32 devices in a mesh: sector: 4 (over z), rows: 8 (over y, x, core).
Axes of the slice: x: 2, y: 2, z: 4, core: 2. Of those that a mesh axis runs over, the one named last changes fastest.
Arguments:
- x_block: bfloat16 [4, 10240, 300], P('sector', 'rows')
- h_diag: bfloat16 [4, 10240, 1280], P('sector', 'rows')
- h_right: bfloat16 [4, 10240, 1280], P('sector', 'rows')
- pattern: int32 [4, 2, 80, 10], P('sector', None, 'rows'), may hold values from 0 to 1, as said below
Outputs:
- q_block: bfloat16 [4, 10240, 300], P('sector', 'rows')
- hproj: float32 [4, 300, 300], P('sector')
- correlation: float32 [4, 300, 300], P('sector')
The draws below stay inside these ranges and needn't reach their ends.
Inputs may be any that keep to these rules, and one draw needn't show every extreme that they name: Within each 1280 x 1280 tile, pattern[s, 0] is symmetric with ones on its diagonal; h_diag's tiles are symmetric.
All inputs are finite; a program needn't handle non-finite values.
Results may differ from the reference program's by a relative error of at most 0.011.
Values may be sent and summed in bfloat16 or wider, within the bound.
No kernel may reach another device: no remote copies, remote signals or barrier semaphores. Data moves between devices by JAX's collectives and lax.ppermute only.
A program may use at most 64 MiB of HBM per device.

```python
import math
import jax
import jax.numpy as jnp
from jax import lax

CHANNELS = 300
SUBBLOCK = 128
BLOCK_ROWS = 1280
NROWS = 10240
SECTORS = 4


def noise_field(key, shape):
    return jax.random.normal(key, shape, jnp.float32)


def draw_x_block(key, part):
    common = noise_field(jax.random.fold_in(key, 11), (1, NROWS, CHANNELS))
    own = noise_field(jax.random.fold_in(key, 12), (SECTORS, NROWS, CHANNELS))
    shared = noise_field(jax.random.fold_in(key, 14), (SECTORS, NROWS, 1))
    values = common + 0.6 * own + 0.5 * shared
    return jnp.clip(values, -6.0, 6.0).astype(jnp.bfloat16)


def coupling_field(key):
    common = noise_field(jax.random.fold_in(key, 21), (1, NROWS, BLOCK_ROWS))
    own = noise_field(jax.random.fold_in(key, 22), (SECTORS, NROWS, BLOCK_ROWS))
    return (common + 0.6 * own) * (0.8 / math.sqrt(BLOCK_ROWS))


def draw_h_diag(key, part):
    count = NROWS // BLOCK_ROWS
    raw = coupling_field(jax.random.fold_in(key, 31)).reshape(SECTORS, count, BLOCK_ROWS, BLOCK_ROWS)
    sym = (raw + jnp.swapaxes(raw, 2, 3)) * (1.0 / math.sqrt(2.0))
    lower, upper = (5.0, 10.0)
    base = jnp.exp(jax.random.uniform(jax.random.fold_in(key, 32), (1, count, BLOCK_ROWS, 1), jnp.float32, math.log(lower), math.log(upper)))
    shift = jax.random.uniform(jax.random.fold_in(key, 33), (SECTORS, count, BLOCK_ROWS, 1), jnp.float32, 0.9, 1.1)
    eye = jnp.eye(BLOCK_ROWS, dtype=jnp.float32)
    tiles = sym + base * shift * eye
    return tiles.reshape(SECTORS, NROWS, BLOCK_ROWS).astype(jnp.bfloat16)


def draw_h_right(key, part):
    return coupling_field(jax.random.fold_in(key, 41)).astype(jnp.bfloat16)


def draw_pattern(key, part):
    count = NROWS // BLOCK_ROWS
    width = BLOCK_ROWS // SUBBLOCK
    bits = jax.random.randint(jax.random.fold_in(key, 51), (SECTORS, 2, count, width, width), 0, 2)
    first = bits[:, 0]
    first = jnp.maximum(first, jnp.swapaxes(first, 2, 3))
    first = jnp.maximum(first, jnp.eye(width, dtype=jnp.int32))
    both = jnp.stack([first, bits[:, 1]], axis=1)
    return both.reshape(SECTORS, 2, count * width, width).astype(jnp.int32)


def setup_inputs(seed: int = 0) -> dict:
    keys = jax.random.split(jax.random.key(seed), 5)
    x_block = draw_x_block(jax.random.fold_in(keys[4], 71), 0)
    h_diag = draw_h_diag(jax.random.fold_in(keys[4], 71), 0)
    h_right = draw_h_right(jax.random.fold_in(keys[4], 71), 0)
    pattern = draw_pattern(jax.random.fold_in(keys[4], 71), 0)
    return dict(x_block=x_block, h_diag=h_diag, h_right=h_right, pattern=pattern)


def expand(blocks):
    return jnp.repeat(jnp.repeat(blocks, SUBBLOCK, axis=-2), SUBBLOCK, axis=-1)

def sector_image(inputs, diag_rows, right_rows, masks):
    count = NROWS // BLOCK_ROWS
    width = BLOCK_ROWS // SUBBLOCK
    starts = inputs.reshape(count, BLOCK_ROWS, CHANNELS).astype(jnp.float32)
    mask_diag = expand(masks[0].reshape(count, width, width)).astype(jnp.bfloat16)
    mask_right = expand(masks[1].reshape(count, width, width)).astype(jnp.bfloat16)
    diag_tile = (diag_rows.reshape(count, BLOCK_ROWS, BLOCK_ROWS) * mask_diag).astype(jnp.float32)
    right_tile = (right_rows.reshape(count, BLOCK_ROWS, BLOCK_ROWS) * mask_right).astype(jnp.float32)
    empty = jnp.zeros((1, BLOCK_ROWS, CHANNELS), jnp.float32)
    later = jnp.concatenate([starts[1:], empty], axis=0)
    first = jnp.einsum('bij,bjk->bik', diag_tile, starts)
    second = jnp.einsum('bij,bjk->bik', right_tile, later)
    carried = jnp.einsum('bji,bjk->bik', right_tile, starts)
    third = jnp.concatenate([empty, carried[:-1]], axis=0)
    image = first + second + third
    return image.reshape(NROWS, CHANNELS).astype(jnp.bfloat16)

def reference(x_block, h_diag, h_right, pattern):
    bases = []
    projected = []
    correlations = []
    eye = jnp.eye(CHANNELS, dtype=jnp.float32)
    for sector_num in range(SECTORS):
        inputs = x_block[sector_num]
        image = sector_image(inputs, h_diag[sector_num], h_right[sector_num], pattern[sector_num])
        gram = jnp.dot(image.T.astype(jnp.float32), image.astype(jnp.float32), preferred_element_type=jnp.float32) / NROWS
        rayleigh = jnp.dot(inputs.T.astype(jnp.float32), image.astype(jnp.float32), preferred_element_type=jnp.float32) / NROWS
        factor = jnp.linalg.cholesky(gram)
        inverse = jax.scipy.linalg.solve_triangular(factor, eye, lower=True)
        basis = jnp.dot(image.astype(jnp.float32), inverse.T, precision=lax.Precision.HIGH).astype(jnp.bfloat16)
        if sector_num == 0:
            correlations.append(jnp.zeros((CHANNELS, CHANNELS), jnp.float32))
        else:
            correlations.append(jnp.dot(bases[-1].T.astype(jnp.float32), basis.astype(jnp.float32), preferred_element_type=jnp.float32) / NROWS)
        bases.append(basis)
        projected.append(rayleigh)
    return (jnp.stack(bases), jnp.stack(projected), jnp.stack(correlations))
```

```python
import functools

import jax
import jax.numpy as jnp
from jax import lax
from jax.experimental import pallas as pl
from jax.experimental.pallas import tpu as pltpu
from jax.sharding import PartitionSpec as P

SUBBLOCK = 128
LANES = 128
PANEL = 16
ROWS_IN = pl.BlockSpec(memory_space=pltpu.VMEM)
SCALARS = pl.BlockSpec(memory_space=pltpu.SMEM)
VMEM_LIMIT = 48 * 1024 * 1024


def params(**more):
    return pltpu.CompilerParams(vmem_limit_bytes=VMEM_LIMIT, **more)


def cost(flops, bytes_accessed):
    return pl.CostEstimate(flops=flops, bytes_accessed=bytes_accessed, transcendentals=0)


def round_up(value, step):
    return (value + step - 1) // step * step


def dot(left, right, dims, precision=None):
    return lax.dot_general(
        left, right, (dims, ((), ())), precision=precision, preferred_element_type=jnp.float32
    )


def masked_strip(tile_ref, mask_ref, which, row0, col0, out_ref):
    rows, cols = tile_ref.shape
    for i in range(rows // SUBBLOCK):
        for j in range(cols // SUBBLOCK):
            here = (slice(i * SUBBLOCK, (i + 1) * SUBBLOCK), slice(j * SUBBLOCK, (j + 1) * SUBBLOCK))
            keep = mask_ref[which, row0 + i, col0 + j]
            out_ref[here] = tile_ref[here] * keep.astype(tile_ref.dtype)


def product_kernel(which, mask_ref, x_ref, tile_ref, out_ref, strip_ref):
    col0 = pl.program_id(0) * (tile_ref.shape[1] // SUBBLOCK)
    masked_strip(tile_ref, mask_ref, which, 0, col0, strip_ref)
    out_ref[...] = dot(x_ref[...], strip_ref[...], ((1,), (0,))).astype(out_ref.dtype)


def tile_product(which, masks, x_t, tile, dtype):
    channels, rows = x_t.shape
    width = 256
    return pl.pallas_call(
        functools.partial(product_kernel, which),
        grid=(rows // width,),
        in_specs=[
            SCALARS,
            pl.BlockSpec((channels, rows), lambda i: (0, 0)),
            pl.BlockSpec((rows, width), lambda i: (0, i)),
        ],
        out_specs=pl.BlockSpec((channels, width), lambda i: (0, i)),
        out_shape=jax.ShapeDtypeStruct((channels, rows), dtype),
        scratch_shapes=[pltpu.VMEM((rows, width), tile.dtype)],
        compiler_params=params(),
        cost_estimate=cost(2 * channels * rows * rows, 2 * rows * rows),
    )(masks, x_t, tile)


def later_kernel(mask_ref, x_ref, tile_ref, first_ref, out_ref, strip_ref):
    row0 = pl.program_id(0) * (tile_ref.shape[0] // SUBBLOCK)
    masked_strip(tile_ref, mask_ref, 1, row0, 0, strip_ref)
    out_ref[...] = first_ref[...] + dot(x_ref[...], strip_ref[...], ((1,), (1,)))


def later_product(masks, x_t, tile, first):
    channels, rows = x_t.shape
    width = 256
    return pl.pallas_call(
        later_kernel,
        grid=(rows // width,),
        in_specs=[
            SCALARS,
            pl.BlockSpec((channels, rows), lambda i: (0, 0)),
            pl.BlockSpec((width, rows), lambda i: (i, 0)),
            pl.BlockSpec((channels, width), lambda i: (0, i)),
        ],
        out_specs=pl.BlockSpec((channels, width), lambda i: (0, i)),
        out_shape=jax.ShapeDtypeStruct((channels, rows), jnp.float32),
        scratch_shapes=[pltpu.VMEM((width, rows), tile.dtype)],
        compiler_params=params(),
        cost_estimate=cost(2 * channels * rows * rows, 2 * rows * rows),
    )(masks, x_t, tile, first)


def store_padded(ref, value):
    ref[...] = jnp.zeros_like(ref)
    ref[0 : value.shape[0], :] = value


def gram_kernel(part_ref, carried_ref, x_ref, y_ref, gram_ref, ray_ref, pad_ref, xpad_ref):
    channels = x_ref.shape[0]
    image = (part_ref[...] + carried_ref[...].astype(jnp.float32)).astype(y_ref.dtype)
    y_ref[...] = image
    store_padded(pad_ref, image)
    store_padded(xpad_ref, x_ref[...])
    tall = gram_ref.shape[1]
    groups = pad_ref.shape[0] // LANES
    offset = 0
    for g in range(groups):
        block = pad_ref[g * LANES : (g + 1) * LANES, :]
        rows = ray_ref.shape[0] // groups
        gram_ref[offset : offset + rows - g * LANES, :] = dot(
            pad_ref[g * LANES : rows, :], block, ((1,), (1,))
        )
        offset += rows - g * LANES
        ray_ref[g * rows : (g + 1) * rows, :] = dot(xpad_ref[0:rows, :], block, ((1,), (1,)))


def packed_rows(channels):
    rows = round_up(channels, PANEL)
    return sum(rows - g * LANES for g in range(round_up(channels, LANES) // LANES))


def gram(part, carried, x_t):
    channels, rows = x_t.shape
    wide = round_up(channels, LANES)
    tall = round_up(channels, PANEL)
    return pl.pallas_call(
        gram_kernel,
        in_specs=[ROWS_IN] * 3,
        out_specs=[ROWS_IN] * 3,
        out_shape=[
            jax.ShapeDtypeStruct((channels, rows), x_t.dtype),
            jax.ShapeDtypeStruct((packed_rows(channels), LANES), jnp.float32),
            jax.ShapeDtypeStruct((tall * wide // LANES, LANES), jnp.float32),
        ],
        scratch_shapes=[pltpu.VMEM((wide, rows), x_t.dtype), pltpu.VMEM((wide, rows), x_t.dtype)],
        compiler_params=params(),
        cost_estimate=cost(4 * channels * channels * rows, 8 * channels * rows),
    )(part, carried, x_t)


def cross_kernel(left_ref, right_ref, out_ref, pad_ref, lpad_ref):
    store_padded(pad_ref, right_ref[...])
    store_padded(lpad_ref, left_ref[...])
    groups = pad_ref.shape[0] // LANES
    rows = out_ref.shape[0] // groups
    for g in range(groups):
        out_ref[g * rows : (g + 1) * rows, :] = dot(
            lpad_ref[0:rows, :], pad_ref[g * LANES : (g + 1) * LANES, :], ((1,), (1,))
        )


def cross(left, right):
    channels, rows = left.shape
    wide = round_up(channels, LANES)
    tall = round_up(channels, PANEL)
    return pl.pallas_call(
        cross_kernel,
        in_specs=[ROWS_IN] * 2,
        out_specs=ROWS_IN,
        out_shape=jax.ShapeDtypeStruct((tall * wide // LANES, LANES), jnp.float32),
        scratch_shapes=[pltpu.VMEM((wide, rows), left.dtype), pltpu.VMEM((wide, rows), left.dtype)],
        compiler_params=params(),
        cost_estimate=cost(2 * channels * channels * rows, 4 * channels * rows),
    )(left, right)


def split3(value):
    high = value.astype(jnp.bfloat16)
    rest = value - high.astype(jnp.float32)
    mid = rest.astype(jnp.bfloat16)
    low = (rest - mid.astype(jnp.float32)).astype(jnp.bfloat16)
    return high, mid, low


def sublane(value, index):
    return jnp.broadcast_to(value[index : index + 1, :], value.shape)


def lane_of(value, index):
    return jnp.take_along_axis(value, jnp.broadcast_to(index, value.shape), axis=1)


def eliminate(columns, panel):
    half = 8
    row = lax.broadcasted_iota(jnp.int32, (half, LANES), 0)
    scales = [jnp.zeros((half, LANES), jnp.float32) for _ in range(2)]
    columns = [list(c) for c in columns]
    panel = [list(p) for p in panel]
    for j in range(PANEL):
        h, r = divmod(j, half)
        pivot = sublane(columns[j][h], r)
        inverse = lax.rsqrt(pivot)
        inverse = inverse * (1.5 - 0.5 * pivot * inverse * inverse)
        square = inverse * inverse
        factor = [None, None]
        factor[h] = jnp.where(row > r, columns[j][h], 0.0) * square
        if h == 0:
            factor[1] = columns[j][1] * square
        for later in range(j + 1, PANEL):
            entry = sublane(columns[j][later // half], later % half)
            for t in range(max(h, later // half), 2):
                columns[later][t] = columns[later][t] - factor[t] * entry
        for group in panel:
            entry = sublane(group[h], r)
            for t in range(h, 2):
                group[t] = group[t] - factor[t] * entry
        scales[h] = jnp.where(row == r, inverse, scales[h])
    return [jnp.concatenate([g[0] * scales[0], g[1] * scales[1]], axis=0) for g in panel]


def factor_kernel(channels, scale, left_ref, right_ref, out_ref, work_ref):
    rows, wide = out_ref.shape
    groups = wide // LANES
    offset = 0
    for g in range(groups):
        top = g * LANES
        size = min(LANES, rows - top)
        column = (left_ref[offset : offset + rows - top, :] + right_ref[offset : offset + rows - top, :]) * scale
        offset += rows - top
        diag = column[0:size, :]
        if top + LANES > channels:
            row = lax.broadcasted_iota(jnp.int32, diag.shape, 0)
            lane = lax.broadcasted_iota(jnp.int32, diag.shape, 1)
            diag = jnp.where((row == lane) & (lane + top >= channels), 1.0, diag)
        work_ref[top : top + size, top : top + LANES] = diag
        for below in range(g + 1, groups):
            start = (below - g) * LANES
            size_b = min(LANES, rows - below * LANES)
            block = column[start : start + size_b, :]
            if size_b < LANES:
                block = jnp.concatenate(
                    [block, jnp.zeros((LANES - size_b, LANES), jnp.float32)], axis=0
                )
            work_ref[top : top + size, below * LANES : (below + 1) * LANES] = block.T
            work_ref[below * LANES : below * LANES + size_b, top : top + LANES] = jnp.zeros(
                (size_b, LANES), jnp.float32
            )

    row = lax.broadcasted_iota(jnp.int32, (PANEL, LANES), 0)
    lane = lax.broadcasted_iota(jnp.int32, (PANEL, LANES), 1)
    for g in range(groups):
        top = g * LANES

        def step(b, carry, g=g, top=top):
            local = b * PANEL
            start = pl.multiple_of(top + local, PANEL)
            parts = [
                work_ref[pl.ds(start, PANEL), q * LANES : (q + 1) * LANES] for q in range(groups)
            ]
            pivots = [parts[g][0:8, :], parts[g][8:16, :]]
            columns = [[lane_of(p, local + j) for p in pivots] for j in range(PANEL)]
            inside = (lane >= local) & (lane < local + PANEL)
            identity = jnp.where(lane - local == row, 1.0, 0.0)
            parts[g] = jnp.where(inside, identity, parts[g])
            done = eliminate(columns, [[p[0:8, :], p[8:16, :]] for p in parts])
            left, right = [], []
            for q in range(groups):
                if q < g:
                    out_ref[pl.ds(start, PANEL), q * LANES : (q + 1) * LANES] = done[q]
                elif q == g:
                    out_ref[pl.ds(start, PANEL), q * LANES : (q + 1) * LANES] = jnp.where(
                        lane < local + PANEL, done[q], 0.0
                    )
                else:
                    out_ref[pl.ds(start, PANEL), q * LANES : (q + 1) * LANES] = jnp.zeros_like(done[q])
                high, mid, low = split3(done[q])
                right.append(jnp.concatenate([high, mid, high, low, mid, high], axis=0))
                if q >= g:
                    if q == g:
                        high, mid, low = split3(jnp.where(lane >= local + PANEL, done[q], 0.0))
                    left.append(jnp.concatenate([high, high, mid, high, mid, low], axis=0))
            for n, q in enumerate(range(g, groups)):
                low_row = q * LANES
                high_row = min(rows, low_row + LANES)
                for c in range(groups):
                    update = dot(left[n], right[c], ((0,), (0,)))[0 : high_row - low_row, :]
                    old = work_ref[low_row:high_row, c * LANES : (c + 1) * LANES]
                    if c == g:
                        lanes = lax.broadcasted_iota(jnp.int32, old.shape, 1)
                        old = jnp.where((lanes >= local) & (lanes < local + PANEL), 0.0, old)
                    work_ref[low_row:high_row, c * LANES : (c + 1) * LANES] = old - update
            return carry

        lax.fori_loop(0, (min(rows, top + LANES) - top) // PANEL, step, 0)


def factor_inverse(left, right, channels, total_rows):
    rows = round_up(channels, PANEL)
    wide = round_up(channels, LANES)
    return pl.pallas_call(
        functools.partial(factor_kernel, channels, 1.0 / total_rows),
        in_specs=[ROWS_IN] * 2,
        out_specs=ROWS_IN,
        out_shape=jax.ShapeDtypeStruct((rows, wide), jnp.float32),
        scratch_shapes=[pltpu.VMEM((rows, wide), jnp.float32)],
        compiler_params=params(),
        cost_estimate=cost(10**9, 10**6),
    )(left, right)


def basis_kernel(inverse_ref, y_ref, q_ref):
    channels = y_ref.shape[0]
    inverse = inverse_ref[0:channels, 0:channels]
    high = inverse.astype(jnp.bfloat16)
    low = (inverse - high.astype(jnp.float32)).astype(jnp.bfloat16)
    image = y_ref[...]
    q_ref[...] = (dot(high, image, ((1,), (0,))) + dot(low, image, ((1,), (0,)))).astype(q_ref.dtype)


def basis(inverse, y_t):
    channels, rows = y_t.shape
    return pl.pallas_call(
        basis_kernel,
        in_specs=[ROWS_IN] * 2,
        out_specs=ROWS_IN,
        out_shape=jax.ShapeDtypeStruct(y_t.shape, y_t.dtype),
        compiler_params=params(),
        cost_estimate=cost(4 * channels * channels * rows, 4 * channels * rows),
    )(inverse, y_t)


def correlation_kernel(scale, previous_ref, inverse_ref, left_ref, right_ref, out_ref):
    rows, wide = inverse_ref.shape
    channels = out_ref.shape[0]
    total = jnp.zeros((rows, rows), jnp.float32)
    groups = wide // LANES
    mixed = jnp.concatenate(
        [left_ref[g * rows : (g + 1) * rows, :] + right_ref[g * rows : (g + 1) * rows, :] for g in range(groups)],
        axis=1,
    )
    half = dot(mixed, inverse_ref[...], ((1,), (1,)), lax.Precision.HIGHEST)
    total = dot(previous_ref[:, 0:rows], half, ((1,), (0,)), lax.Precision.HIGHEST) * scale
    out_ref[...] = total[0:channels, 0:channels]


def correlate(previous, inverse, left, right, channels, total_rows):
    return pl.pallas_call(
        functools.partial(correlation_kernel, 1.0 / total_rows),
        in_specs=[ROWS_IN] * 4,
        out_specs=ROWS_IN,
        out_shape=jax.ShapeDtypeStruct((channels, channels), jnp.float32),
        compiler_params=params(),
        cost_estimate=cost(10**8, 10**6),
    )(previous, inverse, left, right)


def from_behind(value, axis, steps):
    count = lax.axis_size(axis)
    leading, last = (max(0, -steps), min(count, count - steps))
    return lax.ppermute(value, axis, [(source, source + steps) for source in range(leading, last)])


def partner(value, axis, bit):
    count = lax.axis_size(axis)
    return lax.ppermute(value, axis, [(source, source ^ bit) for source in range(count)])


def reduce_pair(value, axis):
    count = lax.axis_size(axis)
    bit = 1
    other = partner(value, axis, bit)
    while 2 * bit < count:
        bit *= 2
        value = value + other
        other = partner(value, axis, bit)
    return value, other


def shards(x_block, h_diag, h_right, pattern):
    x_t = x_block[0].T
    channels, block_rows = x_t.shape
    masks = pattern[0]
    total_rows = lax.axis_size("rows") * block_rows
    later = from_behind(x_t, "rows", -1)
    carried = from_behind(tile_product(1, masks, x_t, h_right[0], jnp.bfloat16), "rows", 1)
    first = tile_product(0, masks, x_t, h_diag[0], jnp.float32)
    part = later_product(masks, later, h_right[0], first)
    y_t, gram_part, ray_part = gram(part, carried, x_t)
    previous_y = from_behind(y_t, "sector", 1)
    gram_left, gram_right = reduce_pair(gram_part, "rows")
    ray_left, ray_right = reduce_pair(ray_part, "rows")
    inverse = factor_inverse(gram_left, gram_right, channels, total_rows)
    previous_inverse = from_behind(inverse, "sector", 1)
    q_t = basis(inverse, y_t)
    cross_left, cross_right = reduce_pair(cross(previous_y, y_t), "rows")
    correlation = correlate(previous_inverse, inverse, cross_left, cross_right, channels, total_rows)
    tall = round_up(channels, PANEL)
    ray = (ray_left + ray_right) * (1.0 / total_rows)
    rayleigh = jnp.concatenate(
        [ray[g * tall : g * tall + channels, :] for g in range(ray.shape[0] // tall)], axis=1
    )[:, 0:channels]
    return (q_t.T[None], rayleigh[None], correlation[None])


def solution(mesh):
    in_specs = (
        P("sector", "rows", None),
        P("sector", "rows", None),
        P("sector", "rows", None),
        P("sector", None, "rows", None),
    )
    out_specs = (P("sector", "rows", None), P("sector", None, None), P("sector", None, None))
    return jax.shard_map(shards, mesh=mesh, in_specs=in_specs, out_specs=out_specs, check_vma=False)
```

```python
import functools

import jax
import jax.numpy as jnp
from jax import lax
from jax.experimental import pallas as pl
from jax.experimental.pallas import tpu as pltpu
from jax.sharding import PartitionSpec as P

SUBBLOCK = 128
LANES = 128
PANEL = 16
WHOLE = pl.BlockSpec(memory_space=pltpu.VMEM)
SCALARS = pl.BlockSpec(memory_space=pltpu.SMEM)
ANYWHERE = pl.BlockSpec(memory_space=pl.ANY)
MIB = 1024 * 1024


def params(mib=48):
    return pltpu.CompilerParams(vmem_limit_bytes=mib * MIB)


def cost(flops, bytes_accessed):
    return pl.CostEstimate(flops=flops, bytes_accessed=bytes_accessed, transcendentals=0)


def round_up(value, step):
    return (value + step - 1) // step * step


def dot(left, right, dims, precision=None):
    return lax.dot_general(
        left, right, (dims, ((), ())), precision=precision, preferred_element_type=jnp.float32
    )


def mask_strip(strip_ref, mask_ref, which, row0, col0, rows, cols):
    for i in range(rows // SUBBLOCK):
        for j in range(cols // SUBBLOCK):
            here = (
                slice(row0 + i * SUBBLOCK, row0 + (i + 1) * SUBBLOCK),
                slice(col0 + j * SUBBLOCK, col0 + (j + 1) * SUBBLOCK),
            )
            keep = mask_ref[row0 // SUBBLOCK + i, which, col0 // SUBBLOCK + j]
            strip_ref[here] = strip_ref[here] * keep.astype(strip_ref.dtype)


def strips(rows):
    width = 2 * SUBBLOCK if rows % (2 * SUBBLOCK) == 0 else SUBBLOCK
    return [(start, width) for start in range(0, rows, width)]


def product_kernel(which, mask_ref, x_hbm, tile_hbm, out_ref, x_ref, tile_ref, x_sem, sems):
    rows = tile_ref.shape[0]
    copy_x = pltpu.make_async_copy(x_hbm, x_ref, x_sem)
    copy_x.start()
    copies = []
    for n, (start, width) in enumerate(strips(rows)):
        here = (slice(None), pl.ds(start, width))
        copies.append(pltpu.make_async_copy(tile_hbm.at[here], tile_ref.at[here], sems.at[n]))
        copies[-1].start()
    copy_x.wait()
    for n, (start, width) in enumerate(strips(rows)):
        copies[n].wait()
        mask_strip(tile_ref, mask_ref, which, 0, start, rows, width)
        out_ref[:, start : start + width] = dot(
            x_ref[...], tile_ref[:, start : start + width], ((1,), (0,))
        ).astype(out_ref.dtype)


def tile_product(which, masks, x_t, tile, dtype):
    channels, rows = x_t.shape
    return pl.pallas_call(
        functools.partial(product_kernel, which),
        in_specs=[SCALARS, ANYWHERE, ANYWHERE],
        out_specs=WHOLE,
        out_shape=jax.ShapeDtypeStruct((channels, rows), dtype),
        scratch_shapes=[
            pltpu.VMEM((channels, rows), x_t.dtype),
            pltpu.VMEM((rows, rows), tile.dtype),
            pltpu.SemaphoreType.DMA,
            pltpu.SemaphoreType.DMA((len(strips(rows)),)),
        ],
        compiler_params=params(60),
        cost_estimate=cost(2 * channels * rows * rows, 2 * rows * rows),
    )(masks, x_t, tile)


def later_kernel(mask_ref, x_ref, tile_hbm, first_ref, out_ref, tile_ref, sems):
    rows = tile_ref.shape[0]
    copies = []
    for n, (start, width) in enumerate(strips(rows)):
        here = (pl.ds(start, width), slice(None))
        copies.append(pltpu.make_async_copy(tile_hbm.at[here], tile_ref.at[here], sems.at[n]))
        copies[-1].start()
    for n, (start, width) in enumerate(strips(rows)):
        copies[n].wait()
        mask_strip(tile_ref, mask_ref, 1, start, 0, width, rows)
        here = (slice(None), slice(start, start + width))
        out_ref[here] = first_ref[here] + dot(
            x_ref[...], tile_ref[start : start + width, :], ((1,), (1,))
        )


def later_product(masks, x_t, tile, first):
    channels, rows = x_t.shape
    return pl.pallas_call(
        later_kernel,
        in_specs=[SCALARS, WHOLE, ANYWHERE, WHOLE],
        out_specs=WHOLE,
        out_shape=jax.ShapeDtypeStruct((channels, rows), jnp.float32),
        scratch_shapes=[
            pltpu.VMEM((rows, rows), tile.dtype),
            pltpu.SemaphoreType.DMA((len(strips(rows)),)),
        ],
        compiler_params=params(),
        cost_estimate=cost(2 * channels * rows * rows, 2 * rows * rows),
    )(masks, x_t, tile, first)


def lower_rows(channels):
    rows = round_up(channels, PANEL)
    return sum(rows - g * LANES for g in range(round_up(channels, LANES) // LANES))


def full_rows(channels):
    rows, wide = round_up(channels, PANEL), round_up(channels, LANES)
    whole = channels // LANES
    rest = rows - whole * LANES
    return round_up(whole * rows + rest * (wide // LANES), 4 * PANEL)


def store_padded(ref, value):
    size, tall = value.shape[0], ref.shape[0]
    start = size // PANEL * PANEL
    ref[start:tall, :] = jnp.zeros((tall - start, ref.shape[1]), ref.dtype)
    ref[0:size, :] = value


def lower_products(pad_ref, rows, out_ref):
    offset = 0
    for g in range(pad_ref.shape[0] // LANES):
        block = pad_ref[g * LANES : (g + 1) * LANES, :]
        out_ref[offset : offset + rows - g * LANES, :] = dot(
            pad_ref[g * LANES : rows, :], block, ((1,), (1,))
        )
        offset += rows - g * LANES


def full_products(left_ref, right_ref, channels, out_ref):
    rows, wide = round_up(channels, PANEL), round_up(channels, LANES)
    whole = channels // LANES
    for g in range(whole):
        out_ref[g * rows : (g + 1) * rows, :] = dot(
            left_ref[0:rows, :], right_ref[g * LANES : (g + 1) * LANES, :], ((1,), (1,))
        )
    rest = rows - whole * LANES
    for g in range(wide // LANES if rest else 0):
        out_ref[whole * rows + g * rest : whole * rows + (g + 1) * rest, :] = dot(
            right_ref[whole * LANES : rows, :],
            left_ref[g * LANES : (g + 1) * LANES, :],
            ((1,), (1,)),
        )
    used = whole * rows + rest * (wide // LANES)
    if used < out_ref.shape[0]:
        out_ref[used:, :] = jnp.zeros((out_ref.shape[0] - used, LANES), out_ref.dtype)


def full_matrix(pack_ref, channels):
    rows, wide = round_up(channels, PANEL), round_up(channels, LANES)
    whole = channels // LANES
    rest = rows - whole * LANES
    parts = [pack_ref[g * rows : (g + 1) * rows, :] for g in range(whole)]
    if rest:
        tail = jnp.concatenate(
            [
                pack_ref[whole * rows + g * rest : whole * rows + (g + 1) * rest, :]
                for g in range(wide // LANES)
            ],
            axis=1,
        )
        tail = jnp.concatenate([tail, jnp.zeros((LANES - rest, wide), tail.dtype)], axis=0)
        parts.append(tail.T[0:rows, :])
    return jnp.concatenate(parts, axis=1)


def cut(pack_ref, core, mine_ref, other_ref):
    half = mine_ref.shape[0]
    mine_ref[...] = pack_ref[pl.ds(pl.multiple_of(core * half, 8), half), :].astype(mine_ref.dtype)
    other_ref[...] = pack_ref[pl.ds(pl.multiple_of((1 - core) * half, 8), half), :].astype(
        other_ref.dtype
    )


def join(pack_ref, core, mine, other):
    half = mine.shape[0]
    pack_ref[pl.ds(pl.multiple_of(core * half, 8), half), :] = mine
    pack_ref[pl.ds(pl.multiple_of((1 - core) * half, 8), half), :] = other


def gram_kernel(
    core_ref, part_ref, carried_ref, x_ref, y_ref, g_mine, g_other, r_mine, r_other,
    pad_ref, xpad_ref, gram_ref, ray_ref,
):
    channels = x_ref.shape[0]
    rows = round_up(channels, PANEL)
    image = (part_ref[...] + carried_ref[...].astype(jnp.float32)).astype(y_ref.dtype)
    y_ref[...] = image
    store_padded(pad_ref, image)
    store_padded(xpad_ref, x_ref[...])
    core = core_ref[0]
    lower_products(pad_ref, rows, gram_ref)
    cut(gram_ref, core, g_mine, g_other)
    full_products(xpad_ref, pad_ref, channels, ray_ref)
    cut(ray_ref, core, r_mine, r_other)


def gram(core, part, carried, x_t):
    channels, rows = x_t.shape
    wide = round_up(channels, LANES)
    lower, full = lower_rows(channels), full_rows(channels)
    return pl.pallas_call(
        gram_kernel,
        in_specs=[SCALARS] + [WHOLE] * 3,
        out_specs=[WHOLE] * 5,
        out_shape=[
            jax.ShapeDtypeStruct((channels, rows), x_t.dtype),
            jax.ShapeDtypeStruct((lower // 2, LANES), jnp.float32),
            jax.ShapeDtypeStruct((lower // 2, LANES), jnp.float32),
            jax.ShapeDtypeStruct((full // 2, LANES), jnp.bfloat16),
            jax.ShapeDtypeStruct((full // 2, LANES), jnp.bfloat16),
        ],
        scratch_shapes=[
            pltpu.VMEM((wide, rows), x_t.dtype),
            pltpu.VMEM((wide, rows), x_t.dtype),
            pltpu.VMEM((lower, LANES), jnp.float32),
            pltpu.VMEM((full, LANES), jnp.float32),
        ],
        compiler_params=params(),
        cost_estimate=cost(4 * channels * channels * rows, 8 * channels * rows),
    )(core, part, carried, x_t)


def cross_kernel(core_ref, left_ref, right_ref, after_ref, m_mine, m_other, lpad_ref, pad_ref, pack_ref):
    store_padded(pad_ref, right_ref[...])
    store_padded(lpad_ref, left_ref[...])
    full_products(lpad_ref, pad_ref, left_ref.shape[0], pack_ref)
    cut(pack_ref, core_ref[0], m_mine, m_other)


def cross(core, left, right, after):
    channels, rows = left.shape
    wide, full = round_up(channels, LANES), full_rows(channels)
    return pl.pallas_call(
        cross_kernel,
        in_specs=[SCALARS, WHOLE, WHOLE, ANYWHERE],
        out_specs=[WHOLE] * 2,
        out_shape=[jax.ShapeDtypeStruct((full // 2, LANES), jnp.float32)] * 2,
        scratch_shapes=[
            pltpu.VMEM((wide, rows), left.dtype),
            pltpu.VMEM((wide, rows), left.dtype),
            pltpu.VMEM((full, LANES), jnp.float32),
        ],
        compiler_params=params(),
        cost_estimate=cost(2 * channels * channels * rows, 4 * channels * rows),
    )(core, left, right, after)


def split3(value):
    high = value.astype(jnp.bfloat16)
    rest = value - high.astype(jnp.float32)
    mid = rest.astype(jnp.bfloat16)
    low = (rest - mid.astype(jnp.float32)).astype(jnp.bfloat16)
    return high, mid, low


def sublane(value, index):
    return jnp.broadcast_to(value[index : index + 1, :], value.shape)


def lane_of(value, index):
    return jnp.take_along_axis(value, jnp.broadcast_to(index, value.shape), axis=1)


def eliminate(columns, panel):
    half = 8
    row = lax.broadcasted_iota(jnp.int32, (half, LANES), 0)
    scales = [jnp.zeros((half, LANES), jnp.float32) for _ in range(2)]
    columns = [list(c) for c in columns]
    panel = [list(p) for p in panel]
    for j in range(PANEL):
        h, r = divmod(j, half)
        pivot = sublane(columns[j][h], r)
        inverse = lax.rsqrt(pivot)
        inverse = inverse * (1.5 - 0.5 * pivot * inverse * inverse)
        square = inverse * inverse
        factor = [None, None]
        factor[h] = jnp.where(row > r, columns[j][h], 0.0) * square
        if h == 0:
            factor[1] = columns[j][1] * square
        for later in range(j + 1, PANEL):
            entry = sublane(columns[j][later // half], later % half)
            for t in range(max(h, later // half), 2):
                columns[later][t] = columns[later][t] - factor[t] * entry
        for group in panel:
            entry = sublane(group[h], r)
            for t in range(h, 2):
                group[t] = group[t] - factor[t] * entry
        scales[h] = jnp.where(row == r, inverse, scales[h])
    return [jnp.concatenate([g[0] * scales[0], g[1] * scales[1]], axis=0) for g in panel]


def fill_work(channels, scale, pack_ref, work_ref):
    rows, wide = work_ref.shape
    groups = wide // LANES
    offset = 0
    for g in range(groups):
        top = g * LANES
        size = min(LANES, rows - top)
        column = pack_ref[offset : offset + rows - top, :] * scale
        offset += rows - top
        diag = column[0:size, :]
        if top + LANES > channels:
            row = lax.broadcasted_iota(jnp.int32, diag.shape, 0)
            lane = lax.broadcasted_iota(jnp.int32, diag.shape, 1)
            diag = jnp.where((row == lane) & (lane + top >= channels), 1.0, diag)
        work_ref[top : top + size, top : top + LANES] = diag
        for below in range(g + 1, groups):
            start = (below - g) * LANES
            size_b = min(LANES, rows - below * LANES)
            block = column[start : start + size_b, :]
            if size_b < LANES:
                block = jnp.concatenate(
                    [block, jnp.zeros((LANES - size_b, LANES), jnp.float32)], axis=0
                )
            work_ref[top : top + size, below * LANES : (below + 1) * LANES] = block.T
            work_ref[below * LANES : below * LANES + size_b, top : top + LANES] = jnp.zeros(
                (size_b, LANES), jnp.float32
            )


def eliminate_group(g, work_ref, out_ref):
    rows, wide = work_ref.shape
    groups = wide // LANES
    row = lax.broadcasted_iota(jnp.int32, (PANEL, LANES), 0)
    lane = lax.broadcasted_iota(jnp.int32, (PANEL, LANES), 1)
    top = g * LANES
    size = min(LANES, rows - top)

    def step(b, carry):
        local = b * PANEL
        start = pl.multiple_of(top + local, PANEL)
        place = pl.ds(pl.multiple_of(local, PANEL), PANEL)
        parts = [work_ref[pl.ds(start, PANEL), q * LANES : (q + 1) * LANES] for q in range(groups)]
        pivots = [parts[g][0:8, :], parts[g][8:16, :]]
        columns = [[lane_of(p, local + j) for p in pivots] for j in range(PANEL)]
        inside = (lane >= local) & (lane < local + PANEL)
        identity = jnp.where(lane - local == row, 1.0, 0.0)
        parts[g] = jnp.where(inside, identity, parts[g])
        done = eliminate(columns, [[p[0:8, :], p[8:16, :]] for p in parts])
        left, right = [], []
        for q in range(groups):
            if q < g:
                out_ref[place, q * LANES : (q + 1) * LANES] = done[q]
            elif q == g:
                out_ref[place, q * LANES : (q + 1) * LANES] = jnp.where(
                    lane < local + PANEL, done[q], 0.0
                )
            high, mid, low = split3(done[q])
            right.append(jnp.concatenate([high, mid, high, low, mid, high], axis=0))
            if q >= g:
                if q == g:
                    high, mid, low = split3(jnp.where(lane >= local + PANEL, done[q], 0.0))
                left.append(jnp.concatenate([high, high, mid, high, mid, low], axis=0))
        for n, q in enumerate(range(g, groups)):
            low_row = q * LANES
            high_row = min(rows, low_row + LANES)
            for c in range(groups):
                update = dot(left[n], right[c], ((0,), (0,)))[0 : high_row - low_row, :]
                old = work_ref[low_row:high_row, c * LANES : (c + 1) * LANES]
                if c == g:
                    lanes = lax.broadcasted_iota(jnp.int32, old.shape, 1)
                    old = jnp.where((lanes >= local) & (lanes < local + PANEL), 0.0, old)
                work_ref[low_row:high_row, c * LANES : (c + 1) * LANES] = old - update
        return carry

    lax.fori_loop(0, size // PANEL, step, 0)


def first_stage_kernel(channels, scale, core_ref, mine_ref, other_ref, work_ref, out_ref, pack_ref):
    join(pack_ref, core_ref[0], mine_ref[...], other_ref[...])
    fill_work(channels, scale, pack_ref, work_ref)
    eliminate_group(0, work_ref, out_ref)


def next_stage_kernel(g, before_ref, after_ref, work_ref, out_ref):
    work_ref[...] = before_ref[...]
    eliminate_group(g, work_ref, out_ref)


def stage_shapes(channels, g):
    rows, wide = round_up(channels, PANEL), round_up(channels, LANES)
    return [
        jax.ShapeDtypeStruct((rows, wide), jnp.float32),
        jax.ShapeDtypeStruct((min(LANES, rows - g * LANES), (g + 1) * LANES), jnp.float32),
    ]


def first_stage(core, mine, other, channels, total_rows):
    return pl.pallas_call(
        functools.partial(first_stage_kernel, channels, 1.0 / total_rows),
        in_specs=[SCALARS] + [WHOLE] * 2,
        out_specs=[WHOLE] * 2,
        out_shape=stage_shapes(channels, 0),
        scratch_shapes=[pltpu.VMEM((lower_rows(channels), LANES), jnp.float32)],
        compiler_params=params(),
        cost_estimate=cost(4 * 10**9, 10**6),
    )(core, mine, other)


def next_stage(g, work, channels, after):
    return pl.pallas_call(
        functools.partial(next_stage_kernel, g),
        in_specs=[WHOLE, ANYWHERE],
        out_specs=[WHOLE] * 2,
        out_shape=stage_shapes(channels, g),
        compiler_params=params(),
        cost_estimate=cost(4 * 10**9, 10**6),
    )(work, after)


def split2(value):
    high = value.astype(jnp.bfloat16)
    return high, (value - high.astype(jnp.float32)).astype(jnp.bfloat16)


def dot3(left, right, dims):
    left_high, left_low = split2(left)
    right_high, right_low = split2(right)
    return (
        dot(left_high, right_high, dims)
        + dot(left_high, right_low, dims)
        + dot(left_low, right_high, dims)
    )


def store_inverse(refs, out_ref):
    rows, wide = out_ref.shape
    for g, ref in enumerate(refs):
        top = g * LANES
        out_ref[top : top + ref.shape[0], 0 : ref.shape[1]] = ref[...]
        if ref.shape[1] < wide:
            out_ref[top : top + ref.shape[0], ref.shape[1] : wide] = jnp.zeros(
                (ref.shape[0], wide - ref.shape[1]), jnp.float32
            )


def basis_kernel(*refs):
    y_ref, q_ref, inverse_ref = refs[-3:]
    channels = y_ref.shape[0]
    store_inverse(refs[:-3], inverse_ref)
    high, low = split2(inverse_ref[0:channels, 0:channels])
    image = y_ref[...]
    q_ref[...] = (dot(high, image, ((1,), (0,))) + dot(low, image, ((1,), (0,)))).astype(q_ref.dtype)


def basis(inverse, y_t):
    channels, rows = y_t.shape
    return pl.pallas_call(
        basis_kernel,
        in_specs=[WHOLE] * (len(inverse) + 1),
        out_specs=WHOLE,
        out_shape=jax.ShapeDtypeStruct(y_t.shape, y_t.dtype),
        scratch_shapes=[
            pltpu.VMEM((round_up(channels, PANEL), round_up(channels, LANES)), jnp.float32)
        ],
        compiler_params=params(),
        cost_estimate=cost(4 * channels * channels * rows, 4 * channels * rows),
    )(*inverse, y_t)


def correlation_kernel(scale, core_ref, mine_ref, other_ref, *refs):
    out_ref, pack_ref, inverse_ref, previous_ref = refs[-4:]
    stages = len(refs[:-4]) // 2
    rows = inverse_ref.shape[0]
    channels = out_ref.shape[0]
    store_inverse(refs[:stages], inverse_ref)
    store_inverse(refs[stages : 2 * stages], previous_ref)
    join(pack_ref, core_ref[0], mine_ref[...], other_ref[...])
    half = dot3(full_matrix(pack_ref, channels), inverse_ref[...], ((1,), (1,)))
    total = dot3(previous_ref[:, 0:rows], half, ((1,), (0,))) * scale
    out_ref[...] = total[0:channels, 0:channels]


def correlate(core, mine, other, inverse, previous, channels, total_rows):
    padded = pltpu.VMEM((round_up(channels, PANEL), round_up(channels, LANES)), jnp.float32)
    return pl.pallas_call(
        functools.partial(correlation_kernel, 1.0 / total_rows),
        in_specs=[SCALARS] + [WHOLE] * (2 + 2 * len(inverse)),
        out_specs=WHOLE,
        out_shape=jax.ShapeDtypeStruct((channels, channels), jnp.float32),
        scratch_shapes=[pltpu.VMEM((full_rows(channels), LANES), jnp.float32), padded, padded],
        compiler_params=params(),
        cost_estimate=cost(10**8, 10**6),
    )(core, mine, other, *inverse, *previous)


def unpack_kernel(scale, core_ref, mine_ref, other_ref, out_ref, pack_ref):
    channels = out_ref.shape[0]
    join(pack_ref, core_ref[0], mine_ref[...], other_ref[...])
    out_ref[...] = full_matrix(pack_ref, channels)[0:channels, 0:channels] * scale


def unpack(core, mine, other, channels, total_rows):
    return pl.pallas_call(
        functools.partial(unpack_kernel, 1.0 / total_rows),
        in_specs=[SCALARS] + [WHOLE] * 2,
        out_specs=WHOLE,
        out_shape=jax.ShapeDtypeStruct((channels, channels), jnp.float32),
        scratch_shapes=[pltpu.VMEM((full_rows(channels), LANES), jnp.float32)],
        compiler_params=params(),
        cost_estimate=cost(10**6, 10**6),
    )(core, mine, other)


def from_behind(value, axis, steps):
    count = lax.axis_size(axis)
    leading, last = (max(0, -steps), min(count, count - steps))
    return lax.ppermute(value, axis, [(source, source + steps) for source in range(leading, last)])


def other_core(value):
    return lax.ppermute(value, "rows", [(s, s ^ 1) for s in range(lax.axis_size("rows"))])


def chip_rounds():
    count = lax.axis_size("rows")
    bits = []
    while 2 << len(bits) < count:
        bits.append(2 << len(bits))
    return [
        [(s, s ^ (bits[n] if s % 2 == 0 else bits[-1 - n])) for s in range(count)]
        for n in range(len(bits))
    ]


def sum_half(mine, other):
    kind = mine.dtype
    value = mine.astype(jnp.float32) + other_core(other).astype(jnp.float32)
    for pairs in chip_rounds():
        sent = value.astype(kind)
        value = sent.astype(jnp.float32) + lax.ppermute(sent, "rows", pairs).astype(jnp.float32)
    return value


def shards(x_block, h_diag, h_right, pattern):
    x_t = x_block[0].T
    channels, block_rows = x_t.shape
    masks = pattern[0].transpose(1, 0, 2)
    total_rows = lax.axis_size("rows") * block_rows
    core = (lax.axis_index("rows") % 2).astype(jnp.int32).reshape(1)
    later = from_behind(x_t, "rows", -1)
    carried = from_behind(tile_product(1, masks, x_t, h_right[0], jnp.bfloat16), "rows", 1)
    first = tile_product(0, masks, x_t, h_diag[0], jnp.float32)
    part = later_product(masks, later, h_right[0], first)
    y_t, g_mine, g_other, r_mine, r_other = gram(core, part, carried, x_t)
    previous_y = from_behind(y_t, "sector", 1)
    g_sum = sum_half(g_mine, g_other)
    r_sum = sum_half(r_mine, r_other)
    work, inverse_0 = first_stage(core, g_sum, other_core(g_sum), channels, total_rows)
    inverse = [inverse_0]
    groups = round_up(channels, LANES) // LANES
    after = inverse_0
    for g in range(1, groups):
        if g == groups - 1:
            m_mine, m_other = cross(core, previous_y, y_t, inverse[-1])
            after = m_mine
        work, rows_g = next_stage(g, work, channels, after)
        inverse.append(rows_g)
    m_sum = sum_half(m_mine, m_other)
    previous = [from_behind(rows_g, "sector", 1) for rows_g in inverse]
    q_t = basis(inverse, y_t)
    rayleigh = unpack(core, r_sum, other_core(r_sum), channels, total_rows)
    correlation = correlate(core, m_sum, other_core(m_sum), inverse, previous, channels, total_rows)
    return (q_t.T[None], rayleigh[None], correlation[None])


def solution(mesh):
    in_specs = (
        P("sector", "rows", None),
        P("sector", "rows", None),
        P("sector", "rows", None),
        P("sector", None, "rows", None),
    )
    out_specs = (P("sector", "rows", None), P("sector", None, None), P("sector", None, None))
    return jax.shard_map(shards, mesh=mesh, in_specs=in_specs, out_specs=out_specs, check_vma=False)
```

```python
import functools

import jax
import jax.numpy as jnp
from jax import lax
from jax.experimental import pallas as pl
from jax.experimental.pallas import tpu as pltpu
from jax.sharding import PartitionSpec as P

SUBBLOCK = 128
LANES = 128
PANEL = 16
WHOLE = pl.BlockSpec(memory_space=pltpu.VMEM)
SCALARS = pl.BlockSpec(memory_space=pltpu.SMEM)
ANYWHERE = pl.BlockSpec(memory_space=pl.ANY)
MIB = 1024 * 1024


def params(mib=48):
    return pltpu.CompilerParams(vmem_limit_bytes=mib * MIB)


def cost(flops, bytes_accessed):
    return pl.CostEstimate(flops=flops, bytes_accessed=bytes_accessed, transcendentals=0)


def round_up(value, step):
    return (value + step - 1) // step * step


def dot(left, right, dims, precision=None):
    return lax.dot_general(
        left, right, (dims, ((), ())), precision=precision, preferred_element_type=jnp.float32
    )


def mask_strip(strip_ref, mask_ref, which, row0, col0, rows, cols):
    for i in range(rows // SUBBLOCK):
        for j in range(cols // SUBBLOCK):
            here = (
                slice(row0 + i * SUBBLOCK, row0 + (i + 1) * SUBBLOCK),
                slice(col0 + j * SUBBLOCK, col0 + (j + 1) * SUBBLOCK),
            )
            keep = mask_ref[row0 // SUBBLOCK + i, which, col0 // SUBBLOCK + j]
            strip_ref[here] = strip_ref[here] * keep.astype(strip_ref.dtype)


def strips(rows):
    width = 2 * SUBBLOCK if rows % (2 * SUBBLOCK) == 0 else SUBBLOCK
    return [(start, width) for start in range(0, rows, width)]


def product_kernel(which, mask_ref, x_hbm, tile_hbm, out_ref, x_ref, tile_ref, sum_ref, x_sem, sems):
    rows = tile_ref.shape[0]
    copy_x = pltpu.make_async_copy(x_hbm, x_ref, x_sem)
    copy_x.start()
    copies = []
    for n, (start, width) in enumerate(strips(rows)):
        here = (pl.ds(start, width), slice(None))
        copies.append(pltpu.make_async_copy(tile_hbm.at[here], tile_ref.at[here], sems.at[n]))
        copies[-1].start()
    copy_x.wait()
    for n, (start, width) in enumerate(strips(rows)):
        copies[n].wait()
        mask_strip(tile_ref, mask_ref, which, start, 0, width, rows)
        term = dot(
            x_ref[:, start : start + width], tile_ref[start : start + width, :], ((1,), (0,))
        )
        if n > 0:
            term = sum_ref[...] + term
        if n + 1 < len(copies):
            sum_ref[...] = term
        else:
            out_ref[...] = term.astype(out_ref.dtype)


def tile_product(which, masks, x_t, tile, dtype, mib):
    channels, rows = x_t.shape
    return pl.pallas_call(
        functools.partial(product_kernel, which),
        in_specs=[SCALARS, ANYWHERE, ANYWHERE],
        out_specs=WHOLE,
        out_shape=jax.ShapeDtypeStruct((channels, rows), dtype),
        scratch_shapes=[
            pltpu.VMEM((channels, rows), x_t.dtype),
            pltpu.VMEM((rows, rows), tile.dtype),
            pltpu.VMEM((channels, rows), jnp.float32),
            pltpu.SemaphoreType.DMA,
            pltpu.SemaphoreType.DMA((len(strips(rows)),)),
        ],
        compiler_params=params(mib),
        cost_estimate=cost(2 * channels * rows * rows, 2 * rows * rows),
    )(masks, x_t, tile)


def later_kernel(mask_ref, x_ref, tile_hbm, first_ref, out_ref, tile_ref, sems):
    rows = tile_ref.shape[0]
    copies = []
    for n, (start, width) in enumerate(strips(rows)):
        here = (pl.ds(start, width), slice(None))
        copies.append(pltpu.make_async_copy(tile_hbm.at[here], tile_ref.at[here], sems.at[n]))
        copies[-1].start()
    for n, (start, width) in enumerate(strips(rows)):
        copies[n].wait()
        mask_strip(tile_ref, mask_ref, 1, start, 0, width, rows)
        here = (slice(None), slice(start, start + width))
        out_ref[here] = first_ref[here] + dot(
            x_ref[...], tile_ref[start : start + width, :], ((1,), (1,))
        )


def later_product(masks, x_t, tile, first):
    channels, rows = x_t.shape
    return pl.pallas_call(
        later_kernel,
        in_specs=[SCALARS, WHOLE, ANYWHERE, WHOLE],
        out_specs=WHOLE,
        out_shape=jax.ShapeDtypeStruct((channels, rows), jnp.float32),
        scratch_shapes=[
            pltpu.VMEM((rows, rows), tile.dtype),
            pltpu.SemaphoreType.DMA((len(strips(rows)),)),
        ],
        compiler_params=params(),
        cost_estimate=cost(2 * channels * rows * rows, 2 * rows * rows),
    )(masks, x_t, tile, first)


def lower_rows(channels):
    rows = round_up(channels, PANEL)
    return sum(rows - g * LANES for g in range(round_up(channels, LANES) // LANES))


def full_rows(channels):
    rows, wide = round_up(channels, PANEL), round_up(channels, LANES)
    whole = channels // LANES
    rest = rows - whole * LANES
    return round_up(whole * rows + rest * (wide // LANES), 4 * PANEL)


def store_padded(ref, value):
    size, tall = value.shape[0], ref.shape[0]
    start = size // PANEL * PANEL
    ref[start:tall, :] = jnp.zeros((tall - start, ref.shape[1]), ref.dtype)
    ref[0:size, :] = value


def lower_products(pad_ref, rows, out_ref):
    offset = 0
    for g in range(pad_ref.shape[0] // LANES):
        block = pad_ref[g * LANES : (g + 1) * LANES, :]
        out_ref[offset : offset + rows - g * LANES, :] = dot(
            pad_ref[g * LANES : rows, :], block, ((1,), (1,))
        )
        offset += rows - g * LANES


def full_products(left_ref, right_ref, channels, out_ref):
    rows, wide = round_up(channels, PANEL), round_up(channels, LANES)
    whole = channels // LANES
    for g in range(whole):
        out_ref[g * rows : (g + 1) * rows, :] = dot(
            left_ref[0:rows, :], right_ref[g * LANES : (g + 1) * LANES, :], ((1,), (1,))
        )
    rest = rows - whole * LANES
    for g in range(wide // LANES if rest else 0):
        out_ref[whole * rows + g * rest : whole * rows + (g + 1) * rest, :] = dot(
            right_ref[whole * LANES : rows, :],
            left_ref[g * LANES : (g + 1) * LANES, :],
            ((1,), (1,)),
        )
    used = whole * rows + rest * (wide // LANES)
    if used < out_ref.shape[0]:
        out_ref[used:, :] = jnp.zeros((out_ref.shape[0] - used, LANES), out_ref.dtype)


def full_matrix(pack_ref, channels):
    rows, wide = round_up(channels, PANEL), round_up(channels, LANES)
    whole = channels // LANES
    rest = rows - whole * LANES
    parts = [pack_ref[g * rows : (g + 1) * rows, :] for g in range(whole)]
    if rest:
        tail = jnp.concatenate(
            [
                pack_ref[whole * rows + g * rest : whole * rows + (g + 1) * rest, :]
                for g in range(wide // LANES)
            ],
            axis=1,
        )
        tail = jnp.concatenate([tail, jnp.zeros((LANES - rest, wide), tail.dtype)], axis=0)
        parts.append(tail.T[0:rows, :])
    return jnp.concatenate(parts, axis=1)


def cut(pack_ref, core, mine_ref, other_ref):
    half = mine_ref.shape[0]
    mine_ref[...] = pack_ref[pl.ds(pl.multiple_of(core * half, 8), half), :].astype(mine_ref.dtype)
    other_ref[...] = pack_ref[pl.ds(pl.multiple_of((1 - core) * half, 8), half), :].astype(
        other_ref.dtype
    )


def join(pack_ref, core, mine, other):
    half = mine.shape[0]
    pack_ref[pl.ds(pl.multiple_of(core * half, 8), half), :] = mine
    pack_ref[pl.ds(pl.multiple_of((1 - core) * half, 8), half), :] = other


def gram_kernel(
    core_ref, part_ref, carried_ref, x_ref, y_ref, g_mine, g_other, r_mine, r_other,
    pad_ref, xpad_ref, gram_ref, ray_ref,
):
    channels = x_ref.shape[0]
    rows = round_up(channels, PANEL)
    image = (part_ref[...] + carried_ref[...].astype(jnp.float32)).astype(y_ref.dtype)
    y_ref[...] = image
    store_padded(pad_ref, image)
    store_padded(xpad_ref, x_ref[...])
    core = core_ref[0]
    lower_products(pad_ref, rows, gram_ref)
    cut(gram_ref, core, g_mine, g_other)
    full_products(xpad_ref, pad_ref, channels, ray_ref)
    cut(ray_ref, core, r_mine, r_other)


def gram(core, part, carried, x_t):
    channels, rows = x_t.shape
    wide = round_up(channels, LANES)
    lower, full = lower_rows(channels), full_rows(channels)
    return pl.pallas_call(
        gram_kernel,
        in_specs=[SCALARS] + [WHOLE] * 3,
        out_specs=[WHOLE] * 5,
        out_shape=[
            jax.ShapeDtypeStruct((channels, rows), x_t.dtype),
            jax.ShapeDtypeStruct((lower // 2, LANES), jnp.float32),
            jax.ShapeDtypeStruct((lower // 2, LANES), jnp.float32),
            jax.ShapeDtypeStruct((full // 2, LANES), jnp.bfloat16),
            jax.ShapeDtypeStruct((full // 2, LANES), jnp.bfloat16),
        ],
        scratch_shapes=[
            pltpu.VMEM((wide, rows), x_t.dtype),
            pltpu.VMEM((wide, rows), x_t.dtype),
            pltpu.VMEM((lower, LANES), jnp.float32),
            pltpu.VMEM((full, LANES), jnp.float32),
        ],
        compiler_params=params(),
        cost_estimate=cost(4 * channels * channels * rows, 8 * channels * rows),
    )(core, part, carried, x_t)


def cross_kernel(core_ref, left_ref, right_ref, after_ref, m_mine, m_other, lpad_ref, pad_ref, pack_ref):
    store_padded(pad_ref, right_ref[...])
    store_padded(lpad_ref, left_ref[...])
    full_products(lpad_ref, pad_ref, left_ref.shape[0], pack_ref)
    cut(pack_ref, core_ref[0], m_mine, m_other)


def cross(core, left, right, after):
    channels, rows = left.shape
    wide, full = round_up(channels, LANES), full_rows(channels)
    return pl.pallas_call(
        cross_kernel,
        in_specs=[SCALARS, WHOLE, WHOLE, ANYWHERE],
        out_specs=[WHOLE] * 2,
        out_shape=[jax.ShapeDtypeStruct((full // 2, LANES), jnp.float32)] * 2,
        scratch_shapes=[
            pltpu.VMEM((wide, rows), left.dtype),
            pltpu.VMEM((wide, rows), left.dtype),
            pltpu.VMEM((full, LANES), jnp.float32),
        ],
        compiler_params=params(),
        cost_estimate=cost(2 * channels * channels * rows, 4 * channels * rows),
    )(core, left, right, after)


def split3(value):
    high = value.astype(jnp.bfloat16)
    rest = value - high.astype(jnp.float32)
    mid = rest.astype(jnp.bfloat16)
    low = (rest - mid.astype(jnp.float32)).astype(jnp.bfloat16)
    return high, mid, low


def sublane(value, index):
    return jnp.broadcast_to(value[index : index + 1, :], value.shape)


def lane_of(value, index):
    return jnp.take_along_axis(value, jnp.broadcast_to(index, value.shape), axis=1)


def eliminate(columns, panel):
    half = 8
    row = lax.broadcasted_iota(jnp.int32, (half, LANES), 0)
    scales = [jnp.zeros((half, LANES), jnp.float32) for _ in range(2)]
    columns = [list(c) for c in columns]
    panel = [list(p) for p in panel]
    for j in range(PANEL):
        h, r = divmod(j, half)
        pivot = sublane(columns[j][h], r)
        inverse = lax.rsqrt(pivot)
        inverse = inverse * (1.5 - 0.5 * pivot * inverse * inverse)
        square = inverse * inverse
        factor = [None, None]
        factor[h] = jnp.where(row > r, columns[j][h], 0.0) * square
        if h == 0:
            factor[1] = columns[j][1] * square
        for later in range(j + 1, PANEL):
            entry = sublane(columns[j][later // half], later % half)
            for t in range(max(h, later // half), 2):
                columns[later][t] = columns[later][t] - factor[t] * entry
        for group in panel:
            entry = sublane(group[h], r)
            for t in range(h, 2):
                group[t] = group[t] - factor[t] * entry
        scales[h] = jnp.where(row == r, inverse, scales[h])
    return [jnp.concatenate([g[0] * scales[0], g[1] * scales[1]], axis=0) for g in panel]


def fill_work(channels, scale, pack_ref, work_ref):
    rows, wide = work_ref.shape
    groups = wide // LANES
    offset = 0
    for g in range(groups):
        top = g * LANES
        size = min(LANES, rows - top)
        column = pack_ref[offset : offset + rows - top, :] * scale
        offset += rows - top
        diag = column[0:size, :]
        if top + LANES > channels:
            row = lax.broadcasted_iota(jnp.int32, diag.shape, 0)
            lane = lax.broadcasted_iota(jnp.int32, diag.shape, 1)
            diag = jnp.where((row == lane) & (lane + top >= channels), 1.0, diag)
        work_ref[top : top + size, top : top + LANES] = diag
        for below in range(g + 1, groups):
            start = (below - g) * LANES
            size_b = min(LANES, rows - below * LANES)
            block = column[start : start + size_b, :]
            if size_b < LANES:
                block = jnp.concatenate(
                    [block, jnp.zeros((LANES - size_b, LANES), jnp.float32)], axis=0
                )
            work_ref[top : top + size, below * LANES : (below + 1) * LANES] = block.T
            work_ref[below * LANES : below * LANES + size_b, top : top + LANES] = jnp.zeros(
                (size_b, LANES), jnp.float32
            )


def eliminate_group(g, work_ref):
    rows, wide = work_ref.shape
    groups = wide // LANES
    row = lax.broadcasted_iota(jnp.int32, (PANEL, LANES), 0)
    lane = lax.broadcasted_iota(jnp.int32, (PANEL, LANES), 1)
    top = g * LANES
    size = min(LANES, rows - top)

    def step(b, carry):
        local = b * PANEL
        start = pl.multiple_of(top + local, PANEL)
        parts = [work_ref[pl.ds(start, PANEL), q * LANES : (q + 1) * LANES] for q in range(groups)]
        pivots = [parts[g][0:8, :], parts[g][8:16, :]]
        columns = [[lane_of(p, local + j) for p in pivots] for j in range(PANEL)]
        inside = (lane >= local) & (lane < local + PANEL)
        identity = jnp.where(lane - local == row, 1.0, 0.0)
        parts[g] = jnp.where(inside, identity, parts[g])
        done = eliminate(columns, [[p[0:8, :], p[8:16, :]] for p in parts])
        left, right = [], []
        for q in range(groups):
            high, mid, low = split3(done[q])
            right.append(jnp.concatenate([high, mid, high, low, mid, high], axis=0))
            if q >= g:
                if q == g:
                    high, mid, low = split3(jnp.where(lane >= local + PANEL, done[q], 0.0))
                left.append(jnp.concatenate([high, high, mid, high, mid, low], axis=0))
        for n, q in enumerate(range(g, groups)):
            low_row = q * LANES
            high_row = min(rows, low_row + LANES)
            for c in range(groups):
                update = dot(left[n], right[c], ((0,), (0,)))[0 : high_row - low_row, :]
                old = work_ref[low_row:high_row, c * LANES : (c + 1) * LANES]
                if c == g:
                    lanes = lax.broadcasted_iota(jnp.int32, old.shape, 1)
                    old = jnp.where((lanes >= local) & (lanes < local + PANEL), 0.0, old)
                work_ref[low_row:high_row, c * LANES : (c + 1) * LANES] = old - update
        for q in range(groups):
            if q == g:
                done[q] = jnp.where(lane < local + PANEL, done[q], 0.0)
            elif q > g:
                done[q] = jnp.zeros_like(done[q])
            work_ref[pl.ds(start, PANEL), q * LANES : (q + 1) * LANES] = done[q]
        return carry

    lax.fori_loop(0, size // PANEL, step, 0)


def first_stage_kernel(channels, scale, core_ref, mine_ref, other_ref, work_ref, pack_ref):
    join(pack_ref, core_ref[0], mine_ref[...], other_ref[...])
    fill_work(channels, scale, pack_ref, work_ref)
    eliminate_group(0, work_ref)


def next_stage_kernel(g, before_ref, after_ref, work_ref, *pack_ref):
    work_ref[...] = before_ref[...]
    eliminate_group(g, work_ref)
    if pack_ref:
        rows, wide = work_ref.shape
        offset = 0
        for q in range(wide // LANES):
            tall = rows - q * LANES
            pack_ref[0][offset : offset + tall, :] = work_ref[q * LANES : rows, q * LANES : (q + 1) * LANES]
            offset += tall


def work_shape(channels):
    return jax.ShapeDtypeStruct((round_up(channels, PANEL), round_up(channels, LANES)), jnp.float32)


def first_stage(core, mine, other, channels, total_rows):
    return pl.pallas_call(
        functools.partial(first_stage_kernel, channels, 1.0 / total_rows),
        in_specs=[SCALARS] + [WHOLE] * 2,
        out_specs=WHOLE,
        out_shape=work_shape(channels),
        scratch_shapes=[pltpu.VMEM((lower_rows(channels), LANES), jnp.float32)],
        compiler_params=params(),
        cost_estimate=cost(10**6, 10**6),
    )(core, mine, other)


def next_stage(g, work, channels, after, last):
    shapes = [work_shape(channels)]
    if last:
        shapes.append(jax.ShapeDtypeStruct((lower_rows(channels), LANES), jnp.float32))
    return pl.pallas_call(
        functools.partial(next_stage_kernel, g),
        in_specs=[WHOLE, ANYWHERE],
        out_specs=[WHOLE] * len(shapes),
        out_shape=shapes,
        compiler_params=params(),
        cost_estimate=cost(10**6, 10**6),
    )(work, after)


def split2(value):
    high = value.astype(jnp.bfloat16)
    return high, (value - high.astype(jnp.float32)).astype(jnp.bfloat16)


def dot3(left, right, dims):
    left_high, left_low = split2(left)
    right_high, right_low = split2(right)
    return (
        dot(left_high, right_high, dims)
        + dot(left_high, right_low, dims)
        + dot(left_low, right_high, dims)
    )


def lower_matrix(pack_ref, out_ref):
    rows, wide = out_ref.shape
    offset = 0
    for g in range(wide // LANES):
        top = g * LANES
        lanes = slice(top, top + LANES)
        if top:
            out_ref[0:top, lanes] = jnp.zeros((top, LANES), jnp.float32)
        out_ref[top:rows, lanes] = pack_ref[offset : offset + rows - top, :]
        offset += rows - top


def basis_kernel(inverse_ref, y_ref, q_ref):
    channels = y_ref.shape[0]
    high, low = split2(inverse_ref[0:channels, 0:channels])
    image = y_ref[...]
    q_ref[...] = (dot(high, image, ((1,), (0,))) + dot(low, image, ((1,), (0,)))).astype(q_ref.dtype)


def basis(inverse, y_t):
    channels, rows = y_t.shape
    return pl.pallas_call(
        basis_kernel,
        in_specs=[WHOLE] * 2,
        out_specs=WHOLE,
        out_shape=jax.ShapeDtypeStruct(y_t.shape, y_t.dtype),
        compiler_params=params(),
        cost_estimate=cost(4 * channels * channels * rows, 4 * channels * rows),
    )(inverse, y_t)


def correlation_kernel(
    scale, core_ref, mine_ref, other_ref, inverse_ref, previous_ref, out_ref, pack_ref, before_ref
):
    rows = inverse_ref.shape[0]
    channels = out_ref.shape[0]
    lower_matrix(previous_ref, before_ref)
    join(pack_ref, core_ref[0], mine_ref[...], other_ref[...])
    half = dot3(full_matrix(pack_ref, channels), inverse_ref[...], ((1,), (1,)))
    total = dot3(before_ref[:, 0:rows], half, ((1,), (0,))) * scale
    out_ref[:, 0, :] = total[0:channels, 0:channels]


def matrix_shape(channels):
    return jax.ShapeDtypeStruct((channels, 1, channels), jnp.float32)


def correlate(core, mine, other, inverse, previous, channels, total_rows):
    return pl.pallas_call(
        functools.partial(correlation_kernel, 1.0 / total_rows),
        in_specs=[SCALARS] + [WHOLE] * 4,
        out_specs=WHOLE,
        out_shape=matrix_shape(channels),
        scratch_shapes=[
            pltpu.VMEM((full_rows(channels), LANES), jnp.float32),
            pltpu.VMEM(inverse.shape, jnp.float32),
        ],
        compiler_params=params(),
        cost_estimate=cost(10**8, 10**6),
    )(core, mine, other, inverse, previous)


def unpack_kernel(scale, core_ref, mine_ref, other_ref, out_ref, pack_ref):
    channels = out_ref.shape[0]
    join(pack_ref, core_ref[0], mine_ref[...], other_ref[...])
    out_ref[:, 0, :] = full_matrix(pack_ref, channels)[0:channels, 0:channels] * scale


def unpack(core, mine, other, channels, total_rows):
    return pl.pallas_call(
        functools.partial(unpack_kernel, 1.0 / total_rows),
        in_specs=[SCALARS] + [WHOLE] * 2,
        out_specs=WHOLE,
        out_shape=matrix_shape(channels),
        scratch_shapes=[pltpu.VMEM((full_rows(channels), LANES), jnp.float32)],
        compiler_params=params(),
        cost_estimate=cost(10**6, 10**6),
    )(core, mine, other)


def from_behind(value, axis, steps):
    count = lax.axis_size(axis)
    leading, last = (max(0, -steps), min(count, count - steps))
    return lax.ppermute(value, axis, [(source, source + steps) for source in range(leading, last)])


def other_core(value):
    return lax.ppermute(value, "rows", [(s, s ^ 1) for s in range(lax.axis_size("rows"))])


def chip_rounds():
    count = lax.axis_size("rows")
    bits = []
    while 2 << len(bits) < count:
        bits.append(2 << len(bits))
    return [
        [(s, s ^ (bits[n] if s % 2 == 0 else bits[-1 - n])) for s in range(count)]
        for n in range(len(bits))
    ]


def sum_half(mine, other):
    kind = mine.dtype
    value = mine.astype(jnp.float32) + other_core(other).astype(jnp.float32)
    for pairs in chip_rounds():
        sent = value.astype(kind)
        value = sent.astype(jnp.float32) + lax.ppermute(sent, "rows", pairs).astype(jnp.float32)
    return value


def shards(x_block, h_diag, h_right, pattern):
    x_t = x_block[0].T
    channels, block_rows = x_t.shape
    masks = pattern[0].transpose(1, 0, 2)
    total_rows = lax.axis_size("rows") * block_rows
    core = (lax.axis_index("rows") % 2).astype(jnp.int32).reshape(1)
    later = from_behind(x_t, "rows", -1)
    carried = from_behind(tile_product(1, masks, x_t, h_right[0], jnp.bfloat16, 58), "rows", 1)
    first = tile_product(0, masks, x_t, h_diag[0], jnp.float32, 48)
    part = later_product(masks, later, h_right[0], first)
    y_t, g_mine, g_other, r_mine, r_other = gram(core, part, carried, x_t)
    previous_y = from_behind(y_t, "sector", 1)
    g_sum = sum_half(g_mine, g_other)
    r_sum = sum_half(r_mine, r_other)
    work = first_stage(core, g_sum, other_core(g_sum), channels, total_rows)
    groups = round_up(channels, LANES) // LANES
    for g in range(1, groups):
        last = g == groups - 1
        if last:
            m_mine, m_other = cross(core, previous_y, y_t, work)
        work, *pack = next_stage(g, work, channels, m_mine if last else core, last)
    inverse = work
    previous = from_behind(pack[0], "sector", 1)
    m_sum = sum_half(m_mine, m_other)
    q_t = basis(inverse, y_t)
    rayleigh = unpack(core, r_sum, other_core(r_sum), channels, total_rows)
    correlation = correlate(core, m_sum, other_core(m_sum), inverse, previous, channels, total_rows)
    return (q_t.T[None], rayleigh.transpose(1, 0, 2), correlation.transpose(1, 0, 2))


def solution(mesh):
    in_specs = (
        P("sector", "rows", None),
        P("sector", "rows", None),
        P("sector", "rows", None),
        P("sector", None, "rows", None),
    )
    out_specs = (P("sector", "rows", None), P("sector", None, None), P("sector", None, None))
    return jax.shard_map(shards, mesh=mesh, in_specs=in_specs, out_specs=out_specs, check_vma=False)
```

```python
import functools

import jax
import jax.numpy as jnp
from jax import lax
from jax.experimental import pallas as pl
from jax.experimental.pallas import tpu as pltpu
from jax.sharding import PartitionSpec as P

SUBBLOCK = 128
LANES = 128
PANEL = 16
WHOLE = pl.BlockSpec(memory_space=pltpu.VMEM)
SCALARS = pl.BlockSpec(memory_space=pltpu.SMEM)
ANYWHERE = pl.BlockSpec(memory_space=pl.ANY)
MIB = 1024 * 1024
FIRST_STAGE_FLOPS = 4 * 10**9


def params(mib=48):
    return pltpu.CompilerParams(vmem_limit_bytes=mib * MIB)


def cost(flops, bytes_accessed):
    return pl.CostEstimate(flops=flops, bytes_accessed=bytes_accessed, transcendentals=0)


def round_up(value, step):
    return (value + step - 1) // step * step


def dot(left, right, dims, precision=None):
    return lax.dot_general(
        left, right, (dims, ((), ())), precision=precision, preferred_element_type=jnp.float32
    )


def block_mask(mask_ref, which, cols):
    blocks = mask_ref[:, which, :].astype(jnp.float32)
    col = lax.broadcasted_iota(jnp.int32, (blocks.shape[1], cols), 1)
    block = lax.broadcasted_iota(jnp.int32, (blocks.shape[1], cols), 0)
    return dot(blocks, jnp.where(col // SUBBLOCK == block, 1.0, 0.0), ((1,), (0,)))


def mask_rows(tile_ref, mask, start, size):
    cols = tile_ref.shape[1]
    for i in range(start // SUBBLOCK, (start + size) // SUBBLOCK):
        keep = jnp.broadcast_to(mask[i : i + 1, :], (PANEL, cols)).astype(tile_ref.dtype)
        for row in range(i * SUBBLOCK, (i + 1) * SUBBLOCK, PANEL):
            tile_ref[row : row + PANEL, :] = tile_ref[row : row + PANEL, :] * keep


def strips(rows, width):
    return [(start, min(width, rows - start)) for start in range(0, rows, width)]


def copies_of(source, target, sems, width):
    copies = []
    for n, (start, size) in enumerate(strips(target.shape[0], width)):
        here = (pl.ds(start, size), slice(None))
        copies.append(pltpu.make_async_copy(source.at[here], target.at[here], sems.at[n]))
    return copies


def product(x_ref, tile_ref, copies, mask, width, sum_ref, out_ref):
    rows = tile_ref.shape[0]
    for n, (start, size) in enumerate(strips(rows, width)):
        copies[n].wait()
        mask_rows(tile_ref, mask, start, size)
        last = n + 1 == len(copies)
        for col, cols in strips(rows, 2 * SUBBLOCK):
            here = (slice(None), slice(col, col + cols))
            term = dot(
                x_ref[:, start : start + size],
                tile_ref[start : start + size, col : col + cols],
                ((1,), (0,)),
            )
            if n > 0:
                term = sum_ref[here] + term
            if last:
                out_ref[here] = term.astype(out_ref.dtype)
            else:
                sum_ref[here] = term


def half_width(rows):
    return rows // 2 if rows // 2 % SUBBLOCK == 0 else rows


def carried_kernel(mask_ref, x_hbm, tile_hbm, out_ref, x_ref, tile_ref, sum_ref, x_sem, sems):
    rows = tile_ref.shape[0]
    width = half_width(rows)
    copies = copies_of(tile_hbm, tile_ref, sems, width)
    copy_x = pltpu.make_async_copy(x_hbm, x_ref, x_sem)
    copy_x.start()
    for copy in copies:
        copy.start()
    mask = block_mask(mask_ref, 1, rows)
    copy_x.wait()
    product(x_ref, tile_ref, copies, mask, width, sum_ref, out_ref)


def carried_product(masks, x_t, tile):
    channels, rows = x_t.shape
    return pl.pallas_call(
        carried_kernel,
        in_specs=[WHOLE, ANYWHERE, ANYWHERE],
        out_specs=WHOLE,
        out_shape=jax.ShapeDtypeStruct((channels, rows), x_t.dtype),
        scratch_shapes=[
            pltpu.VMEM((channels, rows), x_t.dtype),
            pltpu.VMEM((rows, rows), tile.dtype),
            pltpu.VMEM((channels, rows), jnp.float32),
            pltpu.SemaphoreType.DMA,
            pltpu.SemaphoreType.DMA((2,)),
        ],
        compiler_params=params(58),
        cost_estimate=cost(2 * channels * rows * rows, 2 * rows * rows),
    )(masks, x_t, tile)


def image_kernel(
    mask_ref, x_hbm, diag_hbm, later_ref, right_hbm, out_ref,
    x_ref, diag_ref, right_ref, sum_ref, x_sem, diag_sems, right_sems,
):
    rows = diag_ref.shape[0]
    width = half_width(rows)
    diag_copies = copies_of(diag_hbm, diag_ref, diag_sems, width)
    right_copies = copies_of(right_hbm, right_ref, right_sems, width)
    copy_x = pltpu.make_async_copy(x_hbm, x_ref, x_sem)
    copy_x.start()
    for copy in diag_copies + right_copies:
        copy.start()
    diag_mask = block_mask(mask_ref, 0, rows)
    right_mask = block_mask(mask_ref, 1, rows)
    copy_x.wait()
    product(x_ref, diag_ref, diag_copies, diag_mask, width, sum_ref, sum_ref)
    for n, (start, size) in enumerate(strips(rows, width)):
        right_copies[n].wait()
        mask_rows(right_ref, right_mask, start, size)
        for row, count in strips(size, 2 * SUBBLOCK):
            here = (slice(None), slice(start + row, start + row + count))
            out_ref[here] = sum_ref[here] + dot(
                later_ref[...], right_ref[start + row : start + row + count, :], ((1,), (1,))
            )


def image_product(masks, x_t, diag, later, right):
    channels, rows = x_t.shape
    return pl.pallas_call(
        image_kernel,
        in_specs=[WHOLE, ANYWHERE, ANYWHERE, WHOLE, ANYWHERE],
        out_specs=WHOLE,
        out_shape=jax.ShapeDtypeStruct((channels, rows), jnp.float32),
        scratch_shapes=[
            pltpu.VMEM((channels, rows), x_t.dtype),
            pltpu.VMEM((rows, rows), diag.dtype),
            pltpu.VMEM((rows, rows), right.dtype),
            pltpu.VMEM((channels, rows), jnp.float32),
            pltpu.SemaphoreType.DMA,
            pltpu.SemaphoreType.DMA((2,)),
            pltpu.SemaphoreType.DMA((2,)),
        ],
        compiler_params=params(),
        cost_estimate=cost(4 * channels * rows * rows, 4 * rows * rows),
    )(masks, x_t, diag, later, right)


def lower_rows(channels):
    rows = round_up(channels, PANEL)
    return sum(rows - g * LANES for g in range(round_up(channels, LANES) // LANES))


def full_rows(channels):
    rows, wide = round_up(channels, PANEL), round_up(channels, LANES)
    whole = channels // LANES
    rest = rows - whole * LANES
    return round_up(whole * rows + rest * (wide // LANES), 4 * PANEL)


def store_padded(ref, value):
    size, tall = value.shape[0], ref.shape[0]
    start = size // PANEL * PANEL
    ref[start:tall, :] = jnp.zeros((tall - start, ref.shape[1]), ref.dtype)
    ref[0:size, :] = value


def lower_products(pad_ref, rows, out_ref):
    offset = 0
    for g in range(pad_ref.shape[0] // LANES):
        block = pad_ref[g * LANES : (g + 1) * LANES, :]
        out_ref[offset : offset + rows - g * LANES, :] = dot(
            pad_ref[g * LANES : rows, :], block, ((1,), (1,))
        )
        offset += rows - g * LANES


def full_products(left_ref, right_ref, channels, out_ref):
    rows, wide = round_up(channels, PANEL), round_up(channels, LANES)
    whole = channels // LANES
    for g in range(whole):
        out_ref[g * rows : (g + 1) * rows, :] = dot(
            left_ref[0:rows, :], right_ref[g * LANES : (g + 1) * LANES, :], ((1,), (1,))
        )
    rest = rows - whole * LANES
    for g in range(wide // LANES if rest else 0):
        out_ref[whole * rows + g * rest : whole * rows + (g + 1) * rest, :] = dot(
            right_ref[whole * LANES : rows, :],
            left_ref[g * LANES : (g + 1) * LANES, :],
            ((1,), (1,)),
        )
    used = whole * rows + rest * (wide // LANES)
    if used < out_ref.shape[0]:
        out_ref[used:, :] = jnp.zeros((out_ref.shape[0] - used, LANES), out_ref.dtype)


def full_matrix(pack_ref, channels):
    rows, wide = round_up(channels, PANEL), round_up(channels, LANES)
    whole = channels // LANES
    rest = rows - whole * LANES
    parts = [pack_ref[g * rows : (g + 1) * rows, :] for g in range(whole)]
    if rest:
        tail = jnp.concatenate(
            [
                pack_ref[whole * rows + g * rest : whole * rows + (g + 1) * rest, :]
                for g in range(wide // LANES)
            ],
            axis=1,
        )
        tail = jnp.concatenate([tail, jnp.zeros((LANES - rest, wide), tail.dtype)], axis=0)
        parts.append(tail.T[0:rows, :])
    return jnp.concatenate(parts, axis=1)


def cut(pack_ref, core, mine_ref, other_ref):
    half = mine_ref.shape[0]
    mine_ref[...] = pack_ref[pl.ds(pl.multiple_of(core * half, 8), half), :].astype(mine_ref.dtype)
    other_ref[...] = pack_ref[pl.ds(pl.multiple_of((1 - core) * half, 8), half), :].astype(
        other_ref.dtype
    )


def join(pack_ref, core, mine, other):
    half = mine.shape[0]
    pack_ref[pl.ds(pl.multiple_of(core * half, 8), half), :] = mine
    pack_ref[pl.ds(pl.multiple_of((1 - core) * half, 8), half), :] = other


def gram_kernel(core_ref, part_ref, carried_ref, y_ref, g_mine, g_other, pad_ref, gram_ref):
    image = (part_ref[...] + carried_ref[...].astype(jnp.float32)).astype(y_ref.dtype)
    y_ref[...] = image
    store_padded(pad_ref, image)
    lower_products(pad_ref, round_up(image.shape[0], PANEL), gram_ref)
    cut(gram_ref, core_ref[0], g_mine, g_other)


def gram(core, part, carried):
    channels, rows = carried.shape
    lower = lower_rows(channels)
    half = jax.ShapeDtypeStruct((lower // 2, LANES), jnp.float32)
    return pl.pallas_call(
        gram_kernel,
        in_specs=[SCALARS] + [WHOLE] * 2,
        out_specs=[WHOLE] * 3,
        out_shape=[jax.ShapeDtypeStruct((channels, rows), carried.dtype), half, half],
        scratch_shapes=[
            pltpu.VMEM((round_up(channels, LANES), rows), carried.dtype),
            pltpu.VMEM((lower, LANES), jnp.float32),
        ],
        compiler_params=params(),
        cost_estimate=cost(2 * channels * channels * rows, 8 * channels * rows),
    )(core, part, carried)


def cross_kernel(core_ref, left_ref, right_ref, after_ref, m_mine, m_other, lpad_ref, pad_ref, pack_ref):
    store_padded(pad_ref, right_ref[...])
    store_padded(lpad_ref, left_ref[...])
    full_products(lpad_ref, pad_ref, left_ref.shape[0], pack_ref)
    cut(pack_ref, core_ref[0], m_mine, m_other)


def cross(core, left, right, after, dtype):
    channels, rows = left.shape
    wide, full = round_up(channels, LANES), full_rows(channels)
    return pl.pallas_call(
        cross_kernel,
        in_specs=[SCALARS, WHOLE, WHOLE, ANYWHERE],
        out_specs=[WHOLE] * 2,
        out_shape=[jax.ShapeDtypeStruct((full // 2, LANES), dtype)] * 2,
        scratch_shapes=[
            pltpu.VMEM((wide, rows), left.dtype),
            pltpu.VMEM((wide, rows), left.dtype),
            pltpu.VMEM((full, LANES), jnp.float32),
        ],
        compiler_params=params(),
        cost_estimate=cost(2 * channels * channels * rows, 4 * channels * rows),
    )(core, left, right, after)


def ray_kernel(
    core_ref, x_ref, y_any, after_ref, y_out, r_mine, r_other, y_ref, xpad_ref, ypad_ref, pack_ref, sem
):
    copy = pltpu.make_async_copy(y_any, y_ref, sem)
    copy.start()
    store_padded(xpad_ref, x_ref[...])
    copy.wait()
    store_padded(ypad_ref, y_ref[...])
    full_products(xpad_ref, ypad_ref, x_ref.shape[0], pack_ref)
    cut(pack_ref, core_ref[0], r_mine, r_other)


def ray(core, x_t, y_t, after):
    channels, rows = x_t.shape
    wide, full = round_up(channels, LANES), full_rows(channels)
    half = jax.ShapeDtypeStruct((full // 2, LANES), jnp.bfloat16)
    return pl.pallas_call(
        ray_kernel,
        in_specs=[SCALARS, WHOLE, ANYWHERE, ANYWHERE],
        out_specs=[ANYWHERE, WHOLE, WHOLE],
        out_shape=[jax.ShapeDtypeStruct(y_t.shape, y_t.dtype), half, half],
        input_output_aliases={2: 0},
        scratch_shapes=[
            pltpu.VMEM((channels, rows), x_t.dtype),
            pltpu.VMEM((wide, rows), x_t.dtype),
            pltpu.VMEM((wide, rows), x_t.dtype),
            pltpu.VMEM((full, LANES), jnp.float32),
            pltpu.SemaphoreType.DMA,
        ],
        compiler_params=params(),
        cost_estimate=cost(2 * channels * channels * rows, 4 * channels * rows),
    )(core, x_t, y_t, after)


def split3(value):
    high = value.astype(jnp.bfloat16)
    rest = value - high.astype(jnp.float32)
    mid = rest.astype(jnp.bfloat16)
    low = (rest - mid.astype(jnp.float32)).astype(jnp.bfloat16)
    return high, mid, low


def sublane(value, index):
    return jnp.broadcast_to(value[index : index + 1, :], value.shape)


def lane_of(value, index):
    return jnp.take_along_axis(value, jnp.broadcast_to(index, value.shape), axis=1)


def eliminate(columns, panel):
    half = 8
    row = lax.broadcasted_iota(jnp.int32, (half, LANES), 0)
    scales = [jnp.zeros((half, LANES), jnp.float32) for _ in range(2)]
    columns = [list(c) for c in columns]
    panel = [list(p) for p in panel]
    for j in range(PANEL):
        h, r = divmod(j, half)
        pivot = sublane(columns[j][h], r)
        inverse = lax.rsqrt(pivot)
        inverse = inverse * (1.5 - 0.5 * pivot * inverse * inverse)
        square = inverse * inverse
        factor = [None, None]
        factor[h] = jnp.where(row > r, columns[j][h], 0.0) * square
        if h == 0:
            factor[1] = columns[j][1] * square
        for later in range(j + 1, PANEL):
            entry = sublane(columns[j][later // half], later % half)
            for t in range(max(h, later // half), 2):
                columns[later][t] = columns[later][t] - factor[t] * entry
        for group in panel:
            entry = sublane(group[h], r)
            for t in range(h, 2):
                group[t] = group[t] - factor[t] * entry
        scales[h] = jnp.where(row == r, inverse, scales[h])
    return [jnp.concatenate([g[0] * scales[0], g[1] * scales[1]], axis=0) for g in panel]


def fill_work(channels, scale, pack_ref, work_ref):
    rows, wide = work_ref.shape
    groups = wide // LANES
    offset = 0
    for g in range(groups):
        top = g * LANES
        size = min(LANES, rows - top)
        column = pack_ref[offset : offset + rows - top, :] * scale
        offset += rows - top
        diag = column[0:size, :]
        if top + LANES > channels:
            row = lax.broadcasted_iota(jnp.int32, diag.shape, 0)
            lane = lax.broadcasted_iota(jnp.int32, diag.shape, 1)
            diag = jnp.where((row == lane) & (lane + top >= channels), 1.0, diag)
        work_ref[top : top + size, top : top + LANES] = diag
        for below in range(g + 1, groups):
            start = (below - g) * LANES
            size_b = min(LANES, rows - below * LANES)
            block = column[start : start + size_b, :]
            if size_b < LANES:
                block = jnp.concatenate(
                    [block, jnp.zeros((LANES - size_b, LANES), jnp.float32)], axis=0
                )
            work_ref[top : top + size, below * LANES : (below + 1) * LANES] = block.T
            work_ref[below * LANES : below * LANES + size_b, top : top + LANES] = jnp.zeros(
                (size_b, LANES), jnp.float32
            )


def eliminate_group(g, work_ref):
    rows, wide = work_ref.shape
    groups = wide // LANES
    row = lax.broadcasted_iota(jnp.int32, (PANEL, LANES), 0)
    lane = lax.broadcasted_iota(jnp.int32, (PANEL, LANES), 1)
    top = g * LANES
    size = min(LANES, rows - top)

    def step(b, carry):
        local = b * PANEL
        start = pl.multiple_of(top + local, PANEL)
        parts = [work_ref[pl.ds(start, PANEL), q * LANES : (q + 1) * LANES] for q in range(groups)]
        pivots = [parts[g][0:8, :], parts[g][8:16, :]]
        columns = [[lane_of(p, local + j) for p in pivots] for j in range(PANEL)]
        inside = (lane >= local) & (lane < local + PANEL)
        identity = jnp.where(lane - local == row, 1.0, 0.0)
        parts[g] = jnp.where(inside, identity, parts[g])
        done = eliminate(columns, [[p[0:8, :], p[8:16, :]] for p in parts])
        left, right = [], []
        for q in range(groups):
            high, mid, low = split3(done[q])
            right.append(jnp.concatenate([high, mid, high, low, mid, high], axis=0))
            if q >= g:
                if q == g:
                    high, mid, low = split3(jnp.where(lane >= local + PANEL, done[q], 0.0))
                left.append(jnp.concatenate([high, high, mid, high, mid, low], axis=0))
        for n, q in enumerate(range(g, groups)):
            low_row = q * LANES
            high_row = min(rows, low_row + LANES)
            for c in range(groups):
                update = dot(left[n], right[c], ((0,), (0,)))[0 : high_row - low_row, :]
                old = work_ref[low_row:high_row, c * LANES : (c + 1) * LANES]
                if c == g:
                    lanes = lax.broadcasted_iota(jnp.int32, old.shape, 1)
                    old = jnp.where((lanes >= local) & (lanes < local + PANEL), 0.0, old)
                work_ref[low_row:high_row, c * LANES : (c + 1) * LANES] = old - update
        for q in range(groups):
            if q == g:
                done[q] = jnp.where(lane < local + PANEL, done[q], 0.0)
            elif q > g:
                done[q] = jnp.zeros_like(done[q])
            work_ref[pl.ds(start, PANEL), q * LANES : (q + 1) * LANES] = done[q]
        return carry

    lax.fori_loop(0, size // PANEL, step, 0)


def first_stage_kernel(channels, scale, core_ref, mine_ref, other_ref, work_ref, pack_ref):
    join(pack_ref, core_ref[0], mine_ref[...], other_ref[...])
    fill_work(channels, scale, pack_ref, work_ref)
    eliminate_group(0, work_ref)


def next_stage_kernel(g, before_ref, after_ref, work_ref, *pack_ref):
    work_ref[...] = before_ref[...]
    eliminate_group(g, work_ref)
    if pack_ref:
        rows, wide = work_ref.shape
        offset = 0
        for q in range(wide // LANES):
            tall = rows - q * LANES
            pack_ref[0][offset : offset + tall, :] = work_ref[q * LANES : rows, q * LANES : (q + 1) * LANES]
            offset += tall


def work_shape(channels):
    return jax.ShapeDtypeStruct((round_up(channels, PANEL), round_up(channels, LANES)), jnp.float32)


def first_stage(core, mine, other, channels, total_rows):
    return pl.pallas_call(
        functools.partial(first_stage_kernel, channels, 1.0 / total_rows),
        in_specs=[SCALARS] + [WHOLE] * 2,
        out_specs=WHOLE,
        out_shape=work_shape(channels),
        scratch_shapes=[pltpu.VMEM((lower_rows(channels), LANES), jnp.float32)],
        compiler_params=params(),
        cost_estimate=cost(FIRST_STAGE_FLOPS, 10**6),
    )(core, mine, other)


def next_stage(g, work, channels, after, last):
    shapes = [work_shape(channels)]
    if last:
        shapes.append(jax.ShapeDtypeStruct((lower_rows(channels), LANES), jnp.float32))
    blocks = (min(LANES, work.shape[0] - g * LANES)) // PANEL
    return pl.pallas_call(
        functools.partial(next_stage_kernel, g),
        in_specs=[WHOLE, ANYWHERE],
        out_specs=[WHOLE] * len(shapes),
        out_shape=shapes,
        compiler_params=params(),
        cost_estimate=cost(blocks * 6 * 10**8, 10**6),
    )(work, after)


def split2(value):
    high = value.astype(jnp.bfloat16)
    return high, (value - high.astype(jnp.float32)).astype(jnp.bfloat16)


def dot3(left, right, dims):
    left_high, left_low = split2(left)
    right_high, right_low = split2(right)
    return (
        dot(left_high, right_high, dims)
        + dot(left_high, right_low, dims)
        + dot(left_low, right_high, dims)
    )


def lower_matrix(pack_ref, out_ref):
    rows, wide = out_ref.shape
    offset = 0
    for g in range(wide // LANES):
        top = g * LANES
        lanes = slice(top, top + LANES)
        if top:
            out_ref[0:top, lanes] = jnp.zeros((top, LANES), jnp.float32)
        out_ref[top:rows, lanes] = pack_ref[offset : offset + rows - top, :]
        offset += rows - top


def basis_kernel(inverse_ref, y_ref, q_ref):
    channels = y_ref.shape[0]
    image = y_ref[...]
    for start, size in strips(channels, 2 * LANES):
        used = min(channels, start + size)
        high, low = split2(inverse_ref[start : start + size, 0:used])
        both = dot(jnp.concatenate([high, low], axis=0), image[0:used, :], ((1,), (0,)))
        q_ref[start : start + size, :] = (both[0:size, :] + both[size:, :]).astype(q_ref.dtype)


def basis(inverse, y_t):
    channels, rows = y_t.shape
    return pl.pallas_call(
        basis_kernel,
        in_specs=[WHOLE] * 2,
        out_specs=WHOLE,
        out_shape=jax.ShapeDtypeStruct(y_t.shape, y_t.dtype),
        compiler_params=params(),
        cost_estimate=cost(4 * channels * channels * rows, 4 * channels * rows),
    )(inverse, y_t)


def correlation_kernel(
    scale, core_ref, mine_ref, other_ref, inverse_ref, previous_ref, out_ref, pack_ref, before_ref
):
    rows = inverse_ref.shape[0]
    channels = out_ref.shape[0]
    lower_matrix(previous_ref, before_ref)
    join(pack_ref, core_ref[0], mine_ref[...], other_ref[...])
    half = dot3(full_matrix(pack_ref, channels), inverse_ref[...], ((1,), (1,)))
    total = dot3(before_ref[:, 0:rows], half, ((1,), (0,))) * scale
    out_ref[:, 0, :] = total[0:channels, 0:channels]


def matrix_shape(channels):
    return jax.ShapeDtypeStruct((channels, 1, channels), jnp.float32)


def correlate(core, mine, other, inverse, previous, channels, total_rows):
    return pl.pallas_call(
        functools.partial(correlation_kernel, 1.0 / total_rows),
        in_specs=[SCALARS] + [WHOLE] * 4,
        out_specs=WHOLE,
        out_shape=matrix_shape(channels),
        scratch_shapes=[
            pltpu.VMEM((full_rows(channels), LANES), jnp.float32),
            pltpu.VMEM(inverse.shape, jnp.float32),
        ],
        compiler_params=params(),
        cost_estimate=cost(10**8, 10**6),
    )(core, mine, other, inverse, previous)


def unpack_kernel(scale, core_ref, mine_ref, other_ref, out_ref, pack_ref):
    channels = out_ref.shape[0]
    join(pack_ref, core_ref[0], mine_ref[...], other_ref[...])
    out_ref[:, 0, :] = full_matrix(pack_ref, channels)[0:channels, 0:channels] * scale


def unpack(core, mine, other, channels, total_rows):
    return pl.pallas_call(
        functools.partial(unpack_kernel, 1.0 / total_rows),
        in_specs=[SCALARS] + [WHOLE] * 2,
        out_specs=WHOLE,
        out_shape=matrix_shape(channels),
        scratch_shapes=[pltpu.VMEM((full_rows(channels), LANES), jnp.float32)],
        compiler_params=params(),
        cost_estimate=cost(10**6, 10**6),
    )(core, mine, other)


def from_behind(value, axis, steps):
    count = lax.axis_size(axis)
    leading, last = (max(0, -steps), min(count, count - steps))
    return lax.ppermute(value, axis, [(source, source + steps) for source in range(leading, last)])


def other_core(value):
    return lax.ppermute(value, "rows", [(s, s ^ 1) for s in range(lax.axis_size("rows"))])


def chip_rounds():
    count = lax.axis_size("rows")
    bits = []
    while 2 << len(bits) < count:
        bits.append(2 << len(bits))
    return [
        [(s, s ^ (bits[n] if s % 2 == 0 else bits[-1 - n])) for s in range(count)]
        for n in range(len(bits))
    ]


def sum_cores(mine, other):
    return mine.astype(jnp.float32) + other_core(other).astype(jnp.float32)


def sum_chips(value, kind):
    for pairs in chip_rounds():
        sent = value.astype(kind)
        value = sent.astype(jnp.float32) + lax.ppermute(sent, "rows", pairs).astype(jnp.float32)
    return value


def shards(x_block, h_diag, h_right, pattern):
    x_t = x_block[0].T
    channels, block_rows = x_t.shape
    masks = pattern[0].transpose(1, 0, 2)
    total_rows = lax.axis_size("rows") * block_rows
    core = (lax.axis_index("rows") % 2).astype(jnp.int32).reshape(1)
    later = from_behind(x_t, "rows", -1)
    carried = from_behind(carried_product(masks, x_t, h_right[0]), "rows", 1)
    part = image_product(masks, x_t, h_diag[0], later, h_right[0])
    y_t, g_mine, g_other = gram(core, part, carried)
    g_sum = sum_cores(g_mine, g_other)
    y_t, r_mine, r_other = ray(core, x_t, y_t, g_sum)
    previous_y = from_behind(y_t, "sector", 1)
    g_sum = sum_chips(g_sum, jnp.float32)
    r_sum = sum_chips(sum_cores(r_mine, r_other), jnp.bfloat16)
    work = first_stage(core, g_sum, other_core(g_sum), channels, total_rows)
    groups = round_up(channels, LANES) // LANES
    m_mine, m_other = cross(core, previous_y, y_t, work, jnp.float32)
    for g in range(1, groups):
        work, *pack = next_stage(g, work, channels, m_other, g == groups - 1)
    inverse = work
    previous = from_behind(pack[0], "sector", 1)
    m_sum = sum_chips(sum_cores(m_mine, m_other), jnp.float32)
    q_t = basis(inverse, y_t)
    rayleigh = unpack(core, r_sum, other_core(r_sum), channels, total_rows)
    correlation = correlate(core, m_sum, other_core(m_sum), inverse, previous, channels, total_rows)
    return (q_t.T[None], rayleigh.transpose(1, 0, 2), correlation.transpose(1, 0, 2))


def solution(mesh):
    in_specs = (
        P("sector", "rows", None),
        P("sector", "rows", None),
        P("sector", "rows", None),
        P("sector", None, "rows", None),
    )
    out_specs = (P("sector", "rows", None), P("sector", None, None), P("sector", None, None))
    return jax.shard_map(shards, mesh=mesh, in_specs=in_specs, out_specs=out_specs, check_vma=False)
```

```python
import functools

import jax
import jax.numpy as jnp
from jax import lax
from jax.experimental import pallas as pl
from jax.experimental.pallas import tpu as pltpu
from jax.sharding import PartitionSpec as P

SUBBLOCK = 128
LANES = 128
PANEL = 16
WHOLE = pl.BlockSpec(memory_space=pltpu.VMEM)
SCALARS = pl.BlockSpec(memory_space=pltpu.SMEM)
ANYWHERE = pl.BlockSpec(memory_space=pl.ANY)
MIB = 1024 * 1024
FIRST_STAGE_FLOPS = 4*10**9


def params(mib=48):
    return pltpu.CompilerParams(vmem_limit_bytes=mib * MIB)


def cost(flops, bytes_accessed):
    return pl.CostEstimate(flops=flops, bytes_accessed=bytes_accessed, transcendentals=0)


def round_up(value, step):
    return (value + step - 1) // step * step


def dot(left, right, dims, precision=None):
    return lax.dot_general(
        left, right, (dims, ((), ())), precision=precision, preferred_element_type=jnp.float32
    )


def block_mask(mask_ref, which, cols):
    blocks = mask_ref[:, which, :].astype(jnp.float32)
    col = lax.broadcasted_iota(jnp.int32, (blocks.shape[1], cols), 1)
    block = lax.broadcasted_iota(jnp.int32, (blocks.shape[1], cols), 0)
    return dot(blocks, jnp.where(col // SUBBLOCK == block, 1.0, 0.0), ((1,), (0,)))


def mask_rows(tile_ref, mask, start, size):
    cols = tile_ref.shape[1]
    for i in range(start // SUBBLOCK, (start + size) // SUBBLOCK):
        keep = jnp.broadcast_to(mask[i : i + 1, :], (PANEL, cols)).astype(tile_ref.dtype)
        for row in range(i * SUBBLOCK, (i + 1) * SUBBLOCK, PANEL):
            tile_ref[row : row + PANEL, :] = tile_ref[row : row + PANEL, :] * keep


def strips(rows, width):
    return [(start, min(width, rows - start)) for start in range(0, rows, width)]


def copies_of(source, target, sems, width):
    copies = []
    for n, (start, size) in enumerate(strips(target.shape[0], width)):
        here = (pl.ds(start, size), slice(None))
        copies.append(pltpu.make_async_copy(source.at[here], target.at[here], sems.at[n]))
    return copies


def product(x_ref, tile_ref, copies, mask, width, sum_ref, out_ref):
    rows = tile_ref.shape[0]
    for n, (start, size) in enumerate(strips(rows, width)):
        copies[n].wait()
        mask_rows(tile_ref, mask, start, size)
        last = n + 1 == len(copies)
        for col, cols in strips(rows, 2 * SUBBLOCK):
            here = (slice(None), slice(col, col + cols))
            term = dot(
                x_ref[:, start : start + size],
                tile_ref[start : start + size, col : col + cols],
                ((1,), (0,)),
            )
            if n > 0:
                term = sum_ref[here] + term
            if last:
                out_ref[here] = term.astype(out_ref.dtype)
            else:
                sum_ref[here] = term


def half_width(rows):
    return rows // 2 if rows // 2 % SUBBLOCK == 0 else rows


def carried_kernel(mask_ref, x_hbm, tile_hbm, out_ref, x_ref, tile_ref, sum_ref, x_sem, sems):
    rows = tile_ref.shape[0]
    width = half_width(rows)
    copies = copies_of(tile_hbm, tile_ref, sems, width)
    copy_x = pltpu.make_async_copy(x_hbm, x_ref, x_sem)
    copy_x.start()
    for copy in copies:
        copy.start()
    mask = block_mask(mask_ref, 1, rows)
    copy_x.wait()
    product(x_ref, tile_ref, copies, mask, width, sum_ref, out_ref)


def carried_product(masks, x_t, tile):
    channels, rows = x_t.shape
    return pl.pallas_call(
        carried_kernel,
        in_specs=[WHOLE, ANYWHERE, ANYWHERE],
        out_specs=WHOLE,
        out_shape=jax.ShapeDtypeStruct((channels, rows), x_t.dtype),
        scratch_shapes=[
            pltpu.VMEM((channels, rows), x_t.dtype),
            pltpu.VMEM((rows, rows), tile.dtype),
            pltpu.VMEM((channels, rows), jnp.float32),
            pltpu.SemaphoreType.DMA,
            pltpu.SemaphoreType.DMA((2,)),
        ],
        compiler_params=params(58),
        cost_estimate=cost(2 * channels * rows * rows, 2 * rows * rows),
    )(masks, x_t, tile)


def image_kernel(
    mask_ref, x_hbm, diag_hbm, later_ref, right_hbm, out_ref,
    x_ref, diag_ref, right_ref, sum_ref, x_sem, diag_sems, right_sems,
):
    rows = diag_ref.shape[0]
    width = half_width(rows)
    diag_copies = copies_of(diag_hbm, diag_ref, diag_sems, width)
    right_copies = copies_of(right_hbm, right_ref, right_sems, width)
    copy_x = pltpu.make_async_copy(x_hbm, x_ref, x_sem)
    copy_x.start()
    for copy in diag_copies + right_copies:
        copy.start()
    diag_mask = block_mask(mask_ref, 0, rows)
    right_mask = block_mask(mask_ref, 1, rows)
    copy_x.wait()
    product(x_ref, diag_ref, diag_copies, diag_mask, width, sum_ref, sum_ref)
    for n, (start, size) in enumerate(strips(rows, width)):
        right_copies[n].wait()
        mask_rows(right_ref, right_mask, start, size)
        for row, count in strips(size, 2 * SUBBLOCK):
            here = (slice(None), slice(start + row, start + row + count))
            out_ref[here] = sum_ref[here] + dot(
                later_ref[...], right_ref[start + row : start + row + count, :], ((1,), (1,))
            )


def image_product(masks, x_t, diag, later, right):
    channels, rows = x_t.shape
    return pl.pallas_call(
        image_kernel,
        in_specs=[WHOLE, ANYWHERE, ANYWHERE, WHOLE, ANYWHERE],
        out_specs=WHOLE,
        out_shape=jax.ShapeDtypeStruct((channels, rows), jnp.float32),
        scratch_shapes=[
            pltpu.VMEM((channels, rows), x_t.dtype),
            pltpu.VMEM((rows, rows), diag.dtype),
            pltpu.VMEM((rows, rows), right.dtype),
            pltpu.VMEM((channels, rows), jnp.float32),
            pltpu.SemaphoreType.DMA,
            pltpu.SemaphoreType.DMA((2,)),
            pltpu.SemaphoreType.DMA((2,)),
        ],
        compiler_params=params(),
        cost_estimate=cost(4 * channels * rows * rows, 4 * rows * rows),
    )(masks, x_t, diag, later, right)


def lower_rows(channels):
    rows = round_up(channels, PANEL)
    return sum(rows - g * LANES for g in range(round_up(channels, LANES) // LANES))


def full_rows(channels):
    rows, wide = round_up(channels, PANEL), round_up(channels, LANES)
    whole = channels // LANES
    rest = rows - whole * LANES
    return round_up(whole * rows + rest * (wide // LANES), 4 * PANEL)


def store_padded(ref, value):
    size, tall = value.shape[0], ref.shape[0]
    start = size // PANEL * PANEL
    ref[start:tall, :] = jnp.zeros((tall - start, ref.shape[1]), ref.dtype)
    ref[0:size, :] = value


def lower_products(pad_ref, rows, out_ref):
    offset = 0
    for g in range(pad_ref.shape[0] // LANES):
        block = pad_ref[g * LANES : (g + 1) * LANES, :]
        out_ref[offset : offset + rows - g * LANES, :] = dot(
            pad_ref[g * LANES : rows, :], block, ((1,), (1,))
        )
        offset += rows - g * LANES


def full_products(left_ref, right_ref, channels, out_ref):
    rows, wide = round_up(channels, PANEL), round_up(channels, LANES)
    whole = channels // LANES
    for g in range(whole):
        out_ref[g * rows : (g + 1) * rows, :] = dot(
            left_ref[0:rows, :], right_ref[g * LANES : (g + 1) * LANES, :], ((1,), (1,))
        )
    rest = rows - whole * LANES
    for g in range(wide // LANES if rest else 0):
        out_ref[whole * rows + g * rest : whole * rows + (g + 1) * rest, :] = dot(
            right_ref[whole * LANES : rows, :],
            left_ref[g * LANES : (g + 1) * LANES, :],
            ((1,), (1,)),
        )
    used = whole * rows + rest * (wide // LANES)
    if used < out_ref.shape[0]:
        out_ref[used:, :] = jnp.zeros((out_ref.shape[0] - used, LANES), out_ref.dtype)


def full_matrix(pack_ref, channels):
    rows, wide = round_up(channels, PANEL), round_up(channels, LANES)
    whole = channels // LANES
    rest = rows - whole * LANES
    parts = [pack_ref[g * rows : (g + 1) * rows, :] for g in range(whole)]
    if rest:
        tail = jnp.concatenate(
            [
                pack_ref[whole * rows + g * rest : whole * rows + (g + 1) * rest, :]
                for g in range(wide // LANES)
            ],
            axis=1,
        )
        tail = jnp.concatenate([tail, jnp.zeros((LANES - rest, wide), tail.dtype)], axis=0)
        parts.append(tail.T[0:rows, :])
    return jnp.concatenate(parts, axis=1)


def cut(pack_ref, core, mine_ref, other_ref):
    half = mine_ref.shape[0]
    mine_ref[...] = pack_ref[pl.ds(pl.multiple_of(core * half, 8), half), :].astype(mine_ref.dtype)
    other_ref[...] = pack_ref[pl.ds(pl.multiple_of((1 - core) * half, 8), half), :].astype(
        other_ref.dtype
    )


def join(pack_ref, core, mine, other):
    half = mine.shape[0]
    pack_ref[pl.ds(pl.multiple_of(core * half, 8), half), :] = mine
    pack_ref[pl.ds(pl.multiple_of((1 - core) * half, 8), half), :] = other


def gram_kernel(core_ref, part_ref, carried_ref, y_ref, g_mine, g_other, pad_ref, gram_ref):
    image = (part_ref[...] + carried_ref[...].astype(jnp.float32)).astype(y_ref.dtype)
    y_ref[...] = image
    store_padded(pad_ref, image)
    lower_products(pad_ref, round_up(image.shape[0], PANEL), gram_ref)
    cut(gram_ref, core_ref[0], g_mine, g_other)


def gram(core, part, carried):
    channels, rows = carried.shape
    lower = lower_rows(channels)
    half = jax.ShapeDtypeStruct((lower // 2, LANES), jnp.float32)
    return pl.pallas_call(
        gram_kernel,
        in_specs=[SCALARS] + [WHOLE] * 2,
        out_specs=[WHOLE] * 3,
        out_shape=[jax.ShapeDtypeStruct((channels, rows), carried.dtype), half, half],
        scratch_shapes=[
            pltpu.VMEM((round_up(channels, LANES), rows), carried.dtype),
            pltpu.VMEM((lower, LANES), jnp.float32),
        ],
        compiler_params=params(),
        cost_estimate=cost(2 * channels * channels * rows, 8 * channels * rows),
    )(core, part, carried)


def split2(value):
    high = value.astype(jnp.bfloat16)
    return high, (value - high.astype(jnp.float32)).astype(jnp.bfloat16)


def store_payload(ref, mixed, ray):
    half = mixed.shape[0]
    high, low = split2(mixed)
    ref[0:half, :] = high
    ref[half : 2 * half, :] = low
    ref[2 * half : 3 * half, :] = ray.astype(jnp.bfloat16)


def load_payload(ref):
    half = ref.shape[0] // 3
    mixed = ref[0:half, :].astype(jnp.float32) + ref[half : 2 * half, :].astype(jnp.float32)
    return mixed, ref[2 * half : 3 * half, :].astype(jnp.float32)


def payload_shape(channels):
    return jax.ShapeDtypeStruct((3 * full_rows(channels) // 2, LANES), jnp.bfloat16)


def cross_kernel(
    core_ref, before_ref, x_ref, y_ref, after_ref, mine_ref, other_ref,
    left_ref, pad_ref, mixed_ref, ray_ref,
):
    channels = x_ref.shape[0]
    core = core_ref[0]
    half = mixed_ref.shape[0] // 2
    store_padded(pad_ref, y_ref[...])
    store_padded(left_ref, before_ref[...])
    full_products(left_ref, pad_ref, channels, mixed_ref)
    store_padded(left_ref, x_ref[...])
    full_products(left_ref, pad_ref, channels, ray_ref)
    mine = pl.ds(pl.multiple_of(core * half, 8), half)
    other = pl.ds(pl.multiple_of((1 - core) * half, 8), half)
    store_payload(mine_ref, mixed_ref[mine, :], ray_ref[mine, :])
    store_payload(other_ref, mixed_ref[other, :], ray_ref[other, :])


def cross(core, before, x_t, y_t, after):
    channels, rows = x_t.shape
    padded = pltpu.VMEM((round_up(channels, LANES), rows), x_t.dtype)
    pack = pltpu.VMEM((full_rows(channels), LANES), jnp.float32)
    return pl.pallas_call(
        cross_kernel,
        in_specs=[SCALARS, WHOLE, WHOLE, WHOLE, ANYWHERE],
        out_specs=[WHOLE] * 2,
        out_shape=[payload_shape(channels)] * 2,
        scratch_shapes=[padded, padded, pack, pack],
        compiler_params=params(),
        cost_estimate=cost(4 * channels * channels * rows, 6 * channels * rows),
    )(core, before, x_t, y_t, after)


def add_kernel(left_ref, right_ref, *refs):
    left, right = load_payload(left_ref), load_payload(right_ref)
    store_payload(refs[-1], left[0] + right[0], left[1] + right[1])


def last_add_kernel(left_ref, right_ref, mixed_ref, ray_ref):
    left, right = load_payload(left_ref), load_payload(right_ref)
    mixed_ref[...] = left[0] + right[0]
    ray_ref[...] = (left[1] + right[1]).astype(ray_ref.dtype)


def last_add(left, right):
    half = left.shape[0] // 3
    return pl.pallas_call(
        last_add_kernel,
        in_specs=[WHOLE] * 2,
        out_specs=[WHOLE] * 2,
        out_shape=[
            jax.ShapeDtypeStruct((half, LANES), jnp.float32),
            jax.ShapeDtypeStruct((half, LANES), jnp.bfloat16),
        ],
        compiler_params=params(),
        cost_estimate=cost(10**5, 10**5),
    )(left, right)


def add_payloads(left, right, *after):
    return pl.pallas_call(
        add_kernel,
        in_specs=[WHOLE] * 2 + [ANYWHERE] * len(after),
        out_specs=WHOLE,
        out_shape=jax.ShapeDtypeStruct(left.shape, left.dtype),
        compiler_params=params(),
        cost_estimate=cost(10**5, 10**6),
    )(left, right, *after)


def split3(value):
    high = value.astype(jnp.bfloat16)
    rest = value - high.astype(jnp.float32)
    mid = rest.astype(jnp.bfloat16)
    low = (rest - mid.astype(jnp.float32)).astype(jnp.bfloat16)
    return high, mid, low


def sublane(value, index):
    return jnp.broadcast_to(value[index : index + 1, :], value.shape)


def lane_of(value, index):
    return jnp.take_along_axis(value, jnp.broadcast_to(index, value.shape), axis=1)


def eliminate(columns, panel):
    half = 8
    row = lax.broadcasted_iota(jnp.int32, (half, LANES), 0)
    scales = [jnp.zeros((half, LANES), jnp.float32) for _ in range(2)]
    columns = [list(c) for c in columns]
    panel = [list(p) for p in panel]
    for j in range(PANEL):
        h, r = divmod(j, half)
        pivot = sublane(columns[j][h], r)
        inverse = lax.rsqrt(pivot)
        inverse = inverse * (1.5 - 0.5 * pivot * inverse * inverse)
        square = inverse * inverse
        factor = [None, None]
        factor[h] = jnp.where(row > r, columns[j][h], 0.0) * square
        if h == 0:
            factor[1] = columns[j][1] * square
        for later in range(j + 1, PANEL):
            entry = sublane(columns[j][later // half], later % half)
            for t in range(max(h, later // half), 2):
                columns[later][t] = columns[later][t] - factor[t] * entry
        for group in panel:
            entry = sublane(group[h], r)
            for t in range(h, 2):
                group[t] = group[t] - factor[t] * entry
        scales[h] = jnp.where(row == r, inverse, scales[h])
    return [jnp.concatenate([g[0] * scales[0], g[1] * scales[1]], axis=0) for g in panel]


def fill_work(channels, scale, pack_ref, work_ref):
    rows, wide = work_ref.shape
    groups = wide // LANES
    offset = 0
    for g in range(groups):
        top = g * LANES
        size = min(LANES, rows - top)
        column = pack_ref[offset : offset + rows - top, :] * scale
        offset += rows - top
        diag = column[0:size, :]
        if top + LANES > channels:
            row = lax.broadcasted_iota(jnp.int32, diag.shape, 0)
            lane = lax.broadcasted_iota(jnp.int32, diag.shape, 1)
            diag = jnp.where((row == lane) & (lane + top >= channels), 1.0, diag)
        work_ref[top : top + size, top : top + LANES] = diag
        for below in range(g + 1, groups):
            start = (below - g) * LANES
            size_b = min(LANES, rows - below * LANES)
            block = column[start : start + size_b, :]
            if size_b < LANES:
                block = jnp.concatenate(
                    [block, jnp.zeros((LANES - size_b, LANES), jnp.float32)], axis=0
                )
            work_ref[top : top + size, below * LANES : (below + 1) * LANES] = block.T
            work_ref[below * LANES : below * LANES + size_b, top : top + LANES] = jnp.zeros(
                (size_b, LANES), jnp.float32
            )


def eliminate_group(g, work_ref):
    rows, wide = work_ref.shape
    groups = wide // LANES
    row = lax.broadcasted_iota(jnp.int32, (PANEL, LANES), 0)
    lane = lax.broadcasted_iota(jnp.int32, (PANEL, LANES), 1)
    top = g * LANES
    size = min(LANES, rows - top)

    def step(b, carry):
        local = b * PANEL
        start = pl.multiple_of(top + local, PANEL)
        parts = [work_ref[pl.ds(start, PANEL), q * LANES : (q + 1) * LANES] for q in range(groups)]
        pivots = [parts[g][0:8, :], parts[g][8:16, :]]
        columns = [[lane_of(p, local + j) for p in pivots] for j in range(PANEL)]
        inside = (lane >= local) & (lane < local + PANEL)
        identity = jnp.where(lane - local == row, 1.0, 0.0)
        parts[g] = jnp.where(inside, identity, parts[g])
        done = eliminate(columns, [[p[0:8, :], p[8:16, :]] for p in parts])
        left, right = [], []
        for q in range(groups):
            high, mid, low = split3(done[q])
            right.append(jnp.concatenate([high, mid, high, low, mid, high], axis=0))
            if q >= g:
                if q == g:
                    high, mid, low = split3(jnp.where(lane >= local + PANEL, done[q], 0.0))
                left.append(jnp.concatenate([high, high, mid, high, mid, low], axis=0))
        for n, q in enumerate(range(g, groups)):
            low_row = q * LANES
            high_row = min(rows, low_row + LANES)
            for c in range(groups):
                update = dot(left[n], right[c], ((0,), (0,)))[0 : high_row - low_row, :]
                old = work_ref[low_row:high_row, c * LANES : (c + 1) * LANES]
                if c == g:
                    lanes = lax.broadcasted_iota(jnp.int32, old.shape, 1)
                    old = jnp.where((lanes >= local) & (lanes < local + PANEL), 0.0, old)
                work_ref[low_row:high_row, c * LANES : (c + 1) * LANES] = old - update
        for q in range(groups):
            if q == g:
                done[q] = jnp.where(lane < local + PANEL, done[q], 0.0)
            elif q > g:
                done[q] = jnp.zeros_like(done[q])
            work_ref[pl.ds(start, PANEL), q * LANES : (q + 1) * LANES] = done[q]
        return carry

    lax.fori_loop(0, size // PANEL, step, 0)


def first_stage_kernel(channels, scale, core_ref, mine_ref, other_ref, work_ref, pack_ref):
    join(pack_ref, core_ref[0], mine_ref[...], other_ref[...])
    fill_work(channels, scale, pack_ref, work_ref)
    eliminate_group(0, work_ref)


def next_stage_kernel(g, before_ref, after_ref, work_ref, *pack_ref):
    work_ref[...] = before_ref[...]
    eliminate_group(g, work_ref)
    if pack_ref:
        rows, wide = work_ref.shape
        offset = 0
        for q in range(wide // LANES):
            tall = rows - q * LANES
            pack_ref[0][offset : offset + tall, :] = work_ref[q * LANES : rows, q * LANES : (q + 1) * LANES]
            offset += tall


def work_shape(channels):
    return jax.ShapeDtypeStruct((round_up(channels, PANEL), round_up(channels, LANES)), jnp.float32)


def first_stage(core, mine, other, channels, total_rows):
    return pl.pallas_call(
        functools.partial(first_stage_kernel, channels, 1.0 / total_rows),
        in_specs=[SCALARS] + [WHOLE] * 2,
        out_specs=WHOLE,
        out_shape=work_shape(channels),
        scratch_shapes=[pltpu.VMEM((lower_rows(channels), LANES), jnp.float32)],
        compiler_params=params(),
        cost_estimate=cost(FIRST_STAGE_FLOPS, 10**6),
    )(core, mine, other)


def next_stage(g, work, channels, after, last):
    shapes = [work_shape(channels)]
    if last:
        shapes.append(jax.ShapeDtypeStruct((lower_rows(channels), LANES), jnp.float32))
    blocks = (min(LANES, work.shape[0] - g * LANES)) // PANEL
    return pl.pallas_call(
        functools.partial(next_stage_kernel, g),
        in_specs=[WHOLE, ANYWHERE],
        out_specs=[WHOLE] * len(shapes),
        out_shape=shapes,
        compiler_params=params(),
        cost_estimate=cost(blocks * 10**8, 10**5),
    )(work, after)


def dot3(left, right, dims):
    left_high, left_low = split2(left)
    right_high, right_low = split2(right)
    return (
        dot(left_high, right_high, dims)
        + dot(left_high, right_low, dims)
        + dot(left_low, right_high, dims)
    )


def lower_matrix(pack_ref, out_ref):
    rows, wide = out_ref.shape
    offset = 0
    for g in range(wide // LANES):
        top = g * LANES
        lanes = slice(top, top + LANES)
        if top:
            out_ref[0:top, lanes] = jnp.zeros((top, LANES), jnp.float32)
        out_ref[top:rows, lanes] = pack_ref[offset : offset + rows - top, :]
        offset += rows - top


def basis_kernel(inverse_ref, y_ref, q_ref):
    channels = y_ref.shape[0]
    image = y_ref[...]
    for start, size in strips(channels, 2 * LANES):
        used = min(channels, start + size)
        high, low = split2(inverse_ref[start : start + size, 0:used])
        both = dot(jnp.concatenate([high, low], axis=0), image[0:used, :], ((1,), (0,)))
        q_ref[start : start + size, :] = (both[0:size, :] + both[size:, :]).astype(q_ref.dtype)


def basis(inverse, y_t):
    channels, rows = y_t.shape
    return pl.pallas_call(
        basis_kernel,
        in_specs=[WHOLE] * 2,
        out_specs=WHOLE,
        out_shape=jax.ShapeDtypeStruct(y_t.shape, y_t.dtype),
        compiler_params=params(),
        cost_estimate=cost(10**5, 10**5),
    )(inverse, y_t)


def matrix_shape(channels):
    return jax.ShapeDtypeStruct((channels, 1, channels), jnp.float32)


def ray_kernel(scale, core_ref, mine_ref, other_ref, out_ref, pack_ref):
    channels = out_ref.shape[0]
    join(pack_ref, core_ref[0], mine_ref[...].astype(jnp.float32), other_ref[...].astype(jnp.float32))
    out_ref[:, 0, :] = full_matrix(pack_ref, channels)[0:channels, 0:channels] * scale


def unpack_ray(core, mine, other, channels, total_rows):
    return pl.pallas_call(
        functools.partial(ray_kernel, 1.0 / total_rows),
        in_specs=[SCALARS] + [WHOLE] * 2,
        out_specs=WHOLE,
        out_shape=matrix_shape(channels),
        scratch_shapes=[pltpu.VMEM((full_rows(channels), LANES), jnp.float32)],
        compiler_params=params(),
        cost_estimate=cost(10**5, 10**5),
    )(core, mine, other)


def half_kernel(core_ref, mine_ref, other_ref, inverse_ref, out_ref, pack_ref):
    join(pack_ref, core_ref[0], mine_ref[...], other_ref[...])
    mixed = full_matrix(pack_ref, inverse_ref.shape[0])
    out_ref[...] = dot3(mixed, inverse_ref[...], ((1,), (1,)))


def half_product(core, mine, other, inverse):
    rows = inverse.shape[0]
    return pl.pallas_call(
        half_kernel,
        in_specs=[SCALARS] + [WHOLE] * 3,
        out_specs=WHOLE,
        out_shape=jax.ShapeDtypeStruct((rows, rows), jnp.float32),
        scratch_shapes=[pltpu.VMEM((2 * mine.shape[0], LANES), jnp.float32)],
        compiler_params=params(),
        cost_estimate=cost(10**5, 10**5),
    )(core, mine, other, inverse)


def correlation_kernel(scale, previous_ref, half_ref, out_ref, before_ref):
    channels = out_ref.shape[0]
    rows = half_ref.shape[0]
    lower_matrix(previous_ref, before_ref)
    total = dot3(before_ref[:, 0:rows], half_ref[...], ((1,), (0,))) * scale
    out_ref[:, 0, :] = total[0:channels, 0:channels]


def correlate(previous, half, channels, total_rows):
    return pl.pallas_call(
        functools.partial(correlation_kernel, 1.0 / total_rows),
        in_specs=[WHOLE] * 2,
        out_specs=WHOLE,
        out_shape=matrix_shape(channels),
        scratch_shapes=[
            pltpu.VMEM((half.shape[0], round_up(channels, LANES)), jnp.float32),
        ],
        compiler_params=params(),
        cost_estimate=cost(10**8, 10**6),
    )(previous, half)


def from_behind(value, axis, steps):
    count = lax.axis_size(axis)
    leading, last = (max(0, -steps), min(count, count - steps))
    return lax.ppermute(value, axis, [(source, source + steps) for source in range(leading, last)])


def other_core(value):
    return lax.ppermute(value, "rows", [(s, s ^ 1) for s in range(lax.axis_size("rows"))])


def chip_rounds():
    count = lax.axis_size("rows")
    bits = []
    while 2 << len(bits) < count:
        bits.append(2 << len(bits))
    return [
        [(s, s ^ (bits[n] if s % 2 == 0 else bits[-1 - n])) for s in range(count)]
        for n in range(len(bits))
    ]


def shards(x_block, h_diag, h_right, pattern):
    x_t = x_block[0].T
    channels, block_rows = x_t.shape
    masks = pattern[0].transpose(1, 0, 2)
    total_rows = lax.axis_size("rows") * block_rows
    core = (lax.axis_index("rows") % 2).astype(jnp.int32).reshape(1)
    later = from_behind(x_t, "rows", -1)
    carried = from_behind(carried_product(masks, x_t, h_right[0]), "rows", 1)
    part = image_product(masks, x_t, h_diag[0], later, h_right[0])
    y_t, g_mine, g_other = gram(core, part, carried)
    previous_y = from_behind(y_t, "sector", 1)
    g_sum = g_mine + other_core(g_other)
    for pairs in chip_rounds():
        g_sum = g_sum + lax.ppermute(g_sum, "rows", pairs)
    work = first_stage(core, g_sum, other_core(g_sum), channels, total_rows)
    groups = round_up(channels, LANES) // LANES
    for g in range(1, groups - 1):
        work = next_stage(g, work, channels, core, False)[0]
    m_mine, m_other = cross(core, previous_y, x_t, y_t, work)
    m_sum = add_payloads(m_mine, other_core(m_other))
    work, pack = next_stage(groups - 1, work, channels, m_other, True)
    previous = from_behind(pack, "sector", 1)
    q_t = basis(work, y_t)
    rounds = chip_rounds()
    for pairs in rounds[:-1]:
        m_sum = add_payloads(m_sum, lax.ppermute(m_sum, "rows", pairs), work)
    m_half, r_half = last_add(m_sum, lax.ppermute(m_sum, "rows", rounds[-1]))
    half = half_product(core, m_half, other_core(m_half), work)
    correlation = correlate(previous, half, channels, total_rows)
    rayleigh = unpack_ray(core, r_half, other_core(r_half), channels, total_rows)
    return (q_t.T[None], rayleigh.transpose(1, 0, 2), correlation.transpose(1, 0, 2))


def solution(mesh):
    in_specs = (
        P("sector", "rows", None),
        P("sector", "rows", None),
        P("sector", "rows", None),
        P("sector", None, "rows", None),
    )
    out_specs = (P("sector", "rows", None), P("sector", None, None), P("sector", None, None))
    return jax.shard_map(shards, mesh=mesh, in_specs=in_specs, out_specs=out_specs, check_vma=False)
```

```python
import functools

import jax
import jax.numpy as jnp
from jax import lax
from jax.experimental import pallas as pl
from jax.experimental.pallas import tpu as pltpu
from jax.sharding import PartitionSpec as P

SUBBLOCK = 128
LANES = 128
PANEL = 16
WHOLE = pl.BlockSpec(memory_space=pltpu.VMEM)
SCALARS = pl.BlockSpec(memory_space=pltpu.SMEM)
ANYWHERE = pl.BlockSpec(memory_space=pl.ANY)
MIB = 1024 * 1024
FIRST_STAGE_FLOPS = 2 * 10**9
LAST_STAGES_FLOPS = 4 * 10**9


def params(mib=48):
    return pltpu.CompilerParams(vmem_limit_bytes=mib * MIB)


def cost(flops, bytes_accessed):
    return pl.CostEstimate(flops=flops, bytes_accessed=bytes_accessed, transcendentals=0)


def round_up(value, step):
    return (value + step - 1) // step * step


def dot(left, right, dims, precision=None):
    return lax.dot_general(
        left, right, (dims, ((), ())), precision=precision, preferred_element_type=jnp.float32
    )


def block_mask(mask_ref, which, cols):
    blocks = mask_ref[:, which, :].astype(jnp.float32)
    col = lax.broadcasted_iota(jnp.int32, (blocks.shape[1], cols), 1)
    block = lax.broadcasted_iota(jnp.int32, (blocks.shape[1], cols), 0)
    return dot(blocks, jnp.where(col // SUBBLOCK == block, 1.0, 0.0), ((1,), (0,)))


def mask_rows(tile_ref, mask, start, size):
    cols = tile_ref.shape[1]
    for i in range(start // SUBBLOCK, (start + size) // SUBBLOCK):
        keep = jnp.broadcast_to(mask[i : i + 1, :], (PANEL, cols)).astype(tile_ref.dtype)
        for row in range(i * SUBBLOCK, (i + 1) * SUBBLOCK, PANEL):
            tile_ref[row : row + PANEL, :] = tile_ref[row : row + PANEL, :] * keep


def strips(rows, width):
    return [(start, min(width, rows - start)) for start in range(0, rows, width)]


def halves(rows):
    first = rows // 512 * 256
    return [(0, first), (first, rows - first)] if first else [(0, rows)]


def copies_of(source, target, sems):
    copies = []
    for n, (start, size) in enumerate(halves(target.shape[0])):
        here = (pl.ds(start, size), slice(None))
        copies.append(pltpu.make_async_copy(source.at[here], target.at[here], sems.at[n]))
    return copies


def product(x_ref, tile_ref, copies, mask, sum_ref, out_ref):
    rows = tile_ref.shape[0]
    for n, (start, size) in enumerate(halves(rows)):
        copies[n].wait()
        mask_rows(tile_ref, mask, start, size)
        last = n + 1 == len(copies)
        for col, cols in strips(rows, 2 * SUBBLOCK):
            here = (slice(None), slice(col, col + cols))
            term = dot(
                x_ref[:, start : start + size],
                tile_ref[start : start + size, col : col + cols],
                ((1,), (0,)),
            )
            if n > 0:
                term = sum_ref[here] + term
            if last:
                out_ref[here] = term.astype(out_ref.dtype)
            else:
                sum_ref[here] = term


def tile_kernel(which, mask_ref, x_hbm, tile_hbm, out_ref, x_ref, tile_ref, sum_ref, x_sem, sems):
    rows = tile_ref.shape[0]
    copies = copies_of(tile_hbm, tile_ref, sems)
    copy_x = pltpu.make_async_copy(x_hbm, x_ref, x_sem)
    copy_x.start()
    for copy in copies:
        copy.start()
    mask = block_mask(mask_ref, which, rows)
    copy_x.wait()
    product(x_ref, tile_ref, copies, mask, sum_ref, out_ref)


def tile_product(which, masks, x_t, tile, dtype, mib):
    channels, rows = x_t.shape
    return pl.pallas_call(
        functools.partial(tile_kernel, which),
        in_specs=[WHOLE, ANYWHERE, ANYWHERE],
        out_specs=WHOLE,
        out_shape=jax.ShapeDtypeStruct((channels, rows), dtype),
        scratch_shapes=[
            pltpu.VMEM((channels, rows), x_t.dtype),
            pltpu.VMEM((rows, rows), tile.dtype),
            pltpu.VMEM((channels, rows), jnp.float32),
            pltpu.SemaphoreType.DMA,
            pltpu.SemaphoreType.DMA((2,)),
        ],
        compiler_params=params(mib),
        cost_estimate=cost(2 * channels * rows * rows, 2 * rows * rows),
    )(masks, x_t, tile)


def later_kernel(mask_ref, later_ref, tile_hbm, first_ref, out_ref, tile_ref, sems):
    rows = tile_ref.shape[0]
    copies = copies_of(tile_hbm, tile_ref, sems)
    for copy in copies:
        copy.start()
    mask = block_mask(mask_ref, 1, rows)
    for n, (start, size) in enumerate(halves(rows)):
        copies[n].wait()
        mask_rows(tile_ref, mask, start, size)
        for row, count in strips(size, 2 * SUBBLOCK):
            here = (slice(None), slice(start + row, start + row + count))
            out_ref[here] = first_ref[here] + dot(
                later_ref[...], tile_ref[start + row : start + row + count, :], ((1,), (1,))
            )


def later_product(masks, later, tile, first):
    channels, rows = later.shape
    return pl.pallas_call(
        later_kernel,
        in_specs=[WHOLE, WHOLE, ANYWHERE, WHOLE],
        out_specs=WHOLE,
        out_shape=jax.ShapeDtypeStruct((channels, rows), jnp.float32),
        scratch_shapes=[
            pltpu.VMEM((rows, rows), tile.dtype),
            pltpu.SemaphoreType.DMA((2,)),
        ],
        compiler_params=params(),
        cost_estimate=cost(2 * channels * rows * rows, 2 * rows * rows),
    )(masks, later, tile, first)


def lower_rows(channels):
    rows = round_up(channels, PANEL)
    return sum(rows - g * LANES for g in range(round_up(channels, LANES) // LANES))


def full_rows(channels):
    rows, wide = round_up(channels, PANEL), round_up(channels, LANES)
    whole = channels // LANES
    rest = rows - whole * LANES
    return round_up(whole * rows + rest * (wide // LANES), 4 * PANEL)


def store_padded(ref, value):
    size, tall = value.shape[0], ref.shape[0]
    start = size // PANEL * PANEL
    ref[start:tall, :] = jnp.zeros((tall - start, ref.shape[1]), ref.dtype)
    ref[0:size, :] = value


def lower_products(pad_ref, rows, out_ref):
    offset = 0
    for g in range(pad_ref.shape[0] // LANES):
        block = pad_ref[g * LANES : (g + 1) * LANES, :]
        out_ref[offset : offset + rows - g * LANES, :] = dot(
            pad_ref[g * LANES : rows, :], block, ((1,), (1,))
        )
        offset += rows - g * LANES


def full_products(left_ref, right_ref, channels, out_ref):
    rows, wide = round_up(channels, PANEL), round_up(channels, LANES)
    whole = channels // LANES
    for g in range(whole):
        out_ref[g * rows : (g + 1) * rows, :] = dot(
            left_ref[0:rows, :], right_ref[g * LANES : (g + 1) * LANES, :], ((1,), (1,))
        )
    rest = rows - whole * LANES
    for g in range(wide // LANES if rest else 0):
        out_ref[whole * rows + g * rest : whole * rows + (g + 1) * rest, :] = dot(
            right_ref[whole * LANES : rows, :],
            left_ref[g * LANES : (g + 1) * LANES, :],
            ((1,), (1,)),
        )
    used = whole * rows + rest * (wide // LANES)
    if used < out_ref.shape[0]:
        out_ref[used:, :] = jnp.zeros((out_ref.shape[0] - used, LANES), out_ref.dtype)


def full_matrix(pack_ref, channels):
    rows, wide = round_up(channels, PANEL), round_up(channels, LANES)
    whole = channels // LANES
    rest = rows - whole * LANES
    parts = [pack_ref[g * rows : (g + 1) * rows, :] for g in range(whole)]
    if rest:
        tail = jnp.concatenate(
            [
                pack_ref[whole * rows + g * rest : whole * rows + (g + 1) * rest, :]
                for g in range(wide // LANES)
            ],
            axis=1,
        )
        tail = jnp.concatenate([tail, jnp.zeros((LANES - rest, wide), tail.dtype)], axis=0)
        parts.append(tail.T[0:rows, :])
    return jnp.concatenate(parts, axis=1)


def cut(pack_ref, core, mine_ref, other_ref):
    half = mine_ref.shape[0]
    mine_ref[...] = pack_ref[pl.ds(pl.multiple_of(core * half, 8), half), :].astype(mine_ref.dtype)
    other_ref[...] = pack_ref[pl.ds(pl.multiple_of((1 - core) * half, 8), half), :].astype(
        other_ref.dtype
    )


def join(pack_ref, core, mine, other):
    half = mine.shape[0]
    pack_ref[pl.ds(pl.multiple_of(core * half, 8), half), :] = mine
    pack_ref[pl.ds(pl.multiple_of((1 - core) * half, 8), half), :] = other


def gram_kernel(core_ref, part_ref, carried_ref, y_ref, g_mine, g_other, pad_ref, gram_ref):
    image = (part_ref[...] + carried_ref[...].astype(jnp.float32)).astype(y_ref.dtype)
    y_ref[...] = image
    store_padded(pad_ref, image)
    lower_products(pad_ref, round_up(image.shape[0], PANEL), gram_ref)
    cut(gram_ref, core_ref[0], g_mine, g_other)


def gram(core, part, carried):
    channels, rows = carried.shape
    lower = lower_rows(channels)
    half = jax.ShapeDtypeStruct((lower // 2, LANES), jnp.float32)
    return pl.pallas_call(
        gram_kernel,
        in_specs=[SCALARS] + [WHOLE] * 2,
        out_specs=[WHOLE] * 3,
        out_shape=[jax.ShapeDtypeStruct((channels, rows), carried.dtype), half, half],
        scratch_shapes=[
            pltpu.VMEM((round_up(channels, LANES), rows), carried.dtype),
            pltpu.VMEM((lower, LANES), jnp.float32),
        ],
        compiler_params=params(),
        cost_estimate=cost(2 * channels * channels * rows, 8 * channels * rows),
    )(core, part, carried)


def split2(value):
    high = value.astype(jnp.bfloat16)
    return high, (value - high.astype(jnp.float32)).astype(jnp.bfloat16)


def store_payload(ref, mixed, ray):
    half = mixed.shape[0]
    high, low = split2(mixed)
    ref[0:half, :] = high
    ref[half : 2 * half, :] = low
    ref[2 * half : 3 * half, :] = ray.astype(jnp.bfloat16)


def load_payload(ref):
    half = ref.shape[0] // 3
    mixed = ref[0:half, :].astype(jnp.float32) + ref[half : 2 * half, :].astype(jnp.float32)
    return mixed, ref[2 * half : 3 * half, :].astype(jnp.float32)


def payload_shape(channels):
    return jax.ShapeDtypeStruct((3 * full_rows(channels) // 2, LANES), jnp.bfloat16)


def cross_kernel(
    core_ref, before_ref, x_ref, y_ref, after_ref, mine_ref, other_ref,
    left_ref, pad_ref, mixed_ref, ray_ref,
):
    channels = x_ref.shape[0]
    core = core_ref[0]
    half = mixed_ref.shape[0] // 2
    store_padded(pad_ref, y_ref[...])
    store_padded(left_ref, before_ref[...])
    full_products(left_ref, pad_ref, channels, mixed_ref)
    store_padded(left_ref, x_ref[...])
    full_products(left_ref, pad_ref, channels, ray_ref)
    mine = pl.ds(pl.multiple_of(core * half, 8), half)
    other = pl.ds(pl.multiple_of((1 - core) * half, 8), half)
    store_payload(mine_ref, mixed_ref[mine, :], ray_ref[mine, :])
    store_payload(other_ref, mixed_ref[other, :], ray_ref[other, :])


def cross(core, before, x_t, y_t, after):
    channels, rows = x_t.shape
    padded = pltpu.VMEM((round_up(channels, LANES), rows), x_t.dtype)
    pack = pltpu.VMEM((full_rows(channels), LANES), jnp.float32)
    return pl.pallas_call(
        cross_kernel,
        in_specs=[SCALARS, WHOLE, WHOLE, WHOLE, ANYWHERE],
        out_specs=[WHOLE] * 2,
        out_shape=[payload_shape(channels)] * 2,
        scratch_shapes=[padded, padded, pack, pack],
        compiler_params=params(),
        cost_estimate=cost(4 * channels * channels * rows, 6 * channels * rows),
    )(core, before, x_t, y_t, after)


def add_kernel(left_ref, right_ref, *refs):
    left, right = load_payload(left_ref), load_payload(right_ref)
    store_payload(refs[-1], left[0] + right[0], left[1] + right[1])


def last_add_kernel(left_ref, right_ref, mixed_ref, ray_ref):
    left, right = load_payload(left_ref), load_payload(right_ref)
    mixed_ref[...] = left[0] + right[0]
    ray_ref[...] = (left[1] + right[1]).astype(ray_ref.dtype)


def last_add(left, right):
    half = left.shape[0] // 3
    return pl.pallas_call(
        last_add_kernel,
        in_specs=[WHOLE] * 2,
        out_specs=[WHOLE] * 2,
        out_shape=[
            jax.ShapeDtypeStruct((half, LANES), jnp.float32),
            jax.ShapeDtypeStruct((half, LANES), jnp.bfloat16),
        ],
        compiler_params=params(),
        cost_estimate=cost(10**5, 10**5),
    )(left, right)


def add_payloads(left, right, *after):
    return pl.pallas_call(
        add_kernel,
        in_specs=[WHOLE] * 2 + [ANYWHERE] * len(after),
        out_specs=WHOLE,
        out_shape=jax.ShapeDtypeStruct(left.shape, left.dtype),
        compiler_params=params(),
        cost_estimate=cost(10**5, 10**6),
    )(left, right, *after)


def split3(value):
    high = value.astype(jnp.bfloat16)
    rest = value - high.astype(jnp.float32)
    mid = rest.astype(jnp.bfloat16)
    low = (rest - mid.astype(jnp.float32)).astype(jnp.bfloat16)
    return high, mid, low


def sublane(value, index):
    return jnp.broadcast_to(value[index : index + 1, :], value.shape)


def lane_of(value, index):
    return jnp.take_along_axis(value, jnp.broadcast_to(index, value.shape), axis=1)


def eliminate(columns, panel):
    half = 8
    row = lax.broadcasted_iota(jnp.int32, (half, LANES), 0)
    scales = [jnp.zeros((half, LANES), jnp.float32) for _ in range(2)]
    columns = [list(c) for c in columns]
    panel = [list(p) for p in panel]
    for j in range(PANEL):
        h, r = divmod(j, half)
        pivot = sublane(columns[j][h], r)
        inverse = lax.rsqrt(pivot)
        inverse = inverse * (1.5 - 0.5 * pivot * inverse * inverse)
        square = inverse * inverse
        factor = [None, None]
        factor[h] = jnp.where(row > r, columns[j][h], 0.0) * square
        if h == 0:
            factor[1] = columns[j][1] * square
        for later in range(j + 1, PANEL):
            entry = sublane(columns[j][later // half], later % half)
            for t in range(max(h, later // half), 2):
                columns[later][t] = columns[later][t] - factor[t] * entry
        for group in panel:
            entry = sublane(group[h], r)
            for t in range(h, 2):
                group[t] = group[t] - factor[t] * entry
        scales[h] = jnp.where(row == r, inverse, scales[h])
    return [jnp.concatenate([g[0] * scales[0], g[1] * scales[1]], axis=0) for g in panel]


def fill_work(channels, scale, pack_ref, work_ref):
    rows, wide = work_ref.shape
    groups = wide // LANES
    offset = 0
    for g in range(groups):
        top = g * LANES
        size = min(LANES, rows - top)
        column = pack_ref[offset : offset + rows - top, :] * scale
        offset += rows - top
        diag = column[0:size, :]
        if top + LANES > channels:
            row = lax.broadcasted_iota(jnp.int32, diag.shape, 0)
            lane = lax.broadcasted_iota(jnp.int32, diag.shape, 1)
            diag = jnp.where((row == lane) & (lane + top >= channels), 1.0, diag)
        work_ref[top : top + size, top : top + LANES] = diag
        for below in range(g + 1, groups):
            start = (below - g) * LANES
            size_b = min(LANES, rows - below * LANES)
            block = column[start : start + size_b, :]
            if size_b < LANES:
                block = jnp.concatenate(
                    [block, jnp.zeros((LANES - size_b, LANES), jnp.float32)], axis=0
                )
            work_ref[top : top + size, below * LANES : (below + 1) * LANES] = block.T
            work_ref[below * LANES : below * LANES + size_b, top : top + LANES] = jnp.zeros(
                (size_b, LANES), jnp.float32
            )


def eliminate_group(g, work_ref):
    rows, wide = work_ref.shape
    groups = wide // LANES
    row = lax.broadcasted_iota(jnp.int32, (PANEL, LANES), 0)
    lane = lax.broadcasted_iota(jnp.int32, (PANEL, LANES), 1)
    top = g * LANES
    size = min(LANES, rows - top)

    def step(b, carry):
        local = b * PANEL
        start = pl.multiple_of(top + local, PANEL)
        parts = [work_ref[pl.ds(start, PANEL), q * LANES : (q + 1) * LANES] for q in range(groups)]
        pivots = [parts[g][0:8, :], parts[g][8:16, :]]
        columns = [[lane_of(p, local + j) for p in pivots] for j in range(PANEL)]
        inside = (lane >= local) & (lane < local + PANEL)
        identity = jnp.where(lane - local == row, 1.0, 0.0)
        parts[g] = jnp.where(inside, identity, parts[g])
        done = eliminate(columns, [[p[0:8, :], p[8:16, :]] for p in parts])
        left, right = [], []
        for q in range(groups):
            high, mid, low = split3(done[q])
            right.append(jnp.concatenate([high, mid, high, low, mid, high], axis=0))
            if q >= g:
                if q == g:
                    high, mid, low = split3(jnp.where(lane >= local + PANEL, done[q], 0.0))
                left.append(jnp.concatenate([high, high, mid, high, mid, low], axis=0))
        for n, q in enumerate(range(g, groups)):
            low_row = q * LANES
            high_row = min(rows, low_row + LANES)
            for c in range(groups):
                update = dot(left[n], right[c], ((0,), (0,)))[0 : high_row - low_row, :]
                old = work_ref[low_row:high_row, c * LANES : (c + 1) * LANES]
                if c == g:
                    lanes = lax.broadcasted_iota(jnp.int32, old.shape, 1)
                    old = jnp.where((lanes >= local) & (lanes < local + PANEL), 0.0, old)
                work_ref[low_row:high_row, c * LANES : (c + 1) * LANES] = old - update
        for q in range(groups):
            if q == g:
                done[q] = jnp.where(lane < local + PANEL, done[q], 0.0)
            elif q > g:
                done[q] = jnp.zeros_like(done[q])
            work_ref[pl.ds(start, PANEL), q * LANES : (q + 1) * LANES] = done[q]
        return carry

    lax.fori_loop(0, size // PANEL, step, 0)


def first_stage_kernel(channels, scale, core_ref, mine_ref, other_ref, work_ref, pack_ref):
    join(pack_ref, core_ref[0], mine_ref[...], other_ref[...])
    fill_work(channels, scale, pack_ref, work_ref)
    eliminate_group(0, work_ref)


def last_stages_kernel(before_ref, after_ref, work_ref, pack_ref):
    work_ref[...] = before_ref[...]
    rows, wide = work_ref.shape
    for g in range(1, wide // LANES):
        eliminate_group(g, work_ref)
    offset = 0
    for q in range(wide // LANES):
        tall = rows - q * LANES
        pack_ref[offset : offset + tall, :] = work_ref[q * LANES : rows, q * LANES : (q + 1) * LANES]
        offset += tall


def work_shape(channels):
    return jax.ShapeDtypeStruct((round_up(channels, PANEL), round_up(channels, LANES)), jnp.float32)


def first_stage(core, mine, other, channels, total_rows):
    return pl.pallas_call(
        functools.partial(first_stage_kernel, channels, 1.0 / total_rows),
        in_specs=[SCALARS] + [WHOLE] * 2,
        out_specs=WHOLE,
        out_shape=work_shape(channels),
        scratch_shapes=[pltpu.VMEM((lower_rows(channels), LANES), jnp.float32)],
        compiler_params=params(),
        cost_estimate=cost(FIRST_STAGE_FLOPS, 10**6),
    )(core, mine, other)


def last_stages(work, channels, after):
    return pl.pallas_call(
        last_stages_kernel,
        in_specs=[WHOLE, ANYWHERE],
        out_specs=[WHOLE] * 2,
        out_shape=[
            work_shape(channels),
            jax.ShapeDtypeStruct((lower_rows(channels), LANES), jnp.float32),
        ],
        compiler_params=params(),
        cost_estimate=cost(LAST_STAGES_FLOPS, 10**5),
    )(work, after)


def dot3(left, right, dims):
    left_high, left_low = split2(left)
    right_high, right_low = split2(right)
    return (
        dot(left_high, right_high, dims)
        + dot(left_high, right_low, dims)
        + dot(left_low, right_high, dims)
    )


def lower_matrix(pack_ref, out_ref):
    rows, wide = out_ref.shape
    offset = 0
    for g in range(wide // LANES):
        top = g * LANES
        lanes = slice(top, top + LANES)
        if top:
            out_ref[0:top, lanes] = jnp.zeros((top, LANES), jnp.float32)
        out_ref[top:rows, lanes] = pack_ref[offset : offset + rows - top, :]
        offset += rows - top


def basis_kernel(inverse_ref, y_ref, q_ref):
    channels = y_ref.shape[0]
    image = y_ref[...]
    for start, size in strips(channels, 2 * LANES):
        used = min(channels, start + size)
        high, low = split2(inverse_ref[start : start + size, 0:used])
        both = dot(jnp.concatenate([high, low], axis=0), image[0:used, :], ((1,), (0,)))
        q_ref[start : start + size, :] = (both[0:size, :] + both[size:, :]).astype(q_ref.dtype)


def basis(inverse, y_t):
    channels, rows = y_t.shape
    return pl.pallas_call(
        basis_kernel,
        in_specs=[WHOLE] * 2,
        out_specs=WHOLE,
        out_shape=jax.ShapeDtypeStruct(y_t.shape, y_t.dtype),
        compiler_params=params(),
        cost_estimate=cost(10**5, 10**5),
    )(inverse, y_t)


def matrix_shape(channels):
    return jax.ShapeDtypeStruct((channels, 1, channels), jnp.float32)


def ray_kernel(scale, core_ref, mine_ref, other_ref, out_ref, pack_ref):
    channels = out_ref.shape[0]
    join(pack_ref, core_ref[0], mine_ref[...].astype(jnp.float32), other_ref[...].astype(jnp.float32))
    out_ref[:, 0, :] = full_matrix(pack_ref, channels)[0:channels, 0:channels] * scale


def unpack_ray(core, mine, other, channels, total_rows):
    return pl.pallas_call(
        functools.partial(ray_kernel, 1.0 / total_rows),
        in_specs=[SCALARS] + [WHOLE] * 2,
        out_specs=WHOLE,
        out_shape=matrix_shape(channels),
        scratch_shapes=[pltpu.VMEM((full_rows(channels), LANES), jnp.float32)],
        compiler_params=params(),
        cost_estimate=cost(10**5, 10**5),
    )(core, mine, other)


def half_kernel(core_ref, mine_ref, other_ref, inverse_ref, out_ref, pack_ref):
    join(pack_ref, core_ref[0], mine_ref[...], other_ref[...])
    mixed = full_matrix(pack_ref, inverse_ref.shape[0])
    out_ref[...] = dot3(mixed, inverse_ref[...], ((1,), (1,)))


def half_product(core, mine, other, inverse):
    rows = inverse.shape[0]
    return pl.pallas_call(
        half_kernel,
        in_specs=[SCALARS] + [WHOLE] * 3,
        out_specs=WHOLE,
        out_shape=jax.ShapeDtypeStruct((rows, rows), jnp.float32),
        scratch_shapes=[pltpu.VMEM((2 * mine.shape[0], LANES), jnp.float32)],
        compiler_params=params(),
        cost_estimate=cost(10**5, 10**5),
    )(core, mine, other, inverse)


def correlation_kernel(scale, previous_ref, half_ref, out_ref, before_ref):
    channels = out_ref.shape[0]
    rows = half_ref.shape[0]
    lower_matrix(previous_ref, before_ref)
    total = dot3(before_ref[:, 0:rows], half_ref[...], ((1,), (0,))) * scale
    out_ref[:, 0, :] = total[0:channels, 0:channels]


def correlate(previous, half, channels, total_rows):
    return pl.pallas_call(
        functools.partial(correlation_kernel, 1.0 / total_rows),
        in_specs=[WHOLE] * 2,
        out_specs=WHOLE,
        out_shape=matrix_shape(channels),
        scratch_shapes=[
            pltpu.VMEM((half.shape[0], round_up(channels, LANES)), jnp.float32),
        ],
        compiler_params=params(),
        cost_estimate=cost(10**8, 10**6),
    )(previous, half)


def from_behind(value, axis, steps):
    count = lax.axis_size(axis)
    leading, last = (max(0, -steps), min(count, count - steps))
    return lax.ppermute(value, axis, [(source, source + steps) for source in range(leading, last)])


def other_core(value):
    return lax.ppermute(value, "rows", [(s, s ^ 1) for s in range(lax.axis_size("rows"))])


def chip_rounds():
    count = lax.axis_size("rows")
    bits = []
    while 2 << len(bits) < count:
        bits.append(2 << len(bits))
    return [
        [(s, s ^ (bits[n] if s % 2 == 0 else bits[-1 - n])) for s in range(count)]
        for n in range(len(bits))
    ]


def shards(x_block, h_diag, h_right, pattern):
    x_t = x_block[0].T
    channels, block_rows = x_t.shape
    masks = pattern[0].transpose(1, 0, 2)
    total_rows = lax.axis_size("rows") * block_rows
    core = (lax.axis_index("rows") % 2).astype(jnp.int32).reshape(1)
    later = from_behind(x_t, "rows", -1)
    carried = from_behind(tile_product(1, masks, x_t, h_right[0], x_t.dtype, 58), "rows", 1)
    first = tile_product(0, masks, x_t, h_diag[0], jnp.float32, 50)
    part = later_product(masks, later, h_right[0], first)
    y_t, g_mine, g_other = gram(core, part, carried)
    previous_y = from_behind(y_t, "sector", 1)
    g_sum = g_mine + other_core(g_other)
    for pairs in chip_rounds():
        g_sum = g_sum + lax.ppermute(g_sum, "rows", pairs)
    work = first_stage(core, g_sum, other_core(g_sum), channels, total_rows)
    m_mine, m_other = cross(core, previous_y, x_t, y_t, work)
    m_sum = add_payloads(m_mine, other_core(m_other))
    work, pack = last_stages(work, channels, m_sum)
    previous = from_behind(pack, "sector", 1)
    q_t = basis(work, y_t)
    rounds = chip_rounds()
    for pairs in rounds[:-1]:
        m_sum = add_payloads(m_sum, lax.ppermute(m_sum, "rows", pairs), work)
    m_half, r_half = last_add(m_sum, lax.ppermute(m_sum, "rows", rounds[-1]))
    half = half_product(core, m_half, other_core(m_half), work)
    correlation = correlate(previous, half, channels, total_rows)
    rayleigh = unpack_ray(core, r_half, other_core(r_half), channels, total_rows)
    return (q_t.T[None], rayleigh.transpose(1, 0, 2), correlation.transpose(1, 0, 2))


def solution(mesh):
    in_specs = (
        P("sector", "rows", None),
        P("sector", "rows", None),
        P("sector", "rows", None),
        P("sector", None, "rows", None),
    )
    out_specs = (P("sector", "rows", None), P("sector", None, None), P("sector", None, None))
    return jax.shard_map(shards, mesh=mesh, in_specs=in_specs, out_specs=out_specs, check_vma=False)
```

```python
import functools

import jax
import jax.numpy as jnp
from jax import lax
from jax.experimental import pallas as pl
from jax.experimental.pallas import tpu as pltpu
from jax.sharding import PartitionSpec as P

SUBBLOCK = 128
LANES = 128
PANEL = 16
WHOLE = pl.BlockSpec(memory_space=pltpu.VMEM)
SCALARS = pl.BlockSpec(memory_space=pltpu.SMEM)
ANYWHERE = pl.BlockSpec(memory_space=pl.ANY)
MIB = 1024 * 1024
FIRST_STAGE_FLOPS = 3 * 10**9
LAST_STAGES_FLOPS = 4 * 10**9


def params(mib=48):
    return pltpu.CompilerParams(vmem_limit_bytes=mib * MIB)


def cost(flops, bytes_accessed):
    return pl.CostEstimate(flops=flops, bytes_accessed=bytes_accessed, transcendentals=0)


def round_up(value, step):
    return (value + step - 1) // step * step


def dot(left, right, dims, precision=None):
    return lax.dot_general(
        left, right, (dims, ((), ())), precision=precision, preferred_element_type=jnp.float32
    )


def block_mask(mask_ref, which, cols):
    blocks = mask_ref[:, which, :].astype(jnp.float32)
    col = lax.broadcasted_iota(jnp.int32, (blocks.shape[1], cols), 1)
    block = lax.broadcasted_iota(jnp.int32, (blocks.shape[1], cols), 0)
    return dot(blocks, jnp.where(col // SUBBLOCK == block, 1.0, 0.0), ((1,), (0,)))


def mask_rows(tile_ref, mask, start, size):
    cols = tile_ref.shape[1]
    for i in range(start // SUBBLOCK, (start + size) // SUBBLOCK):
        keep = jnp.broadcast_to(mask[i : i + 1, :], (PANEL, cols)).astype(tile_ref.dtype)
        for row in range(i * SUBBLOCK, (i + 1) * SUBBLOCK, PANEL):
            tile_ref[row : row + PANEL, :] = tile_ref[row : row + PANEL, :] * keep


def strips(rows, width):
    return [(start, min(width, rows - start)) for start in range(0, rows, width)]


def halves(rows):
    first = rows // 512 * 256
    return [(0, first), (first, rows - first)] if first else [(0, rows)]


def copies_of(source, target, sems):
    copies = []
    for n, (start, size) in enumerate(halves(target.shape[0])):
        here = (pl.ds(start, size), slice(None))
        copies.append(pltpu.make_async_copy(source.at[here], target.at[here], sems.at[n]))
    return copies


def product(x_ref, tile_ref, copies, mask, sum_ref, out_ref):
    rows = tile_ref.shape[0]
    for n, (start, size) in enumerate(halves(rows)):
        copies[n].wait()
        mask_rows(tile_ref, mask, start, size)
        last = n + 1 == len(copies)
        for col, cols in strips(rows, 2 * SUBBLOCK):
            here = (slice(None), slice(col, col + cols))
            term = dot(
                x_ref[:, start : start + size],
                tile_ref[start : start + size, col : col + cols],
                ((1,), (0,)),
            )
            if n > 0:
                term = sum_ref[here] + term
            if last:
                out_ref[here] = term.astype(out_ref.dtype)
            else:
                sum_ref[here] = term


def tile_kernel(which, mask_ref, x_hbm, tile_hbm, out_ref, x_ref, tile_ref, sum_ref, x_sem, sems):
    rows = tile_ref.shape[0]
    copies = copies_of(tile_hbm, tile_ref, sems)
    copy_x = pltpu.make_async_copy(x_hbm, x_ref, x_sem)
    copy_x.start()
    for copy in copies:
        copy.start()
    mask = block_mask(mask_ref, which, rows)
    copy_x.wait()
    product(x_ref, tile_ref, copies, mask, sum_ref, out_ref)


def tile_product(which, masks, x_t, tile, dtype, mib):
    channels, rows = x_t.shape
    return pl.pallas_call(
        functools.partial(tile_kernel, which),
        in_specs=[WHOLE, ANYWHERE, ANYWHERE],
        out_specs=WHOLE,
        out_shape=jax.ShapeDtypeStruct((channels, rows), dtype),
        scratch_shapes=[
            pltpu.VMEM((channels, rows), x_t.dtype),
            pltpu.VMEM((rows, rows), tile.dtype),
            pltpu.VMEM((channels, rows), jnp.float32),
            pltpu.SemaphoreType.DMA,
            pltpu.SemaphoreType.DMA((2,)),
        ],
        compiler_params=params(mib),
        cost_estimate=cost(2 * channels * rows * rows, 2 * rows * rows),
    )(masks, x_t, tile)


def later_kernel(mask_ref, later_ref, tile_hbm, first_ref, out_ref, tile_ref, sems):
    rows = tile_ref.shape[0]
    copies = copies_of(tile_hbm, tile_ref, sems)
    for copy in copies:
        copy.start()
    mask = block_mask(mask_ref, 1, rows)
    for n, (start, size) in enumerate(halves(rows)):
        copies[n].wait()
        mask_rows(tile_ref, mask, start, size)
        for row, count in strips(size, 2 * SUBBLOCK):
            here = (slice(None), slice(start + row, start + row + count))
            out_ref[here] = first_ref[here] + dot(
                later_ref[...], tile_ref[start + row : start + row + count, :], ((1,), (1,))
            )


def later_product(masks, later, tile, first):
    channels, rows = later.shape
    return pl.pallas_call(
        later_kernel,
        in_specs=[WHOLE, WHOLE, ANYWHERE, WHOLE],
        out_specs=WHOLE,
        out_shape=jax.ShapeDtypeStruct((channels, rows), jnp.float32),
        scratch_shapes=[
            pltpu.VMEM((rows, rows), tile.dtype),
            pltpu.SemaphoreType.DMA((2,)),
        ],
        compiler_params=params(),
        cost_estimate=cost(2 * channels * rows * rows, 2 * rows * rows),
    )(masks, later, tile, first)


def lower_rows(channels):
    rows = round_up(channels, PANEL)
    return sum(rows - g * LANES for g in range(round_up(channels, LANES) // LANES))


def full_rows(channels):
    rows, wide = round_up(channels, PANEL), round_up(channels, LANES)
    whole = channels // LANES
    rest = rows - whole * LANES
    return round_up(whole * rows + rest * (wide // LANES), 4 * PANEL)


def store_padded(ref, value):
    size, tall = value.shape[0], ref.shape[0]
    start = size // PANEL * PANEL
    ref[start:tall, :] = jnp.zeros((tall - start, ref.shape[1]), ref.dtype)
    ref[0:size, :] = value


def lower_products(pad_ref, rows, out_ref):
    offset = 0
    for g in range(pad_ref.shape[0] // LANES):
        block = pad_ref[g * LANES : (g + 1) * LANES, :]
        out_ref[offset : offset + rows - g * LANES, :] = dot(
            pad_ref[g * LANES : rows, :], block, ((1,), (1,))
        )
        offset += rows - g * LANES


def full_products(left_ref, right_ref, channels, out_ref):
    rows, wide = round_up(channels, PANEL), round_up(channels, LANES)
    whole = channels // LANES
    for g in range(whole):
        out_ref[g * rows : (g + 1) * rows, :] = dot(
            left_ref[0:rows, :], right_ref[g * LANES : (g + 1) * LANES, :], ((1,), (1,))
        )
    rest = rows - whole * LANES
    for g in range(wide // LANES if rest else 0):
        out_ref[whole * rows + g * rest : whole * rows + (g + 1) * rest, :] = dot(
            right_ref[whole * LANES : rows, :],
            left_ref[g * LANES : (g + 1) * LANES, :],
            ((1,), (1,)),
        )
    used = whole * rows + rest * (wide // LANES)
    if used < out_ref.shape[0]:
        out_ref[used:, :] = jnp.zeros((out_ref.shape[0] - used, LANES), out_ref.dtype)


def full_matrix(pack_ref, channels):
    rows, wide = round_up(channels, PANEL), round_up(channels, LANES)
    whole = channels // LANES
    rest = rows - whole * LANES
    parts = [pack_ref[g * rows : (g + 1) * rows, :] for g in range(whole)]
    if rest:
        tail = jnp.concatenate(
            [
                pack_ref[whole * rows + g * rest : whole * rows + (g + 1) * rest, :]
                for g in range(wide // LANES)
            ],
            axis=1,
        )
        tail = jnp.concatenate([tail, jnp.zeros((LANES - rest, wide), tail.dtype)], axis=0)
        parts.append(tail.T[0:rows, :])
    return jnp.concatenate(parts, axis=1)


def cut(pack_ref, core, mine_ref, other_ref):
    half = mine_ref.shape[0]
    mine_ref[...] = pack_ref[pl.ds(pl.multiple_of(core * half, 8), half), :].astype(mine_ref.dtype)
    other_ref[...] = pack_ref[pl.ds(pl.multiple_of((1 - core) * half, 8), half), :].astype(
        other_ref.dtype
    )


def join(pack_ref, core, mine, other):
    half = mine.shape[0]
    pack_ref[pl.ds(pl.multiple_of(core * half, 8), half), :] = mine
    pack_ref[pl.ds(pl.multiple_of((1 - core) * half, 8), half), :] = other


def gram_kernel(core_ref, part_ref, carried_ref, y_ref, g_mine, g_other, pad_ref, gram_ref):
    image = (part_ref[...] + carried_ref[...].astype(jnp.float32)).astype(y_ref.dtype)
    y_ref[...] = image
    store_padded(pad_ref, image)
    lower_products(pad_ref, round_up(image.shape[0], PANEL), gram_ref)
    cut(gram_ref, core_ref[0], g_mine, g_other)


def gram(core, part, carried):
    channels, rows = carried.shape
    lower = lower_rows(channels)
    half = jax.ShapeDtypeStruct((lower // 2, LANES), jnp.float32)
    return pl.pallas_call(
        gram_kernel,
        in_specs=[SCALARS] + [WHOLE] * 2,
        out_specs=[WHOLE] * 3,
        out_shape=[jax.ShapeDtypeStruct((channels, rows), carried.dtype), half, half],
        scratch_shapes=[
            pltpu.VMEM((round_up(channels, LANES), rows), carried.dtype),
            pltpu.VMEM((lower, LANES), jnp.float32),
        ],
        compiler_params=params(),
        cost_estimate=cost(2 * channels * channels * rows, 8 * channels * rows),
    )(core, part, carried)


def split2(value):
    high = value.astype(jnp.bfloat16)
    return high, (value - high.astype(jnp.float32)).astype(jnp.bfloat16)


def store_payload(ref, mixed, ray):
    half = mixed.shape[0]
    high, low = split2(mixed)
    ref[0:half, :] = high
    ref[half : 2 * half, :] = low
    ref[2 * half : 3 * half, :] = ray.astype(jnp.bfloat16)


def load_payload(ref):
    half = ref.shape[0] // 3
    mixed = ref[0:half, :].astype(jnp.float32) + ref[half : 2 * half, :].astype(jnp.float32)
    return mixed, ref[2 * half : 3 * half, :].astype(jnp.float32)


def payload_shape(channels):
    return jax.ShapeDtypeStruct((3 * full_rows(channels) // 2, LANES), jnp.bfloat16)


def cross_kernel(
    core_ref, before_ref, x_ref, y_ref, after_ref, mine_ref, other_ref,
    left_ref, pad_ref, mixed_ref, ray_ref,
):
    channels = x_ref.shape[0]
    core = core_ref[0]
    half = mixed_ref.shape[0] // 2
    store_padded(pad_ref, y_ref[...])
    store_padded(left_ref, before_ref[...])
    full_products(left_ref, pad_ref, channels, mixed_ref)
    store_padded(left_ref, x_ref[...])
    full_products(left_ref, pad_ref, channels, ray_ref)
    mine = pl.ds(pl.multiple_of(core * half, 8), half)
    other = pl.ds(pl.multiple_of((1 - core) * half, 8), half)
    store_payload(mine_ref, mixed_ref[mine, :], ray_ref[mine, :])
    store_payload(other_ref, mixed_ref[other, :], ray_ref[other, :])


def cross(core, before, x_t, y_t, after):
    channels, rows = x_t.shape
    padded = pltpu.VMEM((round_up(channels, LANES), rows), x_t.dtype)
    pack = pltpu.VMEM((full_rows(channels), LANES), jnp.float32)
    return pl.pallas_call(
        cross_kernel,
        in_specs=[SCALARS, WHOLE, WHOLE, WHOLE, ANYWHERE],
        out_specs=[WHOLE] * 2,
        out_shape=[payload_shape(channels)] * 2,
        scratch_shapes=[padded, padded, pack, pack],
        compiler_params=params(),
        cost_estimate=cost(4 * channels * channels * rows, 6 * channels * rows),
    )(core, before, x_t, y_t, after)


def add_kernel(left_ref, right_ref, *refs):
    left, right = load_payload(left_ref), load_payload(right_ref)
    store_payload(refs[-1], left[0] + right[0], left[1] + right[1])


def last_add_kernel(left_ref, right_ref, after_ref, mixed_ref, ray_ref):
    left, right = load_payload(left_ref), load_payload(right_ref)
    mixed_ref[...] = left[0] + right[0]
    ray_ref[...] = (left[1] + right[1]).astype(ray_ref.dtype)


def last_add(left, right, after):
    half = left.shape[0] // 3
    return pl.pallas_call(
        last_add_kernel,
        in_specs=[WHOLE] * 2 + [ANYWHERE],
        out_specs=[WHOLE] * 2,
        out_shape=[
            jax.ShapeDtypeStruct((half, LANES), jnp.float32),
            jax.ShapeDtypeStruct((half, LANES), jnp.bfloat16),
        ],
        compiler_params=params(),
        cost_estimate=cost(10**5, 10**5),
    )(left, right, after)


def add_payloads(left, right, *after):
    return pl.pallas_call(
        add_kernel,
        in_specs=[WHOLE] * 2 + [ANYWHERE] * len(after),
        out_specs=WHOLE,
        out_shape=jax.ShapeDtypeStruct(left.shape, left.dtype),
        compiler_params=params(),
        cost_estimate=cost(10**5, 10**6),
    )(left, right, *after)


def split3(value):
    high = value.astype(jnp.bfloat16)
    rest = value - high.astype(jnp.float32)
    mid = rest.astype(jnp.bfloat16)
    low = (rest - mid.astype(jnp.float32)).astype(jnp.bfloat16)
    return high, mid, low


def sublane(value, index):
    return jnp.broadcast_to(value[index : index + 1, :], value.shape)


def lane_of(value, index):
    return jnp.take_along_axis(value, jnp.broadcast_to(index, value.shape), axis=1)


def eliminate(columns, panel):
    half = 8
    row = lax.broadcasted_iota(jnp.int32, (half, LANES), 0)
    scales = [jnp.zeros((half, LANES), jnp.float32) for _ in range(2)]
    columns = [list(c) for c in columns]
    panel = [list(p) for p in panel]
    for j in range(PANEL):
        h, r = divmod(j, half)
        pivot = sublane(columns[j][h], r)
        inverse = lax.rsqrt(pivot)
        inverse = inverse * (1.5 - 0.5 * pivot * inverse * inverse)
        square = inverse * inverse
        factor = [None, None]
        factor[h] = jnp.where(row > r, columns[j][h], 0.0) * square
        if h == 0:
            factor[1] = columns[j][1] * square
        for later in range(j + 1, PANEL):
            entry = sublane(columns[j][later // half], later % half)
            for t in range(max(h, later // half), 2):
                columns[later][t] = columns[later][t] - factor[t] * entry
        for group in panel:
            entry = sublane(group[h], r)
            for t in range(h, 2):
                group[t] = group[t] - factor[t] * entry
        scales[h] = jnp.where(row == r, inverse, scales[h])
    return [jnp.concatenate([g[0] * scales[0], g[1] * scales[1]], axis=0) for g in panel]


def fill_work(channels, scale, pack_ref, work_ref):
    rows, wide = work_ref.shape
    groups = wide // LANES
    offset = 0
    for g in range(groups):
        top = g * LANES
        size = min(LANES, rows - top)
        column = pack_ref[offset : offset + rows - top, :] * scale
        offset += rows - top
        diag = column[0:size, :]
        if top + LANES > channels:
            row = lax.broadcasted_iota(jnp.int32, diag.shape, 0)
            lane = lax.broadcasted_iota(jnp.int32, diag.shape, 1)
            diag = jnp.where((row == lane) & (lane + top >= channels), 1.0, diag)
        work_ref[top : top + size, top : top + LANES] = diag
        for below in range(g + 1, groups):
            start = (below - g) * LANES
            size_b = min(LANES, rows - below * LANES)
            block = column[start : start + size_b, :]
            if size_b < LANES:
                block = jnp.concatenate(
                    [block, jnp.zeros((LANES - size_b, LANES), jnp.float32)], axis=0
                )
            work_ref[top : top + size, below * LANES : (below + 1) * LANES] = block.T
            work_ref[below * LANES : below * LANES + size_b, top : top + LANES] = jnp.zeros(
                (size_b, LANES), jnp.float32
            )


def eliminate_group(g, work_ref):
    rows, wide = work_ref.shape
    groups = wide // LANES
    row = lax.broadcasted_iota(jnp.int32, (PANEL, LANES), 0)
    lane = lax.broadcasted_iota(jnp.int32, (PANEL, LANES), 1)
    top = g * LANES
    size = min(LANES, rows - top)

    def step(b, carry):
        local = b * PANEL
        start = pl.multiple_of(top + local, PANEL)
        parts = [work_ref[pl.ds(start, PANEL), q * LANES : (q + 1) * LANES] for q in range(groups)]
        pivots = [parts[g][0:8, :], parts[g][8:16, :]]
        columns = [[lane_of(p, local + j) for p in pivots] for j in range(PANEL)]
        inside = (lane >= local) & (lane < local + PANEL)
        identity = jnp.where(lane - local == row, 1.0, 0.0)
        parts[g] = jnp.where(inside, identity, parts[g])
        done = eliminate(columns, [[p[0:8, :], p[8:16, :]] for p in parts])
        left, right = [], []
        for q in range(groups):
            high, mid, low = split3(done[q])
            right.append(jnp.concatenate([high, mid, high, low, mid, high], axis=0))
            if q >= g:
                if q == g:
                    high, mid, low = split3(jnp.where(lane >= local + PANEL, done[q], 0.0))
                left.append(jnp.concatenate([high, high, mid, high, mid, low], axis=0))
        for n, q in enumerate(range(g, groups)):
            low_row = q * LANES
            high_row = min(rows, low_row + LANES)
            for c in range(groups):
                update = dot(left[n], right[c], ((0,), (0,)))[0 : high_row - low_row, :]
                old = work_ref[low_row:high_row, c * LANES : (c + 1) * LANES]
                if c == g:
                    lanes = lax.broadcasted_iota(jnp.int32, old.shape, 1)
                    old = jnp.where((lanes >= local) & (lanes < local + PANEL), 0.0, old)
                work_ref[low_row:high_row, c * LANES : (c + 1) * LANES] = old - update
        for q in range(groups):
            if q == g:
                done[q] = jnp.where(lane < local + PANEL, done[q], 0.0)
            elif q > g:
                done[q] = jnp.zeros_like(done[q])
            work_ref[pl.ds(start, PANEL), q * LANES : (q + 1) * LANES] = done[q]
        return carry

    lax.fori_loop(0, size // PANEL, step, 0)


def first_stage_kernel(channels, scale, core_ref, mine_ref, other_ref, work_ref, pack_ref):
    join(pack_ref, core_ref[0], mine_ref[...], other_ref[...])
    fill_work(channels, scale, pack_ref, work_ref)
    eliminate_group(0, work_ref)


def last_stages_kernel(before_ref, after_ref, work_ref, pack_ref):
    work_ref[...] = before_ref[...]
    rows, wide = work_ref.shape
    for g in range(1, wide // LANES):
        eliminate_group(g, work_ref)
    offset = 0
    for q in range(wide // LANES):
        tall = rows - q * LANES
        pack_ref[offset : offset + tall, :] = work_ref[q * LANES : rows, q * LANES : (q + 1) * LANES]
        offset += tall


def work_shape(channels):
    return jax.ShapeDtypeStruct((round_up(channels, PANEL), round_up(channels, LANES)), jnp.float32)


def first_stage(core, mine, other, channels, total_rows):
    return pl.pallas_call(
        functools.partial(first_stage_kernel, channels, 1.0 / total_rows),
        in_specs=[SCALARS] + [WHOLE] * 2,
        out_specs=WHOLE,
        out_shape=work_shape(channels),
        scratch_shapes=[pltpu.VMEM((lower_rows(channels), LANES), jnp.float32)],
        compiler_params=params(),
        cost_estimate=cost(FIRST_STAGE_FLOPS, 10**6),
    )(core, mine, other)


def last_stages(work, channels, after):
    return pl.pallas_call(
        last_stages_kernel,
        in_specs=[WHOLE, ANYWHERE],
        out_specs=[WHOLE] * 2,
        out_shape=[
            work_shape(channels),
            jax.ShapeDtypeStruct((lower_rows(channels), LANES), jnp.float32),
        ],
        compiler_params=params(),
        cost_estimate=cost(LAST_STAGES_FLOPS, 10**5),
    )(work, after)


def dot3(left, right, dims):
    left_high, left_low = split2(left)
    right_high, right_low = split2(right)
    return (
        dot(left_high, right_high, dims)
        + dot(left_high, right_low, dims)
        + dot(left_low, right_high, dims)
    )


def lower_matrix(pack_ref, out_ref):
    rows, wide = out_ref.shape
    offset = 0
    for g in range(wide // LANES):
        top = g * LANES
        lanes = slice(top, top + LANES)
        if top:
            out_ref[0:top, lanes] = jnp.zeros((top, LANES), jnp.float32)
        out_ref[top:rows, lanes] = pack_ref[offset : offset + rows - top, :]
        offset += rows - top


def basis_kernel(inverse_ref, y_ref, q_ref, token_ref):
    channels = y_ref.shape[0]
    image = y_ref[...]
    token_ref[...] = jnp.zeros_like(token_ref)
    for start, size in strips(channels, 2 * LANES):
        used = min(channels, start + size)
        high, low = split2(inverse_ref[start : start + size, 0:used])
        both = dot(jnp.concatenate([high, low], axis=0), image[0:used, :], ((1,), (0,)))
        q_ref[start : start + size, :] = (both[0:size, :] + both[size:, :]).astype(q_ref.dtype)


def basis(inverse, y_t):
    channels, rows = y_t.shape
    return pl.pallas_call(
        basis_kernel,
        in_specs=[WHOLE] * 2,
        out_specs=[WHOLE] * 2,
        out_shape=[
            jax.ShapeDtypeStruct(y_t.shape, y_t.dtype),
            jax.ShapeDtypeStruct((8, LANES), jnp.float32),
        ],
        compiler_params=params(),
        cost_estimate=cost(10**5, 10**5),
    )(inverse, y_t)


def matrix_shape(channels):
    return jax.ShapeDtypeStruct((channels, 1, channels), jnp.float32)


def ray_kernel(scale, core_ref, mine_ref, other_ref, out_ref, pack_ref):
    channels = out_ref.shape[0]
    join(pack_ref, core_ref[0], mine_ref[...].astype(jnp.float32), other_ref[...].astype(jnp.float32))
    out_ref[:, 0, :] = full_matrix(pack_ref, channels)[0:channels, 0:channels] * scale


def unpack_ray(core, mine, other, channels, total_rows):
    return pl.pallas_call(
        functools.partial(ray_kernel, 1.0 / total_rows),
        in_specs=[SCALARS] + [WHOLE] * 2,
        out_specs=WHOLE,
        out_shape=matrix_shape(channels),
        scratch_shapes=[pltpu.VMEM((full_rows(channels), LANES), jnp.float32)],
        compiler_params=params(),
        cost_estimate=cost(10**5, 10**5),
    )(core, mine, other)


def half_kernel(core_ref, mine_ref, other_ref, inverse_ref, out_ref, pack_ref):
    join(pack_ref, core_ref[0], mine_ref[...], other_ref[...])
    mixed = full_matrix(pack_ref, inverse_ref.shape[0])
    out_ref[...] = dot3(mixed, inverse_ref[...], ((1,), (1,)))


def half_product(core, mine, other, inverse):
    rows = inverse.shape[0]
    return pl.pallas_call(
        half_kernel,
        in_specs=[SCALARS] + [WHOLE] * 3,
        out_specs=WHOLE,
        out_shape=jax.ShapeDtypeStruct((rows, rows), jnp.float32),
        scratch_shapes=[pltpu.VMEM((2 * mine.shape[0], LANES), jnp.float32)],
        compiler_params=params(),
        cost_estimate=cost(10**5, 10**5),
    )(core, mine, other, inverse)


def correlation_kernel(scale, previous_ref, half_ref, out_ref, before_ref):
    channels = out_ref.shape[0]
    rows = half_ref.shape[0]
    lower_matrix(previous_ref, before_ref)
    total = dot3(before_ref[:, 0:rows], half_ref[...], ((1,), (0,))) * scale
    out_ref[:, 0, :] = total[0:channels, 0:channels]


def correlate(previous, half, channels, total_rows):
    return pl.pallas_call(
        functools.partial(correlation_kernel, 1.0 / total_rows),
        in_specs=[WHOLE] * 2,
        out_specs=WHOLE,
        out_shape=matrix_shape(channels),
        scratch_shapes=[
            pltpu.VMEM((half.shape[0], round_up(channels, LANES)), jnp.float32),
        ],
        compiler_params=params(),
        cost_estimate=cost(10**8, 10**6),
    )(previous, half)


def from_behind(value, axis, steps):
    count = lax.axis_size(axis)
    leading, last = (max(0, -steps), min(count, count - steps))
    return lax.ppermute(value, axis, [(source, source + steps) for source in range(leading, last)])


def other_core(value):
    return lax.ppermute(value, "rows", [(s, s ^ 1) for s in range(lax.axis_size("rows"))])


def chip_rounds():
    count = lax.axis_size("rows")
    bits = []
    while 2 << len(bits) < count:
        bits.append(2 << len(bits))
    return [
        [(s, s ^ (bits[n] if s % 2 == 0 else bits[-1 - n])) for s in range(count)]
        for n in range(len(bits))
    ]


def shards(x_block, h_diag, h_right, pattern):
    x_t = x_block[0].T
    channels, block_rows = x_t.shape
    masks = pattern[0].transpose(1, 0, 2)
    total_rows = lax.axis_size("rows") * block_rows
    core = (lax.axis_index("rows") % 2).astype(jnp.int32).reshape(1)
    later = from_behind(x_t, "rows", -1)
    carried = from_behind(tile_product(1, masks, x_t, h_right[0], x_t.dtype, 53), "rows", 1)
    first = tile_product(0, masks, x_t, h_diag[0], jnp.float32, 50)
    part = later_product(masks, later, h_right[0], first)
    y_t, g_mine, g_other = gram(core, part, carried)
    previous_y = from_behind(y_t, "sector", 1)
    g_sum = g_mine + other_core(g_other)
    for pairs in chip_rounds():
        g_sum = g_sum + lax.ppermute(g_sum, "rows", pairs)
    work = first_stage(core, g_sum, other_core(g_sum), channels, total_rows)
    m_mine, m_other = cross(core, previous_y, x_t, y_t, work)
    m_sum = add_payloads(m_mine, other_core(m_other))
    work, pack = last_stages(work, channels, m_sum)
    previous = from_behind(pack, "sector", 1)
    q_t, token = basis(work, y_t)
    rounds = chip_rounds()
    for pairs in rounds[:-1]:
        m_sum = add_payloads(m_sum, lax.ppermute(m_sum, "rows", pairs), work)
    m_half, r_half = last_add(m_sum, lax.ppermute(m_sum, "rows", rounds[-1]), token)
    half = half_product(core, m_half, other_core(m_half), work)
    correlation = correlate(previous, half, channels, total_rows)
    rayleigh = unpack_ray(core, r_half, other_core(r_half), channels, total_rows)
    return (q_t.T[None], rayleigh.transpose(1, 0, 2), correlation.transpose(1, 0, 2))


def solution(mesh):
    in_specs = (
        P("sector", "rows", None),
        P("sector", "rows", None),
        P("sector", "rows", None),
        P("sector", None, "rows", None),
    )
    out_specs = (P("sector", "rows", None), P("sector", None, None), P("sector", None, None))
    return jax.shard_map(shards, mesh=mesh, in_specs=in_specs, out_specs=out_specs, check_vma=False)
```

```python
import functools

import jax
import jax.numpy as jnp
from jax import lax
from jax.experimental import pallas as pl
from jax.experimental.pallas import tpu as pltpu
from jax.sharding import PartitionSpec as P

SUBBLOCK = 128
LANES = 128
PANEL = 16
WHOLE = pl.BlockSpec(memory_space=pltpu.VMEM)
SCALARS = pl.BlockSpec(memory_space=pltpu.SMEM)
ANYWHERE = pl.BlockSpec(memory_space=pl.ANY)
MIB = 1024 * 1024
FIRST_STAGE_FLOPS = 3 * 10**9
LAST_STAGES_FLOPS = 4 * 10**9


def params(mib=48):
    return pltpu.CompilerParams(vmem_limit_bytes=mib * MIB)


def cost(flops, bytes_accessed):
    return pl.CostEstimate(flops=flops, bytes_accessed=bytes_accessed, transcendentals=0)


def round_up(value, step):
    return (value + step - 1) // step * step


def dot(left, right, dims, precision=None):
    return lax.dot_general(
        left, right, (dims, ((), ())), precision=precision, preferred_element_type=jnp.float32
    )


def block_mask(mask_ref, which, cols):
    blocks = mask_ref[:, which, :].astype(jnp.float32)
    col = lax.broadcasted_iota(jnp.int32, (blocks.shape[1], cols), 1)
    block = lax.broadcasted_iota(jnp.int32, (blocks.shape[1], cols), 0)
    return dot(blocks, jnp.where(col // SUBBLOCK == block, 1.0, 0.0), ((1,), (0,)))


def mask_rows(tile_ref, mask, start, size):
    cols = tile_ref.shape[1]
    for i in range(start // SUBBLOCK, (start + size) // SUBBLOCK):
        keep = jnp.broadcast_to(mask[i : i + 1, :], (PANEL, cols)).astype(tile_ref.dtype)
        for row in range(i * SUBBLOCK, (i + 1) * SUBBLOCK, PANEL):
            tile_ref[row : row + PANEL, :] = tile_ref[row : row + PANEL, :] * keep


def strips(rows, width):
    return [(start, min(width, rows - start)) for start in range(0, rows, width)]


def halves(rows):
    first = rows // 512 * 256
    return [(0, first), (first, rows - first)] if first else [(0, rows)]


def copies_of(source, target, sems):
    copies = []
    for n, (start, size) in enumerate(halves(target.shape[0])):
        here = (pl.ds(start, size), slice(None))
        copies.append(pltpu.make_async_copy(source.at[here], target.at[here], sems.at[n]))
    return copies


def product(x_ref, tile_ref, copies, mask, sum_ref, out_ref):
    rows = tile_ref.shape[0]
    for n, (start, size) in enumerate(halves(rows)):
        copies[n].wait()
        mask_rows(tile_ref, mask, start, size)
        last = n + 1 == len(copies)
        for col, cols in strips(rows, 2 * SUBBLOCK):
            here = (slice(None), slice(col, col + cols))
            term = dot(
                x_ref[:, start : start + size],
                tile_ref[start : start + size, col : col + cols],
                ((1,), (0,)),
            )
            if n > 0:
                term = sum_ref[here] + term
            if last:
                out_ref[here] = term.astype(out_ref.dtype)
            else:
                sum_ref[here] = term


def tile_kernel(which, mask_ref, x_hbm, tile_hbm, out_ref, x_ref, tile_ref, sum_ref, x_sem, sems):
    rows = tile_ref.shape[0]
    copies = copies_of(tile_hbm, tile_ref, sems)
    copy_x = pltpu.make_async_copy(x_hbm, x_ref, x_sem)
    copy_x.start()
    for copy in copies:
        copy.start()
    mask = block_mask(mask_ref, which, rows)
    copy_x.wait()
    product(x_ref, tile_ref, copies, mask, sum_ref, out_ref)


def tile_product(which, masks, x_t, tile, dtype, mib):
    channels, rows = x_t.shape
    return pl.pallas_call(
        functools.partial(tile_kernel, which),
        in_specs=[WHOLE, ANYWHERE, ANYWHERE],
        out_specs=WHOLE,
        out_shape=jax.ShapeDtypeStruct((channels, rows), dtype),
        scratch_shapes=[
            pltpu.VMEM((channels, rows), x_t.dtype),
            pltpu.VMEM((rows, rows), tile.dtype),
            pltpu.VMEM((channels, rows), jnp.float32),
            pltpu.SemaphoreType.DMA,
            pltpu.SemaphoreType.DMA((2,)),
        ],
        compiler_params=params(mib),
        cost_estimate=cost(2 * channels * rows * rows, 2 * rows * rows),
    )(masks, x_t, tile)


def later_kernel(mask_ref, later_ref, tile_hbm, first_ref, out_ref, tile_ref, sems):
    rows = tile_ref.shape[0]
    copies = copies_of(tile_hbm, tile_ref, sems)
    for copy in copies:
        copy.start()
    mask = block_mask(mask_ref, 1, rows)
    for n, (start, size) in enumerate(halves(rows)):
        copies[n].wait()
        mask_rows(tile_ref, mask, start, size)
        for row, count in strips(size, 2 * SUBBLOCK):
            here = (slice(None), slice(start + row, start + row + count))
            out_ref[here] = first_ref[here] + dot(
                later_ref[...], tile_ref[start + row : start + row + count, :], ((1,), (1,))
            )


def later_product(masks, later, tile, first):
    channels, rows = later.shape
    return pl.pallas_call(
        later_kernel,
        in_specs=[WHOLE, WHOLE, ANYWHERE, WHOLE],
        out_specs=WHOLE,
        out_shape=jax.ShapeDtypeStruct((channels, rows), jnp.float32),
        scratch_shapes=[
            pltpu.VMEM((rows, rows), tile.dtype),
            pltpu.SemaphoreType.DMA((2,)),
        ],
        compiler_params=params(),
        cost_estimate=cost(2 * channels * rows * rows, 2 * rows * rows),
    )(masks, later, tile, first)


def lower_rows(channels):
    rows = round_up(channels, PANEL)
    return sum(rows - g * LANES for g in range(round_up(channels, LANES) // LANES))


def full_rows(channels):
    rows, wide = round_up(channels, PANEL), round_up(channels, LANES)
    whole = channels // LANES
    rest = rows - whole * LANES
    return round_up(whole * rows + rest * (wide // LANES), 4 * PANEL)


def lower_products(ref, out_ref):
    channels = ref.shape[0]
    rows = round_up(channels, PANEL)
    offset = 0
    for start, size in strips(channels, LANES):
        tall = rows - start
        if size < LANES:
            out_ref[offset : offset + tall, :] = jnp.zeros((tall, LANES), jnp.float32)
        elif rows > channels:
            out_ref[offset + channels - start : offset + tall, :] = jnp.zeros(
                (rows - channels, LANES), jnp.float32
            )
        out_ref[offset : offset + channels - start, 0:size] = dot(
            ref[start:channels, :], ref[start : start + size, :], ((1,), (1,))
        )
        offset += tall


def full_products(left_ref, right_ref, out_ref):
    channels = left_ref.shape[0]
    rows = round_up(channels, PANEL)
    whole = channels // LANES
    for g in range(whole):
        out_ref[g * rows : g * rows + channels, :] = dot(
            left_ref[...], right_ref[g * LANES : (g + 1) * LANES, :], ((1,), (1,))
        )
        if rows > channels:
            out_ref[g * rows + channels : (g + 1) * rows, :] = jnp.zeros(
                (rows - channels, LANES), jnp.float32
            )
    base = whole * rows
    if base < out_ref.shape[0]:
        out_ref[base:, :] = jnp.zeros((out_ref.shape[0] - base, LANES), jnp.float32)
    first, rest = whole * LANES, rows - whole * LANES
    for n, (start, size) in enumerate(strips(channels, LANES) if first < channels else []):
        place = base + n * rest
        out_ref[place : place + channels - first, 0:size] = dot(
            right_ref[first:channels, :], left_ref[start : start + size, :], ((1,), (1,))
        )


def full_matrix(pack_ref, channels):
    rows, wide = round_up(channels, PANEL), round_up(channels, LANES)
    whole = channels // LANES
    rest = rows - whole * LANES
    parts = [pack_ref[g * rows : (g + 1) * rows, :] for g in range(whole)]
    if rest:
        tail = jnp.concatenate(
            [
                pack_ref[whole * rows + g * rest : whole * rows + (g + 1) * rest, :]
                for g in range(wide // LANES)
            ],
            axis=1,
        )
        tail = jnp.concatenate([tail, jnp.zeros((LANES - rest, wide), tail.dtype)], axis=0)
        parts.append(tail.T[0:rows, :])
    return jnp.concatenate(parts, axis=1)


def cut(pack_ref, core, mine_ref, other_ref):
    half = mine_ref.shape[0]
    mine_ref[...] = pack_ref[pl.ds(pl.multiple_of(core * half, 8), half), :].astype(mine_ref.dtype)
    other_ref[...] = pack_ref[pl.ds(pl.multiple_of((1 - core) * half, 8), half), :].astype(
        other_ref.dtype
    )


def join(pack_ref, core, mine, other):
    half = mine.shape[0]
    pack_ref[pl.ds(pl.multiple_of(core * half, 8), half), :] = mine
    pack_ref[pl.ds(pl.multiple_of((1 - core) * half, 8), half), :] = other


def gram_kernel(core_ref, part_ref, carried_ref, y_ref, g_mine, g_other, gram_ref):
    image = part_ref[...] + carried_ref[...].astype(jnp.float32)
    y_ref[...] = image.astype(y_ref.dtype)
    lower_products(y_ref, gram_ref)
    cut(gram_ref, core_ref[0], g_mine, g_other)


def gram(core, part, carried):
    channels, rows = carried.shape
    lower = lower_rows(channels)
    half = jax.ShapeDtypeStruct((lower // 2, LANES), jnp.float32)
    return pl.pallas_call(
        gram_kernel,
        in_specs=[SCALARS] + [WHOLE] * 2,
        out_specs=[WHOLE] * 3,
        out_shape=[jax.ShapeDtypeStruct((channels, rows), carried.dtype), half, half],
        scratch_shapes=[pltpu.VMEM((lower, LANES), jnp.float32)],
        compiler_params=params(),
        cost_estimate=cost(2 * channels * channels * rows, 8 * channels * rows),
    )(core, part, carried)


def split2(value):
    high = value.astype(jnp.bfloat16)
    return high, (value - high.astype(jnp.float32)).astype(jnp.bfloat16)


def store_payload(ref, mixed, ray):
    half = mixed.shape[0]
    high, low = split2(mixed)
    ref[0:half, :] = high
    ref[half : 2 * half, :] = low
    ref[2 * half : 3 * half, :] = ray.astype(jnp.bfloat16)


def load_payload(ref):
    half = ref.shape[0] // 3
    mixed = ref[0:half, :].astype(jnp.float32) + ref[half : 2 * half, :].astype(jnp.float32)
    return mixed, ref[2 * half : 3 * half, :].astype(jnp.float32)


def payload_shape(channels):
    return jax.ShapeDtypeStruct((3 * full_rows(channels) // 2, LANES), jnp.bfloat16)


def cross_kernel(
    core_ref, before_ref, x_ref, y_ref, after_ref, mine_ref, other_ref, mixed_ref, ray_ref
):
    core = core_ref[0]
    half = mixed_ref.shape[0] // 2
    full_products(before_ref, y_ref, mixed_ref)
    full_products(x_ref, y_ref, ray_ref)
    mine = pl.ds(pl.multiple_of(core * half, 8), half)
    other = pl.ds(pl.multiple_of((1 - core) * half, 8), half)
    store_payload(mine_ref, mixed_ref[mine, :], ray_ref[mine, :])
    store_payload(other_ref, mixed_ref[other, :], ray_ref[other, :])


def cross(core, before, x_t, y_t, after):
    channels, rows = x_t.shape
    pack = pltpu.VMEM((full_rows(channels), LANES), jnp.float32)
    return pl.pallas_call(
        cross_kernel,
        in_specs=[SCALARS, WHOLE, WHOLE, WHOLE, ANYWHERE],
        out_specs=[WHOLE] * 2,
        out_shape=[payload_shape(channels)] * 2,
        scratch_shapes=[pack, pack],
        compiler_params=params(),
        cost_estimate=cost(4 * channels * channels * rows, 6 * channels * rows),
    )(core, before, x_t, y_t, after)


def add_kernel(left_ref, right_ref, *refs):
    left, right = load_payload(left_ref), load_payload(right_ref)
    store_payload(refs[-1], left[0] + right[0], left[1] + right[1])


def last_add_kernel(left_ref, right_ref, after_ref, mixed_ref, ray_ref):
    left, right = load_payload(left_ref), load_payload(right_ref)
    mixed_ref[...] = left[0] + right[0]
    ray_ref[...] = (left[1] + right[1]).astype(ray_ref.dtype)


def last_add(left, right, after):
    half = left.shape[0] // 3
    return pl.pallas_call(
        last_add_kernel,
        in_specs=[WHOLE] * 2 + [ANYWHERE],
        out_specs=[WHOLE] * 2,
        out_shape=[
            jax.ShapeDtypeStruct((half, LANES), jnp.float32),
            jax.ShapeDtypeStruct((half, LANES), jnp.bfloat16),
        ],
        compiler_params=params(),
        cost_estimate=cost(10**5, 10**5),
    )(left, right, after)


def add_payloads(left, right, *after):
    return pl.pallas_call(
        add_kernel,
        in_specs=[WHOLE] * 2 + [ANYWHERE] * len(after),
        out_specs=WHOLE,
        out_shape=jax.ShapeDtypeStruct(left.shape, left.dtype),
        compiler_params=params(),
        cost_estimate=cost(10**5, 10**6),
    )(left, right, *after)


def split3(value):
    high = value.astype(jnp.bfloat16)
    rest = value - high.astype(jnp.float32)
    mid = rest.astype(jnp.bfloat16)
    low = (rest - mid.astype(jnp.float32)).astype(jnp.bfloat16)
    return high, mid, low


def sublane(value, index):
    return jnp.broadcast_to(value[index : index + 1, :], value.shape)


def lane_of(value, index):
    return jnp.take_along_axis(value, jnp.broadcast_to(index, value.shape), axis=1)


def eliminate(columns, panel):
    half = 8
    row = lax.broadcasted_iota(jnp.int32, (half, LANES), 0)
    scales = [jnp.zeros((half, LANES), jnp.float32) for _ in range(2)]
    columns = [list(c) for c in columns]
    panel = [list(p) for p in panel]
    for j in range(0, PANEL, 2):
        h, r = divmod(j, half)
        left, right = columns[j], columns[j + 1]
        a, b, c = sublane(left[h], r), sublane(left[h], r + 1), sublane(right[h], r + 1)
        det = a * c - b * b
        inverse = pl.reciprocal(det, approx=True)
        first, second = [None, None], [None, None]
        for t in range(h, 2):
            x, y = left[t], right[t]
            if t == h:
                x, y = jnp.where(row > r + 1, x, 0.0), jnp.where(row > r + 1, y, 0.0)
            first[t] = (c * x - b * y) * inverse
            second[t] = (a * y - b * x) * inverse
        for later in range(j + 2, PANEL):
            q = later // half
            x, y = sublane(left[q], later % half), sublane(right[q], later % half)
            for t in range(max(h, q), 2):
                columns[later][t] = columns[later][t] - (first[t] * x + second[t] * y)
        inverse_a = pl.reciprocal(a, approx=True)
        first[h] = jnp.where(row == r + 1, b * inverse_a, first[h])
        for group in panel:
            x, y = sublane(group[h], r), sublane(group[h], r + 1)
            for t in range(h, 2):
                group[t] = group[t] - (first[t] * x + second[t] * y)
        scales[h] = jnp.where(row == r, lax.rsqrt(a), scales[h])
        scales[h] = jnp.where(row == r + 1, lax.rsqrt(det * inverse_a), scales[h])
    return [jnp.concatenate([g[0] * scales[0], g[1] * scales[1]], axis=0) for g in panel]


def fill_work(channels, scale, pack_ref, work_ref):
    rows, wide = work_ref.shape
    groups = wide // LANES
    offset = 0
    for g in range(groups):
        top = g * LANES
        size = min(LANES, rows - top)
        column = pack_ref[offset : offset + rows - top, :] * scale
        offset += rows - top
        diag = column[0:size, :]
        if top + LANES > channels:
            row = lax.broadcasted_iota(jnp.int32, diag.shape, 0)
            lane = lax.broadcasted_iota(jnp.int32, diag.shape, 1)
            diag = jnp.where((row == lane) & (lane + top >= channels), 1.0, diag)
        work_ref[top : top + size, top : top + LANES] = diag
        for below in range(g + 1, groups):
            start = (below - g) * LANES
            size_b = min(LANES, rows - below * LANES)
            block = column[start : start + size_b, :]
            if size_b < LANES:
                block = jnp.concatenate(
                    [block, jnp.zeros((LANES - size_b, LANES), jnp.float32)], axis=0
                )
            work_ref[top : top + size, below * LANES : (below + 1) * LANES] = block.T
            work_ref[below * LANES : below * LANES + size_b, top : top + LANES] = jnp.zeros(
                (size_b, LANES), jnp.float32
            )


def eliminate_group(g, work_ref):
    rows, wide = work_ref.shape
    groups = wide // LANES
    row = lax.broadcasted_iota(jnp.int32, (PANEL, LANES), 0)
    lane = lax.broadcasted_iota(jnp.int32, (PANEL, LANES), 1)
    top = g * LANES
    size = min(LANES, rows - top)

    def step(b, carry):
        local = b * PANEL
        start = pl.multiple_of(top + local, PANEL)
        parts = [work_ref[pl.ds(start, PANEL), q * LANES : (q + 1) * LANES] for q in range(groups)]
        pivots = [parts[g][0:8, :], parts[g][8:16, :]]
        columns = [[lane_of(p, local + j) for p in pivots] for j in range(PANEL)]
        inside = (lane >= local) & (lane < local + PANEL)
        identity = jnp.where(lane - local == row, 1.0, 0.0)
        parts[g] = jnp.where(inside, identity, parts[g])
        done = eliminate(columns, [[p[0:8, :], p[8:16, :]] for p in parts])
        left, right = [], []
        for q in range(groups):
            high, mid, low = split3(done[q])
            right.append(jnp.concatenate([high, mid, high, low, mid, high], axis=0))
            if q >= g:
                if q == g:
                    high, mid, low = split3(jnp.where(lane >= local + PANEL, done[q], 0.0))
                left.append(jnp.concatenate([high, high, mid, high, mid, low], axis=0))
        right = jnp.concatenate(right, axis=1)
        for n, q in enumerate(range(g, groups)):
            low_row = q * LANES
            high_row = min(rows, low_row + LANES)
            update = dot(left[n][:, 0 : high_row - low_row], right, ((0,), (0,)))
            for c in range(groups):
                lanes = slice(c * LANES, (c + 1) * LANES)
                old = work_ref[low_row:high_row, lanes]
                if c == g:
                    here = lax.broadcasted_iota(jnp.int32, old.shape, 1)
                    old = jnp.where((here >= local) & (here < local + PANEL), 0.0, old)
                work_ref[low_row:high_row, lanes] = old - update[:, lanes]
        for q in range(groups):
            if q == g:
                done[q] = jnp.where(lane < local + PANEL, done[q], 0.0)
            elif q > g:
                done[q] = jnp.zeros_like(done[q])
            work_ref[pl.ds(start, PANEL), q * LANES : (q + 1) * LANES] = done[q]
        return carry

    lax.fori_loop(0, size // PANEL, step, 0)


def first_stage_kernel(channels, scale, core_ref, mine_ref, other_ref, work_ref, pack_ref):
    join(pack_ref, core_ref[0], mine_ref[...], other_ref[...])
    fill_work(channels, scale, pack_ref, work_ref)
    eliminate_group(0, work_ref)


def last_stages_kernel(before_ref, after_ref, work_ref, pack_ref):
    work_ref[...] = before_ref[...]
    rows, wide = work_ref.shape
    for g in range(1, wide // LANES):
        eliminate_group(g, work_ref)
    offset = 0
    for q in range(wide // LANES):
        tall = rows - q * LANES
        pack_ref[offset : offset + tall, :] = work_ref[q * LANES : rows, q * LANES : (q + 1) * LANES]
        offset += tall


def work_shape(channels):
    return jax.ShapeDtypeStruct((round_up(channels, PANEL), round_up(channels, LANES)), jnp.float32)


def first_stage(core, mine, other, channels, total_rows):
    return pl.pallas_call(
        functools.partial(first_stage_kernel, channels, 1.0 / total_rows),
        in_specs=[SCALARS] + [WHOLE] * 2,
        out_specs=WHOLE,
        out_shape=work_shape(channels),
        scratch_shapes=[pltpu.VMEM((lower_rows(channels), LANES), jnp.float32)],
        compiler_params=params(),
        cost_estimate=cost(FIRST_STAGE_FLOPS, 10**6),
    )(core, mine, other)


def last_stages(work, channels, after):
    return pl.pallas_call(
        last_stages_kernel,
        in_specs=[WHOLE, ANYWHERE],
        out_specs=[WHOLE] * 2,
        out_shape=[
            work_shape(channels),
            jax.ShapeDtypeStruct((lower_rows(channels), LANES), jnp.float32),
        ],
        compiler_params=params(),
        cost_estimate=cost(LAST_STAGES_FLOPS, 10**5),
    )(work, after)


def dot3(left, right, dims):
    left_high, left_low = split2(left)
    right_high, right_low = split2(right)
    return (
        dot(left_high, right_high, dims)
        + dot(left_high, right_low, dims)
        + dot(left_low, right_high, dims)
    )


def lower_matrix(pack_ref, out_ref):
    rows, wide = out_ref.shape
    offset = 0
    for g in range(wide // LANES):
        top = g * LANES
        lanes = slice(top, top + LANES)
        if top:
            out_ref[0:top, lanes] = jnp.zeros((top, LANES), jnp.float32)
        out_ref[top:rows, lanes] = pack_ref[offset : offset + rows - top, :]
        offset += rows - top


def basis_kernel(inverse_ref, y_ref, q_ref, token_ref):
    channels = y_ref.shape[0]
    image = y_ref[...]
    token_ref[...] = jnp.zeros_like(token_ref)
    for start, size in strips(channels, 2 * LANES):
        used = min(channels, start + size)
        high, low = split2(inverse_ref[start : start + size, 0:used])
        both = dot(jnp.concatenate([high, low], axis=0), image[0:used, :], ((1,), (0,)))
        q_ref[start : start + size, :] = (both[0:size, :] + both[size:, :]).astype(q_ref.dtype)


def basis(inverse, y_t):
    channels, rows = y_t.shape
    return pl.pallas_call(
        basis_kernel,
        in_specs=[WHOLE] * 2,
        out_specs=[WHOLE] * 2,
        out_shape=[
            jax.ShapeDtypeStruct(y_t.shape, y_t.dtype),
            jax.ShapeDtypeStruct((8, LANES), jnp.float32),
        ],
        compiler_params=params(),
        cost_estimate=cost(10**5, 10**5),
    )(inverse, y_t)


def matrix_shape(channels):
    return jax.ShapeDtypeStruct((channels, 1, channels), jnp.float32)


def ray_kernel(scale, core_ref, mine_ref, other_ref, out_ref, pack_ref):
    channels = out_ref.shape[0]
    join(pack_ref, core_ref[0], mine_ref[...].astype(jnp.float32), other_ref[...].astype(jnp.float32))
    out_ref[:, 0, :] = full_matrix(pack_ref, channels)[0:channels, 0:channels] * scale


def unpack_ray(core, mine, other, channels, total_rows):
    return pl.pallas_call(
        functools.partial(ray_kernel, 1.0 / total_rows),
        in_specs=[SCALARS] + [WHOLE] * 2,
        out_specs=WHOLE,
        out_shape=matrix_shape(channels),
        scratch_shapes=[pltpu.VMEM((full_rows(channels), LANES), jnp.float32)],
        compiler_params=params(),
        cost_estimate=cost(10**5, 10**5),
    )(core, mine, other)


def half_kernel(core_ref, mine_ref, other_ref, inverse_ref, out_ref, pack_ref):
    join(pack_ref, core_ref[0], mine_ref[...], other_ref[...])
    mixed = full_matrix(pack_ref, inverse_ref.shape[0])
    out_ref[...] = dot3(mixed, inverse_ref[...], ((1,), (1,)))


def half_product(core, mine, other, inverse):
    rows = inverse.shape[0]
    return pl.pallas_call(
        half_kernel,
        in_specs=[SCALARS] + [WHOLE] * 3,
        out_specs=WHOLE,
        out_shape=jax.ShapeDtypeStruct((rows, rows), jnp.float32),
        scratch_shapes=[pltpu.VMEM((2 * mine.shape[0], LANES), jnp.float32)],
        compiler_params=params(),
        cost_estimate=cost(10**5, 10**5),
    )(core, mine, other, inverse)


def correlation_kernel(scale, previous_ref, half_ref, out_ref, before_ref):
    channels = out_ref.shape[0]
    rows = half_ref.shape[0]
    lower_matrix(previous_ref, before_ref)
    total = dot3(before_ref[:, 0:rows], half_ref[...], ((1,), (0,))) * scale
    out_ref[:, 0, :] = total[0:channels, 0:channels]


def correlate(previous, half, channels, total_rows):
    return pl.pallas_call(
        functools.partial(correlation_kernel, 1.0 / total_rows),
        in_specs=[WHOLE] * 2,
        out_specs=WHOLE,
        out_shape=matrix_shape(channels),
        scratch_shapes=[
            pltpu.VMEM((half.shape[0], round_up(channels, LANES)), jnp.float32),
        ],
        compiler_params=params(),
        cost_estimate=cost(10**8, 10**6),
    )(previous, half)


def from_behind(value, axis, steps):
    count = lax.axis_size(axis)
    leading, last = (max(0, -steps), min(count, count - steps))
    return lax.ppermute(value, axis, [(source, source + steps) for source in range(leading, last)])


def other_core(value):
    return lax.ppermute(value, "rows", [(s, s ^ 1) for s in range(lax.axis_size("rows"))])


def chip_rounds():
    count = lax.axis_size("rows")
    bits = []
    while 2 << len(bits) < count:
        bits.append(2 << len(bits))
    return [
        [(s, s ^ (bits[n] if s % 2 == 0 else bits[-1 - n])) for s in range(count)]
        for n in range(len(bits))
    ]


def shards(x_block, h_diag, h_right, pattern):
    x_t = x_block[0].T
    channels, block_rows = x_t.shape
    masks = pattern[0].transpose(1, 0, 2)
    total_rows = lax.axis_size("rows") * block_rows
    core = (lax.axis_index("rows") % 2).astype(jnp.int32).reshape(1)
    later = from_behind(x_t, "rows", -1)
    carried = from_behind(tile_product(1, masks, x_t, h_right[0], x_t.dtype, 53), "rows", 1)
    first = tile_product(0, masks, x_t, h_diag[0], jnp.float32, 50)
    part = later_product(masks, later, h_right[0], first)
    y_t, g_mine, g_other = gram(core, part, carried)
    previous_y = from_behind(y_t, "sector", 1)
    g_sum = g_mine + other_core(g_other)
    for pairs in chip_rounds():
        g_sum = g_sum + lax.ppermute(g_sum, "rows", pairs)
    work = first_stage(core, g_sum, other_core(g_sum), channels, total_rows)
    m_mine, m_other = cross(core, previous_y, x_t, y_t, work)
    m_sum = add_payloads(m_mine, other_core(m_other))
    work, pack = last_stages(work, channels, m_sum)
    previous = from_behind(pack, "sector", 1)
    q_t, token = basis(work, y_t)
    rounds = chip_rounds()
    for pairs in rounds[:-1]:
        m_sum = add_payloads(m_sum, lax.ppermute(m_sum, "rows", pairs), work)
    m_half, r_half = last_add(m_sum, lax.ppermute(m_sum, "rows", rounds[-1]), token)
    half = half_product(core, m_half, other_core(m_half), work)
    correlation = correlate(previous, half, channels, total_rows)
    rayleigh = unpack_ray(core, r_half, other_core(r_half), channels, total_rows)
    return (q_t.T[None], rayleigh.transpose(1, 0, 2), correlation.transpose(1, 0, 2))


def solution(mesh):
    in_specs = (
        P("sector", "rows", None),
        P("sector", "rows", None),
        P("sector", "rows", None),
        P("sector", None, "rows", None),
    )
    out_specs = (P("sector", "rows", None), P("sector", None, None), P("sector", None, None))
    return jax.shard_map(shards, mesh=mesh, in_specs=in_specs, out_specs=out_specs, check_vma=False)
```

```python
import functools

import jax
import jax.numpy as jnp
from jax import lax
from jax.experimental import pallas as pl
from jax.experimental.pallas import tpu as pltpu
from jax.sharding import PartitionSpec as P

SUBBLOCK = 128
LANES = 128
PANEL = 16
WHOLE = pl.BlockSpec(memory_space=pltpu.VMEM)
SCALARS = pl.BlockSpec(memory_space=pltpu.SMEM)
ANYWHERE = pl.BlockSpec(memory_space=pl.ANY)
MIB = 1024 * 1024
FIRST_STAGE_FLOPS = 3500 * 10**6
LAST_STAGES_FLOPS = 4 * 10**9


def params(mib=48):
    return pltpu.CompilerParams(vmem_limit_bytes=mib * MIB)


def cost(flops, bytes_accessed):
    return pl.CostEstimate(flops=flops, bytes_accessed=bytes_accessed, transcendentals=0)


def round_up(value, step):
    return (value + step - 1) // step * step


def dot(left, right, dims, precision=None):
    return lax.dot_general(
        left, right, (dims, ((), ())), precision=precision, preferred_element_type=jnp.float32
    )


def block_mask(mask_ref, which, cols):
    blocks = mask_ref[:, which, :].astype(jnp.float32)
    col = lax.broadcasted_iota(jnp.int32, (blocks.shape[1], cols), 1)
    block = lax.broadcasted_iota(jnp.int32, (blocks.shape[1], cols), 0)
    return dot(blocks, jnp.where(col // SUBBLOCK == block, 1.0, 0.0), ((1,), (0,)))


def mask_rows(tile_ref, mask, start, size):
    cols = tile_ref.shape[1]
    for i in range(start // SUBBLOCK, (start + size) // SUBBLOCK):
        keep = jnp.broadcast_to(mask[i : i + 1, :], (PANEL, cols)).astype(tile_ref.dtype)
        for row in range(i * SUBBLOCK, (i + 1) * SUBBLOCK, PANEL):
            tile_ref[row : row + PANEL, :] = tile_ref[row : row + PANEL, :] * keep


def strips(rows, width):
    return [(start, min(width, rows - start)) for start in range(0, rows, width)]


def halves(rows):
    first = rows // 512 * 256
    return [(0, first), (first, rows - first)] if first else [(0, rows)]


def copies_of(source, target, sems):
    copies = []
    for n, (start, size) in enumerate(halves(target.shape[0])):
        here = (pl.ds(start, size), slice(None))
        copies.append(pltpu.make_async_copy(source.at[here], target.at[here], sems.at[n]))
    return copies


def product(x_ref, tile_ref, copies, mask, sum_ref, out_ref):
    rows = tile_ref.shape[0]
    for n, (start, size) in enumerate(halves(rows)):
        copies[n].wait()
        mask_rows(tile_ref, mask, start, size)
        last = n + 1 == len(copies)
        for col, cols in strips(rows, 2 * SUBBLOCK):
            here = (slice(None), slice(col, col + cols))
            term = dot(
                x_ref[:, start : start + size],
                tile_ref[start : start + size, col : col + cols],
                ((1,), (0,)),
            )
            if n > 0:
                term = sum_ref[here] + term
            if last:
                out_ref[here] = term.astype(out_ref.dtype)
            else:
                sum_ref[here] = term


def tile_kernel(which, mask_ref, x_hbm, tile_hbm, out_ref, x_ref, tile_ref, sum_ref, x_sem, sems):
    rows = tile_ref.shape[0]
    copies = copies_of(tile_hbm, tile_ref, sems)
    copy_x = pltpu.make_async_copy(x_hbm, x_ref, x_sem)
    copy_x.start()
    for copy in copies:
        copy.start()
    mask = block_mask(mask_ref, which, rows)
    copy_x.wait()
    product(x_ref, tile_ref, copies, mask, sum_ref, out_ref)


def tile_product(which, masks, x_t, tile, dtype, mib):
    channels, rows = x_t.shape
    return pl.pallas_call(
        functools.partial(tile_kernel, which),
        in_specs=[WHOLE, ANYWHERE, ANYWHERE],
        out_specs=WHOLE,
        out_shape=jax.ShapeDtypeStruct((channels, rows), dtype),
        scratch_shapes=[
            pltpu.VMEM((channels, rows), x_t.dtype),
            pltpu.VMEM((rows, rows), tile.dtype),
            pltpu.VMEM((channels, rows), jnp.float32),
            pltpu.SemaphoreType.DMA,
            pltpu.SemaphoreType.DMA((2,)),
        ],
        compiler_params=params(mib),
        cost_estimate=cost(2 * channels * rows * rows, 2 * rows * rows),
    )(masks, x_t, tile)


def later_kernel(mask_ref, later_ref, tile_hbm, first_ref, out_ref, tile_ref, sems):
    rows = tile_ref.shape[0]
    copies = copies_of(tile_hbm, tile_ref, sems)
    for copy in copies:
        copy.start()
    mask = block_mask(mask_ref, 1, rows)
    for n, (start, size) in enumerate(halves(rows)):
        copies[n].wait()
        mask_rows(tile_ref, mask, start, size)
        for row, count in strips(size, 2 * SUBBLOCK):
            here = (slice(None), slice(start + row, start + row + count))
            out_ref[here] = first_ref[here] + dot(
                later_ref[...], tile_ref[start + row : start + row + count, :], ((1,), (1,))
            )


def later_product(masks, later, tile, first):
    channels, rows = later.shape
    return pl.pallas_call(
        later_kernel,
        in_specs=[WHOLE, WHOLE, ANYWHERE, WHOLE],
        out_specs=WHOLE,
        out_shape=jax.ShapeDtypeStruct((channels, rows), jnp.float32),
        scratch_shapes=[
            pltpu.VMEM((rows, rows), tile.dtype),
            pltpu.SemaphoreType.DMA((2,)),
        ],
        compiler_params=params(),
        cost_estimate=cost(2 * channels * rows * rows, 2 * rows * rows),
    )(masks, later, tile, first)


def lower_rows(channels):
    rows = round_up(channels, PANEL)
    return sum(rows - g * LANES for g in range(round_up(channels, LANES) // LANES))


def full_rows(channels):
    rows, wide = round_up(channels, PANEL), round_up(channels, LANES)
    whole = channels // LANES
    rest = rows - whole * LANES
    return round_up(whole * rows + rest * (wide // LANES), 4 * PANEL)


def lower_products(ref, out_ref):
    channels = ref.shape[0]
    rows = round_up(channels, PANEL)
    offset = 0
    for start, size in strips(channels, LANES):
        tall = rows - start
        if size < LANES:
            out_ref[offset : offset + tall, :] = jnp.zeros((tall, LANES), jnp.float32)
        elif rows > channels:
            out_ref[offset + channels - start : offset + tall, :] = jnp.zeros(
                (rows - channels, LANES), jnp.float32
            )
        out_ref[offset : offset + channels - start, 0:size] = dot(
            ref[start:channels, :], ref[start : start + size, :], ((1,), (1,))
        )
        offset += tall


def full_products(left_ref, right_ref, out_ref):
    channels = left_ref.shape[0]
    rows = round_up(channels, PANEL)
    whole = channels // LANES
    for g in range(whole):
        out_ref[g * rows : g * rows + channels, :] = dot(
            left_ref[...], right_ref[g * LANES : (g + 1) * LANES, :], ((1,), (1,))
        )
        if rows > channels:
            out_ref[g * rows + channels : (g + 1) * rows, :] = jnp.zeros(
                (rows - channels, LANES), jnp.float32
            )
    base = whole * rows
    if base < out_ref.shape[0]:
        out_ref[base:, :] = jnp.zeros((out_ref.shape[0] - base, LANES), jnp.float32)
    first, rest = whole * LANES, rows - whole * LANES
    for n, (start, size) in enumerate(strips(channels, LANES) if first < channels else []):
        place = base + n * rest
        out_ref[place : place + channels - first, 0:size] = dot(
            right_ref[first:channels, :], left_ref[start : start + size, :], ((1,), (1,))
        )


def full_matrix(pack_ref, channels):
    rows, wide = round_up(channels, PANEL), round_up(channels, LANES)
    whole = channels // LANES
    rest = rows - whole * LANES
    parts = [pack_ref[g * rows : (g + 1) * rows, :] for g in range(whole)]
    if rest:
        tail = jnp.concatenate(
            [
                pack_ref[whole * rows + g * rest : whole * rows + (g + 1) * rest, :]
                for g in range(wide // LANES)
            ],
            axis=1,
        )
        tail = jnp.concatenate([tail, jnp.zeros((LANES - rest, wide), tail.dtype)], axis=0)
        parts.append(tail.T[0:rows, :])
    return jnp.concatenate(parts, axis=1)


def folded_rows(channels):
    if channels < 2 * LANES:
        return lower_rows(channels)
    return lower_rows(channels) - LANES + PANEL


def corner(channels):
    return round_up(channels, PANEL)


def square_index():
    row = lax.broadcasted_iota(jnp.int32, (LANES, LANES), 0)
    return row, lax.broadcasted_iota(jnp.int32, (LANES, LANES), 1)


def fold(pack_ref, out_ref, channels, symmetric):
    if channels < 2 * LANES:
        out_ref[...] = pack_ref[...]
        return
    start = corner(channels)
    end = pack_ref.shape[0]
    row, lane = square_index()
    second = pack_ref[start : start + LANES, :]
    upper = second if symmetric else second.T
    out_ref[0:LANES, :] = jnp.where(row >= lane, pack_ref[0:LANES, :], upper)
    out_ref[LANES:start, :] = pack_ref[LANES:start, :]
    out_ref[start : end - LANES, :] = pack_ref[start + LANES : end, :]
    diagonal = jnp.sum(jnp.where(row == lane, second, 0.0), axis=0, keepdims=True)
    out_ref[end - LANES :, :] = jnp.broadcast_to(diagonal, (PANEL, LANES))


def unfold(folded_ref, pack_ref, channels, symmetric):
    if channels < 2 * LANES:
        pack_ref[...] = folded_ref[...]
        return
    start = corner(channels)
    end = pack_ref.shape[0]
    row, lane = square_index()
    both = folded_ref[0:LANES, :]
    turned = both.T
    first_upper, second_upper = (turned, both) if symmetric else (0.0, 0.0)
    pack_ref[0:LANES, :] = jnp.where(row >= lane, both, first_upper)
    pack_ref[LANES:start, :] = folded_ref[LANES:start, :]
    second = jnp.where(row > lane, turned, second_upper)
    diagonal = folded_ref[end - LANES : end - LANES + 1, :]
    pack_ref[start : start + LANES, :] = jnp.where(row == lane, diagonal, second)
    pack_ref[start + LANES : end, :] = folded_ref[start : end - LANES, :]


def cut(pack_ref, core, mine_ref, other_ref):
    half = mine_ref.shape[0]
    mine_ref[...] = pack_ref[pl.ds(pl.multiple_of(core * half, 8), half), :].astype(mine_ref.dtype)
    other_ref[...] = pack_ref[pl.ds(pl.multiple_of((1 - core) * half, 8), half), :].astype(
        other_ref.dtype
    )


def join(pack_ref, core, mine, other):
    half = mine.shape[0]
    pack_ref[pl.ds(pl.multiple_of(core * half, 8), half), :] = mine
    pack_ref[pl.ds(pl.multiple_of((1 - core) * half, 8), half), :] = other


def gram_kernel(core_ref, part_ref, carried_ref, y_ref, g_mine, g_other, gram_ref, folded_ref):
    image = part_ref[...] + carried_ref[...].astype(jnp.float32)
    y_ref[...] = image.astype(y_ref.dtype)
    lower_products(y_ref, gram_ref)
    fold(gram_ref, folded_ref, y_ref.shape[0], True)
    cut(folded_ref, core_ref[0], g_mine, g_other)


def gram(core, part, carried):
    channels, rows = carried.shape
    lower, folded = lower_rows(channels), folded_rows(channels)
    half = jax.ShapeDtypeStruct((folded // 2, LANES), jnp.float32)
    return pl.pallas_call(
        gram_kernel,
        in_specs=[SCALARS] + [WHOLE] * 2,
        out_specs=[WHOLE] * 3,
        out_shape=[jax.ShapeDtypeStruct((channels, rows), carried.dtype), half, half],
        scratch_shapes=[
            pltpu.VMEM((lower, LANES), jnp.float32),
            pltpu.VMEM((folded, LANES), jnp.float32),
        ],
        compiler_params=params(),
        cost_estimate=cost(2 * channels * channels * rows, 8 * channels * rows),
    )(core, part, carried)


def cross_kernel(core_ref, left_ref, right_ref, after_ref, mine_ref, other_ref, pack_ref):
    full_products(left_ref, right_ref, pack_ref)
    cut(pack_ref, core_ref[0], mine_ref, other_ref)


def cross(core, left, right, after, dtype):
    channels, rows = left.shape
    full = full_rows(channels)
    return pl.pallas_call(
        cross_kernel,
        in_specs=[SCALARS, WHOLE, WHOLE, ANYWHERE],
        out_specs=[WHOLE] * 2,
        out_shape=[jax.ShapeDtypeStruct((full // 2, LANES), dtype)] * 2,
        scratch_shapes=[pltpu.VMEM((full, LANES), jnp.float32)],
        compiler_params=params(),
        cost_estimate=cost(2 * channels * channels * rows, 4 * channels * rows),
    )(core, left, right, after)


def add_kernel(left_ref, right_ref, *refs):
    total = left_ref[...].astype(jnp.float32) + right_ref[...].astype(jnp.float32)
    refs[-1][...] = total.astype(refs[-1].dtype)


def add_after(left, right, *after):
    return pl.pallas_call(
        add_kernel,
        in_specs=[WHOLE] * 2 + [ANYWHERE] * len(after),
        out_specs=WHOLE,
        out_shape=jax.ShapeDtypeStruct(left.shape, left.dtype),
        compiler_params=params(),
        cost_estimate=cost(10**5, 10**5),
    )(left, right, *after)


def split3(value):
    high = value.astype(jnp.bfloat16)
    rest = value - high.astype(jnp.float32)
    mid = rest.astype(jnp.bfloat16)
    low = (rest - mid.astype(jnp.float32)).astype(jnp.bfloat16)
    return high, mid, low


def sublane(value, index):
    return jnp.broadcast_to(value[index : index + 1, :], value.shape)


def lane_of(value, index):
    return jnp.take_along_axis(value, jnp.broadcast_to(index, value.shape), axis=1)


def eliminate(columns, panel):
    half = 8
    row = lax.broadcasted_iota(jnp.int32, (half, LANES), 0)
    scales = [jnp.zeros((half, LANES), jnp.float32) for _ in range(2)]
    columns = [list(c) for c in columns]
    panel = [list(p) for p in panel]
    for j in range(0, PANEL, 2):
        h, r = divmod(j, half)
        left, right = columns[j], columns[j + 1]
        a, b, c = sublane(left[h], r), sublane(left[h], r + 1), sublane(right[h], r + 1)
        det = a * c - b * b
        inverse = pl.reciprocal(det, approx=True)
        first, second = [None, None], [None, None]
        for t in range(h, 2):
            x, y = left[t], right[t]
            if t == h:
                x, y = jnp.where(row > r + 1, x, 0.0), jnp.where(row > r + 1, y, 0.0)
            first[t] = (c * x - b * y) * inverse
            second[t] = (a * y - b * x) * inverse
        for later in range(j + 2, PANEL):
            q = later // half
            x, y = sublane(left[q], later % half), sublane(right[q], later % half)
            for t in range(max(h, q), 2):
                columns[later][t] = columns[later][t] - (first[t] * x + second[t] * y)
        inverse_a = pl.reciprocal(a, approx=True)
        first[h] = jnp.where(row == r + 1, b * inverse_a, first[h])
        for group in panel:
            x, y = sublane(group[h], r), sublane(group[h], r + 1)
            for t in range(h, 2):
                group[t] = group[t] - (first[t] * x + second[t] * y)
        scales[h] = jnp.where(row == r, lax.rsqrt(a), scales[h])
        scales[h] = jnp.where(row == r + 1, lax.rsqrt(det * inverse_a), scales[h])
    return [jnp.concatenate([g[0] * scales[0], g[1] * scales[1]], axis=0) for g in panel]


def fill_work(channels, scale, pack_ref, work_ref):
    rows, wide = work_ref.shape
    groups = wide // LANES
    offset = 0
    for g in range(groups):
        top = g * LANES
        size = min(LANES, rows - top)
        column = pack_ref[offset : offset + rows - top, :] * scale
        offset += rows - top
        diag = column[0:size, :]
        if top + LANES > channels:
            row = lax.broadcasted_iota(jnp.int32, diag.shape, 0)
            lane = lax.broadcasted_iota(jnp.int32, diag.shape, 1)
            diag = jnp.where((row == lane) & (lane + top >= channels), 1.0, diag)
        work_ref[top : top + size, top : top + LANES] = diag
        for below in range(g + 1, groups):
            start = (below - g) * LANES
            size_b = min(LANES, rows - below * LANES)
            block = column[start : start + size_b, :]
            if size_b < LANES:
                block = jnp.concatenate(
                    [block, jnp.zeros((LANES - size_b, LANES), jnp.float32)], axis=0
                )
            work_ref[top : top + size, below * LANES : (below + 1) * LANES] = block.T
            work_ref[below * LANES : below * LANES + size_b, top : top + LANES] = jnp.zeros(
                (size_b, LANES), jnp.float32
            )


def eliminate_group(g, work_ref):
    rows, wide = work_ref.shape
    groups = wide // LANES
    row = lax.broadcasted_iota(jnp.int32, (PANEL, LANES), 0)
    lane = lax.broadcasted_iota(jnp.int32, (PANEL, LANES), 1)
    top = g * LANES
    size = min(LANES, rows - top)

    def step(b, carry):
        local = b * PANEL
        start = pl.multiple_of(top + local, PANEL)
        parts = [work_ref[pl.ds(start, PANEL), q * LANES : (q + 1) * LANES] for q in range(groups)]
        pivots = [parts[g][0:8, :], parts[g][8:16, :]]
        columns = [[lane_of(p, local + j) for p in pivots] for j in range(PANEL)]
        inside = (lane >= local) & (lane < local + PANEL)
        identity = jnp.where(lane - local == row, 1.0, 0.0)
        parts[g] = jnp.where(inside, identity, parts[g])
        done = eliminate(columns, [[p[0:8, :], p[8:16, :]] for p in parts])
        left, right = [], []
        for q in range(groups):
            high, mid, low = split3(done[q])
            right.append(jnp.concatenate([high, mid, high, low, mid, high], axis=0))
            if q >= g:
                if q == g:
                    high, mid, low = split3(jnp.where(lane >= local + PANEL, done[q], 0.0))
                left.append(jnp.concatenate([high, high, mid, high, mid, low], axis=0))
        right = jnp.concatenate(right, axis=1)
        for n, q in enumerate(range(g, groups)):
            low_row = q * LANES
            high_row = min(rows, low_row + LANES)
            update = dot(left[n][:, 0 : high_row - low_row], right, ((0,), (0,)))
            for c in range(groups):
                lanes = slice(c * LANES, (c + 1) * LANES)
                old = work_ref[low_row:high_row, lanes]
                if c == g:
                    here = lax.broadcasted_iota(jnp.int32, old.shape, 1)
                    old = jnp.where((here >= local) & (here < local + PANEL), 0.0, old)
                work_ref[low_row:high_row, lanes] = old - update[:, lanes]
        for q in range(groups):
            if q == g:
                done[q] = jnp.where(lane < local + PANEL, done[q], 0.0)
            elif q > g:
                done[q] = jnp.zeros_like(done[q])
            work_ref[pl.ds(start, PANEL), q * LANES : (q + 1) * LANES] = done[q]
        return carry

    lax.fori_loop(0, size // PANEL, step, 0)


def first_stage_kernel(
    channels, scale, core_ref, mine_ref, other_ref, work_ref, pack_ref, folded_ref
):
    join(folded_ref, core_ref[0], mine_ref[...], other_ref[...])
    unfold(folded_ref, pack_ref, channels, True)
    fill_work(channels, scale, pack_ref, work_ref)
    eliminate_group(0, work_ref)


def last_stages_kernel(channels, before_ref, after_ref, work_ref, folded_ref, pack_ref):
    work_ref[...] = before_ref[...]
    rows, wide = work_ref.shape
    for g in range(1, wide // LANES):
        eliminate_group(g, work_ref)
    offset = 0
    for q in range(wide // LANES):
        tall = rows - q * LANES
        pack_ref[offset : offset + tall, :] = work_ref[q * LANES : rows, q * LANES : (q + 1) * LANES]
        offset += tall
    fold(pack_ref, folded_ref, channels, False)


def work_shape(channels):
    return jax.ShapeDtypeStruct((round_up(channels, PANEL), round_up(channels, LANES)), jnp.float32)


def first_stage(core, mine, other, channels, total_rows):
    return pl.pallas_call(
        functools.partial(first_stage_kernel, channels, 1.0 / total_rows),
        in_specs=[SCALARS] + [WHOLE] * 2,
        out_specs=WHOLE,
        out_shape=work_shape(channels),
        scratch_shapes=[
            pltpu.VMEM((lower_rows(channels), LANES), jnp.float32),
            pltpu.VMEM((folded_rows(channels), LANES), jnp.float32),
        ],
        compiler_params=params(),
        cost_estimate=cost(FIRST_STAGE_FLOPS, 10**6),
    )(core, mine, other)


def last_stages(work, channels, after):
    return pl.pallas_call(
        functools.partial(last_stages_kernel, channels),
        in_specs=[WHOLE, ANYWHERE],
        out_specs=[WHOLE] * 2,
        out_shape=[
            work_shape(channels),
            jax.ShapeDtypeStruct((folded_rows(channels), LANES), jnp.float32),
        ],
        scratch_shapes=[pltpu.VMEM((lower_rows(channels), LANES), jnp.float32)],
        compiler_params=params(),
        cost_estimate=cost(LAST_STAGES_FLOPS, 10**5),
    )(work, after)


def split2(value):
    high = value.astype(jnp.bfloat16)
    return high, (value - high.astype(jnp.float32)).astype(jnp.bfloat16)


def dot3(left, right, dims):
    left_high, left_low = split2(left)
    right_high, right_low = split2(right)
    return (
        dot(left_high, right_high, dims)
        + dot(left_high, right_low, dims)
        + dot(left_low, right_high, dims)
    )


def lower_matrix(pack_ref, out_ref):
    rows, wide = out_ref.shape
    offset = 0
    for g in range(wide // LANES):
        top = g * LANES
        lanes = slice(top, top + LANES)
        if top:
            out_ref[0:top, lanes] = jnp.zeros((top, LANES), jnp.float32)
        out_ref[top:rows, lanes] = pack_ref[offset : offset + rows - top, :]
        offset += rows - top


def basis_kernel(inverse_ref, y_ref, q_ref):
    channels = y_ref.shape[0]
    image = y_ref[...]
    for start, size in strips(channels, 2 * LANES):
        used = min(channels, start + size)
        high, low = split2(inverse_ref[start : start + size, 0:used])
        both = dot(jnp.concatenate([high, low], axis=0), image[0:used, :], ((1,), (0,)))
        q_ref[start : start + size, :] = (both[0:size, :] + both[size:, :]).astype(q_ref.dtype)


def basis(inverse, y_t):
    channels, rows = y_t.shape
    return pl.pallas_call(
        basis_kernel,
        in_specs=[WHOLE] * 2,
        out_specs=WHOLE,
        out_shape=jax.ShapeDtypeStruct(y_t.shape, y_t.dtype),
        compiler_params=params(),
        cost_estimate=cost(10**5, 10**5),
    )(inverse, y_t)


def matrix_shape(channels):
    return jax.ShapeDtypeStruct((channels, 1, channels), jnp.float32)


def ray_kernel(scale, core_ref, mine_ref, other_ref, out_ref, token_ref, pack_ref):
    token_ref[...] = jnp.zeros_like(token_ref)
    channels = out_ref.shape[0]
    join(pack_ref, core_ref[0], mine_ref[...].astype(jnp.float32), other_ref[...].astype(jnp.float32))
    out_ref[:, 0, :] = full_matrix(pack_ref, channels)[0:channels, 0:channels] * scale


def unpack_ray(core, mine, other, channels, total_rows):
    return pl.pallas_call(
        functools.partial(ray_kernel, 1.0 / total_rows),
        in_specs=[SCALARS] + [WHOLE] * 2,
        out_specs=[WHOLE] * 2,
        out_shape=[matrix_shape(channels), jax.ShapeDtypeStruct((8, LANES), jnp.float32)],
        scratch_shapes=[pltpu.VMEM((full_rows(channels), LANES), jnp.float32)],
        compiler_params=params(),
        cost_estimate=cost(10**5, 10**5),
    )(core, mine, other)


def half_kernel(core_ref, mine_ref, other_ref, inverse_ref, out_ref, pack_ref):
    join(pack_ref, core_ref[0], mine_ref[...], other_ref[...])
    mixed = full_matrix(pack_ref, inverse_ref.shape[0])
    out_ref[...] = dot3(mixed, inverse_ref[...], ((1,), (1,)))


def half_product(core, mine, other, inverse):
    rows = inverse.shape[0]
    return pl.pallas_call(
        half_kernel,
        in_specs=[SCALARS] + [WHOLE] * 3,
        out_specs=WHOLE,
        out_shape=jax.ShapeDtypeStruct((rows, rows), jnp.float32),
        scratch_shapes=[pltpu.VMEM((2 * mine.shape[0], LANES), jnp.float32)],
        compiler_params=params(),
        cost_estimate=cost(10**5, 10**5),
    )(core, mine, other, inverse)


def correlation_kernel(scale, previous_ref, half_ref, out_ref, pack_ref, before_ref):
    channels = out_ref.shape[0]
    rows = half_ref.shape[0]
    unfold(previous_ref, pack_ref, channels, False)
    lower_matrix(pack_ref, before_ref)
    total = dot3(before_ref[:, 0:rows], half_ref[...], ((1,), (0,))) * scale
    out_ref[:, 0, :] = total[0:channels, 0:channels]


def correlate(previous, half, channels, total_rows):
    return pl.pallas_call(
        functools.partial(correlation_kernel, 1.0 / total_rows),
        in_specs=[WHOLE] * 2,
        out_specs=WHOLE,
        out_shape=matrix_shape(channels),
        scratch_shapes=[
            pltpu.VMEM((lower_rows(channels), LANES), jnp.float32),
            pltpu.VMEM((half.shape[0], round_up(channels, LANES)), jnp.float32),
        ],
        compiler_params=params(),
        cost_estimate=cost(10**8, 10**6),
    )(previous, half)


def from_behind(value, axis, steps):
    count = lax.axis_size(axis)
    leading, last = (max(0, -steps), min(count, count - steps))
    return lax.ppermute(value, axis, [(source, source + steps) for source in range(leading, last)])


def other_core(value):
    return lax.ppermute(value, "rows", [(s, s ^ 1) for s in range(lax.axis_size("rows"))])


def chip_rounds():
    count = lax.axis_size("rows")
    bits = []
    while 2 << len(bits) < count:
        bits.append(2 << len(bits))
    return [
        [(s, s ^ (bits[n] if s % 2 == 0 else bits[-1 - n])) for s in range(count)]
        for n in range(len(bits))
    ]


def shards(x_block, h_diag, h_right, pattern):
    x_t = x_block[0].T
    channels, block_rows = x_t.shape
    masks = pattern[0].transpose(1, 0, 2)
    total_rows = lax.axis_size("rows") * block_rows
    core = (lax.axis_index("rows") % 2).astype(jnp.int32).reshape(1)
    later = from_behind(x_t, "rows", -1)
    carried = from_behind(tile_product(1, masks, x_t, h_right[0], x_t.dtype, 53), "rows", 1)
    first = tile_product(0, masks, x_t, h_diag[0], jnp.float32, 50)
    part = later_product(masks, later, h_right[0], first)
    y_t, g_mine, g_other = gram(core, part, carried)
    previous_y = from_behind(y_t, "sector", 1)
    rounds = chip_rounds()
    g_sum = g_mine + other_core(g_other)
    r_mine, r_other = cross(core, x_t, y_t, g_sum, jnp.bfloat16)
    r_sum = add_after(r_mine, other_core(r_other))
    for n, pairs in enumerate(rounds):
        g_sum = add_after(g_sum, lax.ppermute(g_sum, "rows", pairs), r_sum)
        if n + 1 < len(rounds):
            r_sum = add_after(r_sum, lax.ppermute(r_sum, "rows", pairs))
    work = first_stage(core, g_sum, other_core(g_sum), channels, total_rows)
    r_sum = add_after(r_sum, lax.ppermute(r_sum, "rows", rounds[-1]), work)
    m_mine, m_other = cross(core, previous_y, y_t, r_sum, jnp.float32)
    m_sum = add_after(m_mine, other_core(m_other))
    inverse, pack = last_stages(work, channels, m_sum)
    previous = from_behind(pack, "sector", 1)
    rayleigh, token = unpack_ray(core, r_sum, other_core(r_sum), channels, total_rows)
    for pairs in rounds[:-1]:
        m_sum = add_after(m_sum, lax.ppermute(m_sum, "rows", pairs), inverse)
    m_sum = add_after(m_sum, lax.ppermute(m_sum, "rows", rounds[-1]), token)
    q_t = basis(inverse, y_t)
    half = half_product(core, m_sum, other_core(m_sum), inverse)
    correlation = correlate(previous, half, channels, total_rows)
    return (q_t.T[None], rayleigh.transpose(1, 0, 2), correlation.transpose(1, 0, 2))


def solution(mesh):
    in_specs = (
        P("sector", "rows", None),
        P("sector", "rows", None),
        P("sector", "rows", None),
        P("sector", None, "rows", None),
    )
    out_specs = (P("sector", "rows", None), P("sector", None, None), P("sector", None, None))
    return jax.shard_map(shards, mesh=mesh, in_specs=in_specs, out_specs=out_specs, check_vma=False)
```

```python
import functools

import jax
import jax.numpy as jnp
from jax import lax
from jax.experimental import pallas as pl
from jax.experimental.pallas import tpu as pltpu
from jax.sharding import PartitionSpec as P

SUBBLOCK = 128
LANES = 128
PANEL = 16
WHOLE = pl.BlockSpec(memory_space=pltpu.VMEM)
SCALARS = pl.BlockSpec(memory_space=pltpu.SMEM)
ANYWHERE = pl.BlockSpec(memory_space=pl.ANY)
MIB = 1024 * 1024
FIRST_STAGE_FLOPS = 3500 * 10**6
LAST_STAGES_FLOPS = 4 * 10**9


def params(mib=48):
    return pltpu.CompilerParams(vmem_limit_bytes=mib * MIB)


def cost(flops, bytes_accessed):
    return pl.CostEstimate(flops=flops, bytes_accessed=bytes_accessed, transcendentals=0)


def round_up(value, step):
    return (value + step - 1) // step * step


def dot(left, right, dims, precision=None):
    return lax.dot_general(
        left, right, (dims, ((), ())), precision=precision, preferred_element_type=jnp.float32
    )


def block_mask(mask_ref, which, cols):
    blocks = mask_ref[:, which, :].astype(jnp.float32)
    col = lax.broadcasted_iota(jnp.int32, (blocks.shape[1], cols), 1)
    block = lax.broadcasted_iota(jnp.int32, (blocks.shape[1], cols), 0)
    return dot(blocks, jnp.where(col // SUBBLOCK == block, 1.0, 0.0), ((1,), (0,)))


def mask_rows(tile_ref, mask, start, size):
    cols = tile_ref.shape[1]
    for i in range(start // SUBBLOCK, (start + size) // SUBBLOCK):
        keep = jnp.broadcast_to(mask[i : i + 1, :], (PANEL, cols)).astype(tile_ref.dtype)
        for row in range(i * SUBBLOCK, (i + 1) * SUBBLOCK, PANEL):
            tile_ref[row : row + PANEL, :] = tile_ref[row : row + PANEL, :] * keep


def strips(rows, width):
    return [(start, min(width, rows - start)) for start in range(0, rows, width)]


def halves(rows):
    first = rows // 512 * 256
    return [(0, first), (first, rows - first)] if first else [(0, rows)]


def copies_of(source, target, sems):
    copies = []
    for n, (start, size) in enumerate(halves(target.shape[0])):
        here = (pl.ds(start, size), slice(None))
        copies.append(pltpu.make_async_copy(source.at[here], target.at[here], sems.at[n]))
    return copies


def product(x_ref, tile_ref, copies, mask, sum_ref, out_ref):
    rows = tile_ref.shape[0]
    for n, (start, size) in enumerate(halves(rows)):
        copies[n].wait()
        mask_rows(tile_ref, mask, start, size)
        last = n + 1 == len(copies)
        for col, cols in strips(rows, 2 * SUBBLOCK):
            here = (slice(None), slice(col, col + cols))
            term = dot(
                x_ref[:, start : start + size],
                tile_ref[start : start + size, col : col + cols],
                ((1,), (0,)),
            )
            if n > 0:
                term = sum_ref[here] + term
            if last:
                out_ref[here] = term.astype(out_ref.dtype)
            else:
                sum_ref[here] = term


def tile_kernel(which, mask_ref, x_hbm, tile_hbm, out_ref, x_ref, tile_ref, sum_ref, x_sem, sems):
    rows = tile_ref.shape[0]
    copies = copies_of(tile_hbm, tile_ref, sems)
    copy_x = pltpu.make_async_copy(x_hbm, x_ref, x_sem)
    copy_x.start()
    for copy in copies:
        copy.start()
    mask = block_mask(mask_ref, which, rows)
    copy_x.wait()
    product(x_ref, tile_ref, copies, mask, sum_ref, out_ref)


def tile_product(which, masks, x_t, tile, dtype, mib):
    channels, rows = x_t.shape
    return pl.pallas_call(
        functools.partial(tile_kernel, which),
        in_specs=[WHOLE, ANYWHERE, ANYWHERE],
        out_specs=WHOLE,
        out_shape=jax.ShapeDtypeStruct((channels, rows), dtype),
        scratch_shapes=[
            pltpu.VMEM((channels, rows), x_t.dtype),
            pltpu.VMEM((rows, rows), tile.dtype),
            pltpu.VMEM((channels, rows), jnp.float32),
            pltpu.SemaphoreType.DMA,
            pltpu.SemaphoreType.DMA((2,)),
        ],
        compiler_params=params(mib),
        cost_estimate=cost(2 * channels * rows * rows, 2 * rows * rows),
    )(masks, x_t, tile)


def later_kernel(mask_ref, later_ref, tile_hbm, first_ref, out_ref, tile_ref, sems):
    rows = tile_ref.shape[0]
    copies = copies_of(tile_hbm, tile_ref, sems)
    for copy in copies:
        copy.start()
    mask = block_mask(mask_ref, 1, rows)
    for n, (start, size) in enumerate(halves(rows)):
        copies[n].wait()
        mask_rows(tile_ref, mask, start, size)
        for row, count in strips(size, 2 * SUBBLOCK):
            here = (slice(None), slice(start + row, start + row + count))
            out_ref[here] = first_ref[here] + dot(
                later_ref[...], tile_ref[start + row : start + row + count, :], ((1,), (1,))
            )


def later_product(masks, later, tile, first):
    channels, rows = later.shape
    return pl.pallas_call(
        later_kernel,
        in_specs=[WHOLE, WHOLE, ANYWHERE, WHOLE],
        out_specs=WHOLE,
        out_shape=jax.ShapeDtypeStruct((channels, rows), jnp.float32),
        scratch_shapes=[
            pltpu.VMEM((rows, rows), tile.dtype),
            pltpu.SemaphoreType.DMA((2,)),
        ],
        compiler_params=params(),
        cost_estimate=cost(2 * channels * rows * rows, 2 * rows * rows),
    )(masks, later, tile, first)


def lower_rows(channels):
    rows = round_up(channels, PANEL)
    return sum(rows - g * LANES for g in range(round_up(channels, LANES) // LANES))


def full_rows(channels):
    rows, wide = round_up(channels, PANEL), round_up(channels, LANES)
    whole = channels // LANES
    rest = rows - whole * LANES
    return round_up(whole * rows + rest * (wide // LANES), 4 * PANEL)


def lower_products(ref, out_ref):
    channels = ref.shape[0]
    rows = round_up(channels, PANEL)
    offset = 0
    for start, size in strips(channels, LANES):
        tall = rows - start
        if size < LANES:
            out_ref[offset : offset + tall, :] = jnp.zeros((tall, LANES), jnp.float32)
        elif rows > channels:
            out_ref[offset + channels - start : offset + tall, :] = jnp.zeros(
                (rows - channels, LANES), jnp.float32
            )
        out_ref[offset : offset + channels - start, 0:size] = dot(
            ref[start:channels, :], ref[start : start + size, :], ((1,), (1,))
        )
        offset += tall


def full_products(left_ref, right_ref, out_ref):
    channels = left_ref.shape[0]
    rows = round_up(channels, PANEL)
    whole = channels // LANES
    for g in range(whole):
        out_ref[g * rows : g * rows + channels, :] = dot(
            left_ref[...], right_ref[g * LANES : (g + 1) * LANES, :], ((1,), (1,))
        )
        if rows > channels:
            out_ref[g * rows + channels : (g + 1) * rows, :] = jnp.zeros(
                (rows - channels, LANES), jnp.float32
            )
    base = whole * rows
    if base < out_ref.shape[0]:
        out_ref[base:, :] = jnp.zeros((out_ref.shape[0] - base, LANES), jnp.float32)
    first, rest = whole * LANES, rows - whole * LANES
    for n, (start, size) in enumerate(strips(channels, LANES) if first < channels else []):
        place = base + n * rest
        out_ref[place : place + channels - first, 0:size] = dot(
            right_ref[first:channels, :], left_ref[start : start + size, :], ((1,), (1,))
        )


def full_matrix(pack_ref, channels):
    rows, wide = round_up(channels, PANEL), round_up(channels, LANES)
    whole = channels // LANES
    rest = rows - whole * LANES
    parts = [pack_ref[g * rows : (g + 1) * rows, :] for g in range(whole)]
    if rest:
        tail = jnp.concatenate(
            [
                pack_ref[whole * rows + g * rest : whole * rows + (g + 1) * rest, :]
                for g in range(wide // LANES)
            ],
            axis=1,
        )
        tail = jnp.concatenate([tail, jnp.zeros((LANES - rest, wide), tail.dtype)], axis=0)
        parts.append(tail.T[0:rows, :])
    return jnp.concatenate(parts, axis=1)


def folded_rows(channels):
    if channels < 2 * LANES:
        return lower_rows(channels)
    return lower_rows(channels) - LANES + PANEL


def corner(channels):
    return round_up(channels, PANEL)


def square_index():
    row = lax.broadcasted_iota(jnp.int32, (LANES, LANES), 0)
    return row, lax.broadcasted_iota(jnp.int32, (LANES, LANES), 1)


def fold(pack_ref, out_ref, channels, symmetric):
    if channels < 2 * LANES:
        out_ref[...] = pack_ref[...]
        return
    start = corner(channels)
    end = pack_ref.shape[0]
    row, lane = square_index()
    second = pack_ref[start : start + LANES, :]
    upper = second if symmetric else second.T
    out_ref[0:LANES, :] = jnp.where(row >= lane, pack_ref[0:LANES, :], upper)
    out_ref[LANES:start, :] = pack_ref[LANES:start, :]
    out_ref[start : end - LANES, :] = pack_ref[start + LANES : end, :]
    diagonal = jnp.sum(jnp.where(row == lane, second, 0.0), axis=0, keepdims=True)
    out_ref[end - LANES :, :] = jnp.broadcast_to(diagonal, (PANEL, LANES))


def unfold(folded_ref, pack_ref, channels, symmetric):
    if channels < 2 * LANES:
        pack_ref[...] = folded_ref[...]
        return
    start = corner(channels)
    end = pack_ref.shape[0]
    row, lane = square_index()
    both = folded_ref[0:LANES, :]
    turned = both.T
    first_upper, second_upper = (turned, both) if symmetric else (0.0, 0.0)
    pack_ref[0:LANES, :] = jnp.where(row >= lane, both, first_upper)
    pack_ref[LANES:start, :] = folded_ref[LANES:start, :]
    second = jnp.where(row > lane, turned, second_upper)
    diagonal = folded_ref[end - LANES : end - LANES + 1, :]
    pack_ref[start : start + LANES, :] = jnp.where(row == lane, diagonal, second)
    pack_ref[start + LANES : end, :] = folded_ref[start : end - LANES, :]


def cut(pack_ref, core, mine_ref, other_ref):
    half = mine_ref.shape[0]
    mine_ref[...] = pack_ref[pl.ds(pl.multiple_of(core * half, 8), half), :].astype(mine_ref.dtype)
    other_ref[...] = pack_ref[pl.ds(pl.multiple_of((1 - core) * half, 8), half), :].astype(
        other_ref.dtype
    )


def join(pack_ref, core, mine, other):
    half = mine.shape[0]
    pack_ref[pl.ds(pl.multiple_of(core * half, 8), half), :] = mine
    pack_ref[pl.ds(pl.multiple_of((1 - core) * half, 8), half), :] = other


def gram_kernel(core_ref, part_ref, carried_ref, y_ref, g_mine, g_other, gram_ref, folded_ref):
    image = part_ref[...] + carried_ref[...].astype(jnp.float32)
    y_ref[...] = image.astype(y_ref.dtype)
    lower_products(y_ref, gram_ref)
    fold(gram_ref, folded_ref, y_ref.shape[0], True)
    cut(folded_ref, core_ref[0], g_mine, g_other)


def gram(core, part, carried):
    channels, rows = carried.shape
    lower, folded = lower_rows(channels), folded_rows(channels)
    half = jax.ShapeDtypeStruct((folded // 2, LANES), jnp.float32)
    return pl.pallas_call(
        gram_kernel,
        in_specs=[SCALARS] + [WHOLE] * 2,
        out_specs=[WHOLE] * 3,
        out_shape=[jax.ShapeDtypeStruct((channels, rows), carried.dtype), half, half],
        scratch_shapes=[
            pltpu.VMEM((lower, LANES), jnp.float32),
            pltpu.VMEM((folded, LANES), jnp.float32),
        ],
        compiler_params=params(),
        cost_estimate=cost(2 * channels * channels * rows, 8 * channels * rows),
    )(core, part, carried)


def cross_kernel(core_ref, left_ref, right_ref, after_ref, mine_ref, other_ref, pack_ref):
    full_products(left_ref, right_ref, pack_ref)
    cut(pack_ref, core_ref[0], mine_ref, other_ref)


def cross(core, left, right, after, dtype):
    channels, rows = left.shape
    full = full_rows(channels)
    return pl.pallas_call(
        cross_kernel,
        in_specs=[SCALARS, WHOLE, WHOLE, ANYWHERE],
        out_specs=[WHOLE] * 2,
        out_shape=[jax.ShapeDtypeStruct((full // 2, LANES), dtype)] * 2,
        scratch_shapes=[pltpu.VMEM((full, LANES), jnp.float32)],
        compiler_params=params(),
        cost_estimate=cost(2 * channels * channels * rows, 4 * channels * rows),
    )(core, left, right, after)


def add_kernel(left_ref, right_ref, *refs):
    total = left_ref[...].astype(jnp.float32) + right_ref[...].astype(jnp.float32)
    refs[-1][...] = total.astype(refs[-1].dtype)


def add_after(left, right, *after):
    return pl.pallas_call(
        add_kernel,
        in_specs=[WHOLE] * 2 + [ANYWHERE] * len(after),
        out_specs=WHOLE,
        out_shape=jax.ShapeDtypeStruct(left.shape, left.dtype),
        compiler_params=params(),
        cost_estimate=cost(10**5, 10**5),
    )(left, right, *after)


def split3(value):
    high = value.astype(jnp.bfloat16)
    rest = value - high.astype(jnp.float32)
    mid = rest.astype(jnp.bfloat16)
    low = (rest - mid.astype(jnp.float32)).astype(jnp.bfloat16)
    return high, mid, low


def sublane(value, index):
    return jnp.broadcast_to(value[index : index + 1, :], value.shape)


def lane_of(value, index):
    return jnp.take_along_axis(value, jnp.broadcast_to(index, value.shape), axis=1)


def eliminate(columns, panel):
    half = 8
    row = lax.broadcasted_iota(jnp.int32, (half, LANES), 0)
    scales = [jnp.zeros((half, LANES), jnp.float32) for _ in range(2)]
    columns = [list(c) for c in columns]
    panel = [list(p) for p in panel]
    for j in range(0, PANEL, 2):
        h, r = divmod(j, half)
        left, right = columns[j], columns[j + 1]
        a, b, c = sublane(left[h], r), sublane(left[h], r + 1), sublane(right[h], r + 1)
        det = a * c - b * b
        inverse = pl.reciprocal(det, approx=True)
        first, second = [None, None], [None, None]
        for t in range(h, 2):
            x, y = left[t], right[t]
            if t == h:
                x, y = jnp.where(row > r + 1, x, 0.0), jnp.where(row > r + 1, y, 0.0)
            first[t] = (c * x - b * y) * inverse
            second[t] = (a * y - b * x) * inverse
        for later in range(j + 2, PANEL):
            q = later // half
            x, y = sublane(left[q], later % half), sublane(right[q], later % half)
            for t in range(max(h, q), 2):
                columns[later][t] = columns[later][t] - (first[t] * x + second[t] * y)
        inverse_a = pl.reciprocal(a, approx=True)
        first[h] = jnp.where(row == r + 1, b * inverse_a, first[h])
        for group in panel:
            x, y = sublane(group[h], r), sublane(group[h], r + 1)
            for t in range(h, 2):
                group[t] = group[t] - (first[t] * x + second[t] * y)
        scales[h] = jnp.where(row == r, lax.rsqrt(a), scales[h])
        scales[h] = jnp.where(row == r + 1, lax.rsqrt(det * inverse_a), scales[h])
    return [jnp.concatenate([g[0] * scales[0], g[1] * scales[1]], axis=0) for g in panel]


def fill_work(channels, scale, pack_ref, work_ref):
    rows, wide = work_ref.shape
    groups = wide // LANES
    offset = 0
    for g in range(groups):
        top = g * LANES
        size = min(LANES, rows - top)
        column = pack_ref[offset : offset + rows - top, :] * scale
        offset += rows - top
        diag = column[0:size, :]
        if top + LANES > channels:
            row = lax.broadcasted_iota(jnp.int32, diag.shape, 0)
            lane = lax.broadcasted_iota(jnp.int32, diag.shape, 1)
            diag = jnp.where((row == lane) & (lane + top >= channels), 1.0, diag)
        work_ref[top : top + size, top : top + LANES] = diag
        for below in range(g + 1, groups):
            start = (below - g) * LANES
            size_b = min(LANES, rows - below * LANES)
            block = column[start : start + size_b, :]
            if size_b < LANES:
                block = jnp.concatenate(
                    [block, jnp.zeros((LANES - size_b, LANES), jnp.float32)], axis=0
                )
            work_ref[top : top + size, below * LANES : (below + 1) * LANES] = block.T
            work_ref[below * LANES : below * LANES + size_b, top : top + LANES] = jnp.zeros(
                (size_b, LANES), jnp.float32
            )


def eliminate_group(g, work_ref, turned_ref):
    rows, wide = work_ref.shape
    groups = wide // LANES
    row = lax.broadcasted_iota(jnp.int32, (PANEL, LANES), 0)
    lane = lax.broadcasted_iota(jnp.int32, (PANEL, LANES), 1)
    top = g * LANES
    count = min(LANES, rows - top) // PANEL

    def load(local):
        place = pl.ds(pl.multiple_of(top + local, PANEL), PANEL)
        return [work_ref[place, q * LANES : (q + 1) * LANES] for q in range(groups)]

    def panel_step(b, parts, slot):
        local = b * PANEL
        following = jnp.minimum(local + PANEL, (count - 1) * PANEL)
        ahead = load(following)
        pivots = [parts[g][0:8, :], parts[g][8:16, :]]
        columns = [[lane_of(p, local + j) for p in pivots] for j in range(PANEL)]
        inside = (lane >= local) & (lane < local + PANEL)
        identity = jnp.where(lane - local == row, 1.0, 0.0)
        parts = list(parts)
        parts[g] = jnp.where(inside, identity, parts[g])
        done = eliminate(columns, [[p[0:8, :], p[8:16, :]] for p in parts])
        right = []
        for q in range(groups):
            high, mid, low = split3(done[q])
            right.append(jnp.concatenate([high, mid, high, low, mid, high], axis=0))
            if q >= g:
                if q == g:
                    high, mid, low = split3(jnp.where(lane >= local + PANEL, done[q], 0.0))
                left = jnp.concatenate([high, high, mid, high, mid, low], axis=0)
                turned_ref[slot, (q - g) * LANES : (q - g + 1) * LANES, :] = left.T
        right = jnp.concatenate(right, axis=1)
        near = turned_ref[slot, pl.ds(pl.multiple_of(following, PANEL), PANEL), :]
        update = dot(near, right, ((1,), (0,)))
        ahead[g] = jnp.where(inside, 0.0, ahead[g])
        ahead = [ahead[q] - update[:, q * LANES : (q + 1) * LANES] for q in range(groups)]
        for q in range(g, groups):
            low_row = q * LANES
            high_row = min(rows, low_row + LANES)
            base = low_row - top
            update = dot(turned_ref[slot, base : base + high_row - low_row, :], right, ((1,), (0,)))
            for c in range(groups):
                lanes = slice(c * LANES, (c + 1) * LANES)
                old = work_ref[low_row:high_row, lanes]
                if c == g:
                    here = lax.broadcasted_iota(jnp.int32, old.shape, 1)
                    old = jnp.where((here >= local) & (here < local + PANEL), 0.0, old)
                work_ref[low_row:high_row, lanes] = old - update[:, lanes]
        for q in range(groups):
            if q == g:
                done[q] = jnp.where(lane < local + PANEL, done[q], 0.0)
            elif q > g:
                done[q] = jnp.zeros_like(done[q])
            place = pl.ds(pl.multiple_of(top + local, PANEL), PANEL)
            work_ref[place, q * LANES : (q + 1) * LANES] = done[q]
        return ahead

    def two_panels(i, parts):
        return panel_step(2 * i + 1, panel_step(2 * i, parts, 0), 1)

    parts = lax.fori_loop(0, count // 2, two_panels, load(0))
    if count % 2:
        panel_step(jnp.int32(count - 1), parts, 0)


def first_stage_kernel(
    channels, scale, core_ref, mine_ref, other_ref, work_ref, pack_ref, folded_ref, turned_ref
):
    join(folded_ref, core_ref[0], mine_ref[...], other_ref[...])
    unfold(folded_ref, pack_ref, channels, True)
    fill_work(channels, scale, pack_ref, work_ref)
    eliminate_group(0, work_ref, turned_ref)


def last_stages_kernel(
    channels, before_ref, after_ref, work_ref, folded_ref, pack_ref, turned_ref
):
    work_ref[...] = before_ref[...]
    rows, wide = work_ref.shape
    for g in range(1, wide // LANES):
        eliminate_group(g, work_ref, turned_ref)
    offset = 0
    for q in range(wide // LANES):
        tall = rows - q * LANES
        pack_ref[offset : offset + tall, :] = work_ref[q * LANES : rows, q * LANES : (q + 1) * LANES]
        offset += tall
    fold(pack_ref, folded_ref, channels, False)


def turned_scratch(channels):
    return pltpu.VMEM((2, round_up(channels, LANES), 6 * PANEL), jnp.bfloat16)


def work_shape(channels):
    return jax.ShapeDtypeStruct((round_up(channels, PANEL), round_up(channels, LANES)), jnp.float32)


def first_stage(core, mine, other, channels, total_rows):
    return pl.pallas_call(
        functools.partial(first_stage_kernel, channels, 1.0 / total_rows),
        in_specs=[SCALARS] + [WHOLE] * 2,
        out_specs=WHOLE,
        out_shape=work_shape(channels),
        scratch_shapes=[
            pltpu.VMEM((lower_rows(channels), LANES), jnp.float32),
            pltpu.VMEM((folded_rows(channels), LANES), jnp.float32),
            turned_scratch(channels),
        ],
        compiler_params=params(),
        cost_estimate=cost(FIRST_STAGE_FLOPS, 10**6),
    )(core, mine, other)


def last_stages(work, channels, after):
    return pl.pallas_call(
        functools.partial(last_stages_kernel, channels),
        in_specs=[WHOLE, ANYWHERE],
        out_specs=[WHOLE] * 2,
        out_shape=[
            work_shape(channels),
            jax.ShapeDtypeStruct((folded_rows(channels), LANES), jnp.float32),
        ],
        scratch_shapes=[
            pltpu.VMEM((lower_rows(channels), LANES), jnp.float32),
            turned_scratch(channels),
        ],
        compiler_params=params(),
        cost_estimate=cost(LAST_STAGES_FLOPS, 10**5),
    )(work, after)


def split2(value):
    high = value.astype(jnp.bfloat16)
    return high, (value - high.astype(jnp.float32)).astype(jnp.bfloat16)


def dot3(left, right, dims):
    left_high, left_low = split2(left)
    right_high, right_low = split2(right)
    return (
        dot(left_high, right_high, dims)
        + dot(left_high, right_low, dims)
        + dot(left_low, right_high, dims)
    )


def lower_matrix(pack_ref, out_ref):
    rows, wide = out_ref.shape
    offset = 0
    for g in range(wide // LANES):
        top = g * LANES
        lanes = slice(top, top + LANES)
        if top:
            out_ref[0:top, lanes] = jnp.zeros((top, LANES), jnp.float32)
        out_ref[top:rows, lanes] = pack_ref[offset : offset + rows - top, :]
        offset += rows - top


def basis_kernel(inverse_ref, y_ref, q_ref):
    channels = y_ref.shape[0]
    image = y_ref[...]
    for start, size in strips(channels, 2 * LANES):
        used = min(channels, start + size)
        high, low = split2(inverse_ref[start : start + size, 0:used])
        both = dot(jnp.concatenate([high, low], axis=0), image[0:used, :], ((1,), (0,)))
        q_ref[start : start + size, :] = (both[0:size, :] + both[size:, :]).astype(q_ref.dtype)


def basis(inverse, y_t):
    channels, rows = y_t.shape
    return pl.pallas_call(
        basis_kernel,
        in_specs=[WHOLE] * 2,
        out_specs=WHOLE,
        out_shape=jax.ShapeDtypeStruct(y_t.shape, y_t.dtype),
        compiler_params=params(),
        cost_estimate=cost(10**5, 10**5),
    )(inverse, y_t)


def matrix_shape(channels):
    return jax.ShapeDtypeStruct((channels, 1, channels), jnp.float32)


def ray_kernel(scale, core_ref, mine_ref, other_ref, out_ref, token_ref, pack_ref):
    token_ref[...] = jnp.zeros_like(token_ref)
    channels = out_ref.shape[0]
    join(pack_ref, core_ref[0], mine_ref[...].astype(jnp.float32), other_ref[...].astype(jnp.float32))
    out_ref[:, 0, :] = full_matrix(pack_ref, channels)[0:channels, 0:channels] * scale


def unpack_ray(core, mine, other, channels, total_rows):
    return pl.pallas_call(
        functools.partial(ray_kernel, 1.0 / total_rows),
        in_specs=[SCALARS] + [WHOLE] * 2,
        out_specs=[WHOLE] * 2,
        out_shape=[matrix_shape(channels), jax.ShapeDtypeStruct((8, LANES), jnp.float32)],
        scratch_shapes=[pltpu.VMEM((full_rows(channels), LANES), jnp.float32)],
        compiler_params=params(),
        cost_estimate=cost(10**5, 10**5),
    )(core, mine, other)


def half_kernel(core_ref, mine_ref, other_ref, inverse_ref, out_ref, pack_ref):
    join(pack_ref, core_ref[0], mine_ref[...], other_ref[...])
    mixed = full_matrix(pack_ref, inverse_ref.shape[0])
    out_ref[...] = dot3(mixed, inverse_ref[...], ((1,), (1,)))


def half_product(core, mine, other, inverse):
    rows = inverse.shape[0]
    return pl.pallas_call(
        half_kernel,
        in_specs=[SCALARS] + [WHOLE] * 3,
        out_specs=WHOLE,
        out_shape=jax.ShapeDtypeStruct((rows, rows), jnp.float32),
        scratch_shapes=[pltpu.VMEM((2 * mine.shape[0], LANES), jnp.float32)],
        compiler_params=params(),
        cost_estimate=cost(10**5, 10**5),
    )(core, mine, other, inverse)


def correlation_kernel(scale, previous_ref, half_ref, out_ref, pack_ref, before_ref):
    channels = out_ref.shape[0]
    rows = half_ref.shape[0]
    unfold(previous_ref, pack_ref, channels, False)
    lower_matrix(pack_ref, before_ref)
    total = dot3(before_ref[:, 0:rows], half_ref[...], ((1,), (0,))) * scale
    out_ref[:, 0, :] = total[0:channels, 0:channels]


def correlate(previous, half, channels, total_rows):
    return pl.pallas_call(
        functools.partial(correlation_kernel, 1.0 / total_rows),
        in_specs=[WHOLE] * 2,
        out_specs=WHOLE,
        out_shape=matrix_shape(channels),
        scratch_shapes=[
            pltpu.VMEM((lower_rows(channels), LANES), jnp.float32),
            pltpu.VMEM((half.shape[0], round_up(channels, LANES)), jnp.float32),
        ],
        compiler_params=params(),
        cost_estimate=cost(10**8, 10**6),
    )(previous, half)


def from_behind(value, axis, steps):
    count = lax.axis_size(axis)
    leading, last = (max(0, -steps), min(count, count - steps))
    return lax.ppermute(value, axis, [(source, source + steps) for source in range(leading, last)])


def other_core(value):
    return lax.ppermute(value, "rows", [(s, s ^ 1) for s in range(lax.axis_size("rows"))])


def chip_rounds():
    count = lax.axis_size("rows")
    bits = []
    while 2 << len(bits) < count:
        bits.append(2 << len(bits))
    return [
        [(s, s ^ (bits[n] if s % 2 == 0 else bits[-1 - n])) for s in range(count)]
        for n in range(len(bits))
    ]


def shards(x_block, h_diag, h_right, pattern):
    x_t = x_block[0].T
    channels, block_rows = x_t.shape
    masks = pattern[0].transpose(1, 0, 2)
    total_rows = lax.axis_size("rows") * block_rows
    core = (lax.axis_index("rows") % 2).astype(jnp.int32).reshape(1)
    later = from_behind(x_t, "rows", -1)
    carried = from_behind(tile_product(1, masks, x_t, h_right[0], x_t.dtype, 53), "rows", 1)
    first = tile_product(0, masks, x_t, h_diag[0], jnp.float32, 50)
    part = later_product(masks, later, h_right[0], first)
    y_t, g_mine, g_other = gram(core, part, carried)
    previous_y = from_behind(y_t, "sector", 1)
    rounds = chip_rounds()
    g_sum = g_mine + other_core(g_other)
    r_mine, r_other = cross(core, x_t, y_t, g_sum, jnp.bfloat16)
    r_sum = add_after(r_mine, other_core(r_other))
    for n, pairs in enumerate(rounds):
        g_sum = add_after(g_sum, lax.ppermute(g_sum, "rows", pairs), r_sum)
        if n + 1 < len(rounds):
            r_sum = add_after(r_sum, lax.ppermute(r_sum, "rows", pairs))
    work = first_stage(core, g_sum, other_core(g_sum), channels, total_rows)
    r_sum = add_after(r_sum, lax.ppermute(r_sum, "rows", rounds[-1]), work)
    m_mine, m_other = cross(core, previous_y, y_t, r_sum, jnp.float32)
    m_sum = add_after(m_mine, other_core(m_other))
    inverse, pack = last_stages(work, channels, m_sum)
    previous = from_behind(pack, "sector", 1)
    rayleigh, token = unpack_ray(core, r_sum, other_core(r_sum), channels, total_rows)
    for pairs in rounds[:-1]:
        m_sum = add_after(m_sum, lax.ppermute(m_sum, "rows", pairs), inverse)
    m_sum = add_after(m_sum, lax.ppermute(m_sum, "rows", rounds[-1]), token)
    q_t = basis(inverse, y_t)
    half = half_product(core, m_sum, other_core(m_sum), inverse)
    correlation = correlate(previous, half, channels, total_rows)
    return (q_t.T[None], rayleigh.transpose(1, 0, 2), correlation.transpose(1, 0, 2))


def solution(mesh):
    in_specs = (
        P("sector", "rows", None),
        P("sector", "rows", None),
        P("sector", "rows", None),
        P("sector", None, "rows", None),
    )
    out_specs = (P("sector", "rows", None), P("sector", None, None), P("sector", None, None))
    return jax.shard_map(shards, mesh=mesh, in_specs=in_specs, out_specs=out_specs, check_vma=False)
```

```python
import functools

import jax
import jax.numpy as jnp
from jax import lax
from jax.experimental import pallas as pl
from jax.experimental.pallas import tpu as pltpu
from jax.sharding import PartitionSpec as P

SUBBLOCK = 128
LANES = 128
PANEL = 16
EARLY_PANELS = 4
WHOLE = pl.BlockSpec(memory_space=pltpu.VMEM)
SCALARS = pl.BlockSpec(memory_space=pltpu.SMEM)
ANYWHERE = pl.BlockSpec(memory_space=pl.ANY)
MIB = 1024 * 1024
FIRST_STAGE_FLOPS = 3500 * 10**6
LAST_STAGES_FLOPS = 4 * 10**9


def params(mib=48):
    return pltpu.CompilerParams(vmem_limit_bytes=mib * MIB)


def cost(flops, bytes_accessed):
    return pl.CostEstimate(flops=flops, bytes_accessed=bytes_accessed, transcendentals=0)


def round_up(value, step):
    return (value + step - 1) // step * step


def dot(left, right, dims, precision=None):
    return lax.dot_general(
        left, right, (dims, ((), ())), precision=precision, preferred_element_type=jnp.float32
    )


def block_mask(mask_ref, which, cols):
    blocks = mask_ref[:, which, :].astype(jnp.float32)
    col = lax.broadcasted_iota(jnp.int32, (blocks.shape[1], cols), 1)
    block = lax.broadcasted_iota(jnp.int32, (blocks.shape[1], cols), 0)
    return dot(blocks, jnp.where(col // SUBBLOCK == block, 1.0, 0.0), ((1,), (0,)))


def mask_rows(tile_ref, mask, start, size):
    cols = tile_ref.shape[1]
    for i in range(start // SUBBLOCK, (start + size) // SUBBLOCK):
        keep = jnp.broadcast_to(mask[i : i + 1, :], (PANEL, cols)).astype(tile_ref.dtype)
        for row in range(i * SUBBLOCK, (i + 1) * SUBBLOCK, PANEL):
            tile_ref[row : row + PANEL, :] = tile_ref[row : row + PANEL, :] * keep


def strips(rows, width):
    return [(start, min(width, rows - start)) for start in range(0, rows, width)]


def halves(rows):
    first = rows // 512 * 256
    return [(0, first), (first, rows - first)] if first else [(0, rows)]


def copies_of(source, target, sems):
    copies = []
    for n, (start, size) in enumerate(halves(target.shape[0])):
        here = (pl.ds(start, size), slice(None))
        copies.append(pltpu.make_async_copy(source.at[here], target.at[here], sems.at[n]))
    return copies


def product(x_ref, tile_ref, copies, mask, sum_ref, out_ref):
    rows = tile_ref.shape[0]
    for n, (start, size) in enumerate(halves(rows)):
        copies[n].wait()
        mask_rows(tile_ref, mask, start, size)
        last = n + 1 == len(copies)
        for col, cols in strips(rows, 2 * SUBBLOCK):
            here = (slice(None), slice(col, col + cols))
            term = dot(
                x_ref[:, start : start + size],
                tile_ref[start : start + size, col : col + cols],
                ((1,), (0,)),
            )
            if n > 0:
                term = sum_ref[here] + term
            if last:
                out_ref[here] = term.astype(out_ref.dtype)
            else:
                sum_ref[here] = term


def tile_kernel(which, mask_ref, x_hbm, tile_hbm, out_ref, x_ref, tile_ref, sum_ref, x_sem, sems):
    rows = tile_ref.shape[0]
    copies = copies_of(tile_hbm, tile_ref, sems)
    copy_x = pltpu.make_async_copy(x_hbm, x_ref, x_sem)
    copy_x.start()
    for copy in copies:
        copy.start()
    mask = block_mask(mask_ref, which, rows)
    copy_x.wait()
    product(x_ref, tile_ref, copies, mask, sum_ref, out_ref)


def tile_product(which, masks, x_t, tile, dtype, mib):
    channels, rows = x_t.shape
    return pl.pallas_call(
        functools.partial(tile_kernel, which),
        in_specs=[WHOLE, ANYWHERE, ANYWHERE],
        out_specs=WHOLE,
        out_shape=jax.ShapeDtypeStruct((channels, rows), dtype),
        scratch_shapes=[
            pltpu.VMEM((channels, rows), x_t.dtype),
            pltpu.VMEM((rows, rows), tile.dtype),
            pltpu.VMEM((channels, rows), jnp.float32),
            pltpu.SemaphoreType.DMA,
            pltpu.SemaphoreType.DMA((2,)),
        ],
        compiler_params=params(mib),
        cost_estimate=cost(2 * channels * rows * rows, 2 * rows * rows),
    )(masks, x_t, tile)


def later_kernel(mask_ref, later_ref, tile_hbm, first_ref, out_ref, tile_ref, sems):
    rows = tile_ref.shape[0]
    copies = copies_of(tile_hbm, tile_ref, sems)
    for copy in copies:
        copy.start()
    mask = block_mask(mask_ref, 1, rows)
    for n, (start, size) in enumerate(halves(rows)):
        copies[n].wait()
        mask_rows(tile_ref, mask, start, size)
        for row, count in strips(size, 2 * SUBBLOCK):
            here = (slice(None), slice(start + row, start + row + count))
            out_ref[here] = first_ref[here] + dot(
                later_ref[...], tile_ref[start + row : start + row + count, :], ((1,), (1,))
            )


def later_product(masks, later, tile, first):
    channels, rows = later.shape
    return pl.pallas_call(
        later_kernel,
        in_specs=[WHOLE, WHOLE, ANYWHERE, WHOLE],
        out_specs=WHOLE,
        out_shape=jax.ShapeDtypeStruct((channels, rows), jnp.float32),
        scratch_shapes=[
            pltpu.VMEM((rows, rows), tile.dtype),
            pltpu.SemaphoreType.DMA((2,)),
        ],
        compiler_params=params(),
        cost_estimate=cost(2 * channels * rows * rows, 2 * rows * rows),
    )(masks, later, tile, first)


def lower_rows(channels):
    rows = round_up(channels, PANEL)
    return sum(rows - g * LANES for g in range(round_up(channels, LANES) // LANES))


def full_rows(channels):
    rows, wide = round_up(channels, PANEL), round_up(channels, LANES)
    whole = channels // LANES
    rest = rows - whole * LANES
    return round_up(whole * rows + rest * (wide // LANES), 4 * PANEL)


def lower_products(ref, out_ref):
    channels = ref.shape[0]
    rows = round_up(channels, PANEL)
    offset = 0
    for start, size in strips(channels, LANES):
        tall = rows - start
        if size < LANES:
            out_ref[offset : offset + tall, :] = jnp.zeros((tall, LANES), jnp.float32)
        elif rows > channels:
            out_ref[offset + channels - start : offset + tall, :] = jnp.zeros(
                (rows - channels, LANES), jnp.float32
            )
        out_ref[offset : offset + channels - start, 0:size] = dot(
            ref[start:channels, :], ref[start : start + size, :], ((1,), (1,))
        )
        offset += tall


def full_products(left_ref, right_ref, out_ref):
    channels = left_ref.shape[0]
    rows = round_up(channels, PANEL)
    whole = channels // LANES
    for g in range(whole):
        out_ref[g * rows : g * rows + channels, :] = dot(
            left_ref[...], right_ref[g * LANES : (g + 1) * LANES, :], ((1,), (1,))
        )
        if rows > channels:
            out_ref[g * rows + channels : (g + 1) * rows, :] = jnp.zeros(
                (rows - channels, LANES), jnp.float32
            )
    base = whole * rows
    if base < out_ref.shape[0]:
        out_ref[base:, :] = jnp.zeros((out_ref.shape[0] - base, LANES), jnp.float32)
    first, rest = whole * LANES, rows - whole * LANES
    for n, (start, size) in enumerate(strips(channels, LANES) if first < channels else []):
        place = base + n * rest
        out_ref[place : place + channels - first, 0:size] = dot(
            right_ref[first:channels, :], left_ref[start : start + size, :], ((1,), (1,))
        )


def full_matrix(pack_ref, channels):
    rows, wide = round_up(channels, PANEL), round_up(channels, LANES)
    whole = channels // LANES
    rest = rows - whole * LANES
    parts = [pack_ref[g * rows : (g + 1) * rows, :] for g in range(whole)]
    if rest:
        tail = jnp.concatenate(
            [
                pack_ref[whole * rows + g * rest : whole * rows + (g + 1) * rest, :]
                for g in range(wide // LANES)
            ],
            axis=1,
        )
        tail = jnp.concatenate([tail, jnp.zeros((LANES - rest, wide), tail.dtype)], axis=0)
        parts.append(tail.T[0:rows, :])
    return jnp.concatenate(parts, axis=1)


def folded_rows(channels):
    if channels < 2 * LANES:
        return lower_rows(channels)
    return lower_rows(channels) - LANES + PANEL


def corner(channels):
    return round_up(channels, PANEL)


def square_index():
    row = lax.broadcasted_iota(jnp.int32, (LANES, LANES), 0)
    return row, lax.broadcasted_iota(jnp.int32, (LANES, LANES), 1)


def fold(pack_ref, out_ref, channels, symmetric):
    if channels < 2 * LANES:
        out_ref[...] = pack_ref[...]
        return
    start = corner(channels)
    end = pack_ref.shape[0]
    row, lane = square_index()
    second = pack_ref[start : start + LANES, :]
    upper = second if symmetric else second.T
    out_ref[0:LANES, :] = jnp.where(row >= lane, pack_ref[0:LANES, :], upper)
    out_ref[LANES:start, :] = pack_ref[LANES:start, :]
    out_ref[start : end - LANES, :] = pack_ref[start + LANES : end, :]
    diagonal = jnp.sum(jnp.where(row == lane, second, 0.0), axis=0, keepdims=True)
    out_ref[end - LANES :, :] = jnp.broadcast_to(diagonal, (PANEL, LANES))


def unfold(folded_ref, pack_ref, channels, symmetric):
    if channels < 2 * LANES:
        pack_ref[...] = folded_ref[...]
        return
    start = corner(channels)
    end = pack_ref.shape[0]
    row, lane = square_index()
    both = folded_ref[0:LANES, :]
    turned = both.T
    first_upper, second_upper = (turned, both) if symmetric else (0.0, 0.0)
    pack_ref[0:LANES, :] = jnp.where(row >= lane, both, first_upper)
    pack_ref[LANES:start, :] = folded_ref[LANES:start, :]
    second = jnp.where(row > lane, turned, second_upper)
    diagonal = folded_ref[end - LANES : end - LANES + 1, :]
    pack_ref[start : start + LANES, :] = jnp.where(row == lane, diagonal, second)
    pack_ref[start + LANES : end, :] = folded_ref[start : end - LANES, :]


def cut(pack_ref, core, mine_ref, other_ref):
    half = mine_ref.shape[0]
    mine_ref[...] = pack_ref[pl.ds(pl.multiple_of(core * half, 8), half), :].astype(mine_ref.dtype)
    other_ref[...] = pack_ref[pl.ds(pl.multiple_of((1 - core) * half, 8), half), :].astype(
        other_ref.dtype
    )


def join(pack_ref, core, mine, other):
    half = mine.shape[0]
    pack_ref[pl.ds(pl.multiple_of(core * half, 8), half), :] = mine
    pack_ref[pl.ds(pl.multiple_of((1 - core) * half, 8), half), :] = other


def gram_kernel(core_ref, part_ref, carried_ref, y_ref, g_mine, g_other, gram_ref, folded_ref):
    image = part_ref[...] + carried_ref[...].astype(jnp.float32)
    y_ref[...] = image.astype(y_ref.dtype)
    lower_products(y_ref, gram_ref)
    fold(gram_ref, folded_ref, y_ref.shape[0], True)
    cut(folded_ref, core_ref[0], g_mine, g_other)


def gram(core, part, carried):
    channels, rows = carried.shape
    lower, folded = lower_rows(channels), folded_rows(channels)
    half = jax.ShapeDtypeStruct((folded // 2, LANES), jnp.float32)
    return pl.pallas_call(
        gram_kernel,
        in_specs=[SCALARS] + [WHOLE] * 2,
        out_specs=[WHOLE] * 3,
        out_shape=[jax.ShapeDtypeStruct((channels, rows), carried.dtype), half, half],
        scratch_shapes=[
            pltpu.VMEM((lower, LANES), jnp.float32),
            pltpu.VMEM((folded, LANES), jnp.float32),
        ],
        compiler_params=params(),
        cost_estimate=cost(2 * channels * channels * rows, 8 * channels * rows),
    )(core, part, carried)


def cross_kernel(core_ref, left_ref, right_ref, after_ref, mine_ref, other_ref, pack_ref):
    full_products(left_ref, right_ref, pack_ref)
    cut(pack_ref, core_ref[0], mine_ref, other_ref)


def cross(core, left, right, after, dtype):
    channels, rows = left.shape
    full = full_rows(channels)
    return pl.pallas_call(
        cross_kernel,
        in_specs=[SCALARS, WHOLE, WHOLE, ANYWHERE],
        out_specs=[WHOLE] * 2,
        out_shape=[jax.ShapeDtypeStruct((full // 2, LANES), dtype)] * 2,
        scratch_shapes=[pltpu.VMEM((full, LANES), jnp.float32)],
        compiler_params=params(),
        cost_estimate=cost(2 * channels * channels * rows, 4 * channels * rows),
    )(core, left, right, after)


def add_kernel(left_ref, right_ref, *refs):
    total = left_ref[...].astype(jnp.float32) + right_ref[...].astype(jnp.float32)
    refs[-1][...] = total.astype(refs[-1].dtype)


def add_after(left, right, *after):
    return pl.pallas_call(
        add_kernel,
        in_specs=[WHOLE] * 2 + [ANYWHERE] * len(after),
        out_specs=WHOLE,
        out_shape=jax.ShapeDtypeStruct(left.shape, left.dtype),
        compiler_params=params(),
        cost_estimate=cost(10**5, 10**5),
    )(left, right, *after)


def split3(value):
    high = value.astype(jnp.bfloat16)
    rest = value - high.astype(jnp.float32)
    mid = rest.astype(jnp.bfloat16)
    low = (rest - mid.astype(jnp.float32)).astype(jnp.bfloat16)
    return high, mid, low


def sublane(value, index):
    return jnp.broadcast_to(value[index : index + 1, :], value.shape)


def lane_of(value, index):
    return jnp.take_along_axis(value, jnp.broadcast_to(index, value.shape), axis=1)


def eliminate(columns, panel):
    half = 8
    row = lax.broadcasted_iota(jnp.int32, (half, LANES), 0)
    scales = [jnp.zeros((half, LANES), jnp.float32) for _ in range(2)]
    columns = [list(c) for c in columns]
    panel = [list(p) for p in panel]
    for j in range(0, PANEL, 2):
        h, r = divmod(j, half)
        left, right = columns[j], columns[j + 1]
        a, b, c = sublane(left[h], r), sublane(left[h], r + 1), sublane(right[h], r + 1)
        det = a * c - b * b
        inverse = pl.reciprocal(det, approx=True)
        first, second = [None, None], [None, None]
        for t in range(h, 2):
            x, y = left[t], right[t]
            if t == h:
                x, y = jnp.where(row > r + 1, x, 0.0), jnp.where(row > r + 1, y, 0.0)
            first[t] = (c * x - b * y) * inverse
            second[t] = (a * y - b * x) * inverse
        for later in range(j + 2, PANEL):
            q = later // half
            x, y = sublane(left[q], later % half), sublane(right[q], later % half)
            for t in range(max(h, q), 2):
                columns[later][t] = columns[later][t] - (first[t] * x + second[t] * y)
        inverse_a = pl.reciprocal(a, approx=True)
        first[h] = jnp.where(row == r + 1, b * inverse_a, first[h])
        for group in panel:
            x, y = sublane(group[h], r), sublane(group[h], r + 1)
            for t in range(h, 2):
                group[t] = group[t] - (first[t] * x + second[t] * y)
        scales[h] = jnp.where(row == r, lax.rsqrt(a), scales[h])
        scales[h] = jnp.where(row == r + 1, lax.rsqrt(det * inverse_a), scales[h])
    return [jnp.concatenate([g[0] * scales[0], g[1] * scales[1]], axis=0) for g in panel]


def fill_work(channels, scale, pack_ref, work_ref):
    rows, wide = work_ref.shape
    groups = wide // LANES
    offset = 0
    for g in range(groups):
        top = g * LANES
        size = min(LANES, rows - top)
        column = pack_ref[offset : offset + rows - top, :] * scale
        offset += rows - top
        diag = column[0:size, :]
        if top + LANES > channels:
            row = lax.broadcasted_iota(jnp.int32, diag.shape, 0)
            lane = lax.broadcasted_iota(jnp.int32, diag.shape, 1)
            diag = jnp.where((row == lane) & (lane + top >= channels), 1.0, diag)
        work_ref[top : top + size, top : top + LANES] = diag
        for below in range(g + 1, groups):
            start = (below - g) * LANES
            size_b = min(LANES, rows - below * LANES)
            block = column[start : start + size_b, :]
            if size_b < LANES:
                block = jnp.concatenate(
                    [block, jnp.zeros((LANES - size_b, LANES), jnp.float32)], axis=0
                )
            work_ref[top : top + size, below * LANES : (below + 1) * LANES] = block.T
            work_ref[below * LANES : below * LANES + size_b, top : top + LANES] = jnp.zeros(
                (size_b, LANES), jnp.float32
            )


def eliminate_group(g, work_ref, turned_ref, first=0, last=LANES // PANEL):
    rows, wide = work_ref.shape
    groups = wide // LANES
    row = lax.broadcasted_iota(jnp.int32, (PANEL, LANES), 0)
    lane = lax.broadcasted_iota(jnp.int32, (PANEL, LANES), 1)
    top = g * LANES
    count = min(LANES, rows - top) // PANEL

    def load(local):
        place = pl.ds(pl.multiple_of(top + local, PANEL), PANEL)
        return [work_ref[place, q * LANES : (q + 1) * LANES] for q in range(groups)]

    def panel_step(b, parts, slot):
        local = b * PANEL
        following = jnp.minimum(local + PANEL, (count - 1) * PANEL)
        ahead = load(following)
        pivots = [parts[g][0:8, :], parts[g][8:16, :]]
        columns = [[lane_of(p, local + j) for p in pivots] for j in range(PANEL)]
        inside = (lane >= local) & (lane < local + PANEL)
        identity = jnp.where(lane - local == row, 1.0, 0.0)
        parts = list(parts)
        parts[g] = jnp.where(inside, identity, parts[g])
        done = eliminate(columns, [[p[0:8, :], p[8:16, :]] for p in parts])
        right = []
        for q in range(groups):
            high, mid, low = split3(done[q])
            right.append(jnp.concatenate([high, mid, high, low, mid, high], axis=0))
            if q >= g:
                if q == g:
                    high, mid, low = split3(jnp.where(lane >= local + PANEL, done[q], 0.0))
                left = jnp.concatenate([high, high, mid, high, mid, low], axis=0)
                turned_ref[slot, (q - g) * LANES : (q - g + 1) * LANES, :] = left.T
        right = jnp.concatenate(right, axis=1)
        near = turned_ref[slot, pl.ds(pl.multiple_of(following, PANEL), PANEL), :]
        update = dot(near, right, ((1,), (0,)))
        ahead[g] = jnp.where(inside, 0.0, ahead[g])
        ahead = [ahead[q] - update[:, q * LANES : (q + 1) * LANES] for q in range(groups)]
        for q in range(g, groups):
            low_row = q * LANES
            high_row = min(rows, low_row + LANES)
            base = low_row - top
            update = dot(turned_ref[slot, base : base + high_row - low_row, :], right, ((1,), (0,)))
            for c in range(groups):
                lanes = slice(c * LANES, (c + 1) * LANES)
                old = work_ref[low_row:high_row, lanes]
                if c == g:
                    here = lax.broadcasted_iota(jnp.int32, old.shape, 1)
                    old = jnp.where((here >= local) & (here < local + PANEL), 0.0, old)
                work_ref[low_row:high_row, lanes] = old - update[:, lanes]
        for q in range(groups):
            if q == g:
                done[q] = jnp.where(lane < local + PANEL, done[q], 0.0)
            elif q > g:
                done[q] = jnp.zeros_like(done[q])
            place = pl.ds(pl.multiple_of(top + local, PANEL), PANEL)
            work_ref[place, q * LANES : (q + 1) * LANES] = done[q]
        return ahead

    def two_panels(i, parts):
        return panel_step(first + 2 * i + 1, panel_step(first + 2 * i, parts, 0), 1)

    last = min(last, count)
    parts = lax.fori_loop(0, (last - first) // 2, two_panels, load(first * PANEL))
    if (last - first) % 2:
        panel_step(jnp.int32(last - 1), parts, 0)


def first_stage_kernel(
    channels, scale, core_ref, mine_ref, other_ref, work_ref, pack_ref, folded_ref, turned_ref
):
    join(folded_ref, core_ref[0], mine_ref[...], other_ref[...])
    unfold(folded_ref, pack_ref, channels, True)
    fill_work(channels, scale, pack_ref, work_ref)
    eliminate_group(0, work_ref, turned_ref)
    if work_ref.shape[1] > LANES:
        eliminate_group(1, work_ref, turned_ref, 0, EARLY_PANELS)


def last_stages_kernel(
    channels, before_ref, after_ref, work_ref, folded_ref, pack_ref, turned_ref
):
    work_ref[...] = before_ref[...]
    rows, wide = work_ref.shape
    for g in range(1, wide // LANES):
        eliminate_group(g, work_ref, turned_ref, EARLY_PANELS if g == 1 else 0)
    offset = 0
    for q in range(wide // LANES):
        tall = rows - q * LANES
        pack_ref[offset : offset + tall, :] = work_ref[q * LANES : rows, q * LANES : (q + 1) * LANES]
        offset += tall
    fold(pack_ref, folded_ref, channels, False)


def turned_scratch(channels):
    return pltpu.VMEM((2, round_up(channels, LANES), 6 * PANEL), jnp.bfloat16)


def work_shape(channels):
    return jax.ShapeDtypeStruct((round_up(channels, PANEL), round_up(channels, LANES)), jnp.float32)


def first_stage(core, mine, other, channels, total_rows):
    return pl.pallas_call(
        functools.partial(first_stage_kernel, channels, 1.0 / total_rows),
        in_specs=[SCALARS] + [WHOLE] * 2,
        out_specs=WHOLE,
        out_shape=work_shape(channels),
        scratch_shapes=[
            pltpu.VMEM((lower_rows(channels), LANES), jnp.float32),
            pltpu.VMEM((folded_rows(channels), LANES), jnp.float32),
            turned_scratch(channels),
        ],
        compiler_params=params(),
        cost_estimate=cost(FIRST_STAGE_FLOPS, 10**6),
    )(core, mine, other)


def last_stages(work, channels, after):
    return pl.pallas_call(
        functools.partial(last_stages_kernel, channels),
        in_specs=[WHOLE, ANYWHERE],
        out_specs=[WHOLE] * 2,
        out_shape=[
            work_shape(channels),
            jax.ShapeDtypeStruct((folded_rows(channels), LANES), jnp.float32),
        ],
        scratch_shapes=[
            pltpu.VMEM((lower_rows(channels), LANES), jnp.float32),
            turned_scratch(channels),
        ],
        compiler_params=params(),
        cost_estimate=cost(LAST_STAGES_FLOPS, 10**5),
    )(work, after)


def split2(value):
    high = value.astype(jnp.bfloat16)
    return high, (value - high.astype(jnp.float32)).astype(jnp.bfloat16)


def dot3(left, right, dims):
    left_high, left_low = split2(left)
    right_high, right_low = split2(right)
    return (
        dot(left_high, right_high, dims)
        + dot(left_high, right_low, dims)
        + dot(left_low, right_high, dims)
    )


def lower_matrix(pack_ref, out_ref):
    rows, wide = out_ref.shape
    offset = 0
    for g in range(wide // LANES):
        top = g * LANES
        lanes = slice(top, top + LANES)
        if top:
            out_ref[0:top, lanes] = jnp.zeros((top, LANES), jnp.float32)
        out_ref[top:rows, lanes] = pack_ref[offset : offset + rows - top, :]
        offset += rows - top


def basis_kernel(inverse_ref, y_ref, q_ref):
    channels = y_ref.shape[0]
    image = y_ref[...]
    for start, size in strips(channels, 2 * LANES):
        used = min(channels, start + size)
        high, low = split2(inverse_ref[start : start + size, 0:used])
        both = dot(jnp.concatenate([high, low], axis=0), image[0:used, :], ((1,), (0,)))
        q_ref[start : start + size, :] = (both[0:size, :] + both[size:, :]).astype(q_ref.dtype)


def basis(inverse, y_t):
    channels, rows = y_t.shape
    return pl.pallas_call(
        basis_kernel,
        in_specs=[WHOLE] * 2,
        out_specs=WHOLE,
        out_shape=jax.ShapeDtypeStruct(y_t.shape, y_t.dtype),
        compiler_params=params(),
        cost_estimate=cost(10**5, 10**5),
    )(inverse, y_t)


def matrix_shape(channels):
    return jax.ShapeDtypeStruct((channels, 1, channels), jnp.float32)


def ray_kernel(scale, core_ref, mine_ref, other_ref, out_ref, token_ref, pack_ref):
    token_ref[...] = jnp.zeros_like(token_ref)
    channels = out_ref.shape[0]
    join(pack_ref, core_ref[0], mine_ref[...].astype(jnp.float32), other_ref[...].astype(jnp.float32))
    out_ref[:, 0, :] = full_matrix(pack_ref, channels)[0:channels, 0:channels] * scale


def unpack_ray(core, mine, other, channels, total_rows):
    return pl.pallas_call(
        functools.partial(ray_kernel, 1.0 / total_rows),
        in_specs=[SCALARS] + [WHOLE] * 2,
        out_specs=[WHOLE] * 2,
        out_shape=[matrix_shape(channels), jax.ShapeDtypeStruct((8, LANES), jnp.float32)],
        scratch_shapes=[pltpu.VMEM((full_rows(channels), LANES), jnp.float32)],
        compiler_params=params(),
        cost_estimate=cost(10**5, 10**5),
    )(core, mine, other)


def part_kernel(
    channels, scale, core_ref, mine_ref, inverse_ref, previous_ref, out_ref,
    pack_ref, lower_ref, before_ref,
):
    rows, wide = inverse_ref.shape
    half = mine_ref.shape[0]
    join(pack_ref, core_ref[0], mine_ref[...], jnp.zeros((half, LANES), jnp.float32))
    turned = dot3(full_matrix(pack_ref, channels), inverse_ref[...], ((1,), (1,)))
    unfold(previous_ref, lower_ref, channels, False)
    lower_matrix(lower_ref, before_ref)
    total = dot3(before_ref[:, 0:rows], turned, ((1,), (0,))) * scale
    out_ref[:, 0:rows] = total.astype(out_ref.dtype)
    if rows < wide:
        out_ref[:, rows:wide] = jnp.zeros((rows, wide - rows), out_ref.dtype)


def correlation_part(core, mine, inverse, previous, channels, total_rows):
    return pl.pallas_call(
        functools.partial(part_kernel, channels, 1.0 / total_rows),
        in_specs=[SCALARS] + [WHOLE] * 3,
        out_specs=WHOLE,
        out_shape=jax.ShapeDtypeStruct(inverse.shape, jnp.bfloat16),
        scratch_shapes=[
            pltpu.VMEM((full_rows(channels), LANES), jnp.float32),
            pltpu.VMEM((lower_rows(channels), LANES), jnp.float32),
            pltpu.VMEM(inverse.shape, jnp.float32),
        ],
        compiler_params=params(),
        cost_estimate=cost(10**5, 10**5),
    )(core, mine, inverse, previous)


def both_kernel(left_ref, right_ref, out_ref):
    channels = out_ref.shape[0]
    total = left_ref[...].astype(jnp.float32) + right_ref[...].astype(jnp.float32)
    out_ref[:, 0, :] = total[0:channels, 0:channels]


def both_parts(left, right, channels):
    return pl.pallas_call(
        both_kernel,
        in_specs=[WHOLE] * 2,
        out_specs=WHOLE,
        out_shape=matrix_shape(channels),
        compiler_params=params(),
        cost_estimate=cost(10**5, 10**5),
    )(left, right)


def from_behind(value, axis, steps):
    count = lax.axis_size(axis)
    leading, last = (max(0, -steps), min(count, count - steps))
    return lax.ppermute(value, axis, [(source, source + steps) for source in range(leading, last)])


def other_core(value):
    return lax.ppermute(value, "rows", [(s, s ^ 1) for s in range(lax.axis_size("rows"))])


def chip_rounds():
    count = lax.axis_size("rows")
    bits = []
    while 2 << len(bits) < count:
        bits.append(2 << len(bits))
    return [
        [(s, s ^ (bits[n] if s % 2 == 0 else bits[-1 - n])) for s in range(count)]
        for n in range(len(bits))
    ]


def shards(x_block, h_diag, h_right, pattern):
    x_t = x_block[0].T
    channels, block_rows = x_t.shape
    masks = pattern[0].transpose(1, 0, 2)
    total_rows = lax.axis_size("rows") * block_rows
    core = (lax.axis_index("rows") % 2).astype(jnp.int32).reshape(1)
    later = from_behind(x_t, "rows", -1)
    carried = from_behind(tile_product(1, masks, x_t, h_right[0], x_t.dtype, 53), "rows", 1)
    first = tile_product(0, masks, x_t, h_diag[0], jnp.float32, 50)
    part = later_product(masks, later, h_right[0], first)
    y_t, g_mine, g_other = gram(core, part, carried)
    previous_y = from_behind(y_t, "sector", 1)
    rounds = chip_rounds()
    g_sum = g_mine + other_core(g_other)
    r_mine, r_other = cross(core, x_t, y_t, g_sum, jnp.bfloat16)
    r_sum = add_after(r_mine, other_core(r_other))
    for n, pairs in enumerate(rounds):
        g_sum = add_after(g_sum, lax.ppermute(g_sum, "rows", pairs), r_sum)
        if n + 1 < len(rounds):
            r_sum = add_after(r_sum, lax.ppermute(r_sum, "rows", pairs))
    work = first_stage(core, g_sum, other_core(g_sum), channels, total_rows)
    r_sum = add_after(r_sum, lax.ppermute(r_sum, "rows", rounds[-1]), work)
    m_mine, m_other = cross(core, previous_y, y_t, r_sum, jnp.float32)
    inverse, pack = last_stages(work, channels, m_other)
    m_sum = add_after(m_mine, other_core(m_other), inverse)
    previous = from_behind(pack, "sector", 1)
    rayleigh, token = unpack_ray(core, r_sum, other_core(r_sum), channels, total_rows)
    q_t = basis(inverse, y_t)
    for pairs in rounds[:-1]:
        m_sum = add_after(m_sum, lax.ppermute(m_sum, "rows", pairs))
    m_sum = add_after(m_sum, lax.ppermute(m_sum, "rows", rounds[-1]), token)
    part = correlation_part(core, m_sum, inverse, previous, channels, total_rows)
    correlation = both_parts(part, other_core(part), channels)
    return (q_t.T[None], rayleigh.transpose(1, 0, 2), correlation.transpose(1, 0, 2))


def solution(mesh):
    in_specs = (
        P("sector", "rows", None),
        P("sector", "rows", None),
        P("sector", "rows", None),
        P("sector", None, "rows", None),
    )
    out_specs = (P("sector", "rows", None), P("sector", None, None), P("sector", None, None))
    return jax.shard_map(shards, mesh=mesh, in_specs=in_specs, out_specs=out_specs, check_vma=False)
```

```python
import functools

import jax
import jax.numpy as jnp
from jax import lax
from jax.experimental import pallas as pl
from jax.experimental.pallas import tpu as pltpu
from jax.sharding import PartitionSpec as P

SUBBLOCK = 128
LANES = 128
PANEL = 16
EARLY_PANELS = 6
WHOLE = pl.BlockSpec(memory_space=pltpu.VMEM)
SCALARS = pl.BlockSpec(memory_space=pltpu.SMEM)
ANYWHERE = pl.BlockSpec(memory_space=pl.ANY)
MIB = 1024 * 1024
FIRST_STAGE_FLOPS = 5500 * 10**6
LAST_STAGES_FLOPS = 4 * 10**9


def params(mib=48):
    return pltpu.CompilerParams(vmem_limit_bytes=mib * MIB)


def cost(flops, bytes_accessed):
    return pl.CostEstimate(flops=flops, bytes_accessed=bytes_accessed, transcendentals=0)


def round_up(value, step):
    return (value + step - 1) // step * step


def dot(left, right, dims, precision=None):
    return lax.dot_general(
        left, right, (dims, ((), ())), precision=precision, preferred_element_type=jnp.float32
    )


def block_mask(mask_ref, which, cols):
    blocks = mask_ref[:, which, :].astype(jnp.float32)
    col = lax.broadcasted_iota(jnp.int32, (blocks.shape[1], cols), 1)
    block = lax.broadcasted_iota(jnp.int32, (blocks.shape[1], cols), 0)
    return dot(blocks, jnp.where(col // SUBBLOCK == block, 1.0, 0.0), ((1,), (0,)))


def mask_rows(tile_ref, mask, start, size):
    cols = tile_ref.shape[1]
    for i in range(start // SUBBLOCK, (start + size) // SUBBLOCK):
        keep = jnp.broadcast_to(mask[i : i + 1, :], (PANEL, cols)).astype(tile_ref.dtype)
        for row in range(i * SUBBLOCK, (i + 1) * SUBBLOCK, PANEL):
            tile_ref[row : row + PANEL, :] = tile_ref[row : row + PANEL, :] * keep


def strips(rows, width):
    return [(start, min(width, rows - start)) for start in range(0, rows, width)]


def halves(rows):
    first = rows // 512 * 256
    return [(0, first), (first, rows - first)] if first else [(0, rows)]


def copies_of(source, target, sems):
    copies = []
    for n, (start, size) in enumerate(halves(target.shape[0])):
        here = (pl.ds(start, size), slice(None))
        copies.append(pltpu.make_async_copy(source.at[here], target.at[here], sems.at[n]))
    return copies


def product(x_ref, tile_ref, copies, mask, sum_ref, out_ref):
    rows = tile_ref.shape[0]
    for n, (start, size) in enumerate(halves(rows)):
        copies[n].wait()
        mask_rows(tile_ref, mask, start, size)
        last = n + 1 == len(copies)
        for col, cols in strips(rows, 2 * SUBBLOCK):
            here = (slice(None), slice(col, col + cols))
            term = dot(
                x_ref[:, start : start + size],
                tile_ref[start : start + size, col : col + cols],
                ((1,), (0,)),
            )
            if n > 0:
                term = sum_ref[here] + term
            if last:
                out_ref[here] = term.astype(out_ref.dtype)
            else:
                sum_ref[here] = term


def tile_kernel(which, mask_ref, x_hbm, tile_hbm, out_ref, x_ref, tile_ref, sum_ref, x_sem, sems):
    rows = tile_ref.shape[0]
    copies = copies_of(tile_hbm, tile_ref, sems)
    copy_x = pltpu.make_async_copy(x_hbm, x_ref, x_sem)
    copy_x.start()
    for copy in copies:
        copy.start()
    mask = block_mask(mask_ref, which, rows)
    copy_x.wait()
    product(x_ref, tile_ref, copies, mask, sum_ref, out_ref)


def tile_product(which, masks, x_t, tile, dtype, mib):
    channels, rows = x_t.shape
    return pl.pallas_call(
        functools.partial(tile_kernel, which),
        in_specs=[WHOLE, ANYWHERE, ANYWHERE],
        out_specs=WHOLE,
        out_shape=jax.ShapeDtypeStruct((channels, rows), dtype),
        scratch_shapes=[
            pltpu.VMEM((channels, rows), x_t.dtype),
            pltpu.VMEM((rows, rows), tile.dtype),
            pltpu.VMEM((channels, rows), jnp.float32),
            pltpu.SemaphoreType.DMA,
            pltpu.SemaphoreType.DMA((2,)),
        ],
        compiler_params=params(mib),
        cost_estimate=cost(2 * channels * rows * rows, 2 * rows * rows),
    )(masks, x_t, tile)


def later_kernel(mask_ref, later_ref, tile_hbm, first_ref, out_ref, tile_ref, sems):
    rows = tile_ref.shape[0]
    copies = copies_of(tile_hbm, tile_ref, sems)
    for copy in copies:
        copy.start()
    mask = block_mask(mask_ref, 1, rows)
    for n, (start, size) in enumerate(halves(rows)):
        copies[n].wait()
        mask_rows(tile_ref, mask, start, size)
        for row, count in strips(size, 2 * SUBBLOCK):
            here = (slice(None), slice(start + row, start + row + count))
            out_ref[here] = first_ref[here] + dot(
                later_ref[...], tile_ref[start + row : start + row + count, :], ((1,), (1,))
            )


def later_product(masks, later, tile, first):
    channels, rows = later.shape
    return pl.pallas_call(
        later_kernel,
        in_specs=[WHOLE, WHOLE, ANYWHERE, WHOLE],
        out_specs=WHOLE,
        out_shape=jax.ShapeDtypeStruct((channels, rows), jnp.float32),
        scratch_shapes=[
            pltpu.VMEM((rows, rows), tile.dtype),
            pltpu.SemaphoreType.DMA((2,)),
        ],
        compiler_params=params(),
        cost_estimate=cost(2 * channels * rows * rows, 2 * rows * rows),
    )(masks, later, tile, first)


def lower_rows(channels):
    rows = round_up(channels, PANEL)
    return sum(rows - g * LANES for g in range(round_up(channels, LANES) // LANES))


def full_rows(channels):
    rows, wide = round_up(channels, PANEL), round_up(channels, LANES)
    whole = channels // LANES
    rest = rows - whole * LANES
    return round_up(whole * rows + rest * (wide // LANES), 4 * PANEL)


def lower_products(ref, out_ref):
    channels = ref.shape[0]
    rows = round_up(channels, PANEL)
    offset = 0
    for start, size in strips(channels, LANES):
        tall = rows - start
        if size < LANES:
            out_ref[offset : offset + tall, :] = jnp.zeros((tall, LANES), jnp.float32)
        elif rows > channels:
            out_ref[offset + channels - start : offset + tall, :] = jnp.zeros(
                (rows - channels, LANES), jnp.float32
            )
        out_ref[offset : offset + channels - start, 0:size] = dot(
            ref[start:channels, :], ref[start : start + size, :], ((1,), (1,))
        )
        offset += tall


def full_products(left_ref, right_ref, out_ref):
    channels = left_ref.shape[0]
    rows = round_up(channels, PANEL)
    whole = channels // LANES
    for g in range(whole):
        out_ref[g * rows : g * rows + channels, :] = dot(
            left_ref[...], right_ref[g * LANES : (g + 1) * LANES, :], ((1,), (1,))
        )
        if rows > channels:
            out_ref[g * rows + channels : (g + 1) * rows, :] = jnp.zeros(
                (rows - channels, LANES), jnp.float32
            )
    base = whole * rows
    if base < out_ref.shape[0]:
        out_ref[base:, :] = jnp.zeros((out_ref.shape[0] - base, LANES), jnp.float32)
    first, rest = whole * LANES, rows - whole * LANES
    for n, (start, size) in enumerate(strips(channels, LANES) if first < channels else []):
        place = base + n * rest
        out_ref[place : place + channels - first, 0:size] = dot(
            right_ref[first:channels, :], left_ref[start : start + size, :], ((1,), (1,))
        )


def full_matrix(pack_ref, channels):
    rows, wide = round_up(channels, PANEL), round_up(channels, LANES)
    whole = channels // LANES
    rest = rows - whole * LANES
    parts = [pack_ref[g * rows : (g + 1) * rows, :] for g in range(whole)]
    if rest:
        tail = jnp.concatenate(
            [
                pack_ref[whole * rows + g * rest : whole * rows + (g + 1) * rest, :]
                for g in range(wide // LANES)
            ],
            axis=1,
        )
        tail = jnp.concatenate([tail, jnp.zeros((LANES - rest, wide), tail.dtype)], axis=0)
        parts.append(tail.T[0:rows, :])
    return jnp.concatenate(parts, axis=1)


def folded_rows(channels):
    if channels < 2 * LANES:
        return lower_rows(channels)
    return lower_rows(channels) - LANES + PANEL


def corner(channels):
    return round_up(channels, PANEL)


def square_index():
    row = lax.broadcasted_iota(jnp.int32, (LANES, LANES), 0)
    return row, lax.broadcasted_iota(jnp.int32, (LANES, LANES), 1)


def fold(pack_ref, out_ref, channels, symmetric):
    if channels < 2 * LANES:
        out_ref[...] = pack_ref[...]
        return
    start = corner(channels)
    end = pack_ref.shape[0]
    row, lane = square_index()
    second = pack_ref[start : start + LANES, :]
    upper = second if symmetric else second.T
    out_ref[0:LANES, :] = jnp.where(row >= lane, pack_ref[0:LANES, :], upper)
    out_ref[LANES:start, :] = pack_ref[LANES:start, :]
    out_ref[start : end - LANES, :] = pack_ref[start + LANES : end, :]
    diagonal = jnp.sum(jnp.where(row == lane, second, 0.0), axis=0, keepdims=True)
    out_ref[end - LANES :, :] = jnp.broadcast_to(diagonal, (PANEL, LANES))


def unfold(folded_ref, pack_ref, channels, symmetric):
    if channels < 2 * LANES:
        pack_ref[...] = folded_ref[...]
        return
    start = corner(channels)
    end = pack_ref.shape[0]
    row, lane = square_index()
    both = folded_ref[0:LANES, :]
    turned = both.T
    first_upper, second_upper = (turned, both) if symmetric else (0.0, 0.0)
    pack_ref[0:LANES, :] = jnp.where(row >= lane, both, first_upper)
    pack_ref[LANES:start, :] = folded_ref[LANES:start, :]
    second = jnp.where(row > lane, turned, second_upper)
    diagonal = folded_ref[end - LANES : end - LANES + 1, :]
    pack_ref[start : start + LANES, :] = jnp.where(row == lane, diagonal, second)
    pack_ref[start + LANES : end, :] = folded_ref[start : end - LANES, :]


def cut(pack_ref, core, mine_ref, other_ref):
    half = mine_ref.shape[0]
    mine_ref[...] = pack_ref[pl.ds(pl.multiple_of(core * half, 8), half), :].astype(mine_ref.dtype)
    other_ref[...] = pack_ref[pl.ds(pl.multiple_of((1 - core) * half, 8), half), :].astype(
        other_ref.dtype
    )


def join(pack_ref, core, mine, other):
    half = mine.shape[0]
    pack_ref[pl.ds(pl.multiple_of(core * half, 8), half), :] = mine
    pack_ref[pl.ds(pl.multiple_of((1 - core) * half, 8), half), :] = other


def gram_kernel(core_ref, part_ref, carried_ref, y_ref, g_mine, g_other, gram_ref, folded_ref):
    image = part_ref[...] + carried_ref[...].astype(jnp.float32)
    y_ref[...] = image.astype(y_ref.dtype)
    lower_products(y_ref, gram_ref)
    fold(gram_ref, folded_ref, y_ref.shape[0], True)
    cut(folded_ref, core_ref[0], g_mine, g_other)


def gram(core, part, carried):
    channels, rows = carried.shape
    lower, folded = lower_rows(channels), folded_rows(channels)
    half = jax.ShapeDtypeStruct((folded // 2, LANES), jnp.float32)
    return pl.pallas_call(
        gram_kernel,
        in_specs=[SCALARS] + [WHOLE] * 2,
        out_specs=[WHOLE] * 3,
        out_shape=[jax.ShapeDtypeStruct((channels, rows), carried.dtype), half, half],
        scratch_shapes=[
            pltpu.VMEM((lower, LANES), jnp.float32),
            pltpu.VMEM((folded, LANES), jnp.float32),
        ],
        compiler_params=params(),
        cost_estimate=cost(2 * channels * channels * rows, 8 * channels * rows),
    )(core, part, carried)


def cross_kernel(core_ref, left_ref, right_ref, after_ref, mine_ref, other_ref, pack_ref):
    full_products(left_ref, right_ref, pack_ref)
    cut(pack_ref, core_ref[0], mine_ref, other_ref)


def cross(core, left, right, after, dtype):
    channels, rows = left.shape
    full = full_rows(channels)
    return pl.pallas_call(
        cross_kernel,
        in_specs=[SCALARS, WHOLE, WHOLE, ANYWHERE],
        out_specs=[WHOLE] * 2,
        out_shape=[jax.ShapeDtypeStruct((full // 2, LANES), dtype)] * 2,
        scratch_shapes=[pltpu.VMEM((full, LANES), jnp.float32)],
        compiler_params=params(),
        cost_estimate=cost(2 * channels * channels * rows, 4 * channels * rows),
    )(core, left, right, after)


def add_kernel(left_ref, right_ref, *refs):
    total = left_ref[...].astype(jnp.float32) + right_ref[...].astype(jnp.float32)
    refs[-1][...] = total.astype(refs[-1].dtype)


def add_four_kernel(own_ref, first_ref, second_ref, both_ref, after_ref, out_ref):
    own, first, second, both = (
        ref[...].astype(jnp.float32) for ref in (own_ref, first_ref, second_ref, both_ref)
    )
    out_ref[...] = ((own + first) + (second + both)).astype(out_ref.dtype)


def add_four(own, first, second, both, after):
    return pl.pallas_call(
        add_four_kernel,
        in_specs=[WHOLE] * 4 + [ANYWHERE],
        out_specs=WHOLE,
        out_shape=jax.ShapeDtypeStruct(own.shape, own.dtype),
        compiler_params=params(),
        cost_estimate=cost(10**5, 10**5),
    )(own, first, second, both, after)


def add_after(left, right, *after):
    return pl.pallas_call(
        add_kernel,
        in_specs=[WHOLE] * 2 + [ANYWHERE] * len(after),
        out_specs=WHOLE,
        out_shape=jax.ShapeDtypeStruct(left.shape, left.dtype),
        compiler_params=params(),
        cost_estimate=cost(10**5, 10**5),
    )(left, right, *after)


def split3(value):
    high = value.astype(jnp.bfloat16)
    rest = value - high.astype(jnp.float32)
    mid = rest.astype(jnp.bfloat16)
    low = (rest - mid.astype(jnp.float32)).astype(jnp.bfloat16)
    return high, mid, low


def sublane(value, index):
    return jnp.broadcast_to(value[index : index + 1, :], value.shape)


def lane_of(value, index):
    return jnp.take_along_axis(value, jnp.broadcast_to(index, value.shape), axis=1)


def eliminate(columns, panel):
    half = 8
    row = lax.broadcasted_iota(jnp.int32, (half, LANES), 0)
    scales = [jnp.zeros((half, LANES), jnp.float32) for _ in range(2)]
    columns = [list(c) for c in columns]
    panel = [list(p) for p in panel]
    for j in range(0, PANEL, 2):
        h, r = divmod(j, half)
        left, right = columns[j], columns[j + 1]
        a, b, c = sublane(left[h], r), sublane(left[h], r + 1), sublane(right[h], r + 1)
        det = a * c - b * b
        inverse = pl.reciprocal(det, approx=True)
        first, second = [None, None], [None, None]
        for t in range(h, 2):
            x, y = left[t], right[t]
            if t == h:
                x, y = jnp.where(row > r + 1, x, 0.0), jnp.where(row > r + 1, y, 0.0)
            first[t] = (c * x - b * y) * inverse
            second[t] = (a * y - b * x) * inverse
        for later in range(j + 2, PANEL):
            q = later // half
            x, y = sublane(left[q], later % half), sublane(right[q], later % half)
            for t in range(max(h, q), 2):
                columns[later][t] = columns[later][t] - (first[t] * x + second[t] * y)
        inverse_a = pl.reciprocal(a, approx=True)
        first[h] = jnp.where(row == r + 1, b * inverse_a, first[h])
        for group in panel:
            x, y = sublane(group[h], r), sublane(group[h], r + 1)
            for t in range(h, 2):
                group[t] = group[t] - (first[t] * x + second[t] * y)
        scales[h] = jnp.where(row == r, lax.rsqrt(a), scales[h])
        scales[h] = jnp.where(row == r + 1, lax.rsqrt(det * inverse_a), scales[h])
    return [jnp.concatenate([g[0] * scales[0], g[1] * scales[1]], axis=0) for g in panel]


def fill_work(channels, scale, pack_ref, work_ref):
    rows, wide = work_ref.shape
    groups = wide // LANES
    offset = 0
    for g in range(groups):
        top = g * LANES
        size = min(LANES, rows - top)
        column = pack_ref[offset : offset + rows - top, :] * scale
        offset += rows - top
        diag = column[0:size, :]
        if top + LANES > channels:
            row = lax.broadcasted_iota(jnp.int32, diag.shape, 0)
            lane = lax.broadcasted_iota(jnp.int32, diag.shape, 1)
            diag = jnp.where((row == lane) & (lane + top >= channels), 1.0, diag)
        work_ref[top : top + size, top : top + LANES] = diag
        for below in range(g + 1, groups):
            start = (below - g) * LANES
            size_b = min(LANES, rows - below * LANES)
            block = column[start : start + size_b, :]
            if size_b < LANES:
                block = jnp.concatenate(
                    [block, jnp.zeros((LANES - size_b, LANES), jnp.float32)], axis=0
                )
            work_ref[top : top + size, below * LANES : (below + 1) * LANES] = block.T
            work_ref[below * LANES : below * LANES + size_b, top : top + LANES] = jnp.zeros(
                (size_b, LANES), jnp.float32
            )


def eliminate_group(g, work_ref, turned_ref, first=0, last=LANES // PANEL):
    rows, wide = work_ref.shape
    groups = wide // LANES
    row = lax.broadcasted_iota(jnp.int32, (PANEL, LANES), 0)
    lane = lax.broadcasted_iota(jnp.int32, (PANEL, LANES), 1)
    top = g * LANES
    count = min(LANES, rows - top) // PANEL

    def load(local):
        place = pl.ds(pl.multiple_of(top + local, PANEL), PANEL)
        return [work_ref[place, q * LANES : (q + 1) * LANES] for q in range(groups)]

    def panel_step(b, parts, slot):
        local = b * PANEL
        following = jnp.minimum(local + PANEL, (count - 1) * PANEL)
        ahead = load(following)
        pivots = [parts[g][0:8, :], parts[g][8:16, :]]
        columns = [[lane_of(p, local + j) for p in pivots] for j in range(PANEL)]
        inside = (lane >= local) & (lane < local + PANEL)
        identity = jnp.where(lane - local == row, 1.0, 0.0)
        parts = list(parts)
        parts[g] = jnp.where(inside, identity, parts[g])
        done = eliminate(columns, [[p[0:8, :], p[8:16, :]] for p in parts])
        right = []
        for q in range(groups):
            high, mid, low = split3(done[q])
            right.append(jnp.concatenate([high, mid, high, low, mid, high], axis=0))
            if q >= g:
                if q == g:
                    high, mid, low = split3(jnp.where(lane >= local + PANEL, done[q], 0.0))
                left = jnp.concatenate([high, high, mid, high, mid, low], axis=0)
                turned_ref[slot, (q - g) * LANES : (q - g + 1) * LANES, :] = left.T
        right = jnp.concatenate(right, axis=1)
        near = turned_ref[slot, pl.ds(pl.multiple_of(following, PANEL), PANEL), :]
        update = dot(near, right, ((1,), (0,)))
        ahead[g] = jnp.where(inside, 0.0, ahead[g])
        ahead = [ahead[q] - update[:, q * LANES : (q + 1) * LANES] for q in range(groups)]
        for q in range(g, groups):
            low_row = q * LANES
            high_row = min(rows, low_row + LANES)
            base = low_row - top
            update = dot(turned_ref[slot, base : base + high_row - low_row, :], right, ((1,), (0,)))
            for c in range(groups):
                lanes = slice(c * LANES, (c + 1) * LANES)
                old = work_ref[low_row:high_row, lanes]
                if c == g:
                    here = lax.broadcasted_iota(jnp.int32, old.shape, 1)
                    old = jnp.where((here >= local) & (here < local + PANEL), 0.0, old)
                work_ref[low_row:high_row, lanes] = old - update[:, lanes]
        for q in range(groups):
            if q == g:
                done[q] = jnp.where(lane < local + PANEL, done[q], 0.0)
            elif q > g:
                done[q] = jnp.zeros_like(done[q])
            place = pl.ds(pl.multiple_of(top + local, PANEL), PANEL)
            work_ref[place, q * LANES : (q + 1) * LANES] = done[q]
        return ahead

    def two_panels(i, parts):
        return panel_step(first + 2 * i + 1, panel_step(first + 2 * i, parts, 0), 1)

    last = min(last, count)
    parts = lax.fori_loop(0, (last - first) // 2, two_panels, load(first * PANEL))
    if (last - first) % 2:
        panel_step(jnp.int32(last - 1), parts, 0)


def first_stage_kernel(
    channels, scale, core_ref, mine_ref, other_ref, work_ref, pack_ref, folded_ref, turned_ref
):
    join(folded_ref, core_ref[0], mine_ref[...], other_ref[...])
    unfold(folded_ref, pack_ref, channels, True)
    fill_work(channels, scale, pack_ref, work_ref)
    eliminate_group(0, work_ref, turned_ref)
    if work_ref.shape[1] > LANES:
        eliminate_group(1, work_ref, turned_ref, 0, EARLY_PANELS)


def last_stages_kernel(
    channels, before_ref, after_ref, work_ref, folded_ref, pack_ref, turned_ref
):
    work_ref[...] = before_ref[...]
    rows, wide = work_ref.shape
    for g in range(1, wide // LANES):
        eliminate_group(g, work_ref, turned_ref, EARLY_PANELS if g == 1 else 0)
    offset = 0
    for q in range(wide // LANES):
        tall = rows - q * LANES
        pack_ref[offset : offset + tall, :] = work_ref[q * LANES : rows, q * LANES : (q + 1) * LANES]
        offset += tall
    fold(pack_ref, folded_ref, channels, False)


def turned_scratch(channels):
    return pltpu.VMEM((2, round_up(channels, LANES), 6 * PANEL), jnp.bfloat16)


def work_shape(channels):
    return jax.ShapeDtypeStruct((round_up(channels, PANEL), round_up(channels, LANES)), jnp.float32)


def first_stage(core, mine, other, channels, total_rows):
    return pl.pallas_call(
        functools.partial(first_stage_kernel, channels, 1.0 / total_rows),
        in_specs=[SCALARS] + [WHOLE] * 2,
        out_specs=WHOLE,
        out_shape=work_shape(channels),
        scratch_shapes=[
            pltpu.VMEM((lower_rows(channels), LANES), jnp.float32),
            pltpu.VMEM((folded_rows(channels), LANES), jnp.float32),
            turned_scratch(channels),
        ],
        compiler_params=params(),
        cost_estimate=cost(FIRST_STAGE_FLOPS, 10**6),
    )(core, mine, other)


def last_stages(work, channels, after):
    return pl.pallas_call(
        functools.partial(last_stages_kernel, channels),
        in_specs=[WHOLE, ANYWHERE],
        out_specs=[WHOLE] * 2,
        out_shape=[
            work_shape(channels),
            jax.ShapeDtypeStruct((folded_rows(channels), LANES), jnp.float32),
        ],
        scratch_shapes=[
            pltpu.VMEM((lower_rows(channels), LANES), jnp.float32),
            turned_scratch(channels),
        ],
        compiler_params=params(),
        cost_estimate=cost(LAST_STAGES_FLOPS, 10**5),
    )(work, after)


def split2(value):
    high = value.astype(jnp.bfloat16)
    return high, (value - high.astype(jnp.float32)).astype(jnp.bfloat16)


def dot3(left, right, dims):
    left_high, left_low = split2(left)
    right_high, right_low = split2(right)
    return (
        dot(left_high, right_high, dims)
        + dot(left_high, right_low, dims)
        + dot(left_low, right_high, dims)
    )


def lower_matrix(pack_ref, out_ref):
    rows, wide = out_ref.shape
    offset = 0
    for g in range(wide // LANES):
        top = g * LANES
        lanes = slice(top, top + LANES)
        if top:
            out_ref[0:top, lanes] = jnp.zeros((top, LANES), jnp.float32)
        out_ref[top:rows, lanes] = pack_ref[offset : offset + rows - top, :]
        offset += rows - top


def basis_kernel(inverse_ref, y_ref, q_ref, token_ref):
    channels = y_ref.shape[0]
    image = y_ref[...]
    token_ref[...] = jnp.zeros_like(token_ref)
    for start, size in strips(channels, 2 * LANES):
        used = min(channels, start + size)
        high, low = split2(inverse_ref[start : start + size, 0:used])
        both = dot(jnp.concatenate([high, low], axis=0), image[0:used, :], ((1,), (0,)))
        q_ref[start : start + size, :] = (both[0:size, :] + both[size:, :]).astype(q_ref.dtype)


def basis(inverse, y_t):
    channels, rows = y_t.shape
    return pl.pallas_call(
        basis_kernel,
        in_specs=[WHOLE] * 2,
        out_specs=[WHOLE] * 2,
        out_shape=[
            jax.ShapeDtypeStruct(y_t.shape, y_t.dtype),
            jax.ShapeDtypeStruct((8, LANES), jnp.float32),
        ],
        compiler_params=params(),
        cost_estimate=cost(10**5, 10**5),
    )(inverse, y_t)


def matrix_shape(channels):
    return jax.ShapeDtypeStruct((channels, 1, channels), jnp.float32)


def ray_kernel(scale, core_ref, mine_ref, other_ref, out_ref, token_ref, pack_ref):
    token_ref[...] = jnp.zeros_like(token_ref)
    channels = out_ref.shape[0]
    join(pack_ref, core_ref[0], mine_ref[...].astype(jnp.float32), other_ref[...].astype(jnp.float32))
    out_ref[:, 0, :] = full_matrix(pack_ref, channels)[0:channels, 0:channels] * scale


def unpack_ray(core, mine, other, channels, total_rows):
    return pl.pallas_call(
        functools.partial(ray_kernel, 1.0 / total_rows),
        in_specs=[SCALARS] + [WHOLE] * 2,
        out_specs=[WHOLE] * 2,
        out_shape=[matrix_shape(channels), jax.ShapeDtypeStruct((8, LANES), jnp.float32)],
        scratch_shapes=[pltpu.VMEM((full_rows(channels), LANES), jnp.float32)],
        compiler_params=params(),
        cost_estimate=cost(10**5, 10**5),
    )(core, mine, other)


def part_kernel(
    channels, scale, core_ref, mine_ref, inverse_ref, previous_ref, out_ref,
    pack_ref, lower_ref, before_ref,
):
    rows, wide = inverse_ref.shape
    half = mine_ref.shape[0]
    join(pack_ref, core_ref[0], mine_ref[...], jnp.zeros((half, LANES), jnp.float32))
    turned = dot3(full_matrix(pack_ref, channels), inverse_ref[...], ((1,), (1,)))
    unfold(previous_ref, lower_ref, channels, False)
    lower_matrix(lower_ref, before_ref)
    total = dot3(before_ref[:, 0:rows], turned, ((1,), (0,))) * scale
    out_ref[:, 0:rows] = total.astype(out_ref.dtype)
    if rows < wide:
        out_ref[:, rows:wide] = jnp.zeros((rows, wide - rows), out_ref.dtype)


def correlation_part(core, mine, inverse, previous, channels, total_rows):
    return pl.pallas_call(
        functools.partial(part_kernel, channels, 1.0 / total_rows),
        in_specs=[SCALARS] + [WHOLE] * 3,
        out_specs=WHOLE,
        out_shape=jax.ShapeDtypeStruct(inverse.shape, jnp.bfloat16),
        scratch_shapes=[
            pltpu.VMEM((full_rows(channels), LANES), jnp.float32),
            pltpu.VMEM((lower_rows(channels), LANES), jnp.float32),
            pltpu.VMEM(inverse.shape, jnp.float32),
        ],
        compiler_params=params(),
        cost_estimate=cost(10**5, 10**5),
    )(core, mine, inverse, previous)


def both_kernel(left_ref, right_ref, out_ref):
    channels = out_ref.shape[0]
    total = left_ref[...].astype(jnp.float32) + right_ref[...].astype(jnp.float32)
    out_ref[:, 0, :] = total[0:channels, 0:channels]


def both_parts(left, right, channels):
    return pl.pallas_call(
        both_kernel,
        in_specs=[WHOLE] * 2,
        out_specs=WHOLE,
        out_shape=matrix_shape(channels),
        compiler_params=params(),
        cost_estimate=cost(10**5, 10**5),
    )(left, right)


def from_behind(value, axis, steps):
    count = lax.axis_size(axis)
    leading, last = (max(0, -steps), min(count, count - steps))
    return lax.ppermute(value, axis, [(source, source + steps) for source in range(leading, last)])


def other_core(value):
    return lax.ppermute(value, "rows", [(s, s ^ 1) for s in range(lax.axis_size("rows"))])


def chip_rounds():
    count = lax.axis_size("rows")
    bits = []
    while 2 << len(bits) < count:
        bits.append(2 << len(bits))
    return [
        [(s, s ^ (bits[n] if s % 2 == 0 else bits[-1 - n])) for s in range(count)]
        for n in range(len(bits))
    ]


def sum_chips(value, after):
    count = lax.axis_size("rows")
    if count == 8:
        others = [
            lax.ppermute(value, "rows", [(s, s ^ bits) for s in range(count)]) for bits in (2, 4, 6)
        ]
        return add_four(value, *others, after)
    for pairs in chip_rounds():
        value = add_after(value, lax.ppermute(value, "rows", pairs), after)
    return value


def shards(x_block, h_diag, h_right, pattern):
    x_t = x_block[0].T
    channels, block_rows = x_t.shape
    masks = pattern[0].transpose(1, 0, 2)
    total_rows = lax.axis_size("rows") * block_rows
    core = (lax.axis_index("rows") % 2).astype(jnp.int32).reshape(1)
    later = from_behind(x_t, "rows", -1)
    carried = from_behind(tile_product(1, masks, x_t, h_right[0], x_t.dtype, 53), "rows", 1)
    first = tile_product(0, masks, x_t, h_diag[0], jnp.float32, 50)
    part = later_product(masks, later, h_right[0], first)
    y_t, g_mine, g_other = gram(core, part, carried)
    previous_y = from_behind(y_t, "sector", 1)
    rounds = chip_rounds()
    g_sum = g_mine + other_core(g_other)
    r_mine, r_other = cross(core, x_t, y_t, g_sum, jnp.bfloat16)
    r_sum = add_after(r_mine, other_core(r_other))
    g_sum = sum_chips(g_sum, r_sum)
    work = first_stage(core, g_sum, other_core(g_sum), channels, total_rows)
    r_sum = sum_chips(r_sum, work)
    m_mine, m_other = cross(core, previous_y, y_t, r_sum, jnp.float32)
    inverse, pack = last_stages(work, channels, m_other)
    m_sum = add_after(m_mine, other_core(m_other), inverse)
    previous = from_behind(pack, "sector", 1)
    rayleigh, token = unpack_ray(core, r_sum, other_core(r_sum), channels, total_rows)
    q_t, basis_token = basis(inverse, y_t)
    for pairs in rounds[:-1]:
        m_sum = add_after(m_sum, lax.ppermute(m_sum, "rows", pairs))
    m_sum = add_after(m_sum, lax.ppermute(m_sum, "rows", rounds[-1]), token, basis_token)
    part = correlation_part(core, m_sum, inverse, previous, channels, total_rows)
    correlation = both_parts(part, other_core(part), channels)
    return (q_t.T[None], rayleigh.transpose(1, 0, 2), correlation.transpose(1, 0, 2))


def solution(mesh):
    in_specs = (
        P("sector", "rows", None),
        P("sector", "rows", None),
        P("sector", "rows", None),
        P("sector", None, "rows", None),
    )
    out_specs = (P("sector", "rows", None), P("sector", None, None), P("sector", None, None))
    return jax.shard_map(shards, mesh=mesh, in_specs=in_specs, out_specs=out_specs, check_vma=False)
```

```python
import functools

import jax
import jax.numpy as jnp
from jax import lax
from jax.experimental import pallas as pl
from jax.experimental.pallas import tpu as pltpu
from jax.sharding import PartitionSpec as P

SUBBLOCK = 128
LANES = 128
PANEL = 16
EARLY_PANELS = 6
WHOLE = pl.BlockSpec(memory_space=pltpu.VMEM)
SCALARS = pl.BlockSpec(memory_space=pltpu.SMEM)
ANYWHERE = pl.BlockSpec(memory_space=pl.ANY)
MIB = 1024 * 1024
FIRST_STAGE_FLOPS = 5000 * 10**6
LAST_STAGES_FLOPS = 4000 * 10**6


def params(mib=48):
    return pltpu.CompilerParams(vmem_limit_bytes=mib * MIB)


def cost(flops, bytes_accessed):
    return pl.CostEstimate(flops=flops, bytes_accessed=bytes_accessed, transcendentals=0)


def round_up(value, step):
    return (value + step - 1) // step * step


def dot(left, right, dims, precision=None):
    return lax.dot_general(
        left, right, (dims, ((), ())), precision=precision, preferred_element_type=jnp.float32
    )


def block_mask(mask_ref, which, cols):
    blocks = mask_ref[:, which, :].astype(jnp.float32)
    col = lax.broadcasted_iota(jnp.int32, (blocks.shape[1], cols), 1)
    block = lax.broadcasted_iota(jnp.int32, (blocks.shape[1], cols), 0)
    return dot(blocks, jnp.where(col // SUBBLOCK == block, 1.0, 0.0), ((1,), (0,)))


def mask_rows(tile_ref, mask, start, size):
    cols = tile_ref.shape[1]
    for i in range(start // SUBBLOCK, (start + size) // SUBBLOCK):
        keep = jnp.broadcast_to(mask[i : i + 1, :], (PANEL, cols)).astype(tile_ref.dtype)
        for row in range(i * SUBBLOCK, (i + 1) * SUBBLOCK, PANEL):
            tile_ref[row : row + PANEL, :] = tile_ref[row : row + PANEL, :] * keep


def strips(rows, width):
    return [(start, min(width, rows - start)) for start in range(0, rows, width)]


def halves(rows):
    first = rows // 512 * 256
    return [(0, first), (first, rows - first)] if first else [(0, rows)]


def copies_of(source, target, sems):
    copies = []
    for n, (start, size) in enumerate(halves(target.shape[0])):
        here = (pl.ds(start, size), slice(None))
        copies.append(pltpu.make_async_copy(source.at[here], target.at[here], sems.at[n]))
    return copies


def product(x_ref, tile_ref, copies, mask, sum_ref, out_ref):
    rows = tile_ref.shape[0]
    for n, (start, size) in enumerate(halves(rows)):
        copies[n].wait()
        mask_rows(tile_ref, mask, start, size)
        last = n + 1 == len(copies)
        for col, cols in strips(rows, 2 * SUBBLOCK):
            here = (slice(None), slice(col, col + cols))
            term = dot(
                x_ref[:, start : start + size],
                tile_ref[start : start + size, col : col + cols],
                ((1,), (0,)),
            )
            if n > 0:
                term = sum_ref[here] + term
            if last:
                out_ref[here] = term.astype(out_ref.dtype)
            else:
                sum_ref[here] = term


def tile_kernel(which, mask_ref, x_hbm, tile_hbm, out_ref, x_ref, tile_ref, sum_ref, x_sem, sems):
    rows = tile_ref.shape[0]
    copies = copies_of(tile_hbm, tile_ref, sems)
    copy_x = pltpu.make_async_copy(x_hbm, x_ref, x_sem)
    copy_x.start()
    for copy in copies:
        copy.start()
    mask = block_mask(mask_ref, which, rows)
    copy_x.wait()
    product(x_ref, tile_ref, copies, mask, sum_ref, out_ref)


def tile_product(which, masks, x_t, tile, dtype, mib):
    channels, rows = x_t.shape
    return pl.pallas_call(
        functools.partial(tile_kernel, which),
        in_specs=[WHOLE, ANYWHERE, ANYWHERE],
        out_specs=WHOLE,
        out_shape=jax.ShapeDtypeStruct((channels, rows), dtype),
        scratch_shapes=[
            pltpu.VMEM((channels, rows), x_t.dtype),
            pltpu.VMEM((rows, rows), tile.dtype),
            pltpu.VMEM((channels, rows), jnp.float32),
            pltpu.SemaphoreType.DMA,
            pltpu.SemaphoreType.DMA((2,)),
        ],
        compiler_params=params(mib),
        cost_estimate=cost(2 * channels * rows * rows, 2 * rows * rows),
    )(masks, x_t, tile)


def later_kernel(mask_ref, later_ref, tile_hbm, first_ref, out_ref, tile_ref, sems):
    rows = tile_ref.shape[0]
    copies = copies_of(tile_hbm, tile_ref, sems)
    for copy in copies:
        copy.start()
    mask = block_mask(mask_ref, 1, rows)
    for n, (start, size) in enumerate(halves(rows)):
        copies[n].wait()
        mask_rows(tile_ref, mask, start, size)
        for row, count in strips(size, 2 * SUBBLOCK):
            here = (slice(None), slice(start + row, start + row + count))
            out_ref[here] = first_ref[here] + dot(
                later_ref[...], tile_ref[start + row : start + row + count, :], ((1,), (1,))
            )


def later_product(masks, later, tile, first):
    channels, rows = later.shape
    return pl.pallas_call(
        later_kernel,
        in_specs=[WHOLE, WHOLE, ANYWHERE, WHOLE],
        out_specs=WHOLE,
        out_shape=jax.ShapeDtypeStruct((channels, rows), jnp.float32),
        scratch_shapes=[
            pltpu.VMEM((rows, rows), tile.dtype),
            pltpu.SemaphoreType.DMA((2,)),
        ],
        compiler_params=params(),
        cost_estimate=cost(2 * channels * rows * rows, 2 * rows * rows),
    )(masks, later, tile, first)


def lower_rows(channels):
    rows = round_up(channels, PANEL)
    return sum(rows - g * LANES for g in range(round_up(channels, LANES) // LANES))


def full_rows(channels):
    rows, wide = round_up(channels, PANEL), round_up(channels, LANES)
    whole = channels // LANES
    rest = rows - whole * LANES
    return round_up(whole * rows + rest * (wide // LANES), 4 * PANEL)


def lower_products(ref, out_ref):
    channels = ref.shape[0]
    rows = round_up(channels, PANEL)
    offset = 0
    for start, size in strips(channels, LANES):
        tall = rows - start
        if size < LANES:
            out_ref[offset : offset + tall, :] = jnp.zeros((tall, LANES), jnp.float32)
        elif rows > channels:
            out_ref[offset + channels - start : offset + tall, :] = jnp.zeros(
                (rows - channels, LANES), jnp.float32
            )
        out_ref[offset : offset + channels - start, 0:size] = dot(
            ref[start:channels, :], ref[start : start + size, :], ((1,), (1,))
        )
        offset += tall


def full_products(left_ref, right_ref, out_ref):
    channels = left_ref.shape[0]
    rows = round_up(channels, PANEL)
    whole = channels // LANES
    for g in range(whole):
        out_ref[g * rows : g * rows + channels, :] = dot(
            left_ref[...], right_ref[g * LANES : (g + 1) * LANES, :], ((1,), (1,))
        )
        if rows > channels:
            out_ref[g * rows + channels : (g + 1) * rows, :] = jnp.zeros(
                (rows - channels, LANES), jnp.float32
            )
    base = whole * rows
    if base < out_ref.shape[0]:
        out_ref[base:, :] = jnp.zeros((out_ref.shape[0] - base, LANES), jnp.float32)
    first, rest = whole * LANES, rows - whole * LANES
    for n, (start, size) in enumerate(strips(channels, LANES) if first < channels else []):
        place = base + n * rest
        out_ref[place : place + channels - first, 0:size] = dot(
            right_ref[first:channels, :], left_ref[start : start + size, :], ((1,), (1,))
        )


def full_matrix(pack_ref, channels):
    rows, wide = round_up(channels, PANEL), round_up(channels, LANES)
    whole = channels // LANES
    rest = rows - whole * LANES
    parts = [pack_ref[g * rows : (g + 1) * rows, :] for g in range(whole)]
    if rest:
        tail = jnp.concatenate(
            [
                pack_ref[whole * rows + g * rest : whole * rows + (g + 1) * rest, :]
                for g in range(wide // LANES)
            ],
            axis=1,
        )
        tail = jnp.concatenate([tail, jnp.zeros((LANES - rest, wide), tail.dtype)], axis=0)
        parts.append(tail.T[0:rows, :])
    return jnp.concatenate(parts, axis=1)


def folded_rows(channels):
    if channels < 2 * LANES:
        return lower_rows(channels)
    return lower_rows(channels) - LANES + PANEL


def corner(channels):
    return round_up(channels, PANEL)


def square_index():
    row = lax.broadcasted_iota(jnp.int32, (LANES, LANES), 0)
    return row, lax.broadcasted_iota(jnp.int32, (LANES, LANES), 1)


def fold(pack_ref, out_ref, channels, symmetric):
    if channels < 2 * LANES:
        out_ref[...] = pack_ref[...]
        return
    start = corner(channels)
    end = pack_ref.shape[0]
    row, lane = square_index()
    second = pack_ref[start : start + LANES, :]
    upper = second if symmetric else second.T
    out_ref[0:LANES, :] = jnp.where(row >= lane, pack_ref[0:LANES, :], upper)
    out_ref[LANES:start, :] = pack_ref[LANES:start, :]
    out_ref[start : end - LANES, :] = pack_ref[start + LANES : end, :]
    diagonal = jnp.sum(jnp.where(row == lane, second, 0.0), axis=0, keepdims=True)
    out_ref[end - LANES :, :] = jnp.broadcast_to(diagonal, (PANEL, LANES))


def unfold(folded_ref, pack_ref, channels, symmetric):
    if channels < 2 * LANES:
        pack_ref[...] = folded_ref[...]
        return
    start = corner(channels)
    end = pack_ref.shape[0]
    row, lane = square_index()
    both = folded_ref[0:LANES, :]
    turned = both.T
    first_upper, second_upper = (turned, both) if symmetric else (0.0, 0.0)
    pack_ref[0:LANES, :] = jnp.where(row >= lane, both, first_upper)
    pack_ref[LANES:start, :] = folded_ref[LANES:start, :]
    second = jnp.where(row > lane, turned, second_upper)
    diagonal = folded_ref[end - LANES : end - LANES + 1, :]
    pack_ref[start : start + LANES, :] = jnp.where(row == lane, diagonal, second)
    pack_ref[start + LANES : end, :] = folded_ref[start : end - LANES, :]


def cut(pack_ref, core, mine_ref, other_ref):
    half = mine_ref.shape[0]
    mine_ref[...] = pack_ref[pl.ds(pl.multiple_of(core * half, 8), half), :].astype(mine_ref.dtype)
    other_ref[...] = pack_ref[pl.ds(pl.multiple_of((1 - core) * half, 8), half), :].astype(
        other_ref.dtype
    )


def join(pack_ref, core, mine, other):
    half = mine.shape[0]
    pack_ref[pl.ds(pl.multiple_of(core * half, 8), half), :] = mine
    pack_ref[pl.ds(pl.multiple_of((1 - core) * half, 8), half), :] = other


def gram_kernel(core_ref, part_ref, carried_ref, y_ref, g_mine, g_other, gram_ref, folded_ref):
    image = part_ref[...] + carried_ref[...].astype(jnp.float32)
    y_ref[...] = image.astype(y_ref.dtype)
    lower_products(y_ref, gram_ref)
    fold(gram_ref, folded_ref, y_ref.shape[0], True)
    cut(folded_ref, core_ref[0], g_mine, g_other)


def gram(core, part, carried):
    channels, rows = carried.shape
    lower, folded = lower_rows(channels), folded_rows(channels)
    half = jax.ShapeDtypeStruct((folded // 2, LANES), jnp.float32)
    return pl.pallas_call(
        gram_kernel,
        in_specs=[SCALARS] + [WHOLE] * 2,
        out_specs=[WHOLE] * 3,
        out_shape=[jax.ShapeDtypeStruct((channels, rows), carried.dtype), half, half],
        scratch_shapes=[
            pltpu.VMEM((lower, LANES), jnp.float32),
            pltpu.VMEM((folded, LANES), jnp.float32),
        ],
        compiler_params=params(),
        cost_estimate=cost(2 * channels * channels * rows, 8 * channels * rows),
    )(core, part, carried)


def cross_kernel(core_ref, left_ref, right_ref, after_ref, mine_ref, other_ref, pack_ref):
    full_products(left_ref, right_ref, pack_ref)
    cut(pack_ref, core_ref[0], mine_ref, other_ref)


def cross(core, left, right, after, dtype):
    channels, rows = left.shape
    full = full_rows(channels)
    return pl.pallas_call(
        cross_kernel,
        in_specs=[SCALARS, WHOLE, WHOLE, ANYWHERE],
        out_specs=[WHOLE] * 2,
        out_shape=[jax.ShapeDtypeStruct((full // 2, LANES), dtype)] * 2,
        scratch_shapes=[pltpu.VMEM((full, LANES), jnp.float32)],
        compiler_params=params(),
        cost_estimate=cost(2 * channels * channels * rows, 4 * channels * rows),
    )(core, left, right, after)


def add_kernel(left_ref, right_ref, *refs):
    total = left_ref[...].astype(jnp.float32) + right_ref[...].astype(jnp.float32)
    refs[-1][...] = total.astype(refs[-1].dtype)


def add_four_kernel(own_ref, first_ref, second_ref, both_ref, after_ref, out_ref):
    own, first, second, both = (
        ref[...].astype(jnp.float32) for ref in (own_ref, first_ref, second_ref, both_ref)
    )
    out_ref[...] = ((own + first) + (second + both)).astype(out_ref.dtype)


def add_four(own, first, second, both, after):
    return pl.pallas_call(
        add_four_kernel,
        in_specs=[WHOLE] * 4 + [ANYWHERE],
        out_specs=WHOLE,
        out_shape=jax.ShapeDtypeStruct(own.shape, own.dtype),
        compiler_params=params(),
        cost_estimate=cost(10**5, 10**5),
    )(own, first, second, both, after)


def add_after(left, right, *after):
    return pl.pallas_call(
        add_kernel,
        in_specs=[WHOLE] * 2 + [ANYWHERE] * len(after),
        out_specs=WHOLE,
        out_shape=jax.ShapeDtypeStruct(left.shape, left.dtype),
        compiler_params=params(),
        cost_estimate=cost(10**5, 10**5),
    )(left, right, *after)


def split3(value):
    high = value.astype(jnp.bfloat16)
    rest = value - high.astype(jnp.float32)
    mid = rest.astype(jnp.bfloat16)
    low = (rest - mid.astype(jnp.float32)).astype(jnp.bfloat16)
    return high, mid, low


def sublane(value, index):
    return jnp.broadcast_to(value[index : index + 1, :], value.shape)


def lane_of(value, index):
    return jnp.take_along_axis(value, jnp.broadcast_to(index, value.shape), axis=1)


def eliminate(columns, panel):
    half = 8
    row = lax.broadcasted_iota(jnp.int32, (half, LANES), 0)
    scales = [jnp.zeros((half, LANES), jnp.float32) for _ in range(2)]
    columns = [list(c) for c in columns]
    panel = [list(p) for p in panel]
    for j in range(0, PANEL, 2):
        h, r = divmod(j, half)
        left, right = columns[j], columns[j + 1]
        a, b, c = sublane(left[h], r), sublane(left[h], r + 1), sublane(right[h], r + 1)
        det = a * c - b * b
        inverse = pl.reciprocal(det, approx=True)
        first, second = [None, None], [None, None]
        for t in range(h, 2):
            x, y = left[t], right[t]
            if t == h:
                x, y = jnp.where(row > r + 1, x, 0.0), jnp.where(row > r + 1, y, 0.0)
            first[t] = (c * x - b * y) * inverse
            second[t] = (a * y - b * x) * inverse
        for later in range(j + 2, PANEL):
            q = later // half
            x, y = sublane(left[q], later % half), sublane(right[q], later % half)
            for t in range(max(h, q), 2):
                columns[later][t] = columns[later][t] - (first[t] * x + second[t] * y)
        inverse_a = pl.reciprocal(a, approx=True)
        first[h] = jnp.where(row == r + 1, b * inverse_a, first[h])
        for group in panel:
            x, y = sublane(group[h], r), sublane(group[h], r + 1)
            for t in range(h, 2):
                group[t] = group[t] - (first[t] * x + second[t] * y)
        scales[h] = jnp.where(row == r, lax.rsqrt(a), scales[h])
        scales[h] = jnp.where(row == r + 1, lax.rsqrt(det * inverse_a), scales[h])
    return [jnp.concatenate([g[0] * scales[0], g[1] * scales[1]], axis=0) for g in panel]


def fill_work(channels, scale, pack_ref, work_ref):
    rows, wide = work_ref.shape
    groups = wide // LANES
    offset = 0
    for g in range(groups):
        top = g * LANES
        size = min(LANES, rows - top)
        column = pack_ref[offset : offset + rows - top, :] * scale
        offset += rows - top
        diag = column[0:size, :]
        if top + LANES > channels:
            row = lax.broadcasted_iota(jnp.int32, diag.shape, 0)
            lane = lax.broadcasted_iota(jnp.int32, diag.shape, 1)
            diag = jnp.where((row == lane) & (lane + top >= channels), 1.0, diag)
        work_ref[top : top + size, top : top + LANES] = diag
        for below in range(g + 1, groups):
            start = (below - g) * LANES
            size_b = min(LANES, rows - below * LANES)
            block = column[start : start + size_b, :]
            if size_b < LANES:
                block = jnp.concatenate(
                    [block, jnp.zeros((LANES - size_b, LANES), jnp.float32)], axis=0
                )
            work_ref[top : top + size, below * LANES : (below + 1) * LANES] = block.T
            work_ref[below * LANES : below * LANES + size_b, top : top + LANES] = jnp.zeros(
                (size_b, LANES), jnp.float32
            )


def eliminate_group(g, work_ref, turned_ref, first=0, last=LANES // PANEL):
    rows, wide = work_ref.shape
    groups = wide // LANES
    row = lax.broadcasted_iota(jnp.int32, (PANEL, LANES), 0)
    lane = lax.broadcasted_iota(jnp.int32, (PANEL, LANES), 1)
    top = g * LANES
    count = min(LANES, rows - top) // PANEL

    def load(local):
        place = pl.ds(pl.multiple_of(top + local, PANEL), PANEL)
        return [work_ref[place, q * LANES : (q + 1) * LANES] for q in range(groups)]

    def panel_step(b, parts, slot):
        local = b * PANEL
        following = jnp.minimum(local + PANEL, (count - 1) * PANEL)
        ahead = load(following)
        pivots = [parts[g][0:8, :], parts[g][8:16, :]]
        columns = [[lane_of(p, local + j) for p in pivots] for j in range(PANEL)]
        inside = (lane >= local) & (lane < local + PANEL)
        identity = jnp.where(lane - local == row, 1.0, 0.0)
        parts = list(parts)
        parts[g] = jnp.where(inside, identity, parts[g])
        done = eliminate(columns, [[p[0:8, :], p[8:16, :]] for p in parts])
        right = []
        for q in range(groups):
            high, mid, low = split3(done[q])
            right.append(jnp.concatenate([high, mid, high, low, mid, high], axis=0))
            if q >= g:
                if q == g:
                    high, mid, low = split3(jnp.where(lane >= local + PANEL, done[q], 0.0))
                left = jnp.concatenate([high, high, mid, high, mid, low], axis=0)
                turned_ref[slot, (q - g) * LANES : (q - g + 1) * LANES, :] = left.T
        right = jnp.concatenate(right, axis=1)
        near = turned_ref[slot, pl.ds(pl.multiple_of(following, PANEL), PANEL), :]
        update = dot(near, right, ((1,), (0,)))
        ahead[g] = jnp.where(inside, 0.0, ahead[g])
        ahead = [ahead[q] - update[:, q * LANES : (q + 1) * LANES] for q in range(groups)]
        for q in range(g, groups):
            low_row = q * LANES
            high_row = min(rows, low_row + LANES)
            base = low_row - top
            update = dot(turned_ref[slot, base : base + high_row - low_row, :], right, ((1,), (0,)))
            for c in range(groups):
                lanes = slice(c * LANES, (c + 1) * LANES)
                old = work_ref[low_row:high_row, lanes]
                if c == g:
                    here = lax.broadcasted_iota(jnp.int32, old.shape, 1)
                    old = jnp.where((here >= local) & (here < local + PANEL), 0.0, old)
                work_ref[low_row:high_row, lanes] = old - update[:, lanes]
        for q in range(groups):
            if q == g:
                done[q] = jnp.where(lane < local + PANEL, done[q], 0.0)
            elif q > g:
                done[q] = jnp.zeros_like(done[q])
            place = pl.ds(pl.multiple_of(top + local, PANEL), PANEL)
            work_ref[place, q * LANES : (q + 1) * LANES] = done[q]
        return ahead

    def two_panels(i, parts):
        return panel_step(first + 2 * i + 1, panel_step(first + 2 * i, parts, 0), 1)

    last = min(last, count)
    parts = lax.fori_loop(0, (last - first) // 2, two_panels, load(first * PANEL))
    if (last - first) % 2:
        panel_step(jnp.int32(last - 1), parts, 0)


def first_stage_kernel(
    channels, scale, core_ref, mine_ref, other_ref, work_ref, pack_ref, folded_ref, turned_ref
):
    join(folded_ref, core_ref[0], mine_ref[...], other_ref[...])
    unfold(folded_ref, pack_ref, channels, True)
    fill_work(channels, scale, pack_ref, work_ref)
    eliminate_group(0, work_ref, turned_ref)
    if work_ref.shape[1] > LANES:
        eliminate_group(1, work_ref, turned_ref, 0, EARLY_PANELS)


def last_stages_kernel(
    channels, before_ref, after_ref, work_ref, folded_ref, pack_ref, turned_ref
):
    work_ref[...] = before_ref[...]
    rows, wide = work_ref.shape
    for g in range(1, wide // LANES):
        eliminate_group(g, work_ref, turned_ref, EARLY_PANELS if g == 1 else 0)
    offset = 0
    for q in range(wide // LANES):
        tall = rows - q * LANES
        pack_ref[offset : offset + tall, :] = work_ref[q * LANES : rows, q * LANES : (q + 1) * LANES]
        offset += tall
    fold(pack_ref, folded_ref, channels, False)


def turned_scratch(channels):
    return pltpu.VMEM((2, round_up(channels, LANES), 6 * PANEL), jnp.bfloat16)


def work_shape(channels):
    return jax.ShapeDtypeStruct((round_up(channels, PANEL), round_up(channels, LANES)), jnp.float32)


def first_stage(core, mine, other, channels, total_rows):
    return pl.pallas_call(
        functools.partial(first_stage_kernel, channels, 1.0 / total_rows),
        in_specs=[SCALARS] + [WHOLE] * 2,
        out_specs=WHOLE,
        out_shape=work_shape(channels),
        scratch_shapes=[
            pltpu.VMEM((lower_rows(channels), LANES), jnp.float32),
            pltpu.VMEM((folded_rows(channels), LANES), jnp.float32),
            turned_scratch(channels),
        ],
        compiler_params=params(),
        cost_estimate=cost(FIRST_STAGE_FLOPS, 10**6),
    )(core, mine, other)


def last_stages(work, channels, after):
    return pl.pallas_call(
        functools.partial(last_stages_kernel, channels),
        in_specs=[WHOLE, ANYWHERE],
        out_specs=[WHOLE] * 2,
        out_shape=[
            work_shape(channels),
            jax.ShapeDtypeStruct((folded_rows(channels), LANES), jnp.float32),
        ],
        scratch_shapes=[
            pltpu.VMEM((lower_rows(channels), LANES), jnp.float32),
            turned_scratch(channels),
        ],
        compiler_params=params(),
        cost_estimate=cost(LAST_STAGES_FLOPS, 10**5),
    )(work, after)


def split2(value):
    high = value.astype(jnp.bfloat16)
    return high, (value - high.astype(jnp.float32)).astype(jnp.bfloat16)


def dot3(left, right, dims):
    left_high, left_low = split2(left)
    right_high, right_low = split2(right)
    return (
        dot(left_high, right_high, dims)
        + dot(left_high, right_low, dims)
        + dot(left_low, right_high, dims)
    )


def lower_matrix(pack_ref, out_ref):
    rows, wide = out_ref.shape
    offset = 0
    for g in range(wide // LANES):
        top = g * LANES
        lanes = slice(top, top + LANES)
        if top:
            out_ref[0:top, lanes] = jnp.zeros((top, LANES), jnp.float32)
        out_ref[top:rows, lanes] = pack_ref[offset : offset + rows - top, :]
        offset += rows - top


def basis_kernel(inverse_ref, y_ref, q_ref, token_ref):
    channels = y_ref.shape[0]
    image = y_ref[...]
    token_ref[...] = jnp.zeros_like(token_ref)
    for start, size in strips(channels, 2 * LANES):
        used = min(channels, start + size)
        high, low = split2(inverse_ref[start : start + size, 0:used])
        both = dot(jnp.concatenate([high, low], axis=0), image[0:used, :], ((1,), (0,)))
        q_ref[start : start + size, :] = (both[0:size, :] + both[size:, :]).astype(q_ref.dtype)


def basis(inverse, y_t):
    channels, rows = y_t.shape
    return pl.pallas_call(
        basis_kernel,
        in_specs=[WHOLE] * 2,
        out_specs=[WHOLE] * 2,
        out_shape=[
            jax.ShapeDtypeStruct(y_t.shape, y_t.dtype),
            jax.ShapeDtypeStruct((8, LANES), jnp.float32),
        ],
        compiler_params=params(),
        cost_estimate=cost(10**5, 10**5),
    )(inverse, y_t)


def matrix_shape(channels):
    return jax.ShapeDtypeStruct((channels, 1, channels), jnp.float32)


def ray_kernel(scale, core_ref, mine_ref, other_ref, out_ref, token_ref, pack_ref):
    token_ref[...] = jnp.zeros_like(token_ref)
    channels = out_ref.shape[0]
    join(pack_ref, core_ref[0], mine_ref[...].astype(jnp.float32), other_ref[...].astype(jnp.float32))
    out_ref[:, 0, :] = full_matrix(pack_ref, channels)[0:channels, 0:channels] * scale


def unpack_ray(core, mine, other, channels, total_rows):
    return pl.pallas_call(
        functools.partial(ray_kernel, 1.0 / total_rows),
        in_specs=[SCALARS] + [WHOLE] * 2,
        out_specs=[WHOLE] * 2,
        out_shape=[matrix_shape(channels), jax.ShapeDtypeStruct((8, LANES), jnp.float32)],
        scratch_shapes=[pltpu.VMEM((full_rows(channels), LANES), jnp.float32)],
        compiler_params=params(),
        cost_estimate=cost(10**5, 10**5),
    )(core, mine, other)


def part_kernel(
    channels, scale, core_ref, mine_ref, inverse_ref, previous_ref, out_ref,
    pack_ref, lower_ref, before_ref,
):
    rows, wide = inverse_ref.shape
    half = mine_ref.shape[0]
    join(pack_ref, core_ref[0], mine_ref[...], jnp.zeros((half, LANES), jnp.float32))
    turned = dot3(full_matrix(pack_ref, channels), inverse_ref[...], ((1,), (1,)))
    unfold(previous_ref, lower_ref, channels, False)
    lower_matrix(lower_ref, before_ref)
    total = dot3(before_ref[:, 0:rows], turned, ((1,), (0,))) * scale
    out_ref[:, 0:rows] = total.astype(out_ref.dtype)
    if rows < wide:
        out_ref[:, rows:wide] = jnp.zeros((rows, wide - rows), out_ref.dtype)


def correlation_part(core, mine, inverse, previous, channels, total_rows):
    return pl.pallas_call(
        functools.partial(part_kernel, channels, 1.0 / total_rows),
        in_specs=[SCALARS] + [WHOLE] * 3,
        out_specs=WHOLE,
        out_shape=jax.ShapeDtypeStruct(inverse.shape, jnp.bfloat16),
        scratch_shapes=[
            pltpu.VMEM((full_rows(channels), LANES), jnp.float32),
            pltpu.VMEM((lower_rows(channels), LANES), jnp.float32),
            pltpu.VMEM(inverse.shape, jnp.float32),
        ],
        compiler_params=params(),
        cost_estimate=cost(10**5, 10**5),
    )(core, mine, inverse, previous)


def both_kernel(left_ref, right_ref, out_ref):
    channels = out_ref.shape[0]
    total = left_ref[...].astype(jnp.float32) + right_ref[...].astype(jnp.float32)
    out_ref[:, 0, :] = total[0:channels, 0:channels]


def both_parts(left, right, channels):
    return pl.pallas_call(
        both_kernel,
        in_specs=[WHOLE] * 2,
        out_specs=WHOLE,
        out_shape=matrix_shape(channels),
        compiler_params=params(),
        cost_estimate=cost(10**5, 10**5),
    )(left, right)


def from_behind(value, axis, steps):
    count = lax.axis_size(axis)
    leading, last = (max(0, -steps), min(count, count - steps))
    return lax.ppermute(value, axis, [(source, source + steps) for source in range(leading, last)])


def other_core(value):
    return lax.ppermute(value, "rows", [(s, s ^ 1) for s in range(lax.axis_size("rows"))])


def chip_rounds():
    count = lax.axis_size("rows")
    bits = []
    while 2 << len(bits) < count:
        bits.append(2 << len(bits))
    return [
        [(s, s ^ (bits[n] if s % 2 == 0 else bits[-1 - n])) for s in range(count)]
        for n in range(len(bits))
    ]


def sum_chips(value, after):
    count = lax.axis_size("rows")
    if count == 8:
        others = [
            lax.ppermute(value, "rows", [(s, s ^ bits) for s in range(count)]) for bits in (2, 4, 6)
        ]
        return add_four(value, *others, after)
    for pairs in chip_rounds():
        value = add_after(value, lax.ppermute(value, "rows", pairs), after)
    return value


def shards(x_block, h_diag, h_right, pattern):
    x_t = x_block[0].T
    channels, block_rows = x_t.shape
    masks = pattern[0].transpose(1, 0, 2)
    total_rows = lax.axis_size("rows") * block_rows
    core = (lax.axis_index("rows") % 2).astype(jnp.int32).reshape(1)
    later = from_behind(x_t, "rows", -1)
    carried = from_behind(tile_product(1, masks, x_t, h_right[0], x_t.dtype, 53), "rows", 1)
    first = tile_product(0, masks, x_t, h_diag[0], jnp.float32, 50)
    part = later_product(masks, later, h_right[0], first)
    y_t, g_mine, g_other = gram(core, part, carried)
    previous_y = from_behind(y_t, "sector", 1)
    rounds = chip_rounds()
    g_sum = g_mine + other_core(g_other)
    r_mine, r_other = cross(core, x_t, y_t, g_sum, jnp.bfloat16)
    r_sum = add_after(r_mine, other_core(r_other))
    g_sum = sum_chips(g_sum, r_sum)
    r_first = lax.ppermute(r_sum, "rows", rounds[0])
    work = first_stage(core, g_sum, other_core(g_sum), channels, total_rows)
    r_sum = add_after(r_sum, r_first, work)
    m_mine, m_other = cross(core, previous_y, y_t, work, jnp.float32)
    inverse, pack = last_stages(work, channels, m_other)
    m_sum = add_after(m_mine, other_core(m_other), inverse)
    previous = from_behind(pack, "sector", 1)
    for pairs in rounds[1:]:
        r_sum = add_after(r_sum, lax.ppermute(r_sum, "rows", pairs))
    rayleigh, token = unpack_ray(core, r_sum, other_core(r_sum), channels, total_rows)
    q_t, basis_token = basis(inverse, y_t)
    for pairs in rounds[:-1]:
        m_sum = add_after(m_sum, lax.ppermute(m_sum, "rows", pairs), r_sum)
    m_sum = add_after(m_sum, lax.ppermute(m_sum, "rows", rounds[-1]), token, basis_token)
    part = correlation_part(core, m_sum, inverse, previous, channels, total_rows)
    correlation = both_parts(part, other_core(part), channels)
    return (q_t.T[None], rayleigh.transpose(1, 0, 2), correlation.transpose(1, 0, 2))


def solution(mesh):
    in_specs = (
        P("sector", "rows", None),
        P("sector", "rows", None),
        P("sector", "rows", None),
        P("sector", None, "rows", None),
    )
    out_specs = (P("sector", "rows", None), P("sector", None, None), P("sector", None, None))
    return jax.shard_map(shards, mesh=mesh, in_specs=in_specs, out_specs=out_specs, check_vma=False)
```

```python
import functools

import jax
import jax.numpy as jnp
from jax import lax
from jax.experimental import pallas as pl
from jax.experimental.pallas import tpu as pltpu
from jax.sharding import PartitionSpec as P

SUBBLOCK = 128
LANES = 128
PANEL = 16
EARLY_PANELS = 6
WHOLE = pl.BlockSpec(memory_space=pltpu.VMEM)
SCALARS = pl.BlockSpec(memory_space=pltpu.SMEM)
ANYWHERE = pl.BlockSpec(memory_space=pl.ANY)
MIB = 1024 * 1024
FIRST_STAGE_FLOPS = 5000 * 10**6
LAST_RAY_FLOPS = 3000 * 10**6
LAST_STAGES_FLOPS = 4000 * 10**6


def params(mib=48):
    return pltpu.CompilerParams(vmem_limit_bytes=mib * MIB)


def cost(flops, bytes_accessed):
    return pl.CostEstimate(flops=flops, bytes_accessed=bytes_accessed, transcendentals=0)


def round_up(value, step):
    return (value + step - 1) // step * step


def dot(left, right, dims, precision=None):
    return lax.dot_general(
        left, right, (dims, ((), ())), precision=precision, preferred_element_type=jnp.float32
    )


def block_mask(mask_ref, which, cols):
    blocks = mask_ref[:, which, :].astype(jnp.float32)
    col = lax.broadcasted_iota(jnp.int32, (blocks.shape[1], cols), 1)
    block = lax.broadcasted_iota(jnp.int32, (blocks.shape[1], cols), 0)
    return dot(blocks, jnp.where(col // SUBBLOCK == block, 1.0, 0.0), ((1,), (0,)))


def mask_rows(tile_ref, mask, start, size):
    cols = tile_ref.shape[1]
    for i in range(start // SUBBLOCK, (start + size) // SUBBLOCK):
        keep = jnp.broadcast_to(mask[i : i + 1, :], (PANEL, cols)).astype(tile_ref.dtype)
        for row in range(i * SUBBLOCK, (i + 1) * SUBBLOCK, PANEL):
            tile_ref[row : row + PANEL, :] = tile_ref[row : row + PANEL, :] * keep


def strips(rows, width):
    return [(start, min(width, rows - start)) for start in range(0, rows, width)]


def halves(rows):
    first = rows // 512 * 256
    return [(0, first), (first, rows - first)] if first else [(0, rows)]


def copies_of(source, target, sems):
    copies = []
    for n, (start, size) in enumerate(halves(target.shape[0])):
        here = (pl.ds(start, size), slice(None))
        copies.append(pltpu.make_async_copy(source.at[here], target.at[here], sems.at[n]))
    return copies


def product(x_ref, tile_ref, copies, mask, sum_ref, out_ref):
    rows = tile_ref.shape[0]
    for n, (start, size) in enumerate(halves(rows)):
        copies[n].wait()
        mask_rows(tile_ref, mask, start, size)
        last = n + 1 == len(copies)
        for col, cols in strips(rows, 2 * SUBBLOCK):
            here = (slice(None), slice(col, col + cols))
            term = dot(
                x_ref[:, start : start + size],
                tile_ref[start : start + size, col : col + cols],
                ((1,), (0,)),
            )
            if n > 0:
                term = sum_ref[here] + term
            if last:
                out_ref[here] = term.astype(out_ref.dtype)
            else:
                sum_ref[here] = term


def tile_kernel(which, mask_ref, x_hbm, tile_hbm, out_ref, x_ref, tile_ref, sum_ref, x_sem, sems):
    rows = tile_ref.shape[0]
    copies = copies_of(tile_hbm, tile_ref, sems)
    copy_x = pltpu.make_async_copy(x_hbm, x_ref, x_sem)
    copy_x.start()
    for copy in copies:
        copy.start()
    mask = block_mask(mask_ref, which, rows)
    copy_x.wait()
    product(x_ref, tile_ref, copies, mask, sum_ref, out_ref)


def tile_product(which, masks, x_t, tile, dtype, mib):
    channels, rows = x_t.shape
    return pl.pallas_call(
        functools.partial(tile_kernel, which),
        in_specs=[WHOLE, ANYWHERE, ANYWHERE],
        out_specs=WHOLE,
        out_shape=jax.ShapeDtypeStruct((channels, rows), dtype),
        scratch_shapes=[
            pltpu.VMEM((channels, rows), x_t.dtype),
            pltpu.VMEM((rows, rows), tile.dtype),
            pltpu.VMEM((channels, rows), jnp.float32),
            pltpu.SemaphoreType.DMA,
            pltpu.SemaphoreType.DMA((2,)),
        ],
        compiler_params=params(mib),
        cost_estimate=cost(2 * channels * rows * rows, 2 * rows * rows),
    )(masks, x_t, tile)


def later_kernel(mask_ref, later_ref, tile_hbm, first_ref, out_ref, tile_ref, sems):
    rows = tile_ref.shape[0]
    copies = copies_of(tile_hbm, tile_ref, sems)
    for copy in copies:
        copy.start()
    mask = block_mask(mask_ref, 1, rows)
    for n, (start, size) in enumerate(halves(rows)):
        copies[n].wait()
        mask_rows(tile_ref, mask, start, size)
        for row, count in strips(size, 2 * SUBBLOCK):
            here = (slice(None), slice(start + row, start + row + count))
            out_ref[here] = first_ref[here] + dot(
                later_ref[...], tile_ref[start + row : start + row + count, :], ((1,), (1,))
            )


def later_product(masks, later, tile, first):
    channels, rows = later.shape
    return pl.pallas_call(
        later_kernel,
        in_specs=[WHOLE, WHOLE, ANYWHERE, WHOLE],
        out_specs=WHOLE,
        out_shape=jax.ShapeDtypeStruct((channels, rows), jnp.float32),
        scratch_shapes=[
            pltpu.VMEM((rows, rows), tile.dtype),
            pltpu.SemaphoreType.DMA((2,)),
        ],
        compiler_params=params(),
        cost_estimate=cost(2 * channels * rows * rows, 2 * rows * rows),
    )(masks, later, tile, first)


def lower_rows(channels):
    rows = round_up(channels, PANEL)
    return sum(rows - g * LANES for g in range(round_up(channels, LANES) // LANES))


def full_rows(channels):
    rows, wide = round_up(channels, PANEL), round_up(channels, LANES)
    whole = channels // LANES
    rest = rows - whole * LANES
    return round_up(whole * rows + rest * (wide // LANES), 4 * PANEL)


def lower_products(ref, out_ref):
    channels = ref.shape[0]
    rows = round_up(channels, PANEL)
    offset = 0
    for start, size in strips(channels, LANES):
        tall = rows - start
        if size < LANES:
            out_ref[offset : offset + tall, :] = jnp.zeros((tall, LANES), jnp.float32)
        elif rows > channels:
            out_ref[offset + channels - start : offset + tall, :] = jnp.zeros(
                (rows - channels, LANES), jnp.float32
            )
        out_ref[offset : offset + channels - start, 0:size] = dot(
            ref[start:channels, :], ref[start : start + size, :], ((1,), (1,))
        )
        offset += tall


def full_products(left_ref, right_ref, out_ref):
    channels = left_ref.shape[0]
    rows = round_up(channels, PANEL)
    whole = channels // LANES
    for g in range(whole):
        out_ref[g * rows : g * rows + channels, :] = dot(
            left_ref[...], right_ref[g * LANES : (g + 1) * LANES, :], ((1,), (1,))
        )
        if rows > channels:
            out_ref[g * rows + channels : (g + 1) * rows, :] = jnp.zeros(
                (rows - channels, LANES), jnp.float32
            )
    base = whole * rows
    if base < out_ref.shape[0]:
        out_ref[base:, :] = jnp.zeros((out_ref.shape[0] - base, LANES), jnp.float32)
    first, rest = whole * LANES, rows - whole * LANES
    for n, (start, size) in enumerate(strips(channels, LANES) if first < channels else []):
        place = base + n * rest
        out_ref[place : place + channels - first, 0:size] = dot(
            right_ref[first:channels, :], left_ref[start : start + size, :], ((1,), (1,))
        )


def full_matrix(pack_ref, channels):
    rows, wide = round_up(channels, PANEL), round_up(channels, LANES)
    whole = channels // LANES
    rest = rows - whole * LANES
    parts = [pack_ref[g * rows : (g + 1) * rows, :] for g in range(whole)]
    if rest:
        tail = jnp.concatenate(
            [
                pack_ref[whole * rows + g * rest : whole * rows + (g + 1) * rest, :]
                for g in range(wide // LANES)
            ],
            axis=1,
        )
        tail = jnp.concatenate([tail, jnp.zeros((LANES - rest, wide), tail.dtype)], axis=0)
        parts.append(tail.T[0:rows, :])
    return jnp.concatenate(parts, axis=1)


def folded_rows(channels):
    if channels < 2 * LANES:
        return lower_rows(channels)
    return lower_rows(channels) - LANES + PANEL


def corner(channels):
    return round_up(channels, PANEL)


def square_index():
    row = lax.broadcasted_iota(jnp.int32, (LANES, LANES), 0)
    return row, lax.broadcasted_iota(jnp.int32, (LANES, LANES), 1)


def fold(pack_ref, out_ref, channels, symmetric):
    if channels < 2 * LANES:
        out_ref[...] = pack_ref[...]
        return
    start = corner(channels)
    end = pack_ref.shape[0]
    row, lane = square_index()
    second = pack_ref[start : start + LANES, :]
    upper = second if symmetric else second.T
    out_ref[0:LANES, :] = jnp.where(row >= lane, pack_ref[0:LANES, :], upper)
    out_ref[LANES:start, :] = pack_ref[LANES:start, :]
    out_ref[start : end - LANES, :] = pack_ref[start + LANES : end, :]
    diagonal = jnp.sum(jnp.where(row == lane, second, 0.0), axis=0, keepdims=True)
    out_ref[end - LANES :, :] = jnp.broadcast_to(diagonal, (PANEL, LANES))


def unfold(folded_ref, pack_ref, channels, symmetric):
    if channels < 2 * LANES:
        pack_ref[...] = folded_ref[...]
        return
    start = corner(channels)
    end = pack_ref.shape[0]
    row, lane = square_index()
    both = folded_ref[0:LANES, :]
    turned = both.T
    first_upper, second_upper = (turned, both) if symmetric else (0.0, 0.0)
    pack_ref[0:LANES, :] = jnp.where(row >= lane, both, first_upper)
    pack_ref[LANES:start, :] = folded_ref[LANES:start, :]
    second = jnp.where(row > lane, turned, second_upper)
    diagonal = folded_ref[end - LANES : end - LANES + 1, :]
    pack_ref[start : start + LANES, :] = jnp.where(row == lane, diagonal, second)
    pack_ref[start + LANES : end, :] = folded_ref[start : end - LANES, :]


def cut(pack_ref, core, mine_ref, other_ref):
    half = mine_ref.shape[0]
    mine_ref[...] = pack_ref[pl.ds(pl.multiple_of(core * half, 8), half), :].astype(mine_ref.dtype)
    other_ref[...] = pack_ref[pl.ds(pl.multiple_of((1 - core) * half, 8), half), :].astype(
        other_ref.dtype
    )


def join(pack_ref, core, mine, other):
    half = mine.shape[0]
    pack_ref[pl.ds(pl.multiple_of(core * half, 8), half), :] = mine
    pack_ref[pl.ds(pl.multiple_of((1 - core) * half, 8), half), :] = other


def gram_kernel(core_ref, part_ref, carried_ref, y_ref, g_mine, g_other, gram_ref, folded_ref):
    image = part_ref[...] + carried_ref[...].astype(jnp.float32)
    y_ref[...] = image.astype(y_ref.dtype)
    lower_products(y_ref, gram_ref)
    fold(gram_ref, folded_ref, y_ref.shape[0], True)
    cut(folded_ref, core_ref[0], g_mine, g_other)


def gram(core, part, carried):
    channels, rows = carried.shape
    lower, folded = lower_rows(channels), folded_rows(channels)
    half = jax.ShapeDtypeStruct((folded // 2, LANES), jnp.float32)
    return pl.pallas_call(
        gram_kernel,
        in_specs=[SCALARS] + [WHOLE] * 2,
        out_specs=[WHOLE] * 3,
        out_shape=[jax.ShapeDtypeStruct((channels, rows), carried.dtype), half, half],
        scratch_shapes=[
            pltpu.VMEM((lower, LANES), jnp.float32),
            pltpu.VMEM((folded, LANES), jnp.float32),
        ],
        compiler_params=params(),
        cost_estimate=cost(2 * channels * channels * rows, 8 * channels * rows),
    )(core, part, carried)


def cross_kernel(core_ref, left_ref, right_ref, after_ref, mine_ref, other_ref, pack_ref):
    full_products(left_ref, right_ref, pack_ref)
    cut(pack_ref, core_ref[0], mine_ref, other_ref)


def cross(core, left, right, after, dtype):
    channels, rows = left.shape
    full = full_rows(channels)
    return pl.pallas_call(
        cross_kernel,
        in_specs=[SCALARS, WHOLE, WHOLE, ANYWHERE],
        out_specs=[WHOLE] * 2,
        out_shape=[jax.ShapeDtypeStruct((full // 2, LANES), dtype)] * 2,
        scratch_shapes=[pltpu.VMEM((full, LANES), jnp.float32)],
        compiler_params=params(),
        cost_estimate=cost(2 * channels * channels * rows, 4 * channels * rows),
    )(core, left, right, after)


def add_kernel(left_ref, right_ref, *refs):
    total = left_ref[...].astype(jnp.float32) + right_ref[...].astype(jnp.float32)
    refs[-1][...] = total.astype(refs[-1].dtype)


def add_four_kernel(own_ref, first_ref, second_ref, both_ref, after_ref, out_ref):
    own, first, second, both = (
        ref[...].astype(jnp.float32) for ref in (own_ref, first_ref, second_ref, both_ref)
    )
    out_ref[...] = ((own + first) + (second + both)).astype(out_ref.dtype)


def add_four(own, first, second, both, after):
    return pl.pallas_call(
        add_four_kernel,
        in_specs=[WHOLE] * 4 + [ANYWHERE],
        out_specs=WHOLE,
        out_shape=jax.ShapeDtypeStruct(own.shape, own.dtype),
        compiler_params=params(),
        cost_estimate=cost(10**5, 10**5),
    )(own, first, second, both, after)


def add_after(left, right, *after, flops=10**5):
    return pl.pallas_call(
        add_kernel,
        in_specs=[WHOLE] * 2 + [ANYWHERE] * len(after),
        out_specs=WHOLE,
        out_shape=jax.ShapeDtypeStruct(left.shape, left.dtype),
        compiler_params=params(),
        cost_estimate=cost(flops, 10**5),
    )(left, right, *after)


def split3(value):
    high = value.astype(jnp.bfloat16)
    rest = value - high.astype(jnp.float32)
    mid = rest.astype(jnp.bfloat16)
    low = (rest - mid.astype(jnp.float32)).astype(jnp.bfloat16)
    return high, mid, low


def sublane(value, index):
    return jnp.broadcast_to(value[index : index + 1, :], value.shape)


def lane_of(value, index):
    return jnp.take_along_axis(value, jnp.broadcast_to(index, value.shape), axis=1)


def eliminate(columns, panel):
    half = 8
    row = lax.broadcasted_iota(jnp.int32, (half, LANES), 0)
    scales = [jnp.zeros((half, LANES), jnp.float32) for _ in range(2)]
    columns = [list(c) for c in columns]
    panel = [list(p) for p in panel]
    for j in range(0, PANEL, 2):
        h, r = divmod(j, half)
        left, right = columns[j], columns[j + 1]
        a, b, c = sublane(left[h], r), sublane(left[h], r + 1), sublane(right[h], r + 1)
        det = a * c - b * b
        inverse = pl.reciprocal(det, approx=True)
        first, second = [None, None], [None, None]
        for t in range(h, 2):
            x, y = left[t], right[t]
            if t == h:
                x, y = jnp.where(row > r + 1, x, 0.0), jnp.where(row > r + 1, y, 0.0)
            first[t] = (c * x - b * y) * inverse
            second[t] = (a * y - b * x) * inverse
        for later in range(j + 2, PANEL):
            q = later // half
            x, y = sublane(left[q], later % half), sublane(right[q], later % half)
            for t in range(max(h, q), 2):
                columns[later][t] = columns[later][t] - (first[t] * x + second[t] * y)
        inverse_a = pl.reciprocal(a, approx=True)
        first[h] = jnp.where(row == r + 1, b * inverse_a, first[h])
        for group in panel:
            x, y = sublane(group[h], r), sublane(group[h], r + 1)
            for t in range(h, 2):
                group[t] = group[t] - (first[t] * x + second[t] * y)
        scales[h] = jnp.where(row == r, lax.rsqrt(a), scales[h])
        scales[h] = jnp.where(row == r + 1, lax.rsqrt(det * inverse_a), scales[h])
    return [jnp.concatenate([g[0] * scales[0], g[1] * scales[1]], axis=0) for g in panel]


def fill_work(channels, scale, pack_ref, work_ref):
    rows, wide = work_ref.shape
    groups = wide // LANES
    offset = 0
    for g in range(groups):
        top = g * LANES
        size = min(LANES, rows - top)
        column = pack_ref[offset : offset + rows - top, :] * scale
        offset += rows - top
        diag = column[0:size, :]
        if top + LANES > channels:
            row = lax.broadcasted_iota(jnp.int32, diag.shape, 0)
            lane = lax.broadcasted_iota(jnp.int32, diag.shape, 1)
            diag = jnp.where((row == lane) & (lane + top >= channels), 1.0, diag)
        work_ref[top : top + size, top : top + LANES] = diag
        for below in range(g + 1, groups):
            start = (below - g) * LANES
            size_b = min(LANES, rows - below * LANES)
            block = column[start : start + size_b, :]
            if size_b < LANES:
                block = jnp.concatenate(
                    [block, jnp.zeros((LANES - size_b, LANES), jnp.float32)], axis=0
                )
            work_ref[top : top + size, below * LANES : (below + 1) * LANES] = block.T
            work_ref[below * LANES : below * LANES + size_b, top : top + LANES] = jnp.zeros(
                (size_b, LANES), jnp.float32
            )


def eliminate_group(g, work_ref, turned_ref, first=0, last=LANES // PANEL):
    rows, wide = work_ref.shape
    groups = wide // LANES
    row = lax.broadcasted_iota(jnp.int32, (PANEL, LANES), 0)
    lane = lax.broadcasted_iota(jnp.int32, (PANEL, LANES), 1)
    top = g * LANES
    count = min(LANES, rows - top) // PANEL

    def load(local):
        place = pl.ds(pl.multiple_of(top + local, PANEL), PANEL)
        return [work_ref[place, q * LANES : (q + 1) * LANES] for q in range(groups)]

    def panel_step(b, parts, slot):
        local = b * PANEL
        following = jnp.minimum(local + PANEL, (count - 1) * PANEL)
        ahead = load(following)
        pivots = [parts[g][0:8, :], parts[g][8:16, :]]
        columns = [[lane_of(p, local + j) for p in pivots] for j in range(PANEL)]
        inside = (lane >= local) & (lane < local + PANEL)
        identity = jnp.where(lane - local == row, 1.0, 0.0)
        parts = list(parts)
        parts[g] = jnp.where(inside, identity, parts[g])
        done = eliminate(columns, [[p[0:8, :], p[8:16, :]] for p in parts])
        right = []
        for q in range(groups):
            high, mid, low = split3(done[q])
            right.append(jnp.concatenate([high, mid, high, low, mid, high], axis=0))
            if q >= g:
                if q == g:
                    high, mid, low = split3(jnp.where(lane >= local + PANEL, done[q], 0.0))
                left = jnp.concatenate([high, high, mid, high, mid, low], axis=0)
                turned_ref[slot, (q - g) * LANES : (q - g + 1) * LANES, :] = left.T
        right = jnp.concatenate(right, axis=1)
        near = turned_ref[slot, pl.ds(pl.multiple_of(following, PANEL), PANEL), :]
        update = dot(near, right, ((1,), (0,)))
        ahead[g] = jnp.where(inside, 0.0, ahead[g])
        ahead = [ahead[q] - update[:, q * LANES : (q + 1) * LANES] for q in range(groups)]
        for q in range(g, groups):
            low_row = q * LANES
            high_row = min(rows, low_row + LANES)
            base = low_row - top
            update = dot(turned_ref[slot, base : base + high_row - low_row, :], right, ((1,), (0,)))
            for c in range(groups):
                lanes = slice(c * LANES, (c + 1) * LANES)
                old = work_ref[low_row:high_row, lanes]
                if c == g:
                    here = lax.broadcasted_iota(jnp.int32, old.shape, 1)
                    old = jnp.where((here >= local) & (here < local + PANEL), 0.0, old)
                work_ref[low_row:high_row, lanes] = old - update[:, lanes]
        for q in range(groups):
            if q == g:
                done[q] = jnp.where(lane < local + PANEL, done[q], 0.0)
            elif q > g:
                done[q] = jnp.zeros_like(done[q])
            place = pl.ds(pl.multiple_of(top + local, PANEL), PANEL)
            work_ref[place, q * LANES : (q + 1) * LANES] = done[q]
        return ahead

    def two_panels(i, parts):
        return panel_step(first + 2 * i + 1, panel_step(first + 2 * i, parts, 0), 1)

    last = min(last, count)
    parts = lax.fori_loop(0, (last - first) // 2, two_panels, load(first * PANEL))
    if (last - first) % 2:
        panel_step(jnp.int32(last - 1), parts, 0)


def first_stage_kernel(
    channels, scale, core_ref, mine_ref, other_ref, work_ref, pack_ref, folded_ref, turned_ref
):
    join(folded_ref, core_ref[0], mine_ref[...], other_ref[...])
    unfold(folded_ref, pack_ref, channels, True)
    fill_work(channels, scale, pack_ref, work_ref)
    eliminate_group(0, work_ref, turned_ref)
    if work_ref.shape[1] > LANES:
        eliminate_group(1, work_ref, turned_ref, 0, EARLY_PANELS)


def last_stages_kernel(
    channels, before_ref, after_ref, work_ref, folded_ref, pack_ref, turned_ref
):
    work_ref[...] = before_ref[...]
    rows, wide = work_ref.shape
    for g in range(1, wide // LANES):
        eliminate_group(g, work_ref, turned_ref, EARLY_PANELS if g == 1 else 0)
    offset = 0
    for q in range(wide // LANES):
        tall = rows - q * LANES
        pack_ref[offset : offset + tall, :] = work_ref[q * LANES : rows, q * LANES : (q + 1) * LANES]
        offset += tall
    fold(pack_ref, folded_ref, channels, False)


def turned_scratch(channels):
    return pltpu.VMEM((2, round_up(channels, LANES), 6 * PANEL), jnp.bfloat16)


def work_shape(channels):
    return jax.ShapeDtypeStruct((round_up(channels, PANEL), round_up(channels, LANES)), jnp.float32)


def first_stage(core, mine, other, channels, total_rows):
    return pl.pallas_call(
        functools.partial(first_stage_kernel, channels, 1.0 / total_rows),
        in_specs=[SCALARS] + [WHOLE] * 2,
        out_specs=WHOLE,
        out_shape=work_shape(channels),
        scratch_shapes=[
            pltpu.VMEM((lower_rows(channels), LANES), jnp.float32),
            pltpu.VMEM((folded_rows(channels), LANES), jnp.float32),
            turned_scratch(channels),
        ],
        compiler_params=params(),
        cost_estimate=cost(FIRST_STAGE_FLOPS, 10**6),
    )(core, mine, other)


def last_stages(work, channels, after):
    return pl.pallas_call(
        functools.partial(last_stages_kernel, channels),
        in_specs=[WHOLE, ANYWHERE],
        out_specs=[WHOLE] * 2,
        out_shape=[
            work_shape(channels),
            jax.ShapeDtypeStruct((folded_rows(channels), LANES), jnp.float32),
        ],
        scratch_shapes=[
            pltpu.VMEM((lower_rows(channels), LANES), jnp.float32),
            turned_scratch(channels),
        ],
        compiler_params=params(),
        cost_estimate=cost(LAST_STAGES_FLOPS, 10**5),
    )(work, after)


def split2(value):
    high = value.astype(jnp.bfloat16)
    return high, (value - high.astype(jnp.float32)).astype(jnp.bfloat16)


def dot3(left, right, dims):
    left_high, left_low = split2(left)
    right_high, right_low = split2(right)
    return (
        dot(left_high, right_high, dims)
        + dot(left_high, right_low, dims)
        + dot(left_low, right_high, dims)
    )


def lower_matrix(pack_ref, out_ref):
    rows, wide = out_ref.shape
    offset = 0
    for g in range(wide // LANES):
        top = g * LANES
        lanes = slice(top, top + LANES)
        if top:
            out_ref[0:top, lanes] = jnp.zeros((top, LANES), jnp.float32)
        out_ref[top:rows, lanes] = pack_ref[offset : offset + rows - top, :]
        offset += rows - top


def basis_kernel(inverse_ref, y_ref, q_ref, token_ref):
    channels = y_ref.shape[0]
    image = y_ref[...]
    token_ref[...] = jnp.zeros_like(token_ref)
    for start, size in strips(channels, 2 * LANES):
        used = min(channels, start + size)
        high, low = split2(inverse_ref[start : start + size, 0:used])
        both = dot(jnp.concatenate([high, low], axis=0), image[0:used, :], ((1,), (0,)))
        q_ref[start : start + size, :] = (both[0:size, :] + both[size:, :]).astype(q_ref.dtype)


def basis(inverse, y_t):
    channels, rows = y_t.shape
    return pl.pallas_call(
        basis_kernel,
        in_specs=[WHOLE] * 2,
        out_specs=[WHOLE] * 2,
        out_shape=[
            jax.ShapeDtypeStruct(y_t.shape, y_t.dtype),
            jax.ShapeDtypeStruct((8, LANES), jnp.float32),
        ],
        compiler_params=params(),
        cost_estimate=cost(10**5, 10**5),
    )(inverse, y_t)


def matrix_shape(channels):
    return jax.ShapeDtypeStruct((channels, 1, channels), jnp.float32)


def part_kernel(
    channels, scale, core_ref, mine_ref, inverse_ref, previous_ref, out_ref,
    pack_ref, lower_ref, before_ref,
):
    rows, wide = inverse_ref.shape
    half = mine_ref.shape[0]
    join(pack_ref, core_ref[0], mine_ref[...], jnp.zeros((half, LANES), jnp.float32))
    turned = dot3(full_matrix(pack_ref, channels), inverse_ref[...], ((1,), (1,)))
    unfold(previous_ref, lower_ref, channels, False)
    lower_matrix(lower_ref, before_ref)
    total = dot3(before_ref[:, 0:rows], turned, ((1,), (0,))) * scale
    out_ref[:, 0:rows] = total.astype(out_ref.dtype)
    if rows < wide:
        out_ref[:, rows:wide] = jnp.zeros((rows, wide - rows), out_ref.dtype)


def correlation_part(core, mine, inverse, previous, channels, total_rows):
    return pl.pallas_call(
        functools.partial(part_kernel, channels, 1.0 / total_rows),
        in_specs=[SCALARS] + [WHOLE] * 3,
        out_specs=WHOLE,
        out_shape=jax.ShapeDtypeStruct(inverse.shape, jnp.bfloat16),
        scratch_shapes=[
            pltpu.VMEM((full_rows(channels), LANES), jnp.float32),
            pltpu.VMEM((lower_rows(channels), LANES), jnp.float32),
            pltpu.VMEM(inverse.shape, jnp.float32),
        ],
        compiler_params=params(),
        cost_estimate=cost(10**5, 10**5),
    )(core, mine, inverse, previous)


def both_kernel(
    scale, core_ref, left_ref, right_ref, mine_ref, other_ref, out_ref, ray_ref, pack_ref
):
    channels = out_ref.shape[0]
    join(pack_ref, core_ref[0], mine_ref[...].astype(jnp.float32), other_ref[...].astype(jnp.float32))
    ray_ref[:, 0, :] = full_matrix(pack_ref, channels)[0:channels, 0:channels] * scale
    total = left_ref[...].astype(jnp.float32) + right_ref[...].astype(jnp.float32)
    out_ref[:, 0, :] = total[0:channels, 0:channels]


def both_parts(core, left, right, mine, other, channels, total_rows):
    return pl.pallas_call(
        functools.partial(both_kernel, 1.0 / total_rows),
        in_specs=[SCALARS] + [WHOLE] * 4,
        out_specs=[WHOLE] * 2,
        out_shape=[matrix_shape(channels)] * 2,
        scratch_shapes=[pltpu.VMEM((full_rows(channels), LANES), jnp.float32)],
        compiler_params=params(),
        cost_estimate=cost(10**5, 10**5),
    )(core, left, right, mine, other)


def from_behind(value, axis, steps):
    count = lax.axis_size(axis)
    leading, last = (max(0, -steps), min(count, count - steps))
    return lax.ppermute(value, axis, [(source, source + steps) for source in range(leading, last)])


def other_core(value):
    return lax.ppermute(value, "rows", [(s, s ^ 1) for s in range(lax.axis_size("rows"))])


def chip_rounds():
    count = lax.axis_size("rows")
    bits = []
    while 2 << len(bits) < count:
        bits.append(2 << len(bits))
    return [
        [(s, s ^ (bits[n] if s % 2 == 0 else bits[-1 - n])) for s in range(count)]
        for n in range(len(bits))
    ]


def sum_chips(value, after):
    count = lax.axis_size("rows")
    if count == 8:
        others = [
            lax.ppermute(value, "rows", [(s, s ^ bits) for s in range(count)]) for bits in (2, 4, 6)
        ]
        return add_four(value, *others, after)
    for pairs in chip_rounds():
        value = add_after(value, lax.ppermute(value, "rows", pairs), after)
    return value


def shards(x_block, h_diag, h_right, pattern):
    x_t = x_block[0].T
    channels, block_rows = x_t.shape
    masks = pattern[0].transpose(1, 0, 2)
    total_rows = lax.axis_size("rows") * block_rows
    core = (lax.axis_index("rows") % 2).astype(jnp.int32).reshape(1)
    later = from_behind(x_t, "rows", -1)
    carried = from_behind(tile_product(1, masks, x_t, h_right[0], x_t.dtype, 53), "rows", 1)
    first = tile_product(0, masks, x_t, h_diag[0], jnp.float32, 50)
    part = later_product(masks, later, h_right[0], first)
    y_t, g_mine, g_other = gram(core, part, carried)
    previous_y = from_behind(y_t, "sector", 1)
    rounds = chip_rounds()
    g_sum = g_mine + other_core(g_other)
    r_mine, r_other = cross(core, x_t, y_t, g_sum, jnp.bfloat16)
    r_sum = add_after(r_mine, other_core(r_other))
    g_sum = sum_chips(g_sum, r_sum)
    r_first = lax.ppermute(r_sum, "rows", rounds[0])
    work = first_stage(core, g_sum, other_core(g_sum), channels, total_rows)
    r_sum = add_after(r_sum, r_first, work)
    m_mine, m_other = cross(core, previous_y, y_t, r_sum, jnp.float32)
    inverse, pack = last_stages(work, channels, m_other)
    m_sum = add_after(m_mine, other_core(m_other), inverse)
    previous = from_behind(pack, "sector", 1)
    q_t, basis_token = basis(inverse, y_t)
    for pairs in rounds[:-1]:
        m_sum = add_after(m_sum, lax.ppermute(m_sum, "rows", pairs))
    m_sum = add_after(m_sum, lax.ppermute(m_sum, "rows", rounds[-1]), basis_token)
    part = correlation_part(core, m_sum, inverse, previous, channels, total_rows)
    for pairs in rounds[1:]:
        r_sum = add_after(r_sum, lax.ppermute(r_sum, "rows", pairs), flops=LAST_RAY_FLOPS)
    correlation, rayleigh = both_parts(
        core, part, other_core(part), r_sum, other_core(r_sum), channels, total_rows
    )
    return (q_t.T[None], rayleigh.transpose(1, 0, 2), correlation.transpose(1, 0, 2))


def solution(mesh):
    in_specs = (
        P("sector", "rows", None),
        P("sector", "rows", None),
        P("sector", "rows", None),
        P("sector", None, "rows", None),
    )
    out_specs = (P("sector", "rows", None), P("sector", None, None), P("sector", None, None))
    return jax.shard_map(shards, mesh=mesh, in_specs=in_specs, out_specs=out_specs, check_vma=False)
```

```python
import functools

import jax
import jax.numpy as jnp
from jax import lax
from jax.experimental import pallas as pl
from jax.experimental.pallas import tpu as pltpu
from jax.sharding import PartitionSpec as P

SUBBLOCK = 128
LANES = 128
PANEL = 16
EARLY_PANELS = 7
WHOLE = pl.BlockSpec(memory_space=pltpu.VMEM)
SCALARS = pl.BlockSpec(memory_space=pltpu.SMEM)
ANYWHERE = pl.BlockSpec(memory_space=pl.ANY)
MIB = 1024 * 1024
FIRST_STAGE_FLOPS = 5000 * 10**6
LAST_RAY_FLOPS = 3000 * 10**6
LAST_STAGES_FLOPS = 4000 * 10**6


def params(mib=48):
    return pltpu.CompilerParams(vmem_limit_bytes=mib * MIB)


def cost(flops, bytes_accessed):
    return pl.CostEstimate(flops=flops, bytes_accessed=bytes_accessed, transcendentals=0)


def round_up(value, step):
    return (value + step - 1) // step * step


def dot(left, right, dims, precision=None):
    return lax.dot_general(
        left, right, (dims, ((), ())), precision=precision, preferred_element_type=jnp.float32
    )


def block_mask(mask_ref, which, cols, dtype):
    blocks = mask_ref[:, which, :].astype(jnp.float32)
    col = lax.broadcasted_iota(jnp.int32, (blocks.shape[1], cols), 1)
    block = lax.broadcasted_iota(jnp.int32, (blocks.shape[1], cols), 0)
    wide = dot(blocks, jnp.where(col // SUBBLOCK == block, 1.0, 0.0), ((1,), (0,)))
    return [
        jnp.broadcast_to(wide[i : i + 1, :], (PANEL, cols)).astype(dtype)
        for i in range(blocks.shape[0])
    ]


def mask_rows(tile_ref, mask, start, size):
    for i in range(start // SUBBLOCK, (start + size) // SUBBLOCK):
        for row in range(i * SUBBLOCK, (i + 1) * SUBBLOCK, PANEL):
            tile_ref[row : row + PANEL, :] = tile_ref[row : row + PANEL, :] * mask[i]


def strips(rows, width):
    return [(start, min(width, rows - start)) for start in range(0, rows, width)]


def halves(rows):
    first = rows // 512 * 256
    return [(0, first), (first, rows - first)] if first else [(0, rows)]


def copies_of(source, target, sems):
    copies = []
    for n, (start, size) in enumerate(halves(target.shape[0])):
        here = (pl.ds(start, size), slice(None))
        copies.append(pltpu.make_async_copy(source.at[here], target.at[here], sems.at[n]))
    return copies


def product(x_ref, tile_ref, copies, mask, sum_ref, out_ref):
    rows = tile_ref.shape[0]
    for n, (start, size) in enumerate(halves(rows)):
        copies[n].wait()
        if n + 1 < len(copies):
            copies[n + 1].start()
        mask_rows(tile_ref, mask, start, size)
        last = n + 1 == len(copies)
        for col, cols in strips(rows, 2 * SUBBLOCK):
            here = (slice(None), slice(col, col + cols))
            term = dot(
                x_ref[:, start : start + size],
                tile_ref[start : start + size, col : col + cols],
                ((1,), (0,)),
            )
            if n > 0:
                term = sum_ref[here] + term
            if last:
                out_ref[here] = term.astype(out_ref.dtype)
            else:
                sum_ref[here] = term


def tile_kernel(which, mask_ref, x_hbm, tile_hbm, out_ref, x_ref, tile_ref, sum_ref, x_sem, sems):
    rows = tile_ref.shape[0]
    copies = copies_of(tile_hbm, tile_ref, sems)
    copy_x = pltpu.make_async_copy(x_hbm, x_ref, x_sem)
    copies[0].start()
    copy_x.start()
    mask = block_mask(mask_ref, which, rows, tile_ref.dtype)
    copy_x.wait()
    product(x_ref, tile_ref, copies, mask, sum_ref, out_ref)


def tile_product(which, masks, x_t, tile, dtype, mib):
    channels, rows = x_t.shape
    return pl.pallas_call(
        functools.partial(tile_kernel, which),
        in_specs=[WHOLE, ANYWHERE, ANYWHERE],
        out_specs=WHOLE,
        out_shape=jax.ShapeDtypeStruct((channels, rows), dtype),
        scratch_shapes=[
            pltpu.VMEM((channels, rows), x_t.dtype),
            pltpu.VMEM((rows, rows), tile.dtype),
            pltpu.VMEM((channels, rows), jnp.float32),
            pltpu.SemaphoreType.DMA,
            pltpu.SemaphoreType.DMA((2,)),
        ],
        compiler_params=params(mib),
        cost_estimate=cost(2 * channels * rows * rows, 2 * rows * rows),
    )(masks, x_t, tile)


def later_kernel(mask_ref, later_ref, tile_hbm, first_ref, out_ref, tile_ref, sems):
    rows = tile_ref.shape[0]
    copies = copies_of(tile_hbm, tile_ref, sems)
    for copy in copies:
        copy.start()
    mask = block_mask(mask_ref, 1, rows, tile_ref.dtype)
    for n, (start, size) in enumerate(halves(rows)):
        copies[n].wait()
        mask_rows(tile_ref, mask, start, size)
        for row, count in strips(size, 2 * SUBBLOCK):
            here = (slice(None), slice(start + row, start + row + count))
            out_ref[here] = first_ref[here] + dot(
                later_ref[...], tile_ref[start + row : start + row + count, :], ((1,), (1,))
            )


def later_product(masks, later, tile, first):
    channels, rows = later.shape
    return pl.pallas_call(
        later_kernel,
        in_specs=[WHOLE, WHOLE, ANYWHERE, WHOLE],
        out_specs=WHOLE,
        out_shape=jax.ShapeDtypeStruct((channels, rows), jnp.float32),
        scratch_shapes=[
            pltpu.VMEM((rows, rows), tile.dtype),
            pltpu.SemaphoreType.DMA((2,)),
        ],
        compiler_params=params(),
        cost_estimate=cost(2 * channels * rows * rows, 2 * rows * rows),
    )(masks, later, tile, first)


def lower_rows(channels):
    rows = round_up(channels, PANEL)
    return sum(rows - g * LANES for g in range(round_up(channels, LANES) // LANES))


def full_rows(channels):
    rows, wide = round_up(channels, PANEL), round_up(channels, LANES)
    whole = channels // LANES
    rest = rows - whole * LANES
    return round_up(whole * rows + rest * (wide // LANES), 4 * PANEL)


def lower_products(ref, out_ref):
    channels = ref.shape[0]
    rows = round_up(channels, PANEL)
    offset = 0
    for start, size in strips(channels, LANES):
        tall = rows - start
        if size < LANES:
            out_ref[offset : offset + tall, :] = jnp.zeros((tall, LANES), jnp.float32)
        elif rows > channels:
            out_ref[offset + channels - start : offset + tall, :] = jnp.zeros(
                (rows - channels, LANES), jnp.float32
            )
        out_ref[offset : offset + channels - start, 0:size] = dot(
            ref[start:channels, :], ref[start : start + size, :], ((1,), (1,))
        )
        offset += tall


def full_products(left_ref, right_ref, out_ref):
    channels = left_ref.shape[0]
    rows = round_up(channels, PANEL)
    whole = channels // LANES
    for g in range(whole):
        out_ref[g * rows : g * rows + channels, :] = dot(
            left_ref[...], right_ref[g * LANES : (g + 1) * LANES, :], ((1,), (1,))
        )
        if rows > channels:
            out_ref[g * rows + channels : (g + 1) * rows, :] = jnp.zeros(
                (rows - channels, LANES), jnp.float32
            )
    base = whole * rows
    if base < out_ref.shape[0]:
        out_ref[base:, :] = jnp.zeros((out_ref.shape[0] - base, LANES), jnp.float32)
    first, rest = whole * LANES, rows - whole * LANES
    for n, (start, size) in enumerate(strips(channels, LANES) if first < channels else []):
        place = base + n * rest
        out_ref[place : place + channels - first, 0:size] = dot(
            right_ref[first:channels, :], left_ref[start : start + size, :], ((1,), (1,))
        )


def full_matrix(pack_ref, channels):
    rows, wide = round_up(channels, PANEL), round_up(channels, LANES)
    whole = channels // LANES
    rest = rows - whole * LANES
    parts = [pack_ref[g * rows : (g + 1) * rows, :] for g in range(whole)]
    if rest:
        tail = jnp.concatenate(
            [
                pack_ref[whole * rows + g * rest : whole * rows + (g + 1) * rest, :]
                for g in range(wide // LANES)
            ],
            axis=1,
        )
        tail = jnp.concatenate([tail, jnp.zeros((LANES - rest, wide), tail.dtype)], axis=0)
        parts.append(tail.T[0:rows, :])
    return jnp.concatenate(parts, axis=1)


def folded_rows(channels):
    if channels < 2 * LANES:
        return lower_rows(channels)
    return lower_rows(channels) - LANES + PANEL


def corner(channels):
    return round_up(channels, PANEL)


def square_index():
    row = lax.broadcasted_iota(jnp.int32, (LANES, LANES), 0)
    return row, lax.broadcasted_iota(jnp.int32, (LANES, LANES), 1)


def fold(pack_ref, out_ref, channels, symmetric):
    if channels < 2 * LANES:
        out_ref[...] = pack_ref[...]
        return
    start = corner(channels)
    end = pack_ref.shape[0]
    row, lane = square_index()
    second = pack_ref[start : start + LANES, :]
    upper = second if symmetric else second.T
    out_ref[0:LANES, :] = jnp.where(row >= lane, pack_ref[0:LANES, :], upper)
    out_ref[LANES:start, :] = pack_ref[LANES:start, :]
    out_ref[start : end - LANES, :] = pack_ref[start + LANES : end, :]
    diagonal = jnp.sum(jnp.where(row == lane, second, 0.0), axis=0, keepdims=True)
    out_ref[end - LANES :, :] = jnp.broadcast_to(diagonal, (PANEL, LANES))


def unfold(folded_ref, pack_ref, channels, symmetric):
    if channels < 2 * LANES:
        pack_ref[...] = folded_ref[...]
        return
    start = corner(channels)
    end = pack_ref.shape[0]
    row, lane = square_index()
    both = folded_ref[0:LANES, :]
    turned = both.T
    first_upper, second_upper = (turned, both) if symmetric else (0.0, 0.0)
    pack_ref[0:LANES, :] = jnp.where(row >= lane, both, first_upper)
    pack_ref[LANES:start, :] = folded_ref[LANES:start, :]
    second = jnp.where(row > lane, turned, second_upper)
    diagonal = folded_ref[end - LANES : end - LANES + 1, :]
    pack_ref[start : start + LANES, :] = jnp.where(row == lane, diagonal, second)
    pack_ref[start + LANES : end, :] = folded_ref[start : end - LANES, :]


def cut(pack_ref, core, mine_ref, other_ref):
    half = mine_ref.shape[0]
    mine_ref[...] = pack_ref[pl.ds(pl.multiple_of(core * half, 8), half), :].astype(mine_ref.dtype)
    other_ref[...] = pack_ref[pl.ds(pl.multiple_of((1 - core) * half, 8), half), :].astype(
        other_ref.dtype
    )


def join(pack_ref, core, mine, other):
    half = mine.shape[0]
    pack_ref[pl.ds(pl.multiple_of(core * half, 8), half), :] = mine
    pack_ref[pl.ds(pl.multiple_of((1 - core) * half, 8), half), :] = other


def gram_kernel(core_ref, part_ref, carried_ref, y_ref, g_mine, g_other, gram_ref, folded_ref):
    image = part_ref[...] + carried_ref[...].astype(jnp.float32)
    y_ref[...] = image.astype(y_ref.dtype)
    lower_products(y_ref, gram_ref)
    fold(gram_ref, folded_ref, y_ref.shape[0], True)
    cut(folded_ref, core_ref[0], g_mine, g_other)


def gram(core, part, carried):
    channels, rows = carried.shape
    lower, folded = lower_rows(channels), folded_rows(channels)
    half = jax.ShapeDtypeStruct((folded // 2, LANES), jnp.float32)
    return pl.pallas_call(
        gram_kernel,
        in_specs=[SCALARS] + [WHOLE] * 2,
        out_specs=[WHOLE] * 3,
        out_shape=[jax.ShapeDtypeStruct((channels, rows), carried.dtype), half, half],
        scratch_shapes=[
            pltpu.VMEM((lower, LANES), jnp.float32),
            pltpu.VMEM((folded, LANES), jnp.float32),
        ],
        compiler_params=params(),
        cost_estimate=cost(2 * channels * channels * rows, 8 * channels * rows),
    )(core, part, carried)


def cross_kernel(core_ref, left_ref, right_ref, after_ref, mine_ref, other_ref, pack_ref):
    full_products(left_ref, right_ref, pack_ref)
    cut(pack_ref, core_ref[0], mine_ref, other_ref)


def cross(core, left, right, after, dtype):
    channels, rows = left.shape
    full = full_rows(channels)
    return pl.pallas_call(
        cross_kernel,
        in_specs=[SCALARS, WHOLE, WHOLE, ANYWHERE],
        out_specs=[WHOLE] * 2,
        out_shape=[jax.ShapeDtypeStruct((full // 2, LANES), dtype)] * 2,
        scratch_shapes=[pltpu.VMEM((full, LANES), jnp.float32)],
        compiler_params=params(),
        cost_estimate=cost(2 * channels * channels * rows, 4 * channels * rows),
    )(core, left, right, after)


def add_kernel(left_ref, right_ref, *refs):
    total = left_ref[...].astype(jnp.float32) + right_ref[...].astype(jnp.float32)
    refs[-1][...] = total.astype(refs[-1].dtype)


def add_four_kernel(own_ref, first_ref, second_ref, both_ref, after_ref, out_ref):
    own, first, second, both = (
        ref[...].astype(jnp.float32) for ref in (own_ref, first_ref, second_ref, both_ref)
    )
    out_ref[...] = ((own + first) + (second + both)).astype(out_ref.dtype)


def add_four(own, first, second, both, after):
    return pl.pallas_call(
        add_four_kernel,
        in_specs=[WHOLE] * 4 + [ANYWHERE],
        out_specs=WHOLE,
        out_shape=jax.ShapeDtypeStruct(own.shape, own.dtype),
        compiler_params=params(),
        cost_estimate=cost(10**5, 10**5),
    )(own, first, second, both, after)


def add_after(left, right, *after, flops=10**5):
    return pl.pallas_call(
        add_kernel,
        in_specs=[WHOLE] * 2 + [ANYWHERE] * len(after),
        out_specs=WHOLE,
        out_shape=jax.ShapeDtypeStruct(left.shape, left.dtype),
        compiler_params=params(),
        cost_estimate=cost(flops, 10**5),
    )(left, right, *after)


def split3(value):
    high = value.astype(jnp.bfloat16)
    rest = value - high.astype(jnp.float32)
    mid = rest.astype(jnp.bfloat16)
    low = (rest - mid.astype(jnp.float32)).astype(jnp.bfloat16)
    return high, mid, low


def sublane(value, index):
    return jnp.broadcast_to(value[index : index + 1, :], value.shape)


def lane_of(value, index):
    return jnp.take_along_axis(value, jnp.broadcast_to(index, value.shape), axis=1)


def eliminate(columns, panel):
    half = 8
    row = lax.broadcasted_iota(jnp.int32, (half, LANES), 0)
    scales = [jnp.zeros((half, LANES), jnp.float32) for _ in range(2)]
    columns = [list(c) for c in columns]
    panel = [list(p) for p in panel]
    for j in range(0, PANEL, 2):
        h, r = divmod(j, half)
        left, right = columns[j], columns[j + 1]
        a, b, c = sublane(left[h], r), sublane(left[h], r + 1), sublane(right[h], r + 1)
        det = a * c - b * b
        inverse = pl.reciprocal(det, approx=True)
        first, second = [None, None], [None, None]
        for t in range(h, 2):
            x, y = left[t], right[t]
            if t == h:
                x, y = jnp.where(row > r + 1, x, 0.0), jnp.where(row > r + 1, y, 0.0)
            first[t] = (c * x - b * y) * inverse
            second[t] = (a * y - b * x) * inverse
        for later in range(j + 2, PANEL):
            q = later // half
            x, y = sublane(left[q], later % half), sublane(right[q], later % half)
            for t in range(max(h, q), 2):
                columns[later][t] = columns[later][t] - (first[t] * x + second[t] * y)
        inverse_a = pl.reciprocal(a, approx=True)
        first[h] = jnp.where(row == r + 1, b * inverse_a, first[h])
        for group in panel:
            x, y = sublane(group[h], r), sublane(group[h], r + 1)
            for t in range(h, 2):
                group[t] = group[t] - (first[t] * x + second[t] * y)
        scales[h] = jnp.where(row == r, lax.rsqrt(a), scales[h])
        scales[h] = jnp.where(row == r + 1, lax.rsqrt(det * inverse_a), scales[h])
    return [jnp.concatenate([g[0] * scales[0], g[1] * scales[1]], axis=0) for g in panel]


def fill_work(channels, scale, pack_ref, work_ref):
    rows, wide = work_ref.shape
    groups = wide // LANES
    offset = 0
    for g in range(groups):
        top = g * LANES
        size = min(LANES, rows - top)
        column = pack_ref[offset : offset + rows - top, :] * scale
        offset += rows - top
        diag = column[0:size, :]
        if top + LANES > channels:
            row = lax.broadcasted_iota(jnp.int32, diag.shape, 0)
            lane = lax.broadcasted_iota(jnp.int32, diag.shape, 1)
            diag = jnp.where((row == lane) & (lane + top >= channels), 1.0, diag)
        work_ref[top : top + size, top : top + LANES] = diag
        for below in range(g + 1, groups):
            start = (below - g) * LANES
            size_b = min(LANES, rows - below * LANES)
            block = column[start : start + size_b, :]
            if size_b < LANES:
                block = jnp.concatenate(
                    [block, jnp.zeros((LANES - size_b, LANES), jnp.float32)], axis=0
                )
            work_ref[top : top + size, below * LANES : (below + 1) * LANES] = block.T
            work_ref[below * LANES : below * LANES + size_b, top : top + LANES] = jnp.zeros(
                (size_b, LANES), jnp.float32
            )


def eliminate_group(g, work_ref, turned_ref, first=0, last=LANES // PANEL):
    rows, wide = work_ref.shape
    groups = wide // LANES
    row = lax.broadcasted_iota(jnp.int32, (PANEL, LANES), 0)
    lane = lax.broadcasted_iota(jnp.int32, (PANEL, LANES), 1)
    top = g * LANES
    count = min(LANES, rows - top) // PANEL

    def load(local):
        place = pl.ds(pl.multiple_of(top + local, PANEL), PANEL)
        return [work_ref[place, q * LANES : (q + 1) * LANES] for q in range(groups)]

    def panel_step(b, parts, slot):
        local = b * PANEL
        following = jnp.minimum(local + PANEL, (count - 1) * PANEL)
        ahead = load(following)
        pivots = [parts[g][0:8, :], parts[g][8:16, :]]
        columns = [[lane_of(p, local + j) for p in pivots] for j in range(PANEL)]
        inside = (lane >= local) & (lane < local + PANEL)
        identity = jnp.where(lane - local == row, 1.0, 0.0)
        parts = list(parts)
        parts[g] = jnp.where(inside, identity, parts[g])
        done = eliminate(columns, [[p[0:8, :], p[8:16, :]] for p in parts])
        right = []
        for q in range(groups):
            high, mid, low = split3(done[q])
            right.append(jnp.concatenate([high, mid, high, low, mid, high], axis=0))
            if q >= g:
                if q == g:
                    high, mid, low = split3(jnp.where(lane >= local + PANEL, done[q], 0.0))
                left = jnp.concatenate([high, high, mid, high, mid, low], axis=0)
                turned_ref[slot, (q - g) * LANES : (q - g + 1) * LANES, :] = left.T
        right = jnp.concatenate(right, axis=1)
        near = turned_ref[slot, pl.ds(pl.multiple_of(following, PANEL), PANEL), :]
        update = dot(near, right, ((1,), (0,)))
        ahead[g] = jnp.where(inside, 0.0, ahead[g])
        ahead = [ahead[q] - update[:, q * LANES : (q + 1) * LANES] for q in range(groups)]
        for q in range(g, groups):
            low_row = q * LANES
            high_row = min(rows, low_row + LANES)
            base = low_row - top
            update = dot(turned_ref[slot, base : base + high_row - low_row, :], right, ((1,), (0,)))
            for c in range(groups):
                lanes = slice(c * LANES, (c + 1) * LANES)
                old = work_ref[low_row:high_row, lanes]
                if c == g:
                    here = lax.broadcasted_iota(jnp.int32, old.shape, 1)
                    old = jnp.where((here >= local) & (here < local + PANEL), 0.0, old)
                work_ref[low_row:high_row, lanes] = old - update[:, lanes]
        for q in range(groups):
            if q == g:
                done[q] = jnp.where(lane < local + PANEL, done[q], 0.0)
            elif q > g:
                done[q] = jnp.zeros_like(done[q])
            place = pl.ds(pl.multiple_of(top + local, PANEL), PANEL)
            work_ref[place, q * LANES : (q + 1) * LANES] = done[q]
        return ahead

    def two_panels(i, parts):
        return panel_step(first + 2 * i + 1, panel_step(first + 2 * i, parts, 0), 1)

    last = min(last, count)
    parts = lax.fori_loop(0, (last - first) // 2, two_panels, load(first * PANEL))
    if (last - first) % 2:
        panel_step(jnp.int32(last - 1), parts, 0)


def first_stage_kernel(
    channels, scale, core_ref, mine_ref, other_ref, work_ref, pack_ref, folded_ref, turned_ref
):
    join(folded_ref, core_ref[0], mine_ref[...], other_ref[...])
    unfold(folded_ref, pack_ref, channels, True)
    fill_work(channels, scale, pack_ref, work_ref)
    eliminate_group(0, work_ref, turned_ref)
    if work_ref.shape[1] > LANES:
        eliminate_group(1, work_ref, turned_ref, 0, EARLY_PANELS)


def last_stages_kernel(
    channels, before_ref, after_ref, work_ref, folded_ref, pack_ref, turned_ref
):
    work_ref[...] = before_ref[...]
    rows, wide = work_ref.shape
    for g in range(1, wide // LANES):
        eliminate_group(g, work_ref, turned_ref, EARLY_PANELS if g == 1 else 0)
    offset = 0
    for q in range(wide // LANES):
        tall = rows - q * LANES
        pack_ref[offset : offset + tall, :] = work_ref[q * LANES : rows, q * LANES : (q + 1) * LANES]
        offset += tall
    fold(pack_ref, folded_ref, channels, False)


def turned_scratch(channels):
    return pltpu.VMEM((2, round_up(channels, LANES), 6 * PANEL), jnp.bfloat16)


def work_shape(channels):
    return jax.ShapeDtypeStruct((round_up(channels, PANEL), round_up(channels, LANES)), jnp.float32)


def first_stage(core, mine, other, channels, total_rows):
    return pl.pallas_call(
        functools.partial(first_stage_kernel, channels, 1.0 / total_rows),
        in_specs=[SCALARS] + [WHOLE] * 2,
        out_specs=WHOLE,
        out_shape=work_shape(channels),
        scratch_shapes=[
            pltpu.VMEM((lower_rows(channels), LANES), jnp.float32),
            pltpu.VMEM((folded_rows(channels), LANES), jnp.float32),
            turned_scratch(channels),
        ],
        compiler_params=params(),
        cost_estimate=cost(FIRST_STAGE_FLOPS, 10**6),
    )(core, mine, other)


def last_stages(work, channels, after):
    return pl.pallas_call(
        functools.partial(last_stages_kernel, channels),
        in_specs=[WHOLE, ANYWHERE],
        out_specs=[WHOLE] * 2,
        out_shape=[
            work_shape(channels),
            jax.ShapeDtypeStruct((folded_rows(channels), LANES), jnp.float32),
        ],
        scratch_shapes=[
            pltpu.VMEM((lower_rows(channels), LANES), jnp.float32),
            turned_scratch(channels),
        ],
        compiler_params=params(),
        cost_estimate=cost(LAST_STAGES_FLOPS, 10**5),
    )(work, after)


def split2(value):
    high = value.astype(jnp.bfloat16)
    return high, (value - high.astype(jnp.float32)).astype(jnp.bfloat16)


def dot3(left, right, dims):
    left_high, left_low = split2(left)
    right_high, right_low = split2(right)
    return (
        dot(left_high, right_high, dims)
        + dot(left_high, right_low, dims)
        + dot(left_low, right_high, dims)
    )


def lower_matrix(pack_ref, out_ref):
    rows, wide = out_ref.shape
    offset = 0
    for g in range(wide // LANES):
        top = g * LANES
        lanes = slice(top, top + LANES)
        if top:
            out_ref[0:top, lanes] = jnp.zeros((top, LANES), jnp.float32)
        out_ref[top:rows, lanes] = pack_ref[offset : offset + rows - top, :]
        offset += rows - top


def basis_kernel(inverse_ref, y_ref, q_ref, token_ref):
    channels = y_ref.shape[0]
    image = y_ref[...]
    token_ref[...] = jnp.zeros_like(token_ref)
    for start, size in strips(channels, 2 * LANES):
        used = min(channels, start + size)
        high, low = split2(inverse_ref[start : start + size, 0:used])
        both = dot(jnp.concatenate([high, low], axis=0), image[0:used, :], ((1,), (0,)))
        q_ref[start : start + size, :] = (both[0:size, :] + both[size:, :]).astype(q_ref.dtype)


def basis(inverse, y_t):
    channels, rows = y_t.shape
    return pl.pallas_call(
        basis_kernel,
        in_specs=[WHOLE] * 2,
        out_specs=[WHOLE] * 2,
        out_shape=[
            jax.ShapeDtypeStruct(y_t.shape, y_t.dtype),
            jax.ShapeDtypeStruct((8, LANES), jnp.float32),
        ],
        compiler_params=params(),
        cost_estimate=cost(10**5, 10**5),
    )(inverse, y_t)


def matrix_shape(channels):
    return jax.ShapeDtypeStruct((channels, 1, channels), jnp.float32)


def part_kernel(
    channels, scale, core_ref, mine_ref, inverse_ref, previous_ref, out_ref,
    pack_ref, lower_ref, before_ref,
):
    rows, wide = inverse_ref.shape
    half = mine_ref.shape[0]
    join(pack_ref, core_ref[0], mine_ref[...], jnp.zeros((half, LANES), jnp.float32))
    turned = dot3(full_matrix(pack_ref, channels), inverse_ref[...], ((1,), (1,)))
    unfold(previous_ref, lower_ref, channels, False)
    lower_matrix(lower_ref, before_ref)
    total = dot3(before_ref[:, 0:rows], turned, ((1,), (0,))) * scale
    out_ref[:, 0:rows] = total.astype(out_ref.dtype)
    if rows < wide:
        out_ref[:, rows:wide] = jnp.zeros((rows, wide - rows), out_ref.dtype)


def correlation_part(core, mine, inverse, previous, channels, total_rows):
    return pl.pallas_call(
        functools.partial(part_kernel, channels, 1.0 / total_rows),
        in_specs=[SCALARS] + [WHOLE] * 3,
        out_specs=WHOLE,
        out_shape=jax.ShapeDtypeStruct(inverse.shape, jnp.bfloat16),
        scratch_shapes=[
            pltpu.VMEM((full_rows(channels), LANES), jnp.float32),
            pltpu.VMEM((lower_rows(channels), LANES), jnp.float32),
            pltpu.VMEM(inverse.shape, jnp.float32),
        ],
        compiler_params=params(),
        cost_estimate=cost(10**5, 10**5),
    )(core, mine, inverse, previous)


def both_kernel(
    scale, core_ref, left_ref, right_ref, mine_ref, other_ref, out_ref, ray_ref, pack_ref
):
    channels = out_ref.shape[0]
    join(pack_ref, core_ref[0], mine_ref[...].astype(jnp.float32), other_ref[...].astype(jnp.float32))
    ray_ref[:, 0, :] = full_matrix(pack_ref, channels)[0:channels, 0:channels] * scale
    total = left_ref[...].astype(jnp.float32) + right_ref[...].astype(jnp.float32)
    out_ref[:, 0, :] = total[0:channels, 0:channels]


def both_parts(core, left, right, mine, other, channels, total_rows):
    return pl.pallas_call(
        functools.partial(both_kernel, 1.0 / total_rows),
        in_specs=[SCALARS] + [WHOLE] * 4,
        out_specs=[WHOLE] * 2,
        out_shape=[matrix_shape(channels)] * 2,
        scratch_shapes=[pltpu.VMEM((full_rows(channels), LANES), jnp.float32)],
        compiler_params=params(),
        cost_estimate=cost(10**5, 10**5),
    )(core, left, right, mine, other)


def from_behind(value, axis, steps):
    count = lax.axis_size(axis)
    leading, last = (max(0, -steps), min(count, count - steps))
    return lax.ppermute(value, axis, [(source, source + steps) for source in range(leading, last)])


def other_core(value):
    return lax.ppermute(value, "rows", [(s, s ^ 1) for s in range(lax.axis_size("rows"))])


def chip_rounds():
    count = lax.axis_size("rows")
    bits = []
    while 2 << len(bits) < count:
        bits.append(2 << len(bits))
    return [
        [(s, s ^ (bits[n] if s % 2 == 0 else bits[-1 - n])) for s in range(count)]
        for n in range(len(bits))
    ]


def sum_chips(value, after):
    count = lax.axis_size("rows")
    if count == 8:
        others = [
            lax.ppermute(value, "rows", [(s, s ^ bits) for s in range(count)]) for bits in (2, 4, 6)
        ]
        return add_four(value, *others, after)
    for pairs in chip_rounds():
        value = add_after(value, lax.ppermute(value, "rows", pairs), after)
    return value


def shards(x_block, h_diag, h_right, pattern):
    x_t = x_block[0].T
    channels, block_rows = x_t.shape
    masks = pattern[0].transpose(1, 0, 2)
    total_rows = lax.axis_size("rows") * block_rows
    core = (lax.axis_index("rows") % 2).astype(jnp.int32).reshape(1)
    later = from_behind(x_t, "rows", -1)
    carried = from_behind(tile_product(1, masks, x_t, h_right[0], x_t.dtype, 53), "rows", 1)
    first = tile_product(0, masks, x_t, h_diag[0], jnp.float32, 50)
    part = later_product(masks, later, h_right[0], first)
    y_t, g_mine, g_other = gram(core, part, carried)
    previous_y = from_behind(y_t, "sector", 1)
    rounds = chip_rounds()
    g_sum = g_mine + other_core(g_other)
    r_mine, r_other = cross(core, x_t, y_t, g_sum, jnp.bfloat16)
    r_sum = add_after(r_mine, other_core(r_other))
    g_sum = sum_chips(g_sum, r_sum)
    r_first = lax.ppermute(r_sum, "rows", rounds[0])
    work = first_stage(core, g_sum, other_core(g_sum), channels, total_rows)
    r_sum = add_after(r_sum, r_first, work)
    m_mine, m_other = cross(core, previous_y, y_t, r_sum, jnp.float32)
    inverse, pack = last_stages(work, channels, m_other)
    m_sum = add_after(m_mine, other_core(m_other), inverse)
    previous = from_behind(pack, "sector", 1)
    q_t, basis_token = basis(inverse, y_t)
    for pairs in rounds[:-1]:
        m_sum = add_after(m_sum, lax.ppermute(m_sum, "rows", pairs))
    m_sum = add_after(m_sum, lax.ppermute(m_sum, "rows", rounds[-1]), basis_token)
    part = correlation_part(core, m_sum, inverse, previous, channels, total_rows)
    for pairs in rounds[1:]:
        r_sum = add_after(r_sum, lax.ppermute(r_sum, "rows", pairs), flops=LAST_RAY_FLOPS)
    correlation, rayleigh = both_parts(
        core, part, other_core(part), r_sum, other_core(r_sum), channels, total_rows
    )
    return (q_t.T[None], rayleigh.transpose(1, 0, 2), correlation.transpose(1, 0, 2))


def solution(mesh):
    in_specs = (
        P("sector", "rows", None),
        P("sector", "rows", None),
        P("sector", "rows", None),
        P("sector", None, "rows", None),
    )
    out_specs = (P("sector", "rows", None), P("sector", None, None), P("sector", None, None))
    return jax.shard_map(shards, mesh=mesh, in_specs=in_specs, out_specs=out_specs, check_vma=False)
```

```python
import functools

import jax
import jax.numpy as jnp
from jax import lax
from jax.experimental import pallas as pl
from jax.experimental.pallas import tpu as pltpu
from jax.sharding import PartitionSpec as P

SUBBLOCK = 128
LANES = 128
PANEL = 16
EARLY_PANELS = 7
WHOLE = pl.BlockSpec(memory_space=pltpu.VMEM)
SCALARS = pl.BlockSpec(memory_space=pltpu.SMEM)
ANYWHERE = pl.BlockSpec(memory_space=pl.ANY)
MIB = 1024 * 1024
FIRST_STAGE_FLOPS = 5000 * 10**6
LAST_RAY_FLOPS = 3000 * 10**6
LAST_STAGES_FLOPS = 4000 * 10**6


def params(mib=48):
    return pltpu.CompilerParams(vmem_limit_bytes=mib * MIB)


def cost(flops, bytes_accessed):
    return pl.CostEstimate(flops=flops, bytes_accessed=bytes_accessed, transcendentals=0)


def round_up(value, step):
    return (value + step - 1) // step * step


def dot(left, right, dims, precision=None):
    return lax.dot_general(
        left, right, (dims, ((), ())), precision=precision, preferred_element_type=jnp.float32
    )


def block_mask(mask_ref, which, cols, dtype):
    blocks = mask_ref[:, which, :].astype(jnp.float32)
    col = lax.broadcasted_iota(jnp.int32, (blocks.shape[1], cols), 1)
    block = lax.broadcasted_iota(jnp.int32, (blocks.shape[1], cols), 0)
    wide = dot(blocks, jnp.where(col // SUBBLOCK == block, 1.0, 0.0), ((1,), (0,)))
    return [
        jnp.broadcast_to(wide[i : i + 1, :], (PANEL, cols)).astype(dtype)
        for i in range(blocks.shape[0])
    ]


def mask_rows(tile_ref, mask, start, size):
    for i in range(start // SUBBLOCK, (start + size) // SUBBLOCK):
        for row in range(i * SUBBLOCK, (i + 1) * SUBBLOCK, PANEL):
            tile_ref[row : row + PANEL, :] = tile_ref[row : row + PANEL, :] * mask[i]


def strips(rows, width):
    return [(start, min(width, rows - start)) for start in range(0, rows, width)]


def halves(rows):
    first = rows // 512 * 256
    return [(0, first), (first, rows - first)] if first else [(0, rows)]


def copies_of(source, target, sems):
    copies = []
    for n, (start, size) in enumerate(halves(target.shape[0])):
        here = (pl.ds(start, size), slice(None))
        copies.append(pltpu.make_async_copy(source.at[here], target.at[here], sems.at[n]))
    return copies


def product(x_ref, tile_ref, copies, mask, sum_ref, out_ref):
    rows = tile_ref.shape[0]
    for n, (start, size) in enumerate(halves(rows)):
        copies[n].wait()
        mask_rows(tile_ref, mask, start, size)
        last = n + 1 == len(copies)
        for col, cols in strips(rows, 2 * SUBBLOCK):
            here = (slice(None), slice(col, col + cols))
            term = dot(
                x_ref[:, start : start + size],
                tile_ref[start : start + size, col : col + cols],
                ((1,), (0,)),
            )
            if n > 0:
                term = sum_ref[here] + term
            if last:
                out_ref[here] = term.astype(out_ref.dtype)
            else:
                sum_ref[here] = term


def tile_kernel(which, mask_ref, x_hbm, tile_hbm, out_ref, x_ref, tile_ref, sum_ref, x_sem, sems):
    rows = tile_ref.shape[0]
    copies = copies_of(tile_hbm, tile_ref, sems)
    copy_x = pltpu.make_async_copy(x_hbm, x_ref, x_sem)
    copy_x.start()
    for copy in copies:
        copy.start()
    mask = block_mask(mask_ref, which, rows, tile_ref.dtype)
    copy_x.wait()
    product(x_ref, tile_ref, copies, mask, sum_ref, out_ref)


def tile_product(which, masks, x_t, tile, dtype, mib):
    channels, rows = x_t.shape
    return pl.pallas_call(
        functools.partial(tile_kernel, which),
        in_specs=[WHOLE, ANYWHERE, ANYWHERE],
        out_specs=WHOLE,
        out_shape=jax.ShapeDtypeStruct((channels, rows), dtype),
        scratch_shapes=[
            pltpu.VMEM((channels, rows), x_t.dtype),
            pltpu.VMEM((rows, rows), tile.dtype),
            pltpu.VMEM((channels, rows), jnp.float32),
            pltpu.SemaphoreType.DMA,
            pltpu.SemaphoreType.DMA((2,)),
        ],
        compiler_params=params(mib),
        cost_estimate=cost(2 * channels * rows * rows, 2 * rows * rows),
    )(masks, x_t, tile)


def later_kernel(mask_ref, later_ref, tile_hbm, first_ref, out_ref, tile_ref, sems):
    rows = tile_ref.shape[0]
    copies = copies_of(tile_hbm, tile_ref, sems)
    for copy in copies:
        copy.start()
    mask = block_mask(mask_ref, 1, rows, tile_ref.dtype)
    for n, (start, size) in enumerate(halves(rows)):
        copies[n].wait()
        mask_rows(tile_ref, mask, start, size)
        for row, count in strips(size, 2 * SUBBLOCK):
            here = (slice(None), slice(start + row, start + row + count))
            out_ref[here] = first_ref[here] + dot(
                later_ref[...], tile_ref[start + row : start + row + count, :], ((1,), (1,))
            )


def later_product(masks, later, tile, first):
    channels, rows = later.shape
    return pl.pallas_call(
        later_kernel,
        in_specs=[WHOLE, WHOLE, ANYWHERE, WHOLE],
        out_specs=WHOLE,
        out_shape=jax.ShapeDtypeStruct((channels, rows), jnp.float32),
        scratch_shapes=[
            pltpu.VMEM((rows, rows), tile.dtype),
            pltpu.SemaphoreType.DMA((2,)),
        ],
        compiler_params=params(),
        cost_estimate=cost(2 * channels * rows * rows, 2 * rows * rows),
    )(masks, later, tile, first)


def lower_rows(channels):
    rows = round_up(channels, PANEL)
    return sum(rows - g * LANES for g in range(round_up(channels, LANES) // LANES))


def full_rows(channels):
    rows, wide = round_up(channels, PANEL), round_up(channels, LANES)
    whole = channels // LANES
    rest = rows - whole * LANES
    return round_up(whole * rows + rest * (wide // LANES), 4 * PANEL)


def lower_products(left_ref, right_ref, out_ref):
    channels = left_ref.shape[0]
    rows = round_up(channels, PANEL)
    offset = 0
    for start, size in strips(channels, LANES):
        tall = rows - start
        if size < LANES:
            out_ref[offset : offset + tall, :] = jnp.zeros((tall, LANES), jnp.float32)
        elif rows > channels:
            out_ref[offset + channels - start : offset + tall, :] = jnp.zeros(
                (rows - channels, LANES), jnp.float32
            )
        out_ref[offset : offset + channels - start, 0:size] = dot(
            left_ref[start:channels, :], right_ref[start : start + size, :], ((1,), (1,))
        )
        offset += tall


def full_products(left_ref, right_ref, out_ref):
    channels = left_ref.shape[0]
    rows = round_up(channels, PANEL)
    whole = channels // LANES
    for g in range(whole):
        out_ref[g * rows : g * rows + channels, :] = dot(
            left_ref[...], right_ref[g * LANES : (g + 1) * LANES, :], ((1,), (1,))
        )
        if rows > channels:
            out_ref[g * rows + channels : (g + 1) * rows, :] = jnp.zeros(
                (rows - channels, LANES), jnp.float32
            )
    base = whole * rows
    if base < out_ref.shape[0]:
        out_ref[base:, :] = jnp.zeros((out_ref.shape[0] - base, LANES), jnp.float32)
    first, rest = whole * LANES, rows - whole * LANES
    for n, (start, size) in enumerate(strips(channels, LANES) if first < channels else []):
        place = base + n * rest
        out_ref[place : place + channels - first, 0:size] = dot(
            right_ref[first:channels, :], left_ref[start : start + size, :], ((1,), (1,))
        )


def full_matrix(pack_ref, channels):
    rows, wide = round_up(channels, PANEL), round_up(channels, LANES)
    whole = channels // LANES
    rest = rows - whole * LANES
    parts = [pack_ref[g * rows : (g + 1) * rows, :] for g in range(whole)]
    if rest:
        tail = jnp.concatenate(
            [
                pack_ref[whole * rows + g * rest : whole * rows + (g + 1) * rest, :]
                for g in range(wide // LANES)
            ],
            axis=1,
        )
        tail = jnp.concatenate([tail, jnp.zeros((LANES - rest, wide), tail.dtype)], axis=0)
        parts.append(tail.T[0:rows, :])
    return jnp.concatenate(parts, axis=1)


def folded_rows(channels):
    if channels < 2 * LANES:
        return lower_rows(channels)
    return lower_rows(channels) - LANES + PANEL


def corner(channels):
    return round_up(channels, PANEL)


def square_index():
    row = lax.broadcasted_iota(jnp.int32, (LANES, LANES), 0)
    return row, lax.broadcasted_iota(jnp.int32, (LANES, LANES), 1)


def fold(pack_ref, out_ref, channels, symmetric):
    if channels < 2 * LANES:
        out_ref[...] = pack_ref[...]
        return
    start = corner(channels)
    end = pack_ref.shape[0]
    row, lane = square_index()
    second = pack_ref[start : start + LANES, :]
    upper = second if symmetric else second.T
    out_ref[0:LANES, :] = jnp.where(row >= lane, pack_ref[0:LANES, :], upper)
    out_ref[LANES:start, :] = pack_ref[LANES:start, :]
    out_ref[start : end - LANES, :] = pack_ref[start + LANES : end, :]
    diagonal = jnp.sum(jnp.where(row == lane, second, 0.0), axis=0, keepdims=True)
    out_ref[end - LANES :, :] = jnp.broadcast_to(diagonal, (PANEL, LANES))


def unfold(folded_ref, pack_ref, channels, symmetric):
    if channels < 2 * LANES:
        pack_ref[...] = folded_ref[...]
        return
    start = corner(channels)
    end = pack_ref.shape[0]
    row, lane = square_index()
    both = folded_ref[0:LANES, :]
    turned = both.T
    first_upper, second_upper = (turned, both) if symmetric else (0.0, 0.0)
    pack_ref[0:LANES, :] = jnp.where(row >= lane, both, first_upper)
    pack_ref[LANES:start, :] = folded_ref[LANES:start, :]
    second = jnp.where(row > lane, turned, second_upper)
    diagonal = folded_ref[end - LANES : end - LANES + 1, :]
    pack_ref[start : start + LANES, :] = jnp.where(row == lane, diagonal, second)
    pack_ref[start + LANES : end, :] = folded_ref[start : end - LANES, :]


def cut(pack_ref, core, mine_ref, other_ref):
    half = mine_ref.shape[0]
    mine_ref[...] = pack_ref[pl.ds(pl.multiple_of(core * half, 8), half), :].astype(mine_ref.dtype)
    other_ref[...] = pack_ref[pl.ds(pl.multiple_of((1 - core) * half, 8), half), :].astype(
        other_ref.dtype
    )


def join(pack_ref, core, mine, other):
    half = mine.shape[0]
    pack_ref[pl.ds(pl.multiple_of(core * half, 8), half), :] = mine
    pack_ref[pl.ds(pl.multiple_of((1 - core) * half, 8), half), :] = other


def gram_kernel(core_ref, part_ref, carried_ref, y_ref, g_mine, g_other, gram_ref, folded_ref):
    image = part_ref[...] + carried_ref[...].astype(jnp.float32)
    y_ref[...] = image.astype(y_ref.dtype)
    lower_products(y_ref, y_ref, gram_ref)
    fold(gram_ref, folded_ref, y_ref.shape[0], True)
    cut(folded_ref, core_ref[0], g_mine, g_other)


def gram(core, part, carried):
    channels, rows = carried.shape
    lower, folded = lower_rows(channels), folded_rows(channels)
    half = jax.ShapeDtypeStruct((folded // 2, LANES), jnp.float32)
    return pl.pallas_call(
        gram_kernel,
        in_specs=[SCALARS] + [WHOLE] * 2,
        out_specs=[WHOLE] * 3,
        out_shape=[jax.ShapeDtypeStruct((channels, rows), carried.dtype), half, half],
        scratch_shapes=[
            pltpu.VMEM((lower, LANES), jnp.float32),
            pltpu.VMEM((folded, LANES), jnp.float32),
        ],
        compiler_params=params(),
        cost_estimate=cost(2 * channels * channels * rows, 8 * channels * rows),
    )(core, part, carried)


def symmetric_matrix(pack_ref, out_ref):
    rows, wide = out_ref.shape
    offset = 0
    for top in range(0, wide, LANES):
        size = min(LANES, rows - top)
        column = pack_ref[offset : offset + rows - top, :]
        offset += rows - top
        out_ref[top:rows, top : top + LANES] = column
        for below in range(top + LANES, wide, LANES):
            count = min(LANES, rows - below)
            block = column[below - top : below - top + count, :]
            if count < LANES:
                block = jnp.concatenate(
                    [block, jnp.zeros((LANES - count, LANES), block.dtype)], axis=0
                )
            out_ref[top : top + size, below : below + LANES] = block.T


def ray_kernel(core_ref, x_ref, y_ref, after_ref, mine_ref, other_ref, pack_ref, folded_ref):
    lower_products(x_ref, y_ref, pack_ref)
    fold(pack_ref, folded_ref, x_ref.shape[0], True)
    cut(folded_ref, core_ref[0], mine_ref, other_ref)


def ray(core, x_t, y_t, after):
    channels, rows = x_t.shape
    lower, folded = lower_rows(channels), folded_rows(channels)
    return pl.pallas_call(
        ray_kernel,
        in_specs=[SCALARS, WHOLE, WHOLE, ANYWHERE],
        out_specs=[WHOLE] * 2,
        out_shape=[jax.ShapeDtypeStruct((folded // 2, LANES), jnp.bfloat16)] * 2,
        scratch_shapes=[
            pltpu.VMEM((lower, LANES), jnp.float32),
            pltpu.VMEM((folded, LANES), jnp.float32),
        ],
        compiler_params=params(),
        cost_estimate=cost(2 * channels * channels * rows, 4 * channels * rows),
    )(core, x_t, y_t, after)


def cross_kernel(core_ref, left_ref, right_ref, after_ref, mine_ref, other_ref, pack_ref):
    full_products(left_ref, right_ref, pack_ref)
    cut(pack_ref, core_ref[0], mine_ref, other_ref)


def cross(core, left, right, after, dtype):
    channels, rows = left.shape
    full = full_rows(channels)
    return pl.pallas_call(
        cross_kernel,
        in_specs=[SCALARS, WHOLE, WHOLE, ANYWHERE],
        out_specs=[WHOLE] * 2,
        out_shape=[jax.ShapeDtypeStruct((full // 2, LANES), dtype)] * 2,
        scratch_shapes=[pltpu.VMEM((full, LANES), jnp.float32)],
        compiler_params=params(),
        cost_estimate=cost(2 * channels * channels * rows, 4 * channels * rows),
    )(core, left, right, after)


def add_kernel(left_ref, right_ref, *refs):
    total = left_ref[...].astype(jnp.float32) + right_ref[...].astype(jnp.float32)
    refs[-1][...] = total.astype(refs[-1].dtype)


def add_four_kernel(own_ref, first_ref, second_ref, both_ref, after_ref, out_ref):
    own, first, second, both = (
        ref[...].astype(jnp.float32) for ref in (own_ref, first_ref, second_ref, both_ref)
    )
    out_ref[...] = ((own + first) + (second + both)).astype(out_ref.dtype)


def add_four(own, first, second, both, after):
    return pl.pallas_call(
        add_four_kernel,
        in_specs=[WHOLE] * 4 + [ANYWHERE],
        out_specs=WHOLE,
        out_shape=jax.ShapeDtypeStruct(own.shape, own.dtype),
        compiler_params=params(),
        cost_estimate=cost(10**5, 10**5),
    )(own, first, second, both, after)


def add_after(left, right, *after, flops=10**5):
    return pl.pallas_call(
        add_kernel,
        in_specs=[WHOLE] * 2 + [ANYWHERE] * len(after),
        out_specs=WHOLE,
        out_shape=jax.ShapeDtypeStruct(left.shape, left.dtype),
        compiler_params=params(),
        cost_estimate=cost(flops, 10**5),
    )(left, right, *after)


def split3(value):
    high = value.astype(jnp.bfloat16)
    rest = value - high.astype(jnp.float32)
    mid = rest.astype(jnp.bfloat16)
    low = (rest - mid.astype(jnp.float32)).astype(jnp.bfloat16)
    return high, mid, low


def sublane(value, index):
    return jnp.broadcast_to(value[index : index + 1, :], value.shape)


def lane_of(value, index):
    return jnp.take_along_axis(value, jnp.broadcast_to(index, value.shape), axis=1)


def eliminate(columns, panel):
    half = 8
    row = lax.broadcasted_iota(jnp.int32, (half, LANES), 0)
    scales = [jnp.zeros((half, LANES), jnp.float32) for _ in range(2)]
    columns = [list(c) for c in columns]
    panel = [list(p) for p in panel]
    for j in range(0, PANEL, 2):
        h, r = divmod(j, half)
        left, right = columns[j], columns[j + 1]
        a, b, c = sublane(left[h], r), sublane(left[h], r + 1), sublane(right[h], r + 1)
        det = a * c - b * b
        inverse = pl.reciprocal(det, approx=True)
        first, second = [None, None], [None, None]
        for t in range(h, 2):
            x, y = left[t], right[t]
            if t == h:
                x, y = jnp.where(row > r + 1, x, 0.0), jnp.where(row > r + 1, y, 0.0)
            first[t] = (c * x - b * y) * inverse
            second[t] = (a * y - b * x) * inverse
        for later in range(j + 2, PANEL):
            q = later // half
            x, y = sublane(left[q], later % half), sublane(right[q], later % half)
            for t in range(max(h, q), 2):
                columns[later][t] = columns[later][t] - (first[t] * x + second[t] * y)
        inverse_a = pl.reciprocal(a, approx=True)
        first[h] = jnp.where(row == r + 1, b * inverse_a, first[h])
        for group in panel:
            x, y = sublane(group[h], r), sublane(group[h], r + 1)
            for t in range(h, 2):
                group[t] = group[t] - (first[t] * x + second[t] * y)
        scales[h] = jnp.where(row == r, lax.rsqrt(a), scales[h])
        scales[h] = jnp.where(row == r + 1, lax.rsqrt(det * inverse_a), scales[h])
    return [jnp.concatenate([g[0] * scales[0], g[1] * scales[1]], axis=0) for g in panel]


def fill_work(channels, scale, pack_ref, work_ref):
    rows, wide = work_ref.shape
    groups = wide // LANES
    offset = 0
    for g in range(groups):
        top = g * LANES
        size = min(LANES, rows - top)
        column = pack_ref[offset : offset + rows - top, :] * scale
        offset += rows - top
        diag = column[0:size, :]
        if top + LANES > channels:
            row = lax.broadcasted_iota(jnp.int32, diag.shape, 0)
            lane = lax.broadcasted_iota(jnp.int32, diag.shape, 1)
            diag = jnp.where((row == lane) & (lane + top >= channels), 1.0, diag)
        work_ref[top : top + size, top : top + LANES] = diag
        for below in range(g + 1, groups):
            start = (below - g) * LANES
            size_b = min(LANES, rows - below * LANES)
            block = column[start : start + size_b, :]
            if size_b < LANES:
                block = jnp.concatenate(
                    [block, jnp.zeros((LANES - size_b, LANES), jnp.float32)], axis=0
                )
            work_ref[top : top + size, below * LANES : (below + 1) * LANES] = block.T
            work_ref[below * LANES : below * LANES + size_b, top : top + LANES] = jnp.zeros(
                (size_b, LANES), jnp.float32
            )


def eliminate_group(g, work_ref, turned_ref, first=0, last=LANES // PANEL):
    rows, wide = work_ref.shape
    groups = wide // LANES
    row = lax.broadcasted_iota(jnp.int32, (PANEL, LANES), 0)
    lane = lax.broadcasted_iota(jnp.int32, (PANEL, LANES), 1)
    top = g * LANES
    count = min(LANES, rows - top) // PANEL

    def load(local):
        place = pl.ds(pl.multiple_of(top + local, PANEL), PANEL)
        return [work_ref[place, q * LANES : (q + 1) * LANES] for q in range(groups)]

    def panel_step(b, parts, slot):
        local = b * PANEL
        following = jnp.minimum(local + PANEL, (count - 1) * PANEL)
        ahead = load(following)
        pivots = [parts[g][0:8, :], parts[g][8:16, :]]
        columns = [[lane_of(p, local + j) for p in pivots] for j in range(PANEL)]
        inside = (lane >= local) & (lane < local + PANEL)
        identity = jnp.where(lane - local == row, 1.0, 0.0)
        parts = list(parts)
        parts[g] = jnp.where(inside, identity, parts[g])
        done = eliminate(columns, [[p[0:8, :], p[8:16, :]] for p in parts])
        right = []
        for q in range(groups):
            high, mid, low = split3(done[q])
            right.append(jnp.concatenate([high, mid, high, low, mid, high], axis=0))
            if q >= g:
                if q == g:
                    high, mid, low = split3(jnp.where(lane >= local + PANEL, done[q], 0.0))
                left = jnp.concatenate([high, high, mid, high, mid, low], axis=0)
                turned_ref[slot, (q - g) * LANES : (q - g + 1) * LANES, :] = left.T
        right = jnp.concatenate(right, axis=1)
        near = turned_ref[slot, pl.ds(pl.multiple_of(following, PANEL), PANEL), :]
        update = dot(near, right, ((1,), (0,)))
        ahead[g] = jnp.where(inside, 0.0, ahead[g])
        ahead = [ahead[q] - update[:, q * LANES : (q + 1) * LANES] for q in range(groups)]
        for q in range(g, groups):
            low_row = q * LANES
            high_row = min(rows, low_row + LANES)
            base = low_row - top
            update = dot(turned_ref[slot, base : base + high_row - low_row, :], right, ((1,), (0,)))
            for c in range(groups):
                lanes = slice(c * LANES, (c + 1) * LANES)
                old = work_ref[low_row:high_row, lanes]
                if c == g:
                    here = lax.broadcasted_iota(jnp.int32, old.shape, 1)
                    old = jnp.where((here >= local) & (here < local + PANEL), 0.0, old)
                work_ref[low_row:high_row, lanes] = old - update[:, lanes]
        for q in range(groups):
            if q == g:
                done[q] = jnp.where(lane < local + PANEL, done[q], 0.0)
            elif q > g:
                done[q] = jnp.zeros_like(done[q])
            place = pl.ds(pl.multiple_of(top + local, PANEL), PANEL)
            work_ref[place, q * LANES : (q + 1) * LANES] = done[q]
        return ahead

    def two_panels(i, parts):
        return panel_step(first + 2 * i + 1, panel_step(first + 2 * i, parts, 0), 1)

    last = min(last, count)
    parts = lax.fori_loop(0, (last - first) // 2, two_panels, load(first * PANEL))
    if (last - first) % 2:
        panel_step(jnp.int32(last - 1), parts, 0)


def first_stage_kernel(
    channels, scale, core_ref, mine_ref, other_ref, work_ref, pack_ref, folded_ref, turned_ref
):
    join(folded_ref, core_ref[0], mine_ref[...], other_ref[...])
    unfold(folded_ref, pack_ref, channels, True)
    fill_work(channels, scale, pack_ref, work_ref)
    eliminate_group(0, work_ref, turned_ref)
    if work_ref.shape[1] > LANES:
        eliminate_group(1, work_ref, turned_ref, 0, EARLY_PANELS)


def last_stages_kernel(
    channels, before_ref, after_ref, work_ref, folded_ref, pack_ref, turned_ref
):
    work_ref[...] = before_ref[...]
    rows, wide = work_ref.shape
    for g in range(1, wide // LANES):
        eliminate_group(g, work_ref, turned_ref, EARLY_PANELS if g == 1 else 0)
    offset = 0
    for q in range(wide // LANES):
        tall = rows - q * LANES
        pack_ref[offset : offset + tall, :] = work_ref[q * LANES : rows, q * LANES : (q + 1) * LANES]
        offset += tall
    fold(pack_ref, folded_ref, channels, False)


def turned_scratch(channels):
    return pltpu.VMEM((2, round_up(channels, LANES), 6 * PANEL), jnp.bfloat16)


def work_shape(channels):
    return jax.ShapeDtypeStruct((round_up(channels, PANEL), round_up(channels, LANES)), jnp.float32)


def first_stage(core, mine, other, channels, total_rows):
    return pl.pallas_call(
        functools.partial(first_stage_kernel, channels, 1.0 / total_rows),
        in_specs=[SCALARS] + [WHOLE] * 2,
        out_specs=WHOLE,
        out_shape=work_shape(channels),
        scratch_shapes=[
            pltpu.VMEM((lower_rows(channels), LANES), jnp.float32),
            pltpu.VMEM((folded_rows(channels), LANES), jnp.float32),
            turned_scratch(channels),
        ],
        compiler_params=params(),
        cost_estimate=cost(FIRST_STAGE_FLOPS, 10**6),
    )(core, mine, other)


def last_stages(work, channels, after):
    return pl.pallas_call(
        functools.partial(last_stages_kernel, channels),
        in_specs=[WHOLE, ANYWHERE],
        out_specs=[WHOLE] * 2,
        out_shape=[
            work_shape(channels),
            jax.ShapeDtypeStruct((folded_rows(channels), LANES), jnp.float32),
        ],
        scratch_shapes=[
            pltpu.VMEM((lower_rows(channels), LANES), jnp.float32),
            turned_scratch(channels),
        ],
        compiler_params=params(),
        cost_estimate=cost(LAST_STAGES_FLOPS, 10**5),
    )(work, after)


def split2(value):
    high = value.astype(jnp.bfloat16)
    return high, (value - high.astype(jnp.float32)).astype(jnp.bfloat16)


def dot3(left, right, dims):
    rows = left.shape[0]
    left_high, left_low = split2(left)
    right_high, right_low = split2(right)
    both = dot(jnp.concatenate([left_high, left_low], axis=0), right_high, dims)
    return both[0:rows, :] + both[rows:, :] + dot(left_high, right_low, dims)


def lower_matrix(pack_ref, out_ref):
    rows, wide = out_ref.shape
    offset = 0
    for g in range(wide // LANES):
        top = g * LANES
        lanes = slice(top, top + LANES)
        if top:
            out_ref[0:top, lanes] = jnp.zeros((top, LANES), jnp.float32)
        out_ref[top:rows, lanes] = pack_ref[offset : offset + rows - top, :]
        offset += rows - top


def basis_kernel(inverse_ref, y_ref, q_ref, token_ref):
    channels = y_ref.shape[0]
    image = y_ref[...]
    token_ref[...] = jnp.zeros_like(token_ref)
    for start, size in strips(channels, 2 * LANES):
        used = min(channels, start + size)
        high, low = split2(inverse_ref[start : start + size, 0:used])
        both = dot(jnp.concatenate([high, low], axis=0), image[0:used, :], ((1,), (0,)))
        q_ref[start : start + size, :] = (both[0:size, :] + both[size:, :]).astype(q_ref.dtype)


def basis(inverse, y_t):
    channels, rows = y_t.shape
    return pl.pallas_call(
        basis_kernel,
        in_specs=[WHOLE] * 2,
        out_specs=[WHOLE] * 2,
        out_shape=[
            jax.ShapeDtypeStruct(y_t.shape, y_t.dtype),
            jax.ShapeDtypeStruct((8, LANES), jnp.float32),
        ],
        compiler_params=params(),
        cost_estimate=cost(10**5, 10**5),
    )(inverse, y_t)


def matrix_shape(channels):
    return jax.ShapeDtypeStruct((channels, 1, channels), jnp.float32)


def part_kernel(
    channels, scale, core_ref, mine_ref, inverse_ref, previous_ref, out_ref,
    pack_ref, lower_ref, before_ref,
):
    rows, wide = inverse_ref.shape
    half = mine_ref.shape[0]
    join(pack_ref, core_ref[0], mine_ref[...], jnp.zeros((half, LANES), jnp.float32))
    turned = dot3(full_matrix(pack_ref, channels), inverse_ref[...], ((1,), (1,)))
    unfold(previous_ref, lower_ref, channels, False)
    lower_matrix(lower_ref, before_ref)
    total = dot3(before_ref[:, 0:rows], turned, ((1,), (0,))) * scale
    out_ref[:, 0:rows] = total.astype(out_ref.dtype)
    if rows < wide:
        out_ref[:, rows:wide] = jnp.zeros((rows, wide - rows), out_ref.dtype)


def correlation_part(core, mine, inverse, previous, channels, total_rows):
    return pl.pallas_call(
        functools.partial(part_kernel, channels, 1.0 / total_rows),
        in_specs=[SCALARS] + [WHOLE] * 3,
        out_specs=WHOLE,
        out_shape=jax.ShapeDtypeStruct(inverse.shape, jnp.bfloat16),
        scratch_shapes=[
            pltpu.VMEM((full_rows(channels), LANES), jnp.float32),
            pltpu.VMEM((lower_rows(channels), LANES), jnp.float32),
            pltpu.VMEM(inverse.shape, jnp.float32),
        ],
        compiler_params=params(),
        cost_estimate=cost(10**5, 10**5),
    )(core, mine, inverse, previous)


def both_kernel(
    scale, core_ref, left_ref, right_ref, mine_ref, other_ref, out_ref, ray_ref,
    folded_ref, pack_ref, full_ref,
):
    channels = out_ref.shape[0]
    mine, other = mine_ref[...].astype(jnp.float32), other_ref[...].astype(jnp.float32)
    join(folded_ref, core_ref[0], mine, other)
    unfold(folded_ref, pack_ref, channels, True)
    symmetric_matrix(pack_ref, full_ref)
    ray_ref[:, 0, :] = full_ref[0:channels, 0:channels] * scale
    total = left_ref[...].astype(jnp.float32) + right_ref[...].astype(jnp.float32)
    out_ref[:, 0, :] = total[0:channels, 0:channels]


def both_parts(core, left, right, mine, other, channels, total_rows):
    return pl.pallas_call(
        functools.partial(both_kernel, 1.0 / total_rows),
        in_specs=[SCALARS] + [WHOLE] * 4,
        out_specs=[WHOLE] * 2,
        out_shape=[matrix_shape(channels)] * 2,
        scratch_shapes=[
            pltpu.VMEM((folded_rows(channels), LANES), jnp.float32),
            pltpu.VMEM((lower_rows(channels), LANES), jnp.float32),
            pltpu.VMEM((round_up(channels, PANEL), round_up(channels, LANES)), jnp.float32),
        ],
        compiler_params=params(),
        cost_estimate=cost(10**5, 10**5),
    )(core, left, right, mine, other)


def from_behind(value, axis, steps):
    count = lax.axis_size(axis)
    leading, last = (max(0, -steps), min(count, count - steps))
    return lax.ppermute(value, axis, [(source, source + steps) for source in range(leading, last)])


def other_core(value):
    return lax.ppermute(value, "rows", [(s, s ^ 1) for s in range(lax.axis_size("rows"))])


def chip_rounds():
    count = lax.axis_size("rows")
    bits = []
    while 2 << len(bits) < count:
        bits.append(2 << len(bits))
    return [
        [(s, s ^ (bits[n] if s % 2 == 0 else bits[-1 - n])) for s in range(count)]
        for n in range(len(bits))
    ]


def sum_chips(value, after):
    count = lax.axis_size("rows")
    if count == 8:
        others = [
            lax.ppermute(value, "rows", [(s, s ^ bits) for s in range(count)]) for bits in (2, 4, 6)
        ]
        return add_four(value, *others, after)
    for pairs in chip_rounds():
        value = add_after(value, lax.ppermute(value, "rows", pairs), after)
    return value


def shards(x_block, h_diag, h_right, pattern):
    x_t = x_block[0].T
    channels, block_rows = x_t.shape
    masks = pattern[0].transpose(1, 0, 2)
    total_rows = lax.axis_size("rows") * block_rows
    core = (lax.axis_index("rows") % 2).astype(jnp.int32).reshape(1)
    later = from_behind(x_t, "rows", -1)
    carried = from_behind(tile_product(1, masks, x_t, h_right[0], x_t.dtype, 53), "rows", 1)
    first = tile_product(0, masks, x_t, h_diag[0], jnp.float32, 50)
    part = later_product(masks, later, h_right[0], first)
    y_t, g_mine, g_other = gram(core, part, carried)
    previous_y = from_behind(y_t, "sector", 1)
    rounds = chip_rounds()
    g_sum = g_mine + other_core(g_other)
    r_mine, r_other = ray(core, x_t, y_t, g_sum)
    r_sum = add_after(r_mine, other_core(r_other))
    g_sum = sum_chips(g_sum, r_sum)
    r_first = lax.ppermute(r_sum, "rows", rounds[0])
    work = first_stage(core, g_sum, other_core(g_sum), channels, total_rows)
    r_sum = add_after(r_sum, r_first, work)
    m_mine, m_other = cross(core, previous_y, y_t, r_sum, jnp.float32)
    inverse, pack = last_stages(work, channels, m_other)
    m_sum = add_after(m_mine, other_core(m_other), inverse)
    previous = from_behind(pack, "sector", 1)
    q_t, basis_token = basis(inverse, y_t)
    for pairs in rounds[:-1]:
        m_sum = add_after(m_sum, lax.ppermute(m_sum, "rows", pairs))
    m_sum = add_after(m_sum, lax.ppermute(m_sum, "rows", rounds[-1]), basis_token)
    part = correlation_part(core, m_sum, inverse, previous, channels, total_rows)
    for pairs in rounds[1:]:
        r_sum = add_after(r_sum, lax.ppermute(r_sum, "rows", pairs), flops=LAST_RAY_FLOPS)
    correlation, rayleigh = both_parts(
        core, part, other_core(part), r_sum, other_core(r_sum), channels, total_rows
    )
    return (q_t.T[None], rayleigh.transpose(1, 0, 2), correlation.transpose(1, 0, 2))


def solution(mesh):
    in_specs = (
        P("sector", "rows", None),
        P("sector", "rows", None),
        P("sector", "rows", None),
        P("sector", None, "rows", None),
    )
    out_specs = (P("sector", "rows", None), P("sector", None, None), P("sector", None, None))
    return jax.shard_map(shards, mesh=mesh, in_specs=in_specs, out_specs=out_specs, check_vma=False)
```

```python
import functools

import jax
import jax.numpy as jnp
from jax import lax
from jax.experimental import pallas as pl
from jax.experimental.pallas import tpu as pltpu
from jax.sharding import PartitionSpec as P

SUBBLOCK = 128
LANES = 128
PANEL = 16
EARLY_PANELS = 8
WHOLE = pl.BlockSpec(memory_space=pltpu.VMEM)
SCALARS = pl.BlockSpec(memory_space=pltpu.SMEM)
ANYWHERE = pl.BlockSpec(memory_space=pl.ANY)
MIB = 1024 * 1024
FIRST_STAGE_FLOPS = 5000 * 10**6
LAST_RAY_FLOPS = 3000 * 10**6
LAST_STAGES_FLOPS = 4000 * 10**6


def params(mib=48):
    return pltpu.CompilerParams(vmem_limit_bytes=mib * MIB)


def cost(flops, bytes_accessed):
    return pl.CostEstimate(flops=flops, bytes_accessed=bytes_accessed, transcendentals=0)


def round_up(value, step):
    return (value + step - 1) // step * step


def dot(left, right, dims, precision=None):
    return lax.dot_general(
        left, right, (dims, ((), ())), precision=precision, preferred_element_type=jnp.float32
    )


def block_mask(mask_ref, which, cols, dtype):
    blocks = mask_ref[:, which, :].astype(jnp.float32)
    col = lax.broadcasted_iota(jnp.int32, (blocks.shape[1], cols), 1)
    block = lax.broadcasted_iota(jnp.int32, (blocks.shape[1], cols), 0)
    wide = dot(blocks, jnp.where(col // SUBBLOCK == block, 1.0, 0.0), ((1,), (0,)))
    return [
        jnp.broadcast_to(wide[i : i + 1, :], (PANEL, cols)).astype(dtype)
        for i in range(blocks.shape[0])
    ]


def mask_rows(tile_ref, mask, start, size):
    for i in range(start // SUBBLOCK, (start + size) // SUBBLOCK):
        for row in range(i * SUBBLOCK, (i + 1) * SUBBLOCK, PANEL):
            tile_ref[row : row + PANEL, :] = tile_ref[row : row + PANEL, :] * mask[i]


def strips(rows, width):
    return [(start, min(width, rows - start)) for start in range(0, rows, width)]


def halves(rows):
    first = rows // 512 * 256
    return [(0, first), (first, rows - first)] if first else [(0, rows)]


def copies_of(source, target, sems):
    copies = []
    for n, (start, size) in enumerate(halves(target.shape[0])):
        here = (pl.ds(start, size), slice(None))
        copies.append(pltpu.make_async_copy(source.at[here], target.at[here], sems.at[n]))
    return copies


def product(x_ref, tile_ref, copies, in_turn, mask, sum_ref, out_ref):
    rows = tile_ref.shape[0]
    for n, (start, size) in enumerate(halves(rows)):
        copies[n].wait()
        if in_turn and n + 1 < len(copies):
            copies[n + 1].start()
        mask_rows(tile_ref, mask, start, size)
        last = n + 1 == len(copies)
        for col, cols in strips(rows, 2 * SUBBLOCK):
            here = (slice(None), slice(col, col + cols))
            term = dot(
                x_ref[:, start : start + size],
                tile_ref[start : start + size, col : col + cols],
                ((1,), (0,)),
            )
            if n > 0:
                term = sum_ref[here] + term
            if last:
                out_ref[here] = term.astype(out_ref.dtype)
            else:
                sum_ref[here] = term


def tile_kernel(which, in_turn, mask_ref, x_hbm, tile_hbm, out_ref, x_ref, tile_ref, sum_ref, x_sem, sems):
    rows = tile_ref.shape[0]
    copies = copies_of(tile_hbm, tile_ref, sems)
    copy_x = pltpu.make_async_copy(x_hbm, x_ref, x_sem)
    copy_x.start()
    for copy in copies[:1] if in_turn else copies:
        copy.start()
    mask = block_mask(mask_ref, which, rows, tile_ref.dtype)
    copy_x.wait()
    product(x_ref, tile_ref, copies, in_turn, mask, sum_ref, out_ref)


def tile_product(which, masks, x_t, tile, dtype, mib, in_turn):
    channels, rows = x_t.shape
    return pl.pallas_call(
        functools.partial(tile_kernel, which, in_turn),
        in_specs=[WHOLE, ANYWHERE, ANYWHERE],
        out_specs=WHOLE,
        out_shape=jax.ShapeDtypeStruct((channels, rows), dtype),
        scratch_shapes=[
            pltpu.VMEM((channels, rows), x_t.dtype),
            pltpu.VMEM((rows, rows), tile.dtype),
            pltpu.VMEM((channels, rows), jnp.float32),
            pltpu.SemaphoreType.DMA,
            pltpu.SemaphoreType.DMA((2,)),
        ],
        compiler_params=params(mib),
        cost_estimate=cost(2 * channels * rows * rows, 2 * rows * rows),
    )(masks, x_t, tile)


def later_kernel(mask_ref, later_ref, tile_hbm, first_ref, out_ref, tile_ref, sems):
    rows = tile_ref.shape[0]
    copies = copies_of(tile_hbm, tile_ref, sems)
    for copy in copies:
        copy.start()
    mask = block_mask(mask_ref, 1, rows, tile_ref.dtype)
    for n, (start, size) in enumerate(halves(rows)):
        copies[n].wait()
        mask_rows(tile_ref, mask, start, size)
        for row, count in strips(size, 2 * SUBBLOCK):
            here = (slice(None), slice(start + row, start + row + count))
            out_ref[here] = first_ref[here] + dot(
                later_ref[...], tile_ref[start + row : start + row + count, :], ((1,), (1,))
            )


def later_product(masks, later, tile, first):
    channels, rows = later.shape
    return pl.pallas_call(
        later_kernel,
        in_specs=[WHOLE, WHOLE, ANYWHERE, WHOLE],
        out_specs=WHOLE,
        out_shape=jax.ShapeDtypeStruct((channels, rows), jnp.float32),
        scratch_shapes=[
            pltpu.VMEM((rows, rows), tile.dtype),
            pltpu.SemaphoreType.DMA((2,)),
        ],
        compiler_params=params(),
        cost_estimate=cost(2 * channels * rows * rows, 2 * rows * rows),
    )(masks, later, tile, first)


def lower_rows(channels):
    rows = round_up(channels, PANEL)
    return sum(rows - g * LANES for g in range(round_up(channels, LANES) // LANES))


def full_rows(channels):
    rows, wide = round_up(channels, PANEL), round_up(channels, LANES)
    whole = channels // LANES
    rest = rows - whole * LANES
    return round_up(whole * rows + rest * (wide // LANES), 4 * PANEL)


def lower_products(left_ref, right_ref, out_ref):
    channels = left_ref.shape[0]
    rows = round_up(channels, PANEL)
    offset = 0
    for start, size in strips(channels, LANES):
        tall = rows - start
        if size < LANES:
            out_ref[offset : offset + tall, :] = jnp.zeros((tall, LANES), jnp.float32)
        elif rows > channels:
            out_ref[offset + channels - start : offset + tall, :] = jnp.zeros(
                (rows - channels, LANES), jnp.float32
            )
        out_ref[offset : offset + channels - start, 0:size] = dot(
            left_ref[start:channels, :], right_ref[start : start + size, :], ((1,), (1,))
        )
        offset += tall


def full_products(left_ref, right_ref, out_ref):
    channels = left_ref.shape[0]
    rows = round_up(channels, PANEL)
    whole = channels // LANES
    for g in range(whole):
        out_ref[g * rows : g * rows + channels, :] = dot(
            left_ref[...], right_ref[g * LANES : (g + 1) * LANES, :], ((1,), (1,))
        )
        if rows > channels:
            out_ref[g * rows + channels : (g + 1) * rows, :] = jnp.zeros(
                (rows - channels, LANES), jnp.float32
            )
    base = whole * rows
    if base < out_ref.shape[0]:
        out_ref[base:, :] = jnp.zeros((out_ref.shape[0] - base, LANES), jnp.float32)
    first, rest = whole * LANES, rows - whole * LANES
    for n, (start, size) in enumerate(strips(channels, LANES) if first < channels else []):
        place = base + n * rest
        out_ref[place : place + channels - first, 0:size] = dot(
            right_ref[first:channels, :], left_ref[start : start + size, :], ((1,), (1,))
        )


def full_matrix(pack_ref, channels):
    rows, wide = round_up(channels, PANEL), round_up(channels, LANES)
    whole = channels // LANES
    rest = rows - whole * LANES
    parts = [pack_ref[g * rows : (g + 1) * rows, :] for g in range(whole)]
    if rest:
        tail = jnp.concatenate(
            [
                pack_ref[whole * rows + g * rest : whole * rows + (g + 1) * rest, :]
                for g in range(wide // LANES)
            ],
            axis=1,
        )
        tail = jnp.concatenate([tail, jnp.zeros((LANES - rest, wide), tail.dtype)], axis=0)
        parts.append(tail.T[0:rows, :])
    return jnp.concatenate(parts, axis=1)


def folded_rows(channels):
    if channels < 2 * LANES:
        return lower_rows(channels)
    return lower_rows(channels) - LANES + PANEL


def corner(channels):
    return round_up(channels, PANEL)


def square_index():
    row = lax.broadcasted_iota(jnp.int32, (LANES, LANES), 0)
    return row, lax.broadcasted_iota(jnp.int32, (LANES, LANES), 1)


def fold(pack_ref, out_ref, channels, symmetric):
    if channels < 2 * LANES:
        out_ref[...] = pack_ref[...]
        return
    start = corner(channels)
    end = pack_ref.shape[0]
    row, lane = square_index()
    second = pack_ref[start : start + LANES, :]
    upper = second if symmetric else second.T
    out_ref[0:LANES, :] = jnp.where(row >= lane, pack_ref[0:LANES, :], upper)
    out_ref[LANES:start, :] = pack_ref[LANES:start, :]
    out_ref[start : end - LANES, :] = pack_ref[start + LANES : end, :]
    diagonal = jnp.sum(jnp.where(row == lane, second, 0.0), axis=0, keepdims=True)
    out_ref[end - LANES :, :] = jnp.broadcast_to(diagonal, (PANEL, LANES))


def unfold(folded_ref, pack_ref, channels, symmetric):
    if channels < 2 * LANES:
        pack_ref[...] = folded_ref[...]
        return
    start = corner(channels)
    end = pack_ref.shape[0]
    row, lane = square_index()
    both = folded_ref[0:LANES, :]
    turned = both.T
    first_upper, second_upper = (turned, both) if symmetric else (0.0, 0.0)
    pack_ref[0:LANES, :] = jnp.where(row >= lane, both, first_upper)
    pack_ref[LANES:start, :] = folded_ref[LANES:start, :]
    second = jnp.where(row > lane, turned, second_upper)
    diagonal = folded_ref[end - LANES : end - LANES + 1, :]
    pack_ref[start : start + LANES, :] = jnp.where(row == lane, diagonal, second)
    pack_ref[start + LANES : end, :] = folded_ref[start : end - LANES, :]


def cut(pack_ref, core, mine_ref, other_ref):
    half = mine_ref.shape[0]
    mine_ref[...] = pack_ref[pl.ds(pl.multiple_of(core * half, 8), half), :].astype(mine_ref.dtype)
    other_ref[...] = pack_ref[pl.ds(pl.multiple_of((1 - core) * half, 8), half), :].astype(
        other_ref.dtype
    )


def join(pack_ref, core, mine, other):
    half = mine.shape[0]
    pack_ref[pl.ds(pl.multiple_of(core * half, 8), half), :] = mine
    pack_ref[pl.ds(pl.multiple_of((1 - core) * half, 8), half), :] = other


def gram_kernel(core_ref, part_ref, carried_ref, y_ref, g_mine, g_other, gram_ref, folded_ref):
    image = part_ref[...] + carried_ref[...].astype(jnp.float32)
    y_ref[...] = image.astype(y_ref.dtype)
    lower_products(y_ref, y_ref, gram_ref)
    fold(gram_ref, folded_ref, y_ref.shape[0], True)
    cut(folded_ref, core_ref[0], g_mine, g_other)


def gram(core, part, carried):
    channels, rows = carried.shape
    lower, folded = lower_rows(channels), folded_rows(channels)
    half = jax.ShapeDtypeStruct((folded // 2, LANES), jnp.float32)
    return pl.pallas_call(
        gram_kernel,
        in_specs=[SCALARS] + [WHOLE] * 2,
        out_specs=[WHOLE] * 3,
        out_shape=[jax.ShapeDtypeStruct((channels, rows), carried.dtype), half, half],
        scratch_shapes=[
            pltpu.VMEM((lower, LANES), jnp.float32),
            pltpu.VMEM((folded, LANES), jnp.float32),
        ],
        compiler_params=params(),
        cost_estimate=cost(2 * channels * channels * rows, 8 * channels * rows),
    )(core, part, carried)


def symmetric_matrix(pack_ref, out_ref):
    rows, wide = out_ref.shape
    offset = 0
    for top in range(0, wide, LANES):
        size = min(LANES, rows - top)
        column = pack_ref[offset : offset + rows - top, :]
        offset += rows - top
        out_ref[top:rows, top : top + LANES] = column
        for below in range(top + LANES, wide, LANES):
            count = min(LANES, rows - below)
            block = column[below - top : below - top + count, :]
            if count < LANES:
                block = jnp.concatenate(
                    [block, jnp.zeros((LANES - count, LANES), block.dtype)], axis=0
                )
            out_ref[top : top + size, below : below + LANES] = block.T


def ray_kernel(core_ref, x_ref, y_ref, after_ref, mine_ref, other_ref, pack_ref, folded_ref):
    lower_products(x_ref, y_ref, pack_ref)
    fold(pack_ref, folded_ref, x_ref.shape[0], True)
    cut(folded_ref, core_ref[0], mine_ref, other_ref)


def ray(core, x_t, y_t, after):
    channels, rows = x_t.shape
    lower, folded = lower_rows(channels), folded_rows(channels)
    return pl.pallas_call(
        ray_kernel,
        in_specs=[SCALARS, WHOLE, WHOLE, ANYWHERE],
        out_specs=[WHOLE] * 2,
        out_shape=[jax.ShapeDtypeStruct((folded // 2, LANES), jnp.bfloat16)] * 2,
        scratch_shapes=[
            pltpu.VMEM((lower, LANES), jnp.float32),
            pltpu.VMEM((folded, LANES), jnp.float32),
        ],
        compiler_params=params(),
        cost_estimate=cost(2 * channels * channels * rows, 4 * channels * rows),
    )(core, x_t, y_t, after)


def cross_kernel(core_ref, left_ref, right_ref, after_ref, mine_ref, other_ref, pack_ref):
    full_products(left_ref, right_ref, pack_ref)
    cut(pack_ref, core_ref[0], mine_ref, other_ref)


def cross(core, left, right, after, dtype):
    channels, rows = left.shape
    full = full_rows(channels)
    return pl.pallas_call(
        cross_kernel,
        in_specs=[SCALARS, WHOLE, WHOLE, ANYWHERE],
        out_specs=[WHOLE] * 2,
        out_shape=[jax.ShapeDtypeStruct((full // 2, LANES), dtype)] * 2,
        scratch_shapes=[pltpu.VMEM((full, LANES), jnp.float32)],
        compiler_params=params(),
        cost_estimate=cost(2 * channels * channels * rows, 4 * channels * rows),
    )(core, left, right, after)


def add_kernel(left_ref, right_ref, *refs):
    total = left_ref[...].astype(jnp.float32) + right_ref[...].astype(jnp.float32)
    refs[-1][...] = total.astype(refs[-1].dtype)


def add_four_kernel(both_ref, own_ref, first_ref, second_ref, after_ref, out_ref):
    both, own, first, second = (
        ref[...].astype(jnp.float32) for ref in (both_ref, own_ref, first_ref, second_ref)
    )
    out_ref[...] = ((own + first) + (second + both)).astype(out_ref.dtype)


def add_four(both, own, first, second, after):
    return pl.pallas_call(
        add_four_kernel,
        in_specs=[WHOLE] * 4 + [ANYWHERE],
        out_specs=WHOLE,
        out_shape=jax.ShapeDtypeStruct(own.shape, own.dtype),
        compiler_params=params(),
        cost_estimate=cost(10**5, 10**5),
    )(both, own, first, second, after)


def add_after(left, right, *after, flops=10**5):
    return pl.pallas_call(
        add_kernel,
        in_specs=[WHOLE] * 2 + [ANYWHERE] * len(after),
        out_specs=WHOLE,
        out_shape=jax.ShapeDtypeStruct(left.shape, left.dtype),
        compiler_params=params(),
        cost_estimate=cost(flops, 10**5),
    )(left, right, *after)


def split3(value):
    high = value.astype(jnp.bfloat16)
    rest = value - high.astype(jnp.float32)
    mid = rest.astype(jnp.bfloat16)
    low = (rest - mid.astype(jnp.float32)).astype(jnp.bfloat16)
    return high, mid, low


def sublane(value, index):
    return jnp.broadcast_to(value[index : index + 1, :], value.shape)


def lane_of(value, index):
    return jnp.take_along_axis(value, jnp.broadcast_to(index, value.shape), axis=1)


def eliminate(columns, panel):
    half = 8
    row = lax.broadcasted_iota(jnp.int32, (half, LANES), 0)
    scales = [jnp.zeros((half, LANES), jnp.float32) for _ in range(2)]
    columns = [list(c) for c in columns]
    panel = [list(p) for p in panel]
    for j in range(0, PANEL, 2):
        h, r = divmod(j, half)
        left, right = columns[j], columns[j + 1]
        a, b, c = sublane(left[h], r), sublane(left[h], r + 1), sublane(right[h], r + 1)
        det = a * c - b * b
        inverse = pl.reciprocal(det, approx=True)
        first, second = [None, None], [None, None]
        for t in range(h, 2):
            x, y = left[t], right[t]
            if t == h:
                x, y = jnp.where(row > r + 1, x, 0.0), jnp.where(row > r + 1, y, 0.0)
            first[t] = (c * x - b * y) * inverse
            second[t] = (a * y - b * x) * inverse
        for later in range(j + 2, PANEL):
            q = later // half
            x, y = sublane(left[q], later % half), sublane(right[q], later % half)
            for t in range(max(h, q), 2):
                columns[later][t] = columns[later][t] - (first[t] * x + second[t] * y)
        inverse_a = pl.reciprocal(a, approx=True)
        first[h] = jnp.where(row == r + 1, b * inverse_a, first[h])
        for group in panel:
            x, y = sublane(group[h], r), sublane(group[h], r + 1)
            for t in range(h, 2):
                group[t] = group[t] - (first[t] * x + second[t] * y)
        scales[h] = jnp.where(row == r, lax.rsqrt(a), scales[h])
        scales[h] = jnp.where(row == r + 1, lax.rsqrt(det * inverse_a), scales[h])
    return [jnp.concatenate([g[0] * scales[0], g[1] * scales[1]], axis=0) for g in panel]


def fill_work(channels, scale, pack_ref, work_ref):
    rows, wide = work_ref.shape
    groups = wide // LANES
    offset = 0
    for g in range(groups):
        top = g * LANES
        size = min(LANES, rows - top)
        column = pack_ref[offset : offset + rows - top, :] * scale
        offset += rows - top
        diag = column[0:size, :]
        if top + LANES > channels:
            row = lax.broadcasted_iota(jnp.int32, diag.shape, 0)
            lane = lax.broadcasted_iota(jnp.int32, diag.shape, 1)
            diag = jnp.where((row == lane) & (lane + top >= channels), 1.0, diag)
        work_ref[top : top + size, top : top + LANES] = diag
        for below in range(g + 1, groups):
            start = (below - g) * LANES
            size_b = min(LANES, rows - below * LANES)
            block = column[start : start + size_b, :]
            if size_b < LANES:
                block = jnp.concatenate(
                    [block, jnp.zeros((LANES - size_b, LANES), jnp.float32)], axis=0
                )
            work_ref[top : top + size, below * LANES : (below + 1) * LANES] = block.T
            work_ref[below * LANES : below * LANES + size_b, top : top + LANES] = jnp.zeros(
                (size_b, LANES), jnp.float32
            )


def eliminate_group(g, work_ref, turned_ref, first=0, last=LANES // PANEL):
    rows, wide = work_ref.shape
    groups = wide // LANES
    row = lax.broadcasted_iota(jnp.int32, (PANEL, LANES), 0)
    lane = lax.broadcasted_iota(jnp.int32, (PANEL, LANES), 1)
    top = g * LANES
    count = min(LANES, rows - top) // PANEL

    def load(local):
        place = pl.ds(pl.multiple_of(top + local, PANEL), PANEL)
        return [work_ref[place, q * LANES : (q + 1) * LANES] for q in range(groups)]

    def panel_step(b, parts, slot):
        local = b * PANEL
        following = jnp.minimum(local + PANEL, (count - 1) * PANEL)
        ahead = load(following)
        pivots = [parts[g][0:8, :], parts[g][8:16, :]]
        columns = [[lane_of(p, local + j) for p in pivots] for j in range(PANEL)]
        inside = (lane >= local) & (lane < local + PANEL)
        identity = jnp.where(lane - local == row, 1.0, 0.0)
        parts = list(parts)
        parts[g] = jnp.where(inside, identity, parts[g])
        done = eliminate(columns, [[p[0:8, :], p[8:16, :]] for p in parts])
        right = []
        for q in range(groups):
            high, mid, low = split3(done[q])
            right.append(jnp.concatenate([high, mid, high, low, mid, high], axis=0))
            if q >= g:
                if q == g:
                    high, mid, low = split3(jnp.where(lane >= local + PANEL, done[q], 0.0))
                left = jnp.concatenate([high, high, mid, high, mid, low], axis=0)
                turned_ref[slot, (q - g) * LANES : (q - g + 1) * LANES, :] = left.T
        right = jnp.concatenate(right, axis=1)
        near = turned_ref[slot, pl.ds(pl.multiple_of(following, PANEL), PANEL), :]
        update = dot(near, right, ((1,), (0,)))
        ahead[g] = jnp.where(inside, 0.0, ahead[g])
        ahead = [ahead[q] - update[:, q * LANES : (q + 1) * LANES] for q in range(groups)]
        for q in range(g, groups):
            low_row = q * LANES
            high_row = min(rows, low_row + LANES)
            base = low_row - top
            update = dot(turned_ref[slot, base : base + high_row - low_row, :], right, ((1,), (0,)))
            for c in range(groups):
                lanes = slice(c * LANES, (c + 1) * LANES)
                old = work_ref[low_row:high_row, lanes]
                if c == g:
                    here = lax.broadcasted_iota(jnp.int32, old.shape, 1)
                    old = jnp.where((here >= local) & (here < local + PANEL), 0.0, old)
                work_ref[low_row:high_row, lanes] = old - update[:, lanes]
        for q in range(groups):
            if q == g:
                done[q] = jnp.where(lane < local + PANEL, done[q], 0.0)
            elif q > g:
                done[q] = jnp.zeros_like(done[q])
            place = pl.ds(pl.multiple_of(top + local, PANEL), PANEL)
            work_ref[place, q * LANES : (q + 1) * LANES] = done[q]
        return ahead

    def two_panels(i, parts):
        return panel_step(first + 2 * i + 1, panel_step(first + 2 * i, parts, 0), 1)

    last = min(last, count)
    parts = lax.fori_loop(0, (last - first) // 2, two_panels, load(first * PANEL))
    if (last - first) % 2:
        panel_step(jnp.int32(last - 1), parts, 0)


def first_stage_kernel(
    channels, scale, core_ref, mine_ref, other_ref, work_ref, pack_ref, folded_ref, turned_ref
):
    join(folded_ref, core_ref[0], mine_ref[...], other_ref[...])
    unfold(folded_ref, pack_ref, channels, True)
    fill_work(channels, scale, pack_ref, work_ref)
    eliminate_group(0, work_ref, turned_ref)
    if work_ref.shape[1] > LANES:
        eliminate_group(1, work_ref, turned_ref, 0, EARLY_PANELS)


def last_stages_kernel(
    channels, before_ref, after_ref, work_ref, folded_ref, pack_ref, turned_ref
):
    work_ref[...] = before_ref[...]
    rows, wide = work_ref.shape
    for g in range(1 if EARLY_PANELS * PANEL < LANES else 2, wide // LANES):
        eliminate_group(g, work_ref, turned_ref, EARLY_PANELS if g == 1 else 0)
    offset = 0
    for q in range(wide // LANES):
        tall = rows - q * LANES
        pack_ref[offset : offset + tall, :] = work_ref[q * LANES : rows, q * LANES : (q + 1) * LANES]
        offset += tall
    fold(pack_ref, folded_ref, channels, False)


def turned_scratch(channels):
    return pltpu.VMEM((2, round_up(channels, LANES), 6 * PANEL), jnp.bfloat16)


def work_shape(channels):
    return jax.ShapeDtypeStruct((round_up(channels, PANEL), round_up(channels, LANES)), jnp.float32)


def first_stage(core, mine, other, channels, total_rows):
    return pl.pallas_call(
        functools.partial(first_stage_kernel, channels, 1.0 / total_rows),
        in_specs=[SCALARS] + [WHOLE] * 2,
        out_specs=WHOLE,
        out_shape=work_shape(channels),
        scratch_shapes=[
            pltpu.VMEM((lower_rows(channels), LANES), jnp.float32),
            pltpu.VMEM((folded_rows(channels), LANES), jnp.float32),
            turned_scratch(channels),
        ],
        compiler_params=params(),
        cost_estimate=cost(FIRST_STAGE_FLOPS, 10**6),
    )(core, mine, other)


def last_stages(work, channels, after):
    return pl.pallas_call(
        functools.partial(last_stages_kernel, channels),
        in_specs=[WHOLE, ANYWHERE],
        out_specs=[WHOLE] * 2,
        out_shape=[
            work_shape(channels),
            jax.ShapeDtypeStruct((folded_rows(channels), LANES), jnp.float32),
        ],
        scratch_shapes=[
            pltpu.VMEM((lower_rows(channels), LANES), jnp.float32),
            turned_scratch(channels),
        ],
        compiler_params=params(),
        cost_estimate=cost(LAST_STAGES_FLOPS, 10**5),
    )(work, after)


def split2(value):
    high = value.astype(jnp.bfloat16)
    return high, (value - high.astype(jnp.float32)).astype(jnp.bfloat16)


def dot3(left, right, dims):
    rows = left.shape[0]
    left_high, left_low = split2(left)
    right_high, right_low = split2(right)
    both = dot(jnp.concatenate([left_high, left_low], axis=0), right_high, dims)
    return both[0:rows, :] + both[rows:, :] + dot(left_high, right_low, dims)


def lower_matrix(pack_ref, out_ref):
    rows, wide = out_ref.shape
    offset = 0
    for g in range(wide // LANES):
        top = g * LANES
        lanes = slice(top, top + LANES)
        if top:
            out_ref[0:top, lanes] = jnp.zeros((top, LANES), jnp.float32)
        out_ref[top:rows, lanes] = pack_ref[offset : offset + rows - top, :]
        offset += rows - top


def basis_kernel(inverse_ref, y_ref, q_ref, token_ref):
    channels = y_ref.shape[0]
    image = y_ref[...]
    token_ref[...] = jnp.zeros_like(token_ref)
    for start, size in strips(channels, 2 * LANES):
        used = min(channels, start + size)
        high, low = split2(inverse_ref[start : start + size, 0:used])
        both = dot(jnp.concatenate([high, low], axis=0), image[0:used, :], ((1,), (0,)))
        q_ref[start : start + size, :] = (both[0:size, :] + both[size:, :]).astype(q_ref.dtype)


def basis(inverse, y_t):
    channels, rows = y_t.shape
    return pl.pallas_call(
        basis_kernel,
        in_specs=[WHOLE] * 2,
        out_specs=[WHOLE] * 2,
        out_shape=[
            jax.ShapeDtypeStruct(y_t.shape, y_t.dtype),
            jax.ShapeDtypeStruct((8, LANES), jnp.float32),
        ],
        compiler_params=params(),
        cost_estimate=cost(10**5, 10**5),
    )(inverse, y_t)


def matrix_shape(channels):
    return jax.ShapeDtypeStruct((channels, 1, channels), jnp.float32)


def part_kernel(
    channels, scale, core_ref, mine_ref, inverse_ref, previous_ref, out_ref,
    pack_ref, lower_ref, before_ref,
):
    rows, wide = inverse_ref.shape
    half = mine_ref.shape[0]
    join(pack_ref, core_ref[0], mine_ref[...], jnp.zeros((half, LANES), jnp.float32))
    turned = dot3(full_matrix(pack_ref, channels), inverse_ref[...], ((1,), (1,)))
    unfold(previous_ref, lower_ref, channels, False)
    lower_matrix(lower_ref, before_ref)
    total = dot3(before_ref[:, 0:rows], turned, ((1,), (0,))) * scale
    out_ref[:, 0:rows] = total.astype(out_ref.dtype)
    if rows < wide:
        out_ref[:, rows:wide] = jnp.zeros((rows, wide - rows), out_ref.dtype)


def correlation_part(core, mine, inverse, previous, channels, total_rows):
    return pl.pallas_call(
        functools.partial(part_kernel, channels, 1.0 / total_rows),
        in_specs=[SCALARS] + [WHOLE] * 3,
        out_specs=WHOLE,
        out_shape=jax.ShapeDtypeStruct(inverse.shape, jnp.bfloat16),
        scratch_shapes=[
            pltpu.VMEM((full_rows(channels), LANES), jnp.float32),
            pltpu.VMEM((lower_rows(channels), LANES), jnp.float32),
            pltpu.VMEM(inverse.shape, jnp.float32),
        ],
        compiler_params=params(),
        cost_estimate=cost(10**5, 10**5),
    )(core, mine, inverse, previous)


def both_kernel(
    scale, core_ref, left_ref, right_ref, mine_ref, other_ref, out_ref, ray_ref,
    folded_ref, pack_ref, full_ref,
):
    channels = out_ref.shape[0]
    mine, other = mine_ref[...].astype(jnp.float32), other_ref[...].astype(jnp.float32)
    join(folded_ref, core_ref[0], mine, other)
    unfold(folded_ref, pack_ref, channels, True)
    symmetric_matrix(pack_ref, full_ref)
    ray_ref[:, 0, :] = full_ref[0:channels, 0:channels] * scale
    total = left_ref[...].astype(jnp.float32) + right_ref[...].astype(jnp.float32)
    out_ref[:, 0, :] = total[0:channels, 0:channels]


def both_parts(core, left, right, mine, other, channels, total_rows):
    return pl.pallas_call(
        functools.partial(both_kernel, 1.0 / total_rows),
        in_specs=[SCALARS] + [WHOLE] * 4,
        out_specs=[WHOLE] * 2,
        out_shape=[matrix_shape(channels)] * 2,
        scratch_shapes=[
            pltpu.VMEM((folded_rows(channels), LANES), jnp.float32),
            pltpu.VMEM((lower_rows(channels), LANES), jnp.float32),
            pltpu.VMEM((round_up(channels, PANEL), round_up(channels, LANES)), jnp.float32),
        ],
        compiler_params=params(),
        cost_estimate=cost(10**5, 10**5),
    )(core, left, right, mine, other)


def from_behind(value, axis, steps):
    count = lax.axis_size(axis)
    leading, last = (max(0, -steps), min(count, count - steps))
    return lax.ppermute(value, axis, [(source, source + steps) for source in range(leading, last)])


def other_core(value):
    return lax.ppermute(value, "rows", [(s, s ^ 1) for s in range(lax.axis_size("rows"))])


def chip_rounds():
    count = lax.axis_size("rows")
    bits = []
    while 2 << len(bits) < count:
        bits.append(2 << len(bits))
    return [
        [(s, s ^ (bits[n] if s % 2 == 0 else bits[-1 - n])) for s in range(count)]
        for n in range(len(bits))
    ]


def sum_chips(value, after):
    count = lax.axis_size("rows")
    if count == 8:
        both, first, second = [
            lax.ppermute(value, "rows", [(s, s ^ bits) for s in range(count)]) for bits in (6, 2, 4)
        ]
        return add_four(both, value, first, second, after)
    for pairs in chip_rounds():
        value = add_after(value, lax.ppermute(value, "rows", pairs), after)
    return value


def shards(x_block, h_diag, h_right, pattern):
    x_t = x_block[0].T
    channels, block_rows = x_t.shape
    masks = pattern[0].transpose(1, 0, 2)
    total_rows = lax.axis_size("rows") * block_rows
    core = (lax.axis_index("rows") % 2).astype(jnp.int32).reshape(1)
    later = from_behind(x_t, "rows", -1)
    carried = from_behind(tile_product(1, masks, x_t, h_right[0], x_t.dtype, 53, True), "rows", 1)
    first = tile_product(0, masks, x_t, h_diag[0], jnp.float32, 50, False)
    part = later_product(masks, later, h_right[0], first)
    y_t, g_mine, g_other = gram(core, part, carried)
    previous_y = from_behind(y_t, "sector", 1)
    rounds = chip_rounds()
    g_sum = g_mine + other_core(g_other)
    r_mine, r_other = ray(core, x_t, y_t, g_sum)
    r_sum = add_after(r_mine, other_core(r_other))
    g_sum = sum_chips(g_sum, r_sum)
    r_first = lax.ppermute(r_sum, "rows", rounds[0])
    work = first_stage(core, g_sum, other_core(g_sum), channels, total_rows)
    r_sum = add_after(r_sum, r_first, work)
    m_mine, m_other = cross(core, previous_y, y_t, r_sum, jnp.float32)
    inverse, pack = last_stages(work, channels, m_other)
    m_sum = add_after(m_mine, other_core(m_other), inverse)
    previous = from_behind(pack, "sector", 1)
    q_t, basis_token = basis(inverse, y_t)
    for pairs in rounds[:-1]:
        m_sum = add_after(m_sum, lax.ppermute(m_sum, "rows", pairs))
    m_sum = add_after(m_sum, lax.ppermute(m_sum, "rows", rounds[-1]), basis_token)
    part = correlation_part(core, m_sum, inverse, previous, channels, total_rows)
    for pairs in rounds[1:]:
        r_sum = add_after(r_sum, lax.ppermute(r_sum, "rows", pairs), flops=LAST_RAY_FLOPS)
    correlation, rayleigh = both_parts(
        core, part, other_core(part), r_sum, other_core(r_sum), channels, total_rows
    )
    return (q_t.T[None], rayleigh.transpose(1, 0, 2), correlation.transpose(1, 0, 2))


def solution(mesh):
    in_specs = (
        P("sector", "rows", None),
        P("sector", "rows", None),
        P("sector", "rows", None),
        P("sector", None, "rows", None),
    )
    out_specs = (P("sector", "rows", None), P("sector", None, None), P("sector", None, None))
    return jax.shard_map(shards, mesh=mesh, in_specs=in_specs, out_specs=out_specs, check_vma=False)
```

```python
import functools

import jax
import jax.numpy as jnp
from jax import lax
from jax.experimental import pallas as pl
from jax.experimental.pallas import tpu as pltpu
from jax.sharding import PartitionSpec as P

SUBBLOCK = 128
LANES = 128
PANEL = 16
EARLY_PANELS = 7
WHOLE = pl.BlockSpec(memory_space=pltpu.VMEM)
SCALARS = pl.BlockSpec(memory_space=pltpu.SMEM)
ANYWHERE = pl.BlockSpec(memory_space=pl.ANY)
MIB = 1024 * 1024
FIRST_STAGE_FLOPS = 6000 * 10**6
LAST_RAY_FLOPS = 3000 * 10**6
LAST_STAGES_FLOPS = 4000 * 10**6


def params(mib=48):
    return pltpu.CompilerParams(vmem_limit_bytes=mib * MIB)


def cost(flops, bytes_accessed):
    return pl.CostEstimate(flops=flops, bytes_accessed=bytes_accessed, transcendentals=0)


def round_up(value, step):
    return (value + step - 1) // step * step


def dot(left, right, dims, precision=None):
    return lax.dot_general(
        left, right, (dims, ((), ())), precision=precision, preferred_element_type=jnp.float32
    )


def block_mask(mask_ref, which, cols, dtype):
    blocks = mask_ref[:, which, :].astype(jnp.float32)
    col = lax.broadcasted_iota(jnp.int32, (blocks.shape[1], cols), 1)
    block = lax.broadcasted_iota(jnp.int32, (blocks.shape[1], cols), 0)
    wide = dot(blocks, jnp.where(col // SUBBLOCK == block, 1.0, 0.0), ((1,), (0,)))
    return [
        jnp.broadcast_to(wide[i : i + 1, :], (PANEL, cols)).astype(dtype)
        for i in range(blocks.shape[0])
    ]


def mask_rows(tile_ref, mask, start, size):
    for i in range(start // SUBBLOCK, (start + size) // SUBBLOCK):
        for row in range(i * SUBBLOCK, (i + 1) * SUBBLOCK, PANEL):
            tile_ref[row : row + PANEL, :] = tile_ref[row : row + PANEL, :] * mask[i]


def strips(rows, width):
    return [(start, min(width, rows - start)) for start in range(0, rows, width)]


def halves(rows):
    first = rows // 512 * 256
    return [(0, first), (first, rows - first)] if first else [(0, rows)]


def copies_of(source, target, sems):
    copies = []
    for n, (start, size) in enumerate(halves(target.shape[0])):
        here = (pl.ds(start, size), slice(None))
        copies.append(pltpu.make_async_copy(source.at[here], target.at[here], sems.at[n]))
    return copies


def product(x_ref, tile_ref, copies, in_turn, mask, sum_ref, out_ref):
    rows = tile_ref.shape[0]
    for n, (start, size) in enumerate(halves(rows)):
        copies[n].wait()
        if in_turn and n + 1 < len(copies):
            copies[n + 1].start()
        mask_rows(tile_ref, mask, start, size)
        last = n + 1 == len(copies)
        for col, cols in strips(rows, 2 * SUBBLOCK):
            here = (slice(None), slice(col, col + cols))
            term = dot(
                x_ref[:, start : start + size],
                tile_ref[start : start + size, col : col + cols],
                ((1,), (0,)),
            )
            if n > 0:
                term = sum_ref[here] + term
            if last:
                out_ref[here] = term.astype(out_ref.dtype)
            else:
                sum_ref[here] = term


def tile_kernel(which, in_turn, mask_ref, x_hbm, tile_hbm, out_ref, x_ref, tile_ref, sum_ref, x_sem, sems):
    rows = tile_ref.shape[0]
    copies = copies_of(tile_hbm, tile_ref, sems)
    copy_x = pltpu.make_async_copy(x_hbm, x_ref, x_sem)
    copy_x.start()
    for copy in copies[:1] if in_turn else copies:
        copy.start()
    mask = block_mask(mask_ref, which, rows, tile_ref.dtype)
    copy_x.wait()
    product(x_ref, tile_ref, copies, in_turn, mask, sum_ref, out_ref)


def tile_product(which, masks, x_t, tile, dtype, mib, in_turn):
    channels, rows = x_t.shape
    return pl.pallas_call(
        functools.partial(tile_kernel, which, in_turn),
        in_specs=[WHOLE, ANYWHERE, ANYWHERE],
        out_specs=WHOLE,
        out_shape=jax.ShapeDtypeStruct((channels, rows), dtype),
        scratch_shapes=[
            pltpu.VMEM((channels, rows), x_t.dtype),
            pltpu.VMEM((rows, rows), tile.dtype),
            pltpu.VMEM((channels, rows), jnp.float32),
            pltpu.SemaphoreType.DMA,
            pltpu.SemaphoreType.DMA((2,)),
        ],
        compiler_params=params(mib),
        cost_estimate=cost(2 * channels * rows * rows, 2 * rows * rows),
    )(masks, x_t, tile)


def later_kernel(mask_ref, later_ref, tile_hbm, first_ref, out_ref, tile_ref, sems):
    rows = tile_ref.shape[0]
    copies = copies_of(tile_hbm, tile_ref, sems)
    for copy in copies:
        copy.start()
    mask = block_mask(mask_ref, 1, rows, tile_ref.dtype)
    for n, (start, size) in enumerate(halves(rows)):
        copies[n].wait()
        mask_rows(tile_ref, mask, start, size)
        for row, count in strips(size, 2 * SUBBLOCK):
            here = (slice(None), slice(start + row, start + row + count))
            out_ref[here] = first_ref[here] + dot(
                later_ref[...], tile_ref[start + row : start + row + count, :], ((1,), (1,))
            )


def later_product(masks, later, tile, first):
    channels, rows = later.shape
    return pl.pallas_call(
        later_kernel,
        in_specs=[WHOLE, WHOLE, ANYWHERE, WHOLE],
        out_specs=WHOLE,
        out_shape=jax.ShapeDtypeStruct((channels, rows), jnp.float32),
        scratch_shapes=[
            pltpu.VMEM((rows, rows), tile.dtype),
            pltpu.SemaphoreType.DMA((2,)),
        ],
        compiler_params=params(),
        cost_estimate=cost(2 * channels * rows * rows, 2 * rows * rows),
    )(masks, later, tile, first)


def lower_rows(channels):
    rows = round_up(channels, PANEL)
    return sum(rows - g * LANES for g in range(round_up(channels, LANES) // LANES))


def full_rows(channels):
    rows, wide = round_up(channels, PANEL), round_up(channels, LANES)
    whole = channels // LANES
    rest = rows - whole * LANES
    return round_up(whole * rows + rest * (wide // LANES), 4 * PANEL)


def lower_products(left_ref, right_ref, out_ref):
    channels = left_ref.shape[0]
    rows = round_up(channels, PANEL)
    offset = 0
    for start, size in strips(channels, LANES):
        tall = rows - start
        if size < LANES:
            out_ref[offset : offset + tall, :] = jnp.zeros((tall, LANES), jnp.float32)
        elif rows > channels:
            out_ref[offset + channels - start : offset + tall, :] = jnp.zeros(
                (rows - channels, LANES), jnp.float32
            )
        out_ref[offset : offset + channels - start, 0:size] = dot(
            left_ref[start:channels, :], right_ref[start : start + size, :], ((1,), (1,))
        )
        offset += tall


def full_products(left_ref, right_ref, out_ref):
    channels = left_ref.shape[0]
    rows = round_up(channels, PANEL)
    whole = channels // LANES
    for g in range(whole):
        out_ref[g * rows : g * rows + channels, :] = dot(
            left_ref[...], right_ref[g * LANES : (g + 1) * LANES, :], ((1,), (1,))
        )
        if rows > channels:
            out_ref[g * rows + channels : (g + 1) * rows, :] = jnp.zeros(
                (rows - channels, LANES), jnp.float32
            )
    base = whole * rows
    if base < out_ref.shape[0]:
        out_ref[base:, :] = jnp.zeros((out_ref.shape[0] - base, LANES), jnp.float32)
    first, rest = whole * LANES, rows - whole * LANES
    for n, (start, size) in enumerate(strips(channels, LANES) if first < channels else []):
        place = base + n * rest
        out_ref[place : place + channels - first, 0:size] = dot(
            right_ref[first:channels, :], left_ref[start : start + size, :], ((1,), (1,))
        )


def full_matrix(pack_ref, channels):
    rows, wide = round_up(channels, PANEL), round_up(channels, LANES)
    whole = channels // LANES
    rest = rows - whole * LANES
    parts = [pack_ref[g * rows : (g + 1) * rows, :] for g in range(whole)]
    if rest:
        tail = jnp.concatenate(
            [
                pack_ref[whole * rows + g * rest : whole * rows + (g + 1) * rest, :]
                for g in range(wide // LANES)
            ],
            axis=1,
        )
        tail = jnp.concatenate([tail, jnp.zeros((LANES - rest, wide), tail.dtype)], axis=0)
        parts.append(tail.T[0:rows, :])
    return jnp.concatenate(parts, axis=1)


def folded_rows(channels):
    if channels < 2 * LANES:
        return lower_rows(channels)
    return lower_rows(channels) - LANES + PANEL


def corner(channels):
    return round_up(channels, PANEL)


def square_index():
    row = lax.broadcasted_iota(jnp.int32, (LANES, LANES), 0)
    return row, lax.broadcasted_iota(jnp.int32, (LANES, LANES), 1)


def fold(pack_ref, out_ref, channels, symmetric):
    if channels < 2 * LANES:
        out_ref[...] = pack_ref[...]
        return
    start = corner(channels)
    end = pack_ref.shape[0]
    row, lane = square_index()
    second = pack_ref[start : start + LANES, :]
    upper = second if symmetric else second.T
    out_ref[0:LANES, :] = jnp.where(row >= lane, pack_ref[0:LANES, :], upper)
    out_ref[LANES:start, :] = pack_ref[LANES:start, :]
    out_ref[start : end - LANES, :] = pack_ref[start + LANES : end, :]
    diagonal = jnp.sum(jnp.where(row == lane, second, 0.0), axis=0, keepdims=True)
    out_ref[end - LANES :, :] = jnp.broadcast_to(diagonal, (PANEL, LANES))


def unfold(folded_ref, pack_ref, channels, symmetric):
    if channels < 2 * LANES:
        pack_ref[...] = folded_ref[...]
        return
    start = corner(channels)
    end = pack_ref.shape[0]
    row, lane = square_index()
    both = folded_ref[0:LANES, :]
    turned = both.T
    first_upper, second_upper = (turned, both) if symmetric else (0.0, 0.0)
    pack_ref[0:LANES, :] = jnp.where(row >= lane, both, first_upper)
    pack_ref[LANES:start, :] = folded_ref[LANES:start, :]
    second = jnp.where(row > lane, turned, second_upper)
    diagonal = folded_ref[end - LANES : end - LANES + 1, :]
    pack_ref[start : start + LANES, :] = jnp.where(row == lane, diagonal, second)
    pack_ref[start + LANES : end, :] = folded_ref[start : end - LANES, :]


def cut(pack_ref, core, mine_ref, other_ref):
    half = mine_ref.shape[0]
    mine_ref[...] = pack_ref[pl.ds(pl.multiple_of(core * half, 8), half), :].astype(mine_ref.dtype)
    other_ref[...] = pack_ref[pl.ds(pl.multiple_of((1 - core) * half, 8), half), :].astype(
        other_ref.dtype
    )


def join(pack_ref, core, mine, other):
    half = mine.shape[0]
    pack_ref[pl.ds(pl.multiple_of(core * half, 8), half), :] = mine
    pack_ref[pl.ds(pl.multiple_of((1 - core) * half, 8), half), :] = other


def early_kernel(part_ref, inner_ref, y_ref):
    y_ref[...] = (part_ref[...] + inner_ref[...].astype(jnp.float32)).astype(y_ref.dtype)


def early_image(part, inner):
    return pl.pallas_call(
        early_kernel,
        in_specs=[WHOLE] * 2,
        out_specs=WHOLE,
        out_shape=jax.ShapeDtypeStruct(inner.shape, inner.dtype),
        compiler_params=params(),
        cost_estimate=cost(10**6, 10**6),
    )(part, inner)


def gram_kernel(
    core_ref, part_ref, inner_ref, outer_ref, y_ref, g_mine, g_other, gram_ref, folded_ref
):
    carried = inner_ref[...].astype(jnp.float32) + outer_ref[...].astype(jnp.float32)
    y_ref[...] = (part_ref[...] + carried).astype(y_ref.dtype)
    lower_products(y_ref, y_ref, gram_ref)
    fold(gram_ref, folded_ref, y_ref.shape[0], True)
    cut(folded_ref, core_ref[0], g_mine, g_other)


def gram(core, part, inner, outer):
    channels, rows = inner.shape
    lower, folded = lower_rows(channels), folded_rows(channels)
    half = jax.ShapeDtypeStruct((folded // 2, LANES), jnp.float32)
    return pl.pallas_call(
        gram_kernel,
        in_specs=[SCALARS] + [WHOLE] * 3,
        out_specs=[WHOLE] * 3,
        out_shape=[jax.ShapeDtypeStruct((channels, rows), inner.dtype), half, half],
        scratch_shapes=[
            pltpu.VMEM((lower, LANES), jnp.float32),
            pltpu.VMEM((folded, LANES), jnp.float32),
        ],
        compiler_params=params(),
        cost_estimate=cost(2 * channels * channels * rows, 8 * channels * rows),
    )(core, part, inner, outer)


def symmetric_matrix(pack_ref, out_ref):
    rows, wide = out_ref.shape
    offset = 0
    for top in range(0, wide, LANES):
        size = min(LANES, rows - top)
        column = pack_ref[offset : offset + rows - top, :]
        offset += rows - top
        out_ref[top:rows, top : top + LANES] = column
        for below in range(top + LANES, wide, LANES):
            count = min(LANES, rows - below)
            block = column[below - top : below - top + count, :]
            if count < LANES:
                block = jnp.concatenate(
                    [block, jnp.zeros((LANES - count, LANES), block.dtype)], axis=0
                )
            out_ref[top : top + size, below : below + LANES] = block.T


def ray_kernel(core_ref, x_ref, y_ref, after_ref, mine_ref, other_ref, pack_ref, folded_ref):
    lower_products(x_ref, y_ref, pack_ref)
    fold(pack_ref, folded_ref, x_ref.shape[0], True)
    cut(folded_ref, core_ref[0], mine_ref, other_ref)


def ray(core, x_t, y_t, after):
    channels, rows = x_t.shape
    lower, folded = lower_rows(channels), folded_rows(channels)
    return pl.pallas_call(
        ray_kernel,
        in_specs=[SCALARS, WHOLE, WHOLE, ANYWHERE],
        out_specs=[WHOLE] * 2,
        out_shape=[jax.ShapeDtypeStruct((folded // 2, LANES), jnp.bfloat16)] * 2,
        scratch_shapes=[
            pltpu.VMEM((lower, LANES), jnp.float32),
            pltpu.VMEM((folded, LANES), jnp.float32),
        ],
        compiler_params=params(),
        cost_estimate=cost(2 * channels * channels * rows, 4 * channels * rows),
    )(core, x_t, y_t, after)


def cross_kernel(
    core_ref, early_ref, late_ref, right_ref, after_ref, mine_ref, other_ref, left_ref, pack_ref
):
    left_ref[...] = early_ref[...] + late_ref[...]
    full_products(left_ref, right_ref, pack_ref)
    cut(pack_ref, core_ref[0], mine_ref, other_ref)


def cross(core, early, late, right, after):
    channels, rows = right.shape
    full = full_rows(channels)
    return pl.pallas_call(
        cross_kernel,
        in_specs=[SCALARS, WHOLE, WHOLE, WHOLE, ANYWHERE],
        out_specs=[WHOLE] * 2,
        out_shape=[jax.ShapeDtypeStruct((full // 2, LANES), jnp.float32)] * 2,
        scratch_shapes=[
            pltpu.VMEM((channels, rows), right.dtype),
            pltpu.VMEM((full, LANES), jnp.float32),
        ],
        compiler_params=params(),
        cost_estimate=cost(2 * channels * channels * rows, 4 * channels * rows),
    )(core, early, late, right, after)


def add_kernel(left_ref, right_ref, *refs):
    total = left_ref[...].astype(jnp.float32) + right_ref[...].astype(jnp.float32)
    refs[-1][...] = total.astype(refs[-1].dtype)


def add_four_kernel(both_ref, own_ref, first_ref, second_ref, after_ref, out_ref):
    both, own, first, second = (
        ref[...].astype(jnp.float32) for ref in (both_ref, own_ref, first_ref, second_ref)
    )
    out_ref[...] = ((own + first) + (second + both)).astype(out_ref.dtype)


def add_four(both, own, first, second, after):
    return pl.pallas_call(
        add_four_kernel,
        in_specs=[WHOLE] * 4 + [ANYWHERE],
        out_specs=WHOLE,
        out_shape=jax.ShapeDtypeStruct(own.shape, own.dtype),
        compiler_params=params(),
        cost_estimate=cost(10**5, 10**5),
    )(both, own, first, second, after)


def add_after(left, right, *after, flops=10**5):
    return pl.pallas_call(
        add_kernel,
        in_specs=[WHOLE] * 2 + [ANYWHERE] * len(after),
        out_specs=WHOLE,
        out_shape=jax.ShapeDtypeStruct(left.shape, left.dtype),
        compiler_params=params(),
        cost_estimate=cost(flops, 10**5),
    )(left, right, *after)


def split3(value):
    high = value.astype(jnp.bfloat16)
    rest = value - high.astype(jnp.float32)
    mid = rest.astype(jnp.bfloat16)
    low = (rest - mid.astype(jnp.float32)).astype(jnp.bfloat16)
    return high, mid, low


def sublane(value, index):
    return jnp.broadcast_to(value[index : index + 1, :], value.shape)


def lane_of(value, index):
    return jnp.take_along_axis(value, jnp.broadcast_to(index, value.shape), axis=1)


def eliminate(columns, panel):
    half = 8
    row = lax.broadcasted_iota(jnp.int32, (half, LANES), 0)
    scales = [jnp.zeros((half, LANES), jnp.float32) for _ in range(2)]
    columns = [list(c) for c in columns]
    panel = [list(p) for p in panel]
    for j in range(0, PANEL, 2):
        h, r = divmod(j, half)
        left, right = columns[j], columns[j + 1]
        a, b, c = sublane(left[h], r), sublane(left[h], r + 1), sublane(right[h], r + 1)
        det = a * c - b * b
        inverse = pl.reciprocal(det, approx=True)
        first, second = [None, None], [None, None]
        for t in range(h, 2):
            x, y = left[t], right[t]
            if t == h:
                x, y = jnp.where(row > r + 1, x, 0.0), jnp.where(row > r + 1, y, 0.0)
            first[t] = (c * x - b * y) * inverse
            second[t] = (a * y - b * x) * inverse
        for later in range(j + 2, PANEL):
            q = later // half
            x, y = sublane(left[q], later % half), sublane(right[q], later % half)
            for t in range(max(h, q), 2):
                columns[later][t] = columns[later][t] - (first[t] * x + second[t] * y)
        inverse_a = pl.reciprocal(a, approx=True)
        first[h] = jnp.where(row == r + 1, b * inverse_a, first[h])
        for group in panel:
            x, y = sublane(group[h], r), sublane(group[h], r + 1)
            for t in range(h, 2):
                group[t] = group[t] - (first[t] * x + second[t] * y)
        scales[h] = jnp.where(row == r, lax.rsqrt(a), scales[h])
        scales[h] = jnp.where(row == r + 1, lax.rsqrt(det * inverse_a), scales[h])
    return [jnp.concatenate([g[0] * scales[0], g[1] * scales[1]], axis=0) for g in panel]


def fill_work(channels, scale, pack_ref, work_ref):
    rows, wide = work_ref.shape
    groups = wide // LANES
    offset = 0
    for g in range(groups):
        top = g * LANES
        size = min(LANES, rows - top)
        column = pack_ref[offset : offset + rows - top, :] * scale
        offset += rows - top
        diag = column[0:size, :]
        if top + LANES > channels:
            row = lax.broadcasted_iota(jnp.int32, diag.shape, 0)
            lane = lax.broadcasted_iota(jnp.int32, diag.shape, 1)
            diag = jnp.where((row == lane) & (lane + top >= channels), 1.0, diag)
        work_ref[top : top + size, top : top + LANES] = diag
        for below in range(g + 1, groups):
            start = (below - g) * LANES
            size_b = min(LANES, rows - below * LANES)
            block = column[start : start + size_b, :]
            if size_b < LANES:
                block = jnp.concatenate(
                    [block, jnp.zeros((LANES - size_b, LANES), jnp.float32)], axis=0
                )
            work_ref[top : top + size, below * LANES : (below + 1) * LANES] = block.T
            work_ref[below * LANES : below * LANES + size_b, top : top + LANES] = jnp.zeros(
                (size_b, LANES), jnp.float32
            )


def eliminate_group(g, work_ref, turned_ref, first=0, last=LANES // PANEL):
    rows, wide = work_ref.shape
    groups = wide // LANES
    row = lax.broadcasted_iota(jnp.int32, (PANEL, LANES), 0)
    lane = lax.broadcasted_iota(jnp.int32, (PANEL, LANES), 1)
    top = g * LANES
    count = min(LANES, rows - top) // PANEL

    def load(local):
        place = pl.ds(pl.multiple_of(top + local, PANEL), PANEL)
        return [work_ref[place, q * LANES : (q + 1) * LANES] for q in range(groups)]

    def panel_step(b, parts, slot):
        local = b * PANEL
        following = jnp.minimum(local + PANEL, (count - 1) * PANEL)
        ahead = load(following)
        pivots = [parts[g][0:8, :], parts[g][8:16, :]]
        columns = [[lane_of(p, local + j) for p in pivots] for j in range(PANEL)]
        inside = (lane >= local) & (lane < local + PANEL)
        identity = jnp.where(lane - local == row, 1.0, 0.0)
        parts = list(parts)
        parts[g] = jnp.where(inside, identity, parts[g])
        done = eliminate(columns, [[p[0:8, :], p[8:16, :]] for p in parts])
        right = []
        for q in range(groups):
            high, mid, low = split3(done[q])
            right.append(jnp.concatenate([high, mid, high, low, mid, high], axis=0))
            if q >= g:
                if q == g:
                    high, mid, low = split3(jnp.where(lane >= local + PANEL, done[q], 0.0))
                left = jnp.concatenate([high, high, mid, high, mid, low], axis=0)
                turned_ref[slot, (q - g) * LANES : (q - g + 1) * LANES, :] = left.T
        right = jnp.concatenate(right, axis=1)
        near = turned_ref[slot, pl.ds(pl.multiple_of(following, PANEL), PANEL), :]
        update = dot(near, right, ((1,), (0,)))
        ahead[g] = jnp.where(inside, 0.0, ahead[g])
        ahead = [ahead[q] - update[:, q * LANES : (q + 1) * LANES] for q in range(groups)]
        for q in range(g, groups):
            low_row = q * LANES
            high_row = min(rows, low_row + LANES)
            base = low_row - top
            update = dot(turned_ref[slot, base : base + high_row - low_row, :], right, ((1,), (0,)))
            for c in range(groups):
                lanes = slice(c * LANES, (c + 1) * LANES)
                old = work_ref[low_row:high_row, lanes]
                if c == g:
                    here = lax.broadcasted_iota(jnp.int32, old.shape, 1)
                    old = jnp.where((here >= local) & (here < local + PANEL), 0.0, old)
                work_ref[low_row:high_row, lanes] = old - update[:, lanes]
        for q in range(groups):
            if q == g:
                done[q] = jnp.where(lane < local + PANEL, done[q], 0.0)
            elif q > g:
                done[q] = jnp.zeros_like(done[q])
            place = pl.ds(pl.multiple_of(top + local, PANEL), PANEL)
            work_ref[place, q * LANES : (q + 1) * LANES] = done[q]
        return ahead

    def two_panels(i, parts):
        return panel_step(first + 2 * i + 1, panel_step(first + 2 * i, parts, 0), 1)

    last = min(last, count)
    parts = lax.fori_loop(0, (last - first) // 2, two_panels, load(first * PANEL))
    if (last - first) % 2:
        panel_step(jnp.int32(last - 1), parts, 0)


def first_stage_kernel(
    channels, scale, core_ref, mine_ref, other_ref, after_ref,
    work_ref, pack_ref, folded_ref, turned_ref,
):
    join(folded_ref, core_ref[0], mine_ref[...], other_ref[...])
    unfold(folded_ref, pack_ref, channels, True)
    fill_work(channels, scale, pack_ref, work_ref)
    eliminate_group(0, work_ref, turned_ref)
    if work_ref.shape[1] > LANES:
        eliminate_group(1, work_ref, turned_ref, 0, EARLY_PANELS)


def last_stages_kernel(
    channels, before_ref, after_ref, work_ref, folded_ref, pack_ref, turned_ref
):
    work_ref[...] = before_ref[...]
    rows, wide = work_ref.shape
    for g in range(1 if EARLY_PANELS * PANEL < LANES else 2, wide // LANES):
        eliminate_group(g, work_ref, turned_ref, EARLY_PANELS if g == 1 else 0)
    offset = 0
    for q in range(wide // LANES):
        tall = rows - q * LANES
        pack_ref[offset : offset + tall, :] = work_ref[q * LANES : rows, q * LANES : (q + 1) * LANES]
        offset += tall
    fold(pack_ref, folded_ref, channels, False)


def turned_scratch(channels):
    return pltpu.VMEM((2, round_up(channels, LANES), 6 * PANEL), jnp.bfloat16)


def work_shape(channels):
    return jax.ShapeDtypeStruct((round_up(channels, PANEL), round_up(channels, LANES)), jnp.float32)


def first_stage(core, mine, other, after, channels, total_rows):
    return pl.pallas_call(
        functools.partial(first_stage_kernel, channels, 1.0 / total_rows),
        in_specs=[SCALARS] + [WHOLE] * 2 + [ANYWHERE],
        out_specs=WHOLE,
        out_shape=work_shape(channels),
        scratch_shapes=[
            pltpu.VMEM((lower_rows(channels), LANES), jnp.float32),
            pltpu.VMEM((folded_rows(channels), LANES), jnp.float32),
            turned_scratch(channels),
        ],
        compiler_params=params(),
        cost_estimate=cost(FIRST_STAGE_FLOPS, 10**6),
    )(core, mine, other, after)


def last_stages(work, channels, after):
    return pl.pallas_call(
        functools.partial(last_stages_kernel, channels),
        in_specs=[WHOLE, ANYWHERE],
        out_specs=[WHOLE] * 2,
        out_shape=[
            work_shape(channels),
            jax.ShapeDtypeStruct((folded_rows(channels), LANES), jnp.float32),
        ],
        scratch_shapes=[
            pltpu.VMEM((lower_rows(channels), LANES), jnp.float32),
            turned_scratch(channels),
        ],
        compiler_params=params(),
        cost_estimate=cost(LAST_STAGES_FLOPS, 10**5),
    )(work, after)


def split2(value):
    high = value.astype(jnp.bfloat16)
    return high, (value - high.astype(jnp.float32)).astype(jnp.bfloat16)


def dot3(left, right, dims):
    rows = left.shape[0]
    left_high, left_low = split2(left)
    right_high, right_low = split2(right)
    both = dot(jnp.concatenate([left_high, left_low], axis=0), right_high, dims)
    return both[0:rows, :] + both[rows:, :] + dot(left_high, right_low, dims)


def lower_matrix(pack_ref, out_ref):
    rows, wide = out_ref.shape
    offset = 0
    for g in range(wide // LANES):
        top = g * LANES
        lanes = slice(top, top + LANES)
        if top:
            out_ref[0:top, lanes] = jnp.zeros((top, LANES), jnp.float32)
        out_ref[top:rows, lanes] = pack_ref[offset : offset + rows - top, :]
        offset += rows - top


def basis_kernel(inverse_ref, y_ref, q_ref, token_ref):
    channels = y_ref.shape[0]
    image = y_ref[...]
    token_ref[...] = jnp.zeros_like(token_ref)
    for start, size in strips(channels, 2 * LANES):
        used = min(channels, start + size)
        high, low = split2(inverse_ref[start : start + size, 0:used])
        both = dot(jnp.concatenate([high, low], axis=0), image[0:used, :], ((1,), (0,)))
        q_ref[start : start + size, :] = (both[0:size, :] + both[size:, :]).astype(q_ref.dtype)


def basis(inverse, y_t):
    channels, rows = y_t.shape
    return pl.pallas_call(
        basis_kernel,
        in_specs=[WHOLE] * 2,
        out_specs=[WHOLE] * 2,
        out_shape=[
            jax.ShapeDtypeStruct(y_t.shape, y_t.dtype),
            jax.ShapeDtypeStruct((8, LANES), jnp.float32),
        ],
        compiler_params=params(),
        cost_estimate=cost(10**5, 10**5),
    )(inverse, y_t)


def matrix_shape(channels):
    return jax.ShapeDtypeStruct((channels, 1, channels), jnp.float32)


def part_kernel(
    channels, scale, core_ref, mine_ref, inverse_ref, previous_ref, out_ref,
    pack_ref, lower_ref, before_ref,
):
    rows, wide = inverse_ref.shape
    half = mine_ref.shape[0]
    join(pack_ref, core_ref[0], mine_ref[...], jnp.zeros((half, LANES), jnp.float32))
    turned = dot3(full_matrix(pack_ref, channels), inverse_ref[...], ((1,), (1,)))
    unfold(previous_ref, lower_ref, channels, False)
    lower_matrix(lower_ref, before_ref)
    total = dot3(before_ref[:, 0:rows], turned, ((1,), (0,))) * scale
    out_ref[:, 0:rows] = total.astype(out_ref.dtype)
    if rows < wide:
        out_ref[:, rows:wide] = jnp.zeros((rows, wide - rows), out_ref.dtype)


def correlation_part(core, mine, inverse, previous, channels, total_rows):
    return pl.pallas_call(
        functools.partial(part_kernel, channels, 1.0 / total_rows),
        in_specs=[SCALARS] + [WHOLE] * 3,
        out_specs=WHOLE,
        out_shape=jax.ShapeDtypeStruct(inverse.shape, jnp.bfloat16),
        scratch_shapes=[
            pltpu.VMEM((full_rows(channels), LANES), jnp.float32),
            pltpu.VMEM((lower_rows(channels), LANES), jnp.float32),
            pltpu.VMEM(inverse.shape, jnp.float32),
        ],
        compiler_params=params(),
        cost_estimate=cost(10**5, 10**5),
    )(core, mine, inverse, previous)


def both_kernel(
    scale, core_ref, left_ref, right_ref, mine_ref, other_ref, out_ref, ray_ref,
    folded_ref, pack_ref, full_ref,
):
    channels = out_ref.shape[0]
    mine, other = mine_ref[...].astype(jnp.float32), other_ref[...].astype(jnp.float32)
    join(folded_ref, core_ref[0], mine, other)
    unfold(folded_ref, pack_ref, channels, True)
    symmetric_matrix(pack_ref, full_ref)
    ray_ref[:, 0, :] = full_ref[0:channels, 0:channels] * scale
    total = left_ref[...].astype(jnp.float32) + right_ref[...].astype(jnp.float32)
    out_ref[:, 0, :] = total[0:channels, 0:channels]


def both_parts(core, left, right, mine, other, channels, total_rows):
    return pl.pallas_call(
        functools.partial(both_kernel, 1.0 / total_rows),
        in_specs=[SCALARS] + [WHOLE] * 4,
        out_specs=[WHOLE] * 2,
        out_shape=[matrix_shape(channels)] * 2,
        scratch_shapes=[
            pltpu.VMEM((folded_rows(channels), LANES), jnp.float32),
            pltpu.VMEM((lower_rows(channels), LANES), jnp.float32),
            pltpu.VMEM((round_up(channels, PANEL), round_up(channels, LANES)), jnp.float32),
        ],
        compiler_params=params(),
        cost_estimate=cost(10**5, 10**5),
    )(core, left, right, mine, other)


def from_behind(value, axis, steps):
    count = lax.axis_size(axis)
    leading, last = (max(0, -steps), min(count, count - steps))
    return lax.ppermute(value, axis, [(source, source + steps) for source in range(leading, last)])


def to_later_rows(value, odd):
    count = lax.axis_size("rows")
    return lax.ppermute(value, "rows", [(s, s + 1) for s in range(odd, count - 1, 2)])


def to_later_sector(value, early):
    sectors, count = lax.axis_size("sector"), lax.axis_size("rows")
    rows = [r for r in range(count) if (r % 2 == 1 or r == 0) == early]
    pairs = [(s * count + r, (s + 1) * count + r) for s in range(sectors - 1) for r in rows]
    return lax.ppermute(value, ("sector", "rows"), pairs)


def other_core(value):
    return lax.ppermute(value, "rows", [(s, s ^ 1) for s in range(lax.axis_size("rows"))])


def chip_rounds():
    count = lax.axis_size("rows")
    bits = []
    while 2 << len(bits) < count:
        bits.append(2 << len(bits))
    return [
        [(s, s ^ (bits[n] if s % 2 == 0 else bits[-1 - n])) for s in range(count)]
        for n in range(len(bits))
    ]


def sum_chips(value, after):
    count = lax.axis_size("rows")
    if count == 8:
        both, first, second = [
            lax.ppermute(value, "rows", [(s, s ^ bits) for s in range(count)]) for bits in (6, 2, 4)
        ]
        return add_four(both, value, first, second, after)
    for pairs in chip_rounds():
        value = add_after(value, lax.ppermute(value, "rows", pairs), after)
    return value


def shards(x_block, h_diag, h_right, pattern):
    x_t = x_block[0].T
    channels, block_rows = x_t.shape
    masks = pattern[0].transpose(1, 0, 2)
    total_rows = lax.axis_size("rows") * block_rows
    core = (lax.axis_index("rows") % 2).astype(jnp.int32).reshape(1)
    later = from_behind(x_t, "rows", -1)
    carried = tile_product(1, masks, x_t, h_right[0], x_t.dtype, 53, True)
    outer, inner = to_later_rows(carried, 1), to_later_rows(carried, 0)
    first = tile_product(0, masks, x_t, h_diag[0], jnp.float32, 50, False)
    part = later_product(masks, later, h_right[0], first)
    early_y = to_later_sector(early_image(part, inner), True)
    y_t, g_mine, g_other = gram(core, part, inner, outer)
    late_y = to_later_sector(y_t, False)
    rounds = chip_rounds()
    g_sum = g_mine + other_core(g_other)
    r_mine, r_other = ray(core, x_t, y_t, g_sum)
    r_sum = add_after(r_mine, other_core(r_other))
    g_sum = sum_chips(g_sum, r_sum)
    r_first = lax.ppermute(r_sum, "rows", rounds[0])
    work = first_stage(core, g_sum, other_core(g_sum), early_y, channels, total_rows)
    r_sum = add_after(r_sum, r_first, work)
    m_mine, m_other = cross(core, early_y, late_y, y_t, r_sum)
    inverse, pack = last_stages(work, channels, m_other)
    m_sum = add_after(m_mine, other_core(m_other), inverse)
    previous = from_behind(pack, "sector", 1)
    q_t, basis_token = basis(inverse, y_t)
    for pairs in rounds[:-1]:
        m_sum = add_after(m_sum, lax.ppermute(m_sum, "rows", pairs))
    m_sum = add_after(m_sum, lax.ppermute(m_sum, "rows", rounds[-1]), basis_token)
    part = correlation_part(core, m_sum, inverse, previous, channels, total_rows)
    for pairs in rounds[1:]:
        r_sum = add_after(r_sum, lax.ppermute(r_sum, "rows", pairs), flops=LAST_RAY_FLOPS)
    correlation, rayleigh = both_parts(
        core, part, other_core(part), r_sum, other_core(r_sum), channels, total_rows
    )
    return (q_t.T[None], rayleigh.transpose(1, 0, 2), correlation.transpose(1, 0, 2))


def solution(mesh):
    in_specs = (
        P("sector", "rows", None),
        P("sector", "rows", None),
        P("sector", "rows", None),
        P("sector", None, "rows", None),
    )
    out_specs = (P("sector", "rows", None), P("sector", None, None), P("sector", None, None))
    return jax.shard_map(shards, mesh=mesh, in_specs=in_specs, out_specs=out_specs, check_vma=False)
```

```python
import functools

import jax
import jax.numpy as jnp
from jax import lax
from jax.experimental import pallas as pl
from jax.experimental.pallas import tpu as pltpu
from jax.sharding import PartitionSpec as P

SUBBLOCK = 128
LANES = 128
PANEL = 16
EARLY_PANELS = 7
WHOLE = pl.BlockSpec(memory_space=pltpu.VMEM)
SCALARS = pl.BlockSpec(memory_space=pltpu.SMEM)
ANYWHERE = pl.BlockSpec(memory_space=pl.ANY)
MIB = 1024 * 1024
FIRST_STAGE_FLOPS = 5000 * 10**6
LAST_RAY_FLOPS = 3000 * 10**6
LAST_STAGES_FLOPS = 4000 * 10**6


def params(mib=48):
    return pltpu.CompilerParams(vmem_limit_bytes=mib * MIB)


def cost(flops, bytes_accessed):
    return pl.CostEstimate(flops=flops, bytes_accessed=bytes_accessed, transcendentals=0)


def round_up(value, step):
    return (value + step - 1) // step * step


def dot(left, right, dims, precision=None):
    return lax.dot_general(
        left, right, (dims, ((), ())), precision=precision, preferred_element_type=jnp.float32
    )


def block_mask(mask_ref, which, cols, dtype):
    blocks = mask_ref[:, which, :].astype(jnp.float32)
    col = lax.broadcasted_iota(jnp.int32, (blocks.shape[1], cols), 1)
    block = lax.broadcasted_iota(jnp.int32, (blocks.shape[1], cols), 0)
    wide = dot(blocks, jnp.where(col // SUBBLOCK == block, 1.0, 0.0), ((1,), (0,)))
    return [
        jnp.broadcast_to(wide[i : i + 1, :], (PANEL, cols)).astype(dtype)
        for i in range(blocks.shape[0])
    ]


def mask_rows(tile_ref, mask, start, size):
    for i in range(start // SUBBLOCK, (start + size) // SUBBLOCK):
        for row in range(i * SUBBLOCK, (i + 1) * SUBBLOCK, PANEL):
            tile_ref[row : row + PANEL, :] = tile_ref[row : row + PANEL, :] * mask[i]


def strips(rows, width):
    return [(start, min(width, rows - start)) for start in range(0, rows, width)]


def halves(rows):
    first = rows // 512 * 256
    return [(0, first), (first, rows - first)] if first else [(0, rows)]


def copies_of(source, target, sems):
    copies = []
    for n, (start, size) in enumerate(halves(target.shape[0])):
        here = (pl.ds(start, size), slice(None))
        copies.append(pltpu.make_async_copy(source.at[here], target.at[here], sems.at[n]))
    return copies


def product(x_ref, tile_ref, copies, in_turn, mask, sum_ref, out_ref):
    rows = tile_ref.shape[0]
    for n, (start, size) in enumerate(halves(rows)):
        copies[n].wait()
        if in_turn and n + 1 < len(copies):
            copies[n + 1].start()
        mask_rows(tile_ref, mask, start, size)
        last = n + 1 == len(copies)
        for col, cols in strips(rows, 2 * SUBBLOCK):
            here = (slice(None), slice(col, col + cols))
            term = dot(
                x_ref[:, start : start + size],
                tile_ref[start : start + size, col : col + cols],
                ((1,), (0,)),
            )
            if n > 0:
                term = sum_ref[here] + term
            if last:
                out_ref[here] = term.astype(out_ref.dtype)
            else:
                sum_ref[here] = term


def tile_kernel(which, in_turn, mask_ref, x_hbm, tile_hbm, out_ref, x_ref, tile_ref, sum_ref, x_sem, sems):
    rows = tile_ref.shape[0]
    copies = copies_of(tile_hbm, tile_ref, sems)
    copy_x = pltpu.make_async_copy(x_hbm, x_ref, x_sem)
    copy_x.start()
    for copy in copies[:1] if in_turn else copies:
        copy.start()
    mask = block_mask(mask_ref, which, rows, tile_ref.dtype)
    copy_x.wait()
    product(x_ref, tile_ref, copies, in_turn, mask, sum_ref, out_ref)


def tile_product(which, masks, x_t, tile, dtype, mib, in_turn):
    channels, rows = x_t.shape
    return pl.pallas_call(
        functools.partial(tile_kernel, which, in_turn),
        in_specs=[WHOLE, ANYWHERE, ANYWHERE],
        out_specs=WHOLE,
        out_shape=jax.ShapeDtypeStruct((channels, rows), dtype),
        scratch_shapes=[
            pltpu.VMEM((channels, rows), x_t.dtype),
            pltpu.VMEM((rows, rows), tile.dtype),
            pltpu.VMEM((channels, rows), jnp.float32),
            pltpu.SemaphoreType.DMA,
            pltpu.SemaphoreType.DMA((2,)),
        ],
        compiler_params=params(mib),
        cost_estimate=cost(2 * channels * rows * rows, 2 * rows * rows),
    )(masks, x_t, tile)


def later_kernel(mask_ref, later_ref, tile_hbm, first_ref, out_ref, tile_ref, sems):
    rows = tile_ref.shape[0]
    copies = copies_of(tile_hbm, tile_ref, sems)
    for copy in copies:
        copy.start()
    mask = block_mask(mask_ref, 1, rows, tile_ref.dtype)
    for n, (start, size) in enumerate(halves(rows)):
        copies[n].wait()
        mask_rows(tile_ref, mask, start, size)
        for row, count in strips(size, 2 * SUBBLOCK):
            here = (slice(None), slice(start + row, start + row + count))
            out_ref[here] = first_ref[here] + dot(
                later_ref[...], tile_ref[start + row : start + row + count, :], ((1,), (1,))
            )


def later_product(masks, later, tile, first):
    channels, rows = later.shape
    return pl.pallas_call(
        later_kernel,
        in_specs=[WHOLE, WHOLE, ANYWHERE, WHOLE],
        out_specs=WHOLE,
        out_shape=jax.ShapeDtypeStruct((channels, rows), jnp.float32),
        scratch_shapes=[
            pltpu.VMEM((rows, rows), tile.dtype),
            pltpu.SemaphoreType.DMA((2,)),
        ],
        compiler_params=params(),
        cost_estimate=cost(2 * channels * rows * rows, 2 * rows * rows),
    )(masks, later, tile, first)


def lower_rows(channels):
    rows = round_up(channels, PANEL)
    return sum(rows - g * LANES for g in range(round_up(channels, LANES) // LANES))


def full_rows(channels):
    rows, wide = round_up(channels, PANEL), round_up(channels, LANES)
    whole = channels // LANES
    rest = rows - whole * LANES
    return round_up(whole * rows + rest * (wide // LANES), 4 * PANEL)


def lower_products(left_ref, right_ref, out_ref):
    channels = left_ref.shape[0]
    rows = round_up(channels, PANEL)
    offset = 0
    for start, size in strips(channels, 2 * LANES):
        product = dot(left_ref[start:channels, :], right_ref[start : start + size, :], ((1,), (1,)))
        for skip in range(0, size, LANES):
            width = min(LANES, size - skip)
            top = start + skip
            tall = rows - top
            if width < LANES:
                out_ref[offset : offset + tall, :] = jnp.zeros((tall, LANES), jnp.float32)
            elif rows > channels:
                out_ref[offset + channels - top : offset + tall, :] = jnp.zeros(
                    (rows - channels, LANES), jnp.float32
                )
            out_ref[offset : offset + channels - top, 0:width] = product[skip:, skip : skip + width]
            offset += tall


def full_products(left_ref, right_ref, out_ref):
    channels = left_ref.shape[0]
    rows = round_up(channels, PANEL)
    whole = channels // LANES
    for g in range(whole):
        out_ref[g * rows : g * rows + channels, :] = dot(
            left_ref[...], right_ref[g * LANES : (g + 1) * LANES, :], ((1,), (1,))
        )
        if rows > channels:
            out_ref[g * rows + channels : (g + 1) * rows, :] = jnp.zeros(
                (rows - channels, LANES), jnp.float32
            )
    base = whole * rows
    if base < out_ref.shape[0]:
        out_ref[base:, :] = jnp.zeros((out_ref.shape[0] - base, LANES), jnp.float32)
    first, rest = whole * LANES, rows - whole * LANES
    for n, (start, size) in enumerate(strips(channels, LANES) if first < channels else []):
        place = base + n * rest
        out_ref[place : place + channels - first, 0:size] = dot(
            right_ref[first:channels, :], left_ref[start : start + size, :], ((1,), (1,))
        )


def folded_rows(channels):
    if channels < 2 * LANES:
        return lower_rows(channels)
    return lower_rows(channels) - LANES + PANEL


def corner(channels):
    return round_up(channels, PANEL)


def square_index():
    row = lax.broadcasted_iota(jnp.int32, (LANES, LANES), 0)
    return row, lax.broadcasted_iota(jnp.int32, (LANES, LANES), 1)


def fold(pack_ref, out_ref, channels, symmetric):
    if channels < 2 * LANES:
        out_ref[...] = pack_ref[...]
        return
    start = corner(channels)
    end = pack_ref.shape[0]
    row, lane = square_index()
    second = pack_ref[start : start + LANES, :]
    upper = second if symmetric else second.T
    out_ref[0:LANES, :] = jnp.where(row >= lane, pack_ref[0:LANES, :], upper)
    out_ref[LANES:start, :] = pack_ref[LANES:start, :]
    out_ref[start : end - LANES, :] = pack_ref[start + LANES : end, :]
    diagonal = jnp.sum(jnp.where(row == lane, second, 0.0), axis=0, keepdims=True)
    out_ref[end - LANES :, :] = jnp.broadcast_to(diagonal, (PANEL, LANES))


def unfold(folded_ref, pack_ref, channels, symmetric):
    if channels < 2 * LANES:
        pack_ref[...] = folded_ref[...]
        return
    start = corner(channels)
    end = pack_ref.shape[0]
    row, lane = square_index()
    both = folded_ref[0:LANES, :]
    turned = both.T
    first_upper, second_upper = (turned, both) if symmetric else (0.0, 0.0)
    pack_ref[0:LANES, :] = jnp.where(row >= lane, both, first_upper)
    pack_ref[LANES:start, :] = folded_ref[LANES:start, :]
    second = jnp.where(row > lane, turned, second_upper)
    diagonal = folded_ref[end - LANES : end - LANES + 1, :]
    pack_ref[start : start + LANES, :] = jnp.where(row == lane, diagonal, second)
    pack_ref[start + LANES : end, :] = folded_ref[start : end - LANES, :]


def cut(pack_ref, core, mine_ref, other_ref):
    half = mine_ref.shape[0]
    mine_ref[...] = pack_ref[pl.ds(pl.multiple_of(core * half, 8), half), :].astype(mine_ref.dtype)
    other_ref[...] = pack_ref[pl.ds(pl.multiple_of((1 - core) * half, 8), half), :].astype(
        other_ref.dtype
    )


def join(pack_ref, core, mine, other):
    half = mine.shape[0]
    pack_ref[pl.ds(pl.multiple_of(core * half, 8), half), :] = mine
    pack_ref[pl.ds(pl.multiple_of((1 - core) * half, 8), half), :] = other


def gram_kernel(core_ref, part_ref, carried_ref, y_ref, g_mine, g_other, gram_ref, folded_ref):
    image = part_ref[...] + carried_ref[...].astype(jnp.float32)
    y_ref[...] = image.astype(y_ref.dtype)
    lower_products(y_ref, y_ref, gram_ref)
    fold(gram_ref, folded_ref, y_ref.shape[0], True)
    cut(folded_ref, core_ref[0], g_mine, g_other)


def gram(core, part, carried):
    channels, rows = carried.shape
    lower, folded = lower_rows(channels), folded_rows(channels)
    half = jax.ShapeDtypeStruct((folded // 2, LANES), jnp.float32)
    return pl.pallas_call(
        gram_kernel,
        in_specs=[SCALARS] + [WHOLE] * 2,
        out_specs=[WHOLE] * 3,
        out_shape=[jax.ShapeDtypeStruct((channels, rows), carried.dtype), half, half],
        scratch_shapes=[
            pltpu.VMEM((lower, LANES), jnp.float32),
            pltpu.VMEM((folded, LANES), jnp.float32),
        ],
        compiler_params=params(),
        cost_estimate=cost(2 * channels * channels * rows, 8 * channels * rows),
    )(core, part, carried)


def symmetric_matrix(pack_ref, out_ref):
    rows, wide = out_ref.shape
    offset = 0
    for top in range(0, wide, LANES):
        size = min(LANES, rows - top)
        column = pack_ref[offset : offset + rows - top, :]
        offset += rows - top
        out_ref[top:rows, top : top + LANES] = column
        for below in range(top + LANES, wide, LANES):
            count = min(LANES, rows - below)
            block = column[below - top : below - top + count, :]
            if count < LANES:
                block = jnp.concatenate(
                    [block, jnp.zeros((LANES - count, LANES), block.dtype)], axis=0
                )
            out_ref[top : top + size, below : below + LANES] = block.T


def ray_kernel(core_ref, x_ref, y_ref, after_ref, mine_ref, other_ref, pack_ref, folded_ref):
    lower_products(x_ref, y_ref, pack_ref)
    fold(pack_ref, folded_ref, x_ref.shape[0], True)
    cut(folded_ref, core_ref[0], mine_ref, other_ref)


def ray(core, x_t, y_t, after):
    channels, rows = x_t.shape
    lower, folded = lower_rows(channels), folded_rows(channels)
    return pl.pallas_call(
        ray_kernel,
        in_specs=[SCALARS, WHOLE, WHOLE, ANYWHERE],
        out_specs=[WHOLE] * 2,
        out_shape=[jax.ShapeDtypeStruct((folded // 2, LANES), jnp.bfloat16)] * 2,
        scratch_shapes=[
            pltpu.VMEM((lower, LANES), jnp.float32),
            pltpu.VMEM((folded, LANES), jnp.float32),
        ],
        compiler_params=params(),
        cost_estimate=cost(2 * channels * channels * rows, 4 * channels * rows),
    )(core, x_t, y_t, after)


def cross_kernel(core_ref, left_ref, right_ref, after_ref, mine_ref, other_ref, pack_ref):
    full_products(left_ref, right_ref, pack_ref)
    cut(pack_ref, core_ref[0], mine_ref, other_ref)


def cross(core, left, right, after, dtype):
    channels, rows = left.shape
    full = full_rows(channels)
    return pl.pallas_call(
        cross_kernel,
        in_specs=[SCALARS, WHOLE, WHOLE, ANYWHERE],
        out_specs=[WHOLE] * 2,
        out_shape=[jax.ShapeDtypeStruct((full // 2, LANES), dtype)] * 2,
        scratch_shapes=[pltpu.VMEM((full, LANES), jnp.float32)],
        compiler_params=params(),
        cost_estimate=cost(2 * channels * channels * rows, 4 * channels * rows),
    )(core, left, right, after)


def add_kernel(left_ref, right_ref, *refs):
    total = left_ref[...].astype(jnp.float32) + right_ref[...].astype(jnp.float32)
    refs[-1][...] = total.astype(refs[-1].dtype)


def add_four_kernel(own_ref, first_ref, second_ref, both_ref, after_ref, out_ref):
    own, first, second, both = (
        ref[...].astype(jnp.float32) for ref in (own_ref, first_ref, second_ref, both_ref)
    )
    out_ref[...] = ((own + first) + (second + both)).astype(out_ref.dtype)


def add_four(own, first, second, both, after):
    return pl.pallas_call(
        add_four_kernel,
        in_specs=[WHOLE] * 4 + [ANYWHERE],
        out_specs=WHOLE,
        out_shape=jax.ShapeDtypeStruct(own.shape, own.dtype),
        compiler_params=params(),
        cost_estimate=cost(10**5, 10**5),
    )(own, first, second, both, after)


def add_after(left, right, *after, flops=10**5):
    return pl.pallas_call(
        add_kernel,
        in_specs=[WHOLE] * 2 + [ANYWHERE] * len(after),
        out_specs=WHOLE,
        out_shape=jax.ShapeDtypeStruct(left.shape, left.dtype),
        compiler_params=params(),
        cost_estimate=cost(flops, 10**5),
    )(left, right, *after)


def split3(value):
    high = value.astype(jnp.bfloat16)
    rest = value - high.astype(jnp.float32)
    mid = rest.astype(jnp.bfloat16)
    low = (rest - mid.astype(jnp.float32)).astype(jnp.bfloat16)
    return high, mid, low


def sublane(value, index):
    return jnp.broadcast_to(value[index : index + 1, :], value.shape)


def lane_of(value, index):
    return jnp.take_along_axis(value, jnp.broadcast_to(index, value.shape), axis=1)


def eliminate(columns, panel):
    half = 8
    row = lax.broadcasted_iota(jnp.int32, (half, LANES), 0)
    scales = [jnp.zeros((half, LANES), jnp.float32) for _ in range(2)]
    columns = [list(c) for c in columns]
    panel = [list(p) for p in panel]
    for j in range(0, PANEL, 2):
        h, r = divmod(j, half)
        left, right = columns[j], columns[j + 1]
        a, b, c = sublane(left[h], r), sublane(left[h], r + 1), sublane(right[h], r + 1)
        det = a * c - b * b
        inverse = pl.reciprocal(det, approx=True)
        first, second = [None, None], [None, None]
        for t in range(h, 2):
            x, y = left[t], right[t]
            if t == h:
                x, y = jnp.where(row > r + 1, x, 0.0), jnp.where(row > r + 1, y, 0.0)
            first[t] = (c * x - b * y) * inverse
            second[t] = (a * y - b * x) * inverse
        for later in range(j + 2, PANEL):
            q = later // half
            x, y = sublane(left[q], later % half), sublane(right[q], later % half)
            for t in range(max(h, q), 2):
                columns[later][t] = columns[later][t] - (first[t] * x + second[t] * y)
        inverse_a = pl.reciprocal(a, approx=True)
        first[h] = jnp.where(row == r + 1, b * inverse_a, first[h])
        for group in panel:
            x, y = sublane(group[h], r), sublane(group[h], r + 1)
            for t in range(h, 2):
                group[t] = group[t] - (first[t] * x + second[t] * y)
        scales[h] = jnp.where(row == r, lax.rsqrt(a), scales[h])
        scales[h] = jnp.where(row == r + 1, lax.rsqrt(det * inverse_a), scales[h])
    return [jnp.concatenate([g[0] * scales[0], g[1] * scales[1]], axis=0) for g in panel]


def fill_work(channels, scale, pack_ref, work_ref):
    rows, wide = work_ref.shape
    groups = wide // LANES
    offset = 0
    for g in range(groups):
        top = g * LANES
        size = min(LANES, rows - top)
        column = pack_ref[offset : offset + rows - top, :] * scale
        offset += rows - top
        diag = column[0:size, :]
        if top + LANES > channels:
            row = lax.broadcasted_iota(jnp.int32, diag.shape, 0)
            lane = lax.broadcasted_iota(jnp.int32, diag.shape, 1)
            diag = jnp.where((row == lane) & (lane + top >= channels), 1.0, diag)
        work_ref[top : top + size, top : top + LANES] = diag
        for below in range(g + 1, groups):
            start = (below - g) * LANES
            size_b = min(LANES, rows - below * LANES)
            block = column[start : start + size_b, :]
            if size_b < LANES:
                block = jnp.concatenate(
                    [block, jnp.zeros((LANES - size_b, LANES), jnp.float32)], axis=0
                )
            work_ref[top : top + size, below * LANES : (below + 1) * LANES] = block.T
            work_ref[below * LANES : below * LANES + size_b, top : top + LANES] = jnp.zeros(
                (size_b, LANES), jnp.float32
            )


def eliminate_group(g, work_ref, turned_ref, first=0, last=LANES // PANEL):
    rows, wide = work_ref.shape
    groups = wide // LANES
    row = lax.broadcasted_iota(jnp.int32, (PANEL, LANES), 0)
    lane = lax.broadcasted_iota(jnp.int32, (PANEL, LANES), 1)
    top = g * LANES
    count = min(LANES, rows - top) // PANEL

    def load(local):
        place = pl.ds(pl.multiple_of(top + local, PANEL), PANEL)
        return [work_ref[place, q * LANES : (q + 1) * LANES] for q in range(groups)]

    def panel_step(b, parts, slot):
        local = b * PANEL
        following = jnp.minimum(local + PANEL, (count - 1) * PANEL)
        ahead = load(following)
        pivots = [parts[g][0:8, :], parts[g][8:16, :]]
        columns = [[lane_of(p, local + j) for p in pivots] for j in range(PANEL)]
        inside = (lane >= local) & (lane < local + PANEL)
        identity = jnp.where(lane - local == row, 1.0, 0.0)
        parts = list(parts)
        parts[g] = jnp.where(inside, identity, parts[g])
        done = eliminate(columns, [[p[0:8, :], p[8:16, :]] for p in parts])
        right = []
        for q in range(groups):
            high, mid, low = split3(done[q])
            right.append(jnp.concatenate([high, mid, high, low, mid, high], axis=0))
            if q >= g:
                if q == g:
                    high, mid, low = split3(jnp.where(lane >= local + PANEL, done[q], 0.0))
                left = jnp.concatenate([high, high, mid, high, mid, low], axis=0)
                turned_ref[slot, (q - g) * LANES : (q - g + 1) * LANES, :] = left.T
        right = jnp.concatenate(right, axis=1)
        near = turned_ref[slot, pl.ds(pl.multiple_of(following, PANEL), PANEL), :]
        update = dot(near, right, ((1,), (0,)))
        ahead[g] = jnp.where(inside, 0.0, ahead[g])
        ahead = [ahead[q] - update[:, q * LANES : (q + 1) * LANES] for q in range(groups)]
        for q in range(g, groups):
            low_row = q * LANES
            high_row = min(rows, low_row + LANES)
            base = low_row - top
            update = dot(turned_ref[slot, base : base + high_row - low_row, :], right, ((1,), (0,)))
            for c in range(groups):
                lanes = slice(c * LANES, (c + 1) * LANES)
                old = work_ref[low_row:high_row, lanes]
                if c == g:
                    here = lax.broadcasted_iota(jnp.int32, old.shape, 1)
                    old = jnp.where((here >= local) & (here < local + PANEL), 0.0, old)
                work_ref[low_row:high_row, lanes] = old - update[:, lanes]
        for q in range(groups):
            if q == g:
                done[q] = jnp.where(lane < local + PANEL, done[q], 0.0)
            elif q > g:
                done[q] = jnp.zeros_like(done[q])
            place = pl.ds(pl.multiple_of(top + local, PANEL), PANEL)
            work_ref[place, q * LANES : (q + 1) * LANES] = done[q]
        return ahead

    def two_panels(i, parts):
        return panel_step(first + 2 * i + 1, panel_step(first + 2 * i, parts, 0), 1)

    last = min(last, count)
    parts = lax.fori_loop(0, (last - first) // 2, two_panels, load(first * PANEL))
    if (last - first) % 2:
        panel_step(jnp.int32(last - 1), parts, 0)


def first_stage_kernel(
    channels, scale, core_ref, mine_ref, other_ref, work_ref, pack_ref, folded_ref, turned_ref
):
    join(folded_ref, core_ref[0], mine_ref[...], other_ref[...])
    unfold(folded_ref, pack_ref, channels, True)
    fill_work(channels, scale, pack_ref, work_ref)
    eliminate_group(0, work_ref, turned_ref)
    if work_ref.shape[1] > LANES:
        eliminate_group(1, work_ref, turned_ref, 0, EARLY_PANELS)


def last_stages_kernel(
    channels, before_ref, after_ref, work_ref, folded_ref, pack_ref, turned_ref
):
    work_ref[...] = before_ref[...]
    rows, wide = work_ref.shape
    for g in range(1 if EARLY_PANELS * PANEL < LANES else 2, wide // LANES):
        eliminate_group(g, work_ref, turned_ref, EARLY_PANELS if g == 1 else 0)
    offset = 0
    for q in range(wide // LANES):
        tall = rows - q * LANES
        pack_ref[offset : offset + tall, :] = work_ref[q * LANES : rows, q * LANES : (q + 1) * LANES]
        offset += tall
    fold(pack_ref, folded_ref, channels, False)


def turned_scratch(channels):
    return pltpu.VMEM((2, round_up(channels, LANES), 6 * PANEL), jnp.bfloat16)


def work_shape(channels):
    return jax.ShapeDtypeStruct((round_up(channels, PANEL), round_up(channels, LANES)), jnp.float32)


def first_stage(core, mine, other, channels, total_rows):
    return pl.pallas_call(
        functools.partial(first_stage_kernel, channels, 1.0 / total_rows),
        in_specs=[SCALARS] + [WHOLE] * 2,
        out_specs=WHOLE,
        out_shape=work_shape(channels),
        scratch_shapes=[
            pltpu.VMEM((lower_rows(channels), LANES), jnp.float32),
            pltpu.VMEM((folded_rows(channels), LANES), jnp.float32),
            turned_scratch(channels),
        ],
        compiler_params=params(),
        cost_estimate=cost(FIRST_STAGE_FLOPS, 10**6),
    )(core, mine, other)


def last_stages(work, channels, after):
    return pl.pallas_call(
        functools.partial(last_stages_kernel, channels),
        in_specs=[WHOLE, ANYWHERE],
        out_specs=[WHOLE] * 2,
        out_shape=[
            work_shape(channels),
            jax.ShapeDtypeStruct((folded_rows(channels), LANES), jnp.float32),
        ],
        scratch_shapes=[
            pltpu.VMEM((lower_rows(channels), LANES), jnp.float32),
            turned_scratch(channels),
        ],
        compiler_params=params(),
        cost_estimate=cost(LAST_STAGES_FLOPS, 10**5),
    )(work, after)


def split2(value):
    high = value.astype(jnp.bfloat16)
    return high, (value - high.astype(jnp.float32)).astype(jnp.bfloat16)


def dot3(left, right, dims):
    rows = left.shape[0]
    left_high, left_low = split2(left)
    right_high, right_low = split2(right)
    both = dot(jnp.concatenate([left_high, left_low], axis=0), right_high, dims)
    return both[0:rows, :] + both[rows:, :] + dot(left_high, right_low, dims)


def lower_matrix(pack_ref, out_ref):
    rows, wide = out_ref.shape
    offset = 0
    for g in range(wide // LANES):
        top = g * LANES
        lanes = slice(top, top + LANES)
        if top:
            out_ref[0:top, lanes] = jnp.zeros((top, LANES), jnp.float32)
        out_ref[top:rows, lanes] = pack_ref[offset : offset + rows - top, :]
        offset += rows - top


def basis_kernel(inverse_ref, y_ref, q_ref, token_ref):
    channels = y_ref.shape[0]
    image = y_ref[...]
    token_ref[...] = jnp.zeros_like(token_ref)
    for start, size in strips(channels, 2 * LANES):
        used = min(channels, start + size)
        high, low = split2(inverse_ref[start : start + size, 0:used])
        both = dot(jnp.concatenate([high, low], axis=0), image[0:used, :], ((1,), (0,)))
        q_ref[start : start + size, :] = (both[0:size, :] + both[size:, :]).astype(q_ref.dtype)


def basis(inverse, y_t):
    channels, rows = y_t.shape
    return pl.pallas_call(
        basis_kernel,
        in_specs=[WHOLE] * 2,
        out_specs=[WHOLE] * 2,
        out_shape=[
            jax.ShapeDtypeStruct(y_t.shape, y_t.dtype),
            jax.ShapeDtypeStruct((8, LANES), jnp.float32),
        ],
        compiler_params=params(),
        cost_estimate=cost(10**5, 10**5),
    )(inverse, y_t)


def matrix_shape(channels):
    return jax.ShapeDtypeStruct((channels, 1, channels), jnp.float32)


def turned_product(inverse_ref, pack_ref, channels):
    rows, wide = round_up(channels, PANEL), round_up(channels, LANES)
    whole = channels // LANES
    total = 0.0
    for g in range(whole):
        total += dot3(
            inverse_ref[:, g * LANES : (g + 1) * LANES],
            pack_ref[g * rows : (g + 1) * rows, :],
            ((1,), (1,)),
        )
    rest = rows - whole * LANES
    if rest:
        tail = jnp.concatenate(
            [
                pack_ref[whole * rows + n * rest : whole * rows + (n + 1) * rest, :]
                for n in range(wide // LANES)
            ],
            axis=1,
        )
        tail = jnp.concatenate([tail, jnp.zeros((LANES - rest, wide), tail.dtype)], axis=0)
        total += dot3(inverse_ref[:, whole * LANES : wide], tail[:, 0:rows], ((1,), (0,)))
    return total


def part_kernel(
    channels, scale, core_ref, mine_ref, inverse_ref, previous_ref, out_ref,
    pack_ref, lower_ref, before_ref,
):
    rows, wide = inverse_ref.shape
    half = mine_ref.shape[0]
    join(pack_ref, core_ref[0], mine_ref[...], jnp.zeros((half, LANES), jnp.float32))
    turned = turned_product(inverse_ref, pack_ref, channels)
    unfold(previous_ref, lower_ref, channels, False)
    lower_matrix(lower_ref, before_ref)
    total = dot3(before_ref[:, 0:rows], turned, ((1,), (1,))) * scale
    out_ref[:, 0:rows] = total.astype(out_ref.dtype)
    if rows < wide:
        out_ref[:, rows:wide] = jnp.zeros((rows, wide - rows), out_ref.dtype)


def correlation_part(core, mine, inverse, previous, channels, total_rows):
    return pl.pallas_call(
        functools.partial(part_kernel, channels, 1.0 / total_rows),
        in_specs=[SCALARS] + [WHOLE] * 3,
        out_specs=WHOLE,
        out_shape=jax.ShapeDtypeStruct(inverse.shape, jnp.bfloat16),
        scratch_shapes=[
            pltpu.VMEM((full_rows(channels), LANES), jnp.float32),
            pltpu.VMEM((lower_rows(channels), LANES), jnp.float32),
            pltpu.VMEM(inverse.shape, jnp.float32),
        ],
        compiler_params=params(),
        cost_estimate=cost(10**5, 10**5),
    )(core, mine, inverse, previous)


def both_kernel(
    scale, core_ref, left_ref, right_ref, mine_ref, other_ref, out_ref, ray_ref,
    folded_ref, pack_ref, full_ref,
):
    channels = out_ref.shape[0]
    mine, other = mine_ref[...].astype(jnp.float32), other_ref[...].astype(jnp.float32)
    join(folded_ref, core_ref[0], mine, other)
    unfold(folded_ref, pack_ref, channels, True)
    symmetric_matrix(pack_ref, full_ref)
    ray_ref[:, 0, :] = full_ref[0:channels, 0:channels] * scale
    total = left_ref[...].astype(jnp.float32) + right_ref[...].astype(jnp.float32)
    out_ref[:, 0, :] = total[0:channels, 0:channels]


def both_parts(core, left, right, mine, other, channels, total_rows):
    return pl.pallas_call(
        functools.partial(both_kernel, 1.0 / total_rows),
        in_specs=[SCALARS] + [WHOLE] * 4,
        out_specs=[WHOLE] * 2,
        out_shape=[matrix_shape(channels)] * 2,
        scratch_shapes=[
            pltpu.VMEM((folded_rows(channels), LANES), jnp.float32),
            pltpu.VMEM((lower_rows(channels), LANES), jnp.float32),
            pltpu.VMEM((round_up(channels, PANEL), round_up(channels, LANES)), jnp.float32),
        ],
        compiler_params=params(),
        cost_estimate=cost(10**5, 10**5),
    )(core, left, right, mine, other)


def from_behind(value, axis, steps):
    count = lax.axis_size(axis)
    leading, last = (max(0, -steps), min(count, count - steps))
    return lax.ppermute(value, axis, [(source, source + steps) for source in range(leading, last)])


def other_core(value):
    return lax.ppermute(value, "rows", [(s, s ^ 1) for s in range(lax.axis_size("rows"))])


def chip_rounds():
    count = lax.axis_size("rows")
    bits = []
    while 2 << len(bits) < count:
        bits.append(2 << len(bits))
    return [
        [(s, s ^ (bits[n] if s % 2 == 0 else bits[-1 - n])) for s in range(count)]
        for n in range(len(bits))
    ]


def sum_chips(value, after):
    count = lax.axis_size("rows")
    if count == 8:
        first, second, both = [
            lax.ppermute(value, "rows", [(s, s ^ bits) for s in range(count)]) for bits in (2, 4, 6)
        ]
        return add_four(value, first, second, both, after)
    for pairs in chip_rounds():
        value = add_after(value, lax.ppermute(value, "rows", pairs), after)
    return value


def shards(x_block, h_diag, h_right, pattern):
    x_t = x_block[0].T
    channels, block_rows = x_t.shape
    masks = pattern[0].transpose(1, 0, 2)
    total_rows = lax.axis_size("rows") * block_rows
    core = (lax.axis_index("rows") % 2).astype(jnp.int32).reshape(1)
    later = from_behind(x_t, "rows", -1)
    carried = from_behind(tile_product(1, masks, x_t, h_right[0], x_t.dtype, 53, True), "rows", 1)
    first = tile_product(0, masks, x_t, h_diag[0], jnp.float32, 50, False)
    part = later_product(masks, later, h_right[0], first)
    y_t, g_mine, g_other = gram(core, part, carried)
    previous_y = from_behind(y_t, "sector", 1)
    rounds = chip_rounds()
    g_sum = g_mine + other_core(g_other)
    r_mine, r_other = ray(core, x_t, y_t, g_sum)
    r_sum = add_after(r_mine, other_core(r_other))
    g_sum = sum_chips(g_sum, r_sum)
    r_first = lax.ppermute(r_sum, "rows", rounds[0])
    work = first_stage(core, g_sum, other_core(g_sum), channels, total_rows)
    r_sum = add_after(r_sum, r_first, work)
    m_mine, m_other = cross(core, previous_y, y_t, r_sum, jnp.float32)
    inverse, pack = last_stages(work, channels, m_other)
    m_sum = add_after(m_mine, other_core(m_other), inverse)
    previous = from_behind(pack, "sector", 1)
    q_t, basis_token = basis(inverse, y_t)
    for pairs in rounds[:-1]:
        m_sum = add_after(m_sum, lax.ppermute(m_sum, "rows", pairs))
    m_sum = add_after(m_sum, lax.ppermute(m_sum, "rows", rounds[-1]), basis_token)
    part = correlation_part(core, m_sum, inverse, previous, channels, total_rows)
    for pairs in rounds[1:]:
        r_sum = add_after(r_sum, lax.ppermute(r_sum, "rows", pairs), flops=LAST_RAY_FLOPS)
    correlation, rayleigh = both_parts(
        core, part, other_core(part), r_sum, other_core(r_sum), channels, total_rows
    )
    return (q_t.T[None], rayleigh.transpose(1, 0, 2), correlation.transpose(1, 0, 2))


def solution(mesh):
    in_specs = (
        P("sector", "rows", None),
        P("sector", "rows", None),
        P("sector", "rows", None),
        P("sector", None, "rows", None),
    )
    out_specs = (P("sector", "rows", None), P("sector", None, None), P("sector", None, None))
    return jax.shard_map(shards, mesh=mesh, in_specs=in_specs, out_specs=out_specs, check_vma=False)
```

```python
import functools

import jax
import jax.numpy as jnp
from jax import lax
from jax.experimental import pallas as pl
from jax.experimental.pallas import tpu as pltpu
from jax.sharding import PartitionSpec as P

SUBBLOCK = 128
LANES = 128
PANEL = 16
EARLY_PANELS = 7
WHOLE = pl.BlockSpec(memory_space=pltpu.VMEM)
SCALARS = pl.BlockSpec(memory_space=pltpu.SMEM)
ANYWHERE = pl.BlockSpec(memory_space=pl.ANY)
MIB = 1024 * 1024
FIRST_STAGE_FLOPS = 5000 * 10**6
LAST_RAY_FLOPS = 3000 * 10**6
LAST_STAGES_FLOPS = 4000 * 10**6


def params(mib=48):
    return pltpu.CompilerParams(vmem_limit_bytes=mib * MIB)


def cost(flops, bytes_accessed):
    return pl.CostEstimate(flops=flops, bytes_accessed=bytes_accessed, transcendentals=0)


def round_up(value, step):
    return (value + step - 1) // step * step


def dot(left, right, dims, precision=None):
    return lax.dot_general(
        left, right, (dims, ((), ())), precision=precision, preferred_element_type=jnp.float32
    )


def block_mask(mask_ref, which, cols, dtype):
    blocks = mask_ref[:, which, :].astype(jnp.float32)
    col = lax.broadcasted_iota(jnp.int32, (blocks.shape[1], cols), 1)
    block = lax.broadcasted_iota(jnp.int32, (blocks.shape[1], cols), 0)
    wide = dot(blocks, jnp.where(col // SUBBLOCK == block, 1.0, 0.0), ((1,), (0,)))
    return [
        jnp.broadcast_to(wide[i : i + 1, :], (PANEL, cols)).astype(dtype)
        for i in range(blocks.shape[0])
    ]


def mask_rows(tile_ref, mask, start, size):
    for i in range(start // SUBBLOCK, (start + size) // SUBBLOCK):
        for row in range(i * SUBBLOCK, (i + 1) * SUBBLOCK, PANEL):
            tile_ref[row : row + PANEL, :] = tile_ref[row : row + PANEL, :] * mask[i]


def strips(rows, width):
    return [(start, min(width, rows - start)) for start in range(0, rows, width)]


def halves(rows):
    first = rows // 512 * 256
    return [(0, first), (first, rows - first)] if first else [(0, rows)]


def copies_of(source, target, sems):
    copies = []
    for n, (start, size) in enumerate(halves(target.shape[0])):
        here = (pl.ds(start, size), slice(None))
        copies.append(pltpu.make_async_copy(source.at[here], target.at[here], sems.at[n]))
    return copies


def product(x_ref, tile_ref, copies, in_turn, mask, sum_ref, out_ref):
    rows = tile_ref.shape[0]
    for n, (start, size) in enumerate(halves(rows)):
        copies[n].wait()
        if in_turn and n + 1 < len(copies):
            copies[n + 1].start()
        mask_rows(tile_ref, mask, start, size)
        last = n + 1 == len(copies)
        for col, cols in strips(rows, 2 * SUBBLOCK):
            here = (slice(None), slice(col, col + cols))
            term = dot(
                x_ref[:, start : start + size],
                tile_ref[start : start + size, col : col + cols],
                ((1,), (0,)),
            )
            if n > 0:
                term = sum_ref[here] + term
            if last:
                out_ref[here] = term.astype(out_ref.dtype)
            else:
                sum_ref[here] = term


def tile_kernel(which, in_turn, mask_ref, x_hbm, tile_hbm, out_ref, x_ref, tile_ref, sum_ref, x_sem, sems):
    rows = tile_ref.shape[0]
    copies = copies_of(tile_hbm, tile_ref, sems)
    copy_x = pltpu.make_async_copy(x_hbm, x_ref, x_sem)
    copy_x.start()
    for copy in copies[:1] if in_turn else copies:
        copy.start()
    mask = block_mask(mask_ref, which, rows, tile_ref.dtype)
    copy_x.wait()
    product(x_ref, tile_ref, copies, in_turn, mask, sum_ref, out_ref)


def tile_product(which, masks, x_t, tile, dtype, mib, in_turn):
    channels, rows = x_t.shape
    return pl.pallas_call(
        functools.partial(tile_kernel, which, in_turn),
        in_specs=[WHOLE, ANYWHERE, ANYWHERE],
        out_specs=WHOLE,
        out_shape=jax.ShapeDtypeStruct((channels, rows), dtype),
        scratch_shapes=[
            pltpu.VMEM((channels, rows), x_t.dtype),
            pltpu.VMEM((rows, rows), tile.dtype),
            pltpu.VMEM((channels, rows), jnp.float32),
            pltpu.SemaphoreType.DMA,
            pltpu.SemaphoreType.DMA((2,)),
        ],
        compiler_params=params(mib),
        cost_estimate=cost(2 * channels * rows * rows, 2 * rows * rows),
    )(masks, x_t, tile)


def later_kernel(mask_ref, later_ref, tile_hbm, first_ref, out_ref, tile_ref, sems):
    rows = tile_ref.shape[0]
    copies = copies_of(tile_hbm, tile_ref, sems)
    for copy in copies:
        copy.start()
    mask = block_mask(mask_ref, 1, rows, tile_ref.dtype)
    for n, (start, size) in enumerate(halves(rows)):
        copies[n].wait()
        mask_rows(tile_ref, mask, start, size)
        for row, count in strips(size, 2 * SUBBLOCK):
            here = (slice(None), slice(start + row, start + row + count))
            out_ref[here] = first_ref[here] + dot(
                later_ref[...], tile_ref[start + row : start + row + count, :], ((1,), (1,))
            )


def later_product(masks, later, tile, first):
    channels, rows = later.shape
    return pl.pallas_call(
        later_kernel,
        in_specs=[WHOLE, WHOLE, ANYWHERE, WHOLE],
        out_specs=WHOLE,
        out_shape=jax.ShapeDtypeStruct((channels, rows), jnp.float32),
        scratch_shapes=[
            pltpu.VMEM((rows, rows), tile.dtype),
            pltpu.SemaphoreType.DMA((2,)),
        ],
        compiler_params=params(),
        cost_estimate=cost(2 * channels * rows * rows, 2 * rows * rows),
    )(masks, later, tile, first)


def lower_rows(channels):
    rows = round_up(channels, PANEL)
    return sum(rows - g * LANES for g in range(round_up(channels, LANES) // LANES))


def full_rows(channels):
    rows, wide = round_up(channels, PANEL), round_up(channels, LANES)
    whole = channels // LANES
    rest = rows - whole * LANES
    return round_up(whole * rows + rest * (wide // LANES), 4 * PANEL)


def lower_products(left_ref, right_ref, out_ref):
    channels = left_ref.shape[0]
    rows = round_up(channels, PANEL)
    offset = 0
    for start, size in strips(channels, 2 * LANES):
        product = dot(left_ref[start:channels, :], right_ref[start : start + size, :], ((1,), (1,)))
        for skip in range(0, size, LANES):
            width = min(LANES, size - skip)
            top = start + skip
            tall = rows - top
            if width < LANES:
                out_ref[offset : offset + tall, :] = jnp.zeros((tall, LANES), jnp.float32)
            elif rows > channels:
                out_ref[offset + channels - top : offset + tall, :] = jnp.zeros(
                    (rows - channels, LANES), jnp.float32
                )
            out_ref[offset : offset + channels - top, 0:width] = product[skip:, skip : skip + width]
            offset += tall


def full_products(left_ref, right_ref, out_ref):
    channels = left_ref.shape[0]
    rows = round_up(channels, PANEL)
    whole = channels // LANES
    for g in range(whole):
        out_ref[g * rows : g * rows + channels, :] = dot(
            left_ref[...], right_ref[g * LANES : (g + 1) * LANES, :], ((1,), (1,))
        )
        if rows > channels:
            out_ref[g * rows + channels : (g + 1) * rows, :] = jnp.zeros(
                (rows - channels, LANES), jnp.float32
            )
    base = whole * rows
    if base < out_ref.shape[0]:
        out_ref[base:, :] = jnp.zeros((out_ref.shape[0] - base, LANES), jnp.float32)
    first, rest = whole * LANES, rows - whole * LANES
    for n, (start, size) in enumerate(strips(channels, LANES) if first < channels else []):
        place = base + n * rest
        out_ref[place : place + channels - first, 0:size] = dot(
            right_ref[first:channels, :], left_ref[start : start + size, :], ((1,), (1,))
        )


def full_matrix(pack_ref, channels):
    rows, wide = round_up(channels, PANEL), round_up(channels, LANES)
    whole = channels // LANES
    rest = rows - whole * LANES
    parts = [pack_ref[g * rows : (g + 1) * rows, :] for g in range(whole)]
    if rest:
        tail = jnp.concatenate(
            [
                pack_ref[whole * rows + g * rest : whole * rows + (g + 1) * rest, :]
                for g in range(wide // LANES)
            ],
            axis=1,
        )
        tail = jnp.concatenate([tail, jnp.zeros((LANES - rest, wide), tail.dtype)], axis=0)
        parts.append(tail.T[0:rows, :])
    return jnp.concatenate(parts, axis=1)


def folded_rows(channels):
    if channels < 2 * LANES:
        return lower_rows(channels)
    return lower_rows(channels) - LANES + PANEL


def corner(channels):
    return round_up(channels, PANEL)


def square_index():
    row = lax.broadcasted_iota(jnp.int32, (LANES, LANES), 0)
    return row, lax.broadcasted_iota(jnp.int32, (LANES, LANES), 1)


def fold(pack_ref, out_ref, channels, symmetric):
    if channels < 2 * LANES:
        out_ref[...] = pack_ref[...]
        return
    start = corner(channels)
    end = pack_ref.shape[0]
    row, lane = square_index()
    second = pack_ref[start : start + LANES, :]
    upper = second if symmetric else second.T
    out_ref[0:LANES, :] = jnp.where(row >= lane, pack_ref[0:LANES, :], upper)
    out_ref[LANES:start, :] = pack_ref[LANES:start, :]
    out_ref[start : end - LANES, :] = pack_ref[start + LANES : end, :]
    diagonal = jnp.sum(jnp.where(row == lane, second, 0.0), axis=0, keepdims=True)
    out_ref[end - LANES :, :] = jnp.broadcast_to(diagonal, (PANEL, LANES))


def unfold(folded_ref, pack_ref, channels, symmetric):
    if channels < 2 * LANES:
        pack_ref[...] = folded_ref[...]
        return
    start = corner(channels)
    end = pack_ref.shape[0]
    row, lane = square_index()
    both = folded_ref[0:LANES, :]
    turned = both.T
    first_upper, second_upper = (turned, both) if symmetric else (0.0, 0.0)
    pack_ref[0:LANES, :] = jnp.where(row >= lane, both, first_upper)
    pack_ref[LANES:start, :] = folded_ref[LANES:start, :]
    second = jnp.where(row > lane, turned, second_upper)
    diagonal = folded_ref[end - LANES : end - LANES + 1, :]
    pack_ref[start : start + LANES, :] = jnp.where(row == lane, diagonal, second)
    pack_ref[start + LANES : end, :] = folded_ref[start : end - LANES, :]


def cut(pack_ref, core, mine_ref, other_ref):
    half = mine_ref.shape[0]
    mine_ref[...] = pack_ref[pl.ds(pl.multiple_of(core * half, 8), half), :].astype(mine_ref.dtype)
    other_ref[...] = pack_ref[pl.ds(pl.multiple_of((1 - core) * half, 8), half), :].astype(
        other_ref.dtype
    )


def join(pack_ref, core, mine, other):
    half = mine.shape[0]
    pack_ref[pl.ds(pl.multiple_of(core * half, 8), half), :] = mine
    pack_ref[pl.ds(pl.multiple_of((1 - core) * half, 8), half), :] = other


def gram_kernel(core_ref, part_ref, carried_ref, y_ref, g_mine, g_other, gram_ref, folded_ref):
    image = part_ref[...] + carried_ref[...].astype(jnp.float32)
    y_ref[...] = image.astype(y_ref.dtype)
    lower_products(y_ref, y_ref, gram_ref)
    fold(gram_ref, folded_ref, y_ref.shape[0], True)
    cut(folded_ref, core_ref[0], g_mine, g_other)


def gram(core, part, carried):
    channels, rows = carried.shape
    lower, folded = lower_rows(channels), folded_rows(channels)
    half = jax.ShapeDtypeStruct((folded // 2, LANES), jnp.float32)
    return pl.pallas_call(
        gram_kernel,
        in_specs=[SCALARS] + [WHOLE] * 2,
        out_specs=[WHOLE] * 3,
        out_shape=[jax.ShapeDtypeStruct((channels, rows), carried.dtype), half, half],
        scratch_shapes=[
            pltpu.VMEM((lower, LANES), jnp.float32),
            pltpu.VMEM((folded, LANES), jnp.float32),
        ],
        compiler_params=params(),
        cost_estimate=cost(2 * channels * channels * rows, 8 * channels * rows),
    )(core, part, carried)


def symmetric_matrix(pack_ref, out_ref):
    rows, wide = out_ref.shape
    offset = 0
    for top in range(0, wide, LANES):
        size = min(LANES, rows - top)
        column = pack_ref[offset : offset + rows - top, :]
        offset += rows - top
        out_ref[top:rows, top : top + LANES] = column
        for below in range(top + LANES, wide, LANES):
            count = min(LANES, rows - below)
            block = column[below - top : below - top + count, :]
            if count < LANES:
                block = jnp.concatenate(
                    [block, jnp.zeros((LANES - count, LANES), block.dtype)], axis=0
                )
            out_ref[top : top + size, below : below + LANES] = block.T


def ray_kernel(core_ref, x_ref, y_ref, after_ref, mine_ref, other_ref, pack_ref, folded_ref):
    lower_products(x_ref, y_ref, pack_ref)
    fold(pack_ref, folded_ref, x_ref.shape[0], True)
    cut(folded_ref, core_ref[0], mine_ref, other_ref)


def ray(core, x_t, y_t, after):
    channels, rows = x_t.shape
    lower, folded = lower_rows(channels), folded_rows(channels)
    return pl.pallas_call(
        ray_kernel,
        in_specs=[SCALARS, WHOLE, WHOLE, ANYWHERE],
        out_specs=[WHOLE] * 2,
        out_shape=[jax.ShapeDtypeStruct((folded // 2, LANES), jnp.bfloat16)] * 2,
        scratch_shapes=[
            pltpu.VMEM((lower, LANES), jnp.float32),
            pltpu.VMEM((folded, LANES), jnp.float32),
        ],
        compiler_params=params(),
        cost_estimate=cost(2 * channels * channels * rows, 4 * channels * rows),
    )(core, x_t, y_t, after)


def cross_kernel(core_ref, left_ref, right_ref, after_ref, mine_ref, other_ref, pack_ref):
    full_products(left_ref, right_ref, pack_ref)
    cut(pack_ref, core_ref[0], mine_ref, other_ref)


def cross(core, left, right, after, dtype):
    channels, rows = left.shape
    full = full_rows(channels)
    return pl.pallas_call(
        cross_kernel,
        in_specs=[SCALARS, WHOLE, WHOLE, ANYWHERE],
        out_specs=[WHOLE] * 2,
        out_shape=[jax.ShapeDtypeStruct((full // 2, LANES), dtype)] * 2,
        scratch_shapes=[pltpu.VMEM((full, LANES), jnp.float32)],
        compiler_params=params(),
        cost_estimate=cost(2 * channels * channels * rows, 4 * channels * rows),
    )(core, left, right, after)


def add_kernel(left_ref, right_ref, *refs):
    total = left_ref[...].astype(jnp.float32) + right_ref[...].astype(jnp.float32)
    refs[-1][...] = total.astype(refs[-1].dtype)


def add_four_kernel(both_ref, own_ref, first_ref, second_ref, after_ref, out_ref):
    both, own, first, second = (
        ref[...].astype(jnp.float32) for ref in (both_ref, own_ref, first_ref, second_ref)
    )
    out_ref[...] = ((own + first) + (second + both)).astype(out_ref.dtype)


def add_four(both, own, first, second, after):
    return pl.pallas_call(
        add_four_kernel,
        in_specs=[WHOLE] * 4 + [ANYWHERE],
        out_specs=WHOLE,
        out_shape=jax.ShapeDtypeStruct(own.shape, own.dtype),
        compiler_params=params(),
        cost_estimate=cost(10**5, 10**5),
    )(both, own, first, second, after)


def add_after(left, right, *after, flops=10**5):
    return pl.pallas_call(
        add_kernel,
        in_specs=[WHOLE] * 2 + [ANYWHERE] * len(after),
        out_specs=WHOLE,
        out_shape=jax.ShapeDtypeStruct(left.shape, left.dtype),
        compiler_params=params(),
        cost_estimate=cost(flops, 10**5),
    )(left, right, *after)


def split3(value):
    high = value.astype(jnp.bfloat16)
    rest = value - high.astype(jnp.float32)
    mid = rest.astype(jnp.bfloat16)
    low = (rest - mid.astype(jnp.float32)).astype(jnp.bfloat16)
    return high, mid, low


def sublane(value, index):
    return jnp.broadcast_to(value[index : index + 1, :], value.shape)


def lane_of(value, index):
    return jnp.take_along_axis(value, jnp.broadcast_to(index, value.shape), axis=1)


def eliminate(columns, panel):
    half = 8
    row = lax.broadcasted_iota(jnp.int32, (half, LANES), 0)
    scales = [jnp.zeros((half, LANES), jnp.float32) for _ in range(2)]
    columns = [list(c) for c in columns]
    panel = [list(p) for p in panel]
    for j in range(0, PANEL, 2):
        h, r = divmod(j, half)
        left, right = columns[j], columns[j + 1]
        a, b, c = sublane(left[h], r), sublane(left[h], r + 1), sublane(right[h], r + 1)
        det = a * c - b * b
        inverse = pl.reciprocal(det, approx=True)
        first, second = [None, None], [None, None]
        for t in range(h, 2):
            x, y = left[t], right[t]
            if t == h:
                x, y = jnp.where(row > r + 1, x, 0.0), jnp.where(row > r + 1, y, 0.0)
            first[t] = (c * x - b * y) * inverse
            second[t] = (a * y - b * x) * inverse
        for later in range(j + 2, PANEL):
            q = later // half
            x, y = sublane(left[q], later % half), sublane(right[q], later % half)
            for t in range(max(h, q), 2):
                columns[later][t] = columns[later][t] - (first[t] * x + second[t] * y)
        inverse_a = pl.reciprocal(a, approx=True)
        first[h] = jnp.where(row == r + 1, b * inverse_a, first[h])
        for group in panel:
            x, y = sublane(group[h], r), sublane(group[h], r + 1)
            for t in range(h, 2):
                group[t] = group[t] - (first[t] * x + second[t] * y)
        scales[h] = jnp.where(row == r, lax.rsqrt(a), scales[h])
        scales[h] = jnp.where(row == r + 1, lax.rsqrt(det * inverse_a), scales[h])
    return [jnp.concatenate([g[0] * scales[0], g[1] * scales[1]], axis=0) for g in panel]


def fill_work(channels, scale, pack_ref, work_ref):
    rows, wide = work_ref.shape
    groups = wide // LANES
    offset = 0
    for g in range(groups):
        top = g * LANES
        size = min(LANES, rows - top)
        column = pack_ref[offset : offset + rows - top, :] * scale
        offset += rows - top
        diag = column[0:size, :]
        if top + LANES > channels:
            row = lax.broadcasted_iota(jnp.int32, diag.shape, 0)
            lane = lax.broadcasted_iota(jnp.int32, diag.shape, 1)
            diag = jnp.where((row == lane) & (lane + top >= channels), 1.0, diag)
        work_ref[top : top + size, top : top + LANES] = diag
        for below in range(g + 1, groups):
            start = (below - g) * LANES
            size_b = min(LANES, rows - below * LANES)
            block = column[start : start + size_b, :]
            if size_b < LANES:
                block = jnp.concatenate(
                    [block, jnp.zeros((LANES - size_b, LANES), jnp.float32)], axis=0
                )
            work_ref[top : top + size, below * LANES : (below + 1) * LANES] = block.T
            work_ref[below * LANES : below * LANES + size_b, top : top + LANES] = jnp.zeros(
                (size_b, LANES), jnp.float32
            )


def eliminate_group(g, work_ref, turned_ref, first=0, last=LANES // PANEL):
    rows, wide = work_ref.shape
    groups = wide // LANES
    row = lax.broadcasted_iota(jnp.int32, (PANEL, LANES), 0)
    lane = lax.broadcasted_iota(jnp.int32, (PANEL, LANES), 1)
    top = g * LANES
    count = min(LANES, rows - top) // PANEL

    def load(local):
        place = pl.ds(pl.multiple_of(top + local, PANEL), PANEL)
        return [work_ref[place, q * LANES : (q + 1) * LANES] for q in range(groups)]

    def panel_step(b, parts, slot):
        local = b * PANEL
        following = jnp.minimum(local + PANEL, (count - 1) * PANEL)
        ahead = load(following)
        pivots = [parts[g][0:8, :], parts[g][8:16, :]]
        columns = [[lane_of(p, local + j) for p in pivots] for j in range(PANEL)]
        inside = (lane >= local) & (lane < local + PANEL)
        identity = jnp.where(lane - local == row, 1.0, 0.0)
        parts = list(parts)
        parts[g] = jnp.where(inside, identity, parts[g])
        done = eliminate(columns, [[p[0:8, :], p[8:16, :]] for p in parts])
        right = []
        for q in range(groups):
            high, mid, low = split3(done[q])
            right.append(jnp.concatenate([high, mid, high, low, mid, high], axis=0))
            if q >= g:
                if q == g:
                    high, mid, low = split3(jnp.where(lane >= local + PANEL, done[q], 0.0))
                left = jnp.concatenate([high, high, mid, high, mid, low], axis=0)
                turned_ref[slot, (q - g) * LANES : (q - g + 1) * LANES, :] = left.T
        right = jnp.concatenate(right, axis=1)
        near = turned_ref[slot, pl.ds(pl.multiple_of(following, PANEL), PANEL), :]
        update = dot(near, right, ((1,), (0,)))
        ahead[g] = jnp.where(inside, 0.0, ahead[g])
        ahead = [ahead[q] - update[:, q * LANES : (q + 1) * LANES] for q in range(groups)]
        for q in range(g, groups):
            low_row = q * LANES
            high_row = min(rows, low_row + LANES)
            base = low_row - top
            update = dot(turned_ref[slot, base : base + high_row - low_row, :], right, ((1,), (0,)))
            for c in range(groups):
                lanes = slice(c * LANES, (c + 1) * LANES)
                old = work_ref[low_row:high_row, lanes]
                if c == g:
                    here = lax.broadcasted_iota(jnp.int32, old.shape, 1)
                    old = jnp.where((here >= local) & (here < local + PANEL), 0.0, old)
                work_ref[low_row:high_row, lanes] = old - update[:, lanes]
        for q in range(groups):
            if q == g:
                done[q] = jnp.where(lane < local + PANEL, done[q], 0.0)
            elif q > g:
                done[q] = jnp.zeros_like(done[q])
            place = pl.ds(pl.multiple_of(top + local, PANEL), PANEL)
            work_ref[place, q * LANES : (q + 1) * LANES] = done[q]
        return ahead

    def two_panels(i, parts):
        return panel_step(first + 2 * i + 1, panel_step(first + 2 * i, parts, 0), 1)

    last = min(last, count)
    parts = lax.fori_loop(0, (last - first) // 2, two_panels, load(first * PANEL))
    if (last - first) % 2:
        panel_step(jnp.int32(last - 1), parts, 0)


def first_stage_kernel(
    channels, scale, core_ref, mine_ref, other_ref, work_ref, pack_ref, folded_ref, turned_ref
):
    join(folded_ref, core_ref[0], mine_ref[...], other_ref[...])
    unfold(folded_ref, pack_ref, channels, True)
    fill_work(channels, scale, pack_ref, work_ref)
    eliminate_group(0, work_ref, turned_ref)
    if work_ref.shape[1] > LANES:
        eliminate_group(1, work_ref, turned_ref, 0, EARLY_PANELS)


def last_stages_kernel(
    channels, before_ref, after_ref, work_ref, folded_ref, pack_ref, turned_ref
):
    work_ref[...] = before_ref[...]
    rows, wide = work_ref.shape
    for g in range(1 if EARLY_PANELS * PANEL < LANES else 2, wide // LANES):
        eliminate_group(g, work_ref, turned_ref, EARLY_PANELS if g == 1 else 0)
    offset = 0
    for q in range(wide // LANES):
        tall = rows - q * LANES
        pack_ref[offset : offset + tall, :] = work_ref[q * LANES : rows, q * LANES : (q + 1) * LANES]
        offset += tall
    fold(pack_ref, folded_ref, channels, False)


def turned_scratch(channels):
    return pltpu.VMEM((2, round_up(channels, LANES), 6 * PANEL), jnp.bfloat16)


def work_shape(channels):
    return jax.ShapeDtypeStruct((round_up(channels, PANEL), round_up(channels, LANES)), jnp.float32)


def first_stage(core, mine, other, channels, total_rows):
    return pl.pallas_call(
        functools.partial(first_stage_kernel, channels, 1.0 / total_rows),
        in_specs=[SCALARS] + [WHOLE] * 2,
        out_specs=WHOLE,
        out_shape=work_shape(channels),
        scratch_shapes=[
            pltpu.VMEM((lower_rows(channels), LANES), jnp.float32),
            pltpu.VMEM((folded_rows(channels), LANES), jnp.float32),
            turned_scratch(channels),
        ],
        compiler_params=params(),
        cost_estimate=cost(FIRST_STAGE_FLOPS, 10**6),
    )(core, mine, other)


def last_stages(work, channels, after):
    return pl.pallas_call(
        functools.partial(last_stages_kernel, channels),
        in_specs=[WHOLE, ANYWHERE],
        out_specs=[WHOLE] * 2,
        out_shape=[
            work_shape(channels),
            jax.ShapeDtypeStruct((folded_rows(channels), LANES), jnp.float32),
        ],
        scratch_shapes=[
            pltpu.VMEM((lower_rows(channels), LANES), jnp.float32),
            turned_scratch(channels),
        ],
        compiler_params=params(),
        cost_estimate=cost(LAST_STAGES_FLOPS, 10**5),
    )(work, after)


def split2(value):
    high = value.astype(jnp.bfloat16)
    return high, (value - high.astype(jnp.float32)).astype(jnp.bfloat16)


def dot3(left, right, dims):
    rows = left.shape[0]
    left_high, left_low = split2(left)
    right_high, right_low = split2(right)
    both = dot(jnp.concatenate([left_high, left_low], axis=0), right_high, dims)
    return both[0:rows, :] + both[rows:, :] + dot(left_high, right_low, dims)


def lower_matrix(pack_ref, out_ref):
    rows, wide = out_ref.shape
    offset = 0
    for g in range(wide // LANES):
        top = g * LANES
        lanes = slice(top, top + LANES)
        if top:
            out_ref[0:top, lanes] = jnp.zeros((top, LANES), jnp.float32)
        out_ref[top:rows, lanes] = pack_ref[offset : offset + rows - top, :]
        offset += rows - top


def basis_kernel(inverse_ref, y_ref, q_ref, token_ref):
    channels = y_ref.shape[0]
    image = y_ref[...]
    token_ref[...] = jnp.zeros_like(token_ref)
    for start, size in strips(channels, 2 * LANES):
        used = min(channels, start + size)
        high, low = split2(inverse_ref[start : start + size, 0:used])
        both = dot(jnp.concatenate([high, low], axis=0), image[0:used, :], ((1,), (0,)))
        q_ref[start : start + size, :] = (both[0:size, :] + both[size:, :]).astype(q_ref.dtype)


def basis(inverse, y_t):
    channels, rows = y_t.shape
    return pl.pallas_call(
        basis_kernel,
        in_specs=[WHOLE] * 2,
        out_specs=[WHOLE] * 2,
        out_shape=[
            jax.ShapeDtypeStruct(y_t.shape, y_t.dtype),
            jax.ShapeDtypeStruct((8, LANES), jnp.float32),
        ],
        compiler_params=params(),
        cost_estimate=cost(10**5, 10**5),
    )(inverse, y_t)


def matrix_shape(channels):
    return jax.ShapeDtypeStruct((channels, 1, channels), jnp.float32)


def part_kernel(
    channels, scale, core_ref, mine_ref, inverse_ref, previous_ref, out_ref,
    pack_ref, lower_ref, before_ref,
):
    rows, wide = inverse_ref.shape
    half = mine_ref.shape[0]
    join(pack_ref, core_ref[0], mine_ref[...], jnp.zeros((half, LANES), jnp.float32))
    turned = dot3(full_matrix(pack_ref, channels), inverse_ref[...], ((1,), (1,)))
    unfold(previous_ref, lower_ref, channels, False)
    lower_matrix(lower_ref, before_ref)
    total = dot3(before_ref[:, 0:rows], turned, ((1,), (0,))) * scale
    out_ref[:, 0:rows] = total.astype(out_ref.dtype)
    if rows < wide:
        out_ref[:, rows:wide] = jnp.zeros((rows, wide - rows), out_ref.dtype)


def correlation_part(core, mine, inverse, previous, channels, total_rows):
    return pl.pallas_call(
        functools.partial(part_kernel, channels, 1.0 / total_rows),
        in_specs=[SCALARS] + [WHOLE] * 3,
        out_specs=WHOLE,
        out_shape=jax.ShapeDtypeStruct(inverse.shape, jnp.bfloat16),
        scratch_shapes=[
            pltpu.VMEM((full_rows(channels), LANES), jnp.float32),
            pltpu.VMEM((lower_rows(channels), LANES), jnp.float32),
            pltpu.VMEM(inverse.shape, jnp.float32),
        ],
        compiler_params=params(),
        cost_estimate=cost(10**5, 10**5),
    )(core, mine, inverse, previous)


def both_kernel(
    scale, core_ref, left_ref, right_ref, mine_ref, other_ref, out_ref, ray_ref,
    folded_ref, pack_ref, full_ref,
):
    channels = out_ref.shape[0]
    mine, other = mine_ref[...].astype(jnp.float32), other_ref[...].astype(jnp.float32)
    join(folded_ref, core_ref[0], mine, other)
    unfold(folded_ref, pack_ref, channels, True)
    symmetric_matrix(pack_ref, full_ref)
    ray_ref[:, 0, :] = full_ref[0:channels, 0:channels] * scale
    total = left_ref[...].astype(jnp.float32) + right_ref[...].astype(jnp.float32)
    out_ref[:, 0, :] = total[0:channels, 0:channels]


def both_parts(core, left, right, mine, other, channels, total_rows):
    return pl.pallas_call(
        functools.partial(both_kernel, 1.0 / total_rows),
        in_specs=[SCALARS] + [WHOLE] * 4,
        out_specs=[WHOLE] * 2,
        out_shape=[matrix_shape(channels)] * 2,
        scratch_shapes=[
            pltpu.VMEM((folded_rows(channels), LANES), jnp.float32),
            pltpu.VMEM((lower_rows(channels), LANES), jnp.float32),
            pltpu.VMEM((round_up(channels, PANEL), round_up(channels, LANES)), jnp.float32),
        ],
        compiler_params=params(),
        cost_estimate=cost(10**5, 10**5),
    )(core, left, right, mine, other)


def from_behind(value, axis, steps):
    count = lax.axis_size(axis)
    leading, last = (max(0, -steps), min(count, count - steps))
    return lax.ppermute(value, axis, [(source, source + steps) for source in range(leading, last)])


def other_core(value):
    return lax.ppermute(value, "rows", [(s, s ^ 1) for s in range(lax.axis_size("rows"))])


def chip_rounds():
    count = lax.axis_size("rows")
    bits = []
    while 2 << len(bits) < count:
        bits.append(2 << len(bits))
    return [
        [(s, s ^ (bits[n] if s % 2 == 0 else bits[-1 - n])) for s in range(count)]
        for n in range(len(bits))
    ]


def sum_chips(value, after):
    count = lax.axis_size("rows")
    if count == 8:
        both, first, second = [
            lax.ppermute(value, "rows", [(s, s ^ bits) for s in range(count)]) for bits in (6, 2, 4)
        ]
        return add_four(both, value, first, second, after)
    for pairs in chip_rounds():
        value = add_after(value, lax.ppermute(value, "rows", pairs), after)
    return value


def shards(x_block, h_diag, h_right, pattern):
    x_t = x_block[0].T
    channels, block_rows = x_t.shape
    masks = pattern[0].transpose(1, 0, 2)
    total_rows = lax.axis_size("rows") * block_rows
    core = (lax.axis_index("rows") % 2).astype(jnp.int32).reshape(1)
    later = from_behind(x_t, "rows", -1)
    carried = from_behind(tile_product(1, masks, x_t, h_right[0], x_t.dtype, 53, True), "rows", 1)
    first = tile_product(0, masks, x_t, h_diag[0], jnp.float32, 50, False)
    part = later_product(masks, later, h_right[0], first)
    y_t, g_mine, g_other = gram(core, part, carried)
    previous_y = from_behind(y_t, "sector", 1)
    rounds = chip_rounds()
    g_sum = g_mine + other_core(g_other)
    r_mine, r_other = ray(core, x_t, y_t, g_sum)
    r_sum = add_after(r_mine, other_core(r_other))
    g_sum = sum_chips(g_sum, r_sum)
    r_first = lax.ppermute(r_sum, "rows", rounds[0])
    work = first_stage(core, g_sum, other_core(g_sum), channels, total_rows)
    r_sum = add_after(r_sum, r_first, work)
    m_mine, m_other = cross(core, previous_y, y_t, r_sum, jnp.float32)
    inverse, pack = last_stages(work, channels, m_other)
    m_sum = add_after(m_mine, other_core(m_other), inverse)
    previous = from_behind(pack, "sector", 1)
    q_t, basis_token = basis(inverse, y_t)
    for pairs in rounds[:-1]:
        m_sum = add_after(m_sum, lax.ppermute(m_sum, "rows", pairs))
    m_sum = add_after(m_sum, lax.ppermute(m_sum, "rows", rounds[-1]), basis_token)
    part = correlation_part(core, m_sum, inverse, previous, channels, total_rows)
    for pairs in rounds[1:]:
        r_sum = add_after(r_sum, lax.ppermute(r_sum, "rows", pairs), flops=LAST_RAY_FLOPS)
    correlation, rayleigh = both_parts(
        core, part, other_core(part), r_sum, other_core(r_sum), channels, total_rows
    )
    return (q_t.T[None], rayleigh.transpose(1, 0, 2), correlation.transpose(1, 0, 2))


def solution(mesh):
    in_specs = (
        P("sector", "rows", None),
        P("sector", "rows", None),
        P("sector", "rows", None),
        P("sector", None, "rows", None),
    )
    out_specs = (P("sector", "rows", None), P("sector", None, None), P("sector", None, None))
    return jax.shard_map(shards, mesh=mesh, in_specs=in_specs, out_specs=out_specs, check_vma=False)
```

```python
import functools

import jax
import jax.numpy as jnp
from jax import lax
from jax.experimental import pallas as pl
from jax.experimental.pallas import tpu as pltpu
from jax.sharding import PartitionSpec as P

SUBBLOCK = 128
LANES = 128
PANEL = 16
EARLY_PANELS = 7
WHOLE = pl.BlockSpec(memory_space=pltpu.VMEM)
SCALARS = pl.BlockSpec(memory_space=pltpu.SMEM)
ANYWHERE = pl.BlockSpec(memory_space=pl.ANY)
MIB = 1024 * 1024
FIRST_STAGE_FLOPS = 5000 * 10**6
LAST_RAY_FLOPS = 3000 * 10**6
LAST_STAGES_FLOPS = 4000 * 10**6


def params(mib=48):
    return pltpu.CompilerParams(vmem_limit_bytes=mib * MIB)


def cost(flops, bytes_accessed):
    return pl.CostEstimate(flops=flops, bytes_accessed=bytes_accessed, transcendentals=0)


def round_up(value, step):
    return (value + step - 1) // step * step


def dot(left, right, dims, precision=None):
    return lax.dot_general(
        left, right, (dims, ((), ())), precision=precision, preferred_element_type=jnp.float32
    )


def block_mask(mask_ref, which, cols, dtype):
    blocks = mask_ref[:, which, :].astype(jnp.float32)
    col = lax.broadcasted_iota(jnp.int32, (blocks.shape[1], cols), 1)
    block = lax.broadcasted_iota(jnp.int32, (blocks.shape[1], cols), 0)
    wide = dot(blocks, jnp.where(col // SUBBLOCK == block, 1.0, 0.0), ((1,), (0,)))
    return [
        jnp.broadcast_to(wide[i : i + 1, :], (PANEL, cols)).astype(dtype)
        for i in range(blocks.shape[0])
    ]


def mask_rows(tile_ref, mask, start, size):
    for i in range(start // SUBBLOCK, (start + size) // SUBBLOCK):
        for row in range(i * SUBBLOCK, (i + 1) * SUBBLOCK, PANEL):
            tile_ref[row : row + PANEL, :] = tile_ref[row : row + PANEL, :] * mask[i]


def strips(rows, width):
    return [(start, min(width, rows - start)) for start in range(0, rows, width)]


def halves(rows):
    first = rows // 512 * 256
    return [(0, first), (first, rows - first)] if first else [(0, rows)]


def copies_of(source, target, sems):
    copies = []
    for n, (start, size) in enumerate(halves(target.shape[0])):
        here = (pl.ds(start, size), slice(None))
        copies.append(pltpu.make_async_copy(source.at[here], target.at[here], sems.at[n]))
    return copies


def product(x_ref, tile_ref, copies, in_turn, mask, sum_ref, out_ref):
    rows = tile_ref.shape[0]
    for n, (start, size) in enumerate(halves(rows)):
        copies[n].wait()
        if in_turn and n + 1 < len(copies):
            copies[n + 1].start()
        mask_rows(tile_ref, mask, start, size)
        last = n + 1 == len(copies)
        for col, cols in strips(rows, 2 * SUBBLOCK):
            here = (slice(None), slice(col, col + cols))
            term = dot(
                x_ref[:, start : start + size],
                tile_ref[start : start + size, col : col + cols],
                ((1,), (0,)),
            )
            if n > 0:
                term = sum_ref[here] + term
            if last:
                out_ref[here] = term.astype(out_ref.dtype)
            else:
                sum_ref[here] = term


def tile_kernel(which, in_turn, mask_ref, x_hbm, tile_hbm, out_ref, x_ref, tile_ref, sum_ref, x_sem, sems):
    rows = tile_ref.shape[0]
    copies = copies_of(tile_hbm, tile_ref, sems)
    copy_x = pltpu.make_async_copy(x_hbm, x_ref, x_sem)
    copy_x.start()
    for copy in copies[:1] if in_turn else copies:
        copy.start()
    mask = block_mask(mask_ref, which, rows, tile_ref.dtype)
    copy_x.wait()
    product(x_ref, tile_ref, copies, in_turn, mask, sum_ref, out_ref)


def tile_product(which, masks, x_t, tile, dtype, mib, in_turn):
    channels, rows = x_t.shape
    return pl.pallas_call(
        functools.partial(tile_kernel, which, in_turn),
        in_specs=[WHOLE, ANYWHERE, ANYWHERE],
        out_specs=WHOLE,
        out_shape=jax.ShapeDtypeStruct((channels, rows), dtype),
        scratch_shapes=[
            pltpu.VMEM((channels, rows), x_t.dtype),
            pltpu.VMEM((rows, rows), tile.dtype),
            pltpu.VMEM((channels, rows), jnp.float32),
            pltpu.SemaphoreType.DMA,
            pltpu.SemaphoreType.DMA((2,)),
        ],
        compiler_params=params(mib),
        cost_estimate=cost(2 * channels * rows * rows, 2 * rows * rows),
    )(masks, x_t, tile)


def later_kernel(mask_ref, later_ref, tile_hbm, first_ref, out_ref, tile_ref, sems):
    rows = tile_ref.shape[0]
    copies = copies_of(tile_hbm, tile_ref, sems)
    for copy in copies:
        copy.start()
    mask = block_mask(mask_ref, 1, rows, tile_ref.dtype)
    for n, (start, size) in enumerate(halves(rows)):
        copies[n].wait()
        mask_rows(tile_ref, mask, start, size)
        for row, count in strips(size, 2 * SUBBLOCK):
            here = (slice(None), slice(start + row, start + row + count))
            out_ref[here] = first_ref[here] + dot(
                later_ref[...], tile_ref[start + row : start + row + count, :], ((1,), (1,))
            )


def later_product(masks, later, tile, first):
    channels, rows = later.shape
    return pl.pallas_call(
        later_kernel,
        in_specs=[WHOLE, WHOLE, ANYWHERE, WHOLE],
        out_specs=WHOLE,
        out_shape=jax.ShapeDtypeStruct((channels, rows), jnp.float32),
        scratch_shapes=[
            pltpu.VMEM((rows, rows), tile.dtype),
            pltpu.SemaphoreType.DMA((2,)),
        ],
        compiler_params=params(),
        cost_estimate=cost(2 * channels * rows * rows, 2 * rows * rows),
    )(masks, later, tile, first)


def lower_rows(channels):
    rows = round_up(channels, PANEL)
    return sum(rows - g * LANES for g in range(round_up(channels, LANES) // LANES))


def full_rows(channels):
    rows, wide = round_up(channels, PANEL), round_up(channels, LANES)
    whole = channels // LANES
    rest = rows - whole * LANES
    return round_up(whole * rows + rest * (wide // LANES), 4 * PANEL)


def lower_products(left_ref, right_ref, out_ref):
    channels = left_ref.shape[0]
    rows = round_up(channels, PANEL)
    offset = 0
    for start, size in strips(channels, 2 * LANES):
        product = dot(left_ref[start:channels, :], right_ref[start : start + size, :], ((1,), (1,)))
        for skip in range(0, size, LANES):
            width = min(LANES, size - skip)
            top = start + skip
            tall = rows - top
            if width < LANES:
                out_ref[offset : offset + tall, :] = jnp.zeros((tall, LANES), jnp.float32)
            elif rows > channels:
                out_ref[offset + channels - top : offset + tall, :] = jnp.zeros(
                    (rows - channels, LANES), jnp.float32
                )
            out_ref[offset : offset + channels - top, 0:width] = product[skip:, skip : skip + width]
            offset += tall


def full_products(left_ref, right_ref, out_ref):
    channels = left_ref.shape[0]
    rows = round_up(channels, PANEL)
    whole = channels // LANES
    for g in range(whole):
        out_ref[g * rows : g * rows + channels, :] = dot(
            left_ref[...], right_ref[g * LANES : (g + 1) * LANES, :], ((1,), (1,))
        )
        if rows > channels:
            out_ref[g * rows + channels : (g + 1) * rows, :] = jnp.zeros(
                (rows - channels, LANES), jnp.float32
            )
    base = whole * rows
    if base < out_ref.shape[0]:
        out_ref[base:, :] = jnp.zeros((out_ref.shape[0] - base, LANES), jnp.float32)
    first, rest = whole * LANES, rows - whole * LANES
    for n, (start, size) in enumerate(strips(channels, LANES) if first < channels else []):
        place = base + n * rest
        out_ref[place : place + channels - first, 0:size] = dot(
            right_ref[first:channels, :], left_ref[start : start + size, :], ((1,), (1,))
        )


def full_matrix(pack_ref, channels):
    rows, wide = round_up(channels, PANEL), round_up(channels, LANES)
    whole = channels // LANES
    rest = rows - whole * LANES
    parts = [pack_ref[g * rows : (g + 1) * rows, :] for g in range(whole)]
    if rest:
        tail = jnp.concatenate(
            [
                pack_ref[whole * rows + g * rest : whole * rows + (g + 1) * rest, :]
                for g in range(wide // LANES)
            ],
            axis=1,
        )
        tail = jnp.concatenate([tail, jnp.zeros((LANES - rest, wide), tail.dtype)], axis=0)
        parts.append(tail.T[0:rows, :])
    return jnp.concatenate(parts, axis=1)


def folded_rows(channels):
    if channels < 2 * LANES:
        return lower_rows(channels)
    return lower_rows(channels) - LANES + PANEL


def corner(channels):
    return round_up(channels, PANEL)


def square_index():
    row = lax.broadcasted_iota(jnp.int32, (LANES, LANES), 0)
    return row, lax.broadcasted_iota(jnp.int32, (LANES, LANES), 1)


def fold(pack_ref, out_ref, channels, symmetric):
    if channels < 2 * LANES:
        out_ref[...] = pack_ref[...]
        return
    start = corner(channels)
    end = pack_ref.shape[0]
    row, lane = square_index()
    second = pack_ref[start : start + LANES, :]
    upper = second if symmetric else second.T
    out_ref[0:LANES, :] = jnp.where(row >= lane, pack_ref[0:LANES, :], upper)
    out_ref[LANES:start, :] = pack_ref[LANES:start, :]
    out_ref[start : end - LANES, :] = pack_ref[start + LANES : end, :]
    diagonal = jnp.sum(jnp.where(row == lane, second, 0.0), axis=0, keepdims=True)
    out_ref[end - LANES :, :] = jnp.broadcast_to(diagonal, (PANEL, LANES))


def unfold(folded_ref, pack_ref, channels, symmetric):
    if channels < 2 * LANES:
        pack_ref[...] = folded_ref[...]
        return
    start = corner(channels)
    end = pack_ref.shape[0]
    row, lane = square_index()
    both = folded_ref[0:LANES, :]
    turned = both.T
    first_upper, second_upper = (turned, both) if symmetric else (0.0, 0.0)
    pack_ref[0:LANES, :] = jnp.where(row >= lane, both, first_upper)
    pack_ref[LANES:start, :] = folded_ref[LANES:start, :]
    second = jnp.where(row > lane, turned, second_upper)
    diagonal = folded_ref[end - LANES : end - LANES + 1, :]
    pack_ref[start : start + LANES, :] = jnp.where(row == lane, diagonal, second)
    pack_ref[start + LANES : end, :] = folded_ref[start : end - LANES, :]


def cut(pack_ref, core, mine_ref, other_ref):
    half = mine_ref.shape[0]
    mine_ref[...] = pack_ref[pl.ds(pl.multiple_of(core * half, 8), half), :].astype(mine_ref.dtype)
    other_ref[...] = pack_ref[pl.ds(pl.multiple_of((1 - core) * half, 8), half), :].astype(
        other_ref.dtype
    )


def join(pack_ref, core, mine, other):
    half = mine.shape[0]
    pack_ref[pl.ds(pl.multiple_of(core * half, 8), half), :] = mine
    pack_ref[pl.ds(pl.multiple_of((1 - core) * half, 8), half), :] = other


def gram_kernel(core_ref, part_ref, carried_ref, y_ref, g_mine, g_other, gram_ref, folded_ref):
    image = part_ref[...] + carried_ref[...].astype(jnp.float32)
    y_ref[...] = image.astype(y_ref.dtype)
    lower_products(y_ref, y_ref, gram_ref)
    fold(gram_ref, folded_ref, y_ref.shape[0], True)
    cut(folded_ref, core_ref[0], g_mine, g_other)


def gram(core, part, carried):
    channels, rows = carried.shape
    lower, folded = lower_rows(channels), folded_rows(channels)
    half = jax.ShapeDtypeStruct((folded // 2, LANES), jnp.float32)
    return pl.pallas_call(
        gram_kernel,
        in_specs=[SCALARS] + [WHOLE] * 2,
        out_specs=[WHOLE] * 3,
        out_shape=[jax.ShapeDtypeStruct((channels, rows), carried.dtype), half, half],
        scratch_shapes=[
            pltpu.VMEM((lower, LANES), jnp.float32),
            pltpu.VMEM((folded, LANES), jnp.float32),
        ],
        compiler_params=params(),
        cost_estimate=cost(2 * channels * channels * rows, 8 * channels * rows),
    )(core, part, carried)


def symmetric_matrix(pack_ref, out_ref):
    rows, wide = out_ref.shape
    offset = 0
    for top in range(0, wide, LANES):
        size = min(LANES, rows - top)
        column = pack_ref[offset : offset + rows - top, :]
        offset += rows - top
        out_ref[top:rows, top : top + LANES] = column
        for below in range(top + LANES, wide, LANES):
            count = min(LANES, rows - below)
            block = column[below - top : below - top + count, :]
            if count < LANES:
                block = jnp.concatenate(
                    [block, jnp.zeros((LANES - count, LANES), block.dtype)], axis=0
                )
            out_ref[top : top + size, below : below + LANES] = block.T


def ray_kernel(core_ref, x_ref, y_ref, after_ref, mine_ref, other_ref, pack_ref, folded_ref):
    lower_products(x_ref, y_ref, pack_ref)
    fold(pack_ref, folded_ref, x_ref.shape[0], True)
    cut(folded_ref, core_ref[0], mine_ref, other_ref)


def ray(core, x_t, y_t, after):
    channels, rows = x_t.shape
    lower, folded = lower_rows(channels), folded_rows(channels)
    return pl.pallas_call(
        ray_kernel,
        in_specs=[SCALARS, WHOLE, WHOLE, ANYWHERE],
        out_specs=[WHOLE] * 2,
        out_shape=[jax.ShapeDtypeStruct((folded // 2, LANES), jnp.bfloat16)] * 2,
        scratch_shapes=[
            pltpu.VMEM((lower, LANES), jnp.float32),
            pltpu.VMEM((folded, LANES), jnp.float32),
        ],
        compiler_params=params(),
        cost_estimate=cost(2 * channels * channels * rows, 4 * channels * rows),
    )(core, x_t, y_t, after)


def cross_kernel(core_ref, left_ref, right_ref, after_ref, mine_ref, other_ref, pack_ref):
    full_products(left_ref, right_ref, pack_ref)
    cut(pack_ref, core_ref[0], mine_ref, other_ref)


def cross(core, left, right, after, dtype):
    channels, rows = left.shape
    full = full_rows(channels)
    return pl.pallas_call(
        cross_kernel,
        in_specs=[SCALARS, WHOLE, WHOLE, ANYWHERE],
        out_specs=[WHOLE] * 2,
        out_shape=[jax.ShapeDtypeStruct((full // 2, LANES), dtype)] * 2,
        scratch_shapes=[pltpu.VMEM((full, LANES), jnp.float32)],
        compiler_params=params(),
        cost_estimate=cost(2 * channels * channels * rows, 4 * channels * rows),
    )(core, left, right, after)


def add_kernel(left_ref, right_ref, *refs):
    total = left_ref[...].astype(jnp.float32) + right_ref[...].astype(jnp.float32)
    refs[-1][...] = total.astype(refs[-1].dtype)


def add_four_kernel(both_ref, own_ref, first_ref, second_ref, after_ref, out_ref):
    both, own, first, second = (
        ref[...].astype(jnp.float32) for ref in (both_ref, own_ref, first_ref, second_ref)
    )
    out_ref[...] = ((own + first) + (second + both)).astype(out_ref.dtype)


def add_four(both, own, first, second, after):
    return pl.pallas_call(
        add_four_kernel,
        in_specs=[WHOLE] * 4 + [ANYWHERE],
        out_specs=WHOLE,
        out_shape=jax.ShapeDtypeStruct(own.shape, own.dtype),
        compiler_params=params(),
        cost_estimate=cost(10**5, 10**5),
    )(both, own, first, second, after)


def add_after(left, right, *after, flops=10**5):
    return pl.pallas_call(
        add_kernel,
        in_specs=[WHOLE] * 2 + [ANYWHERE] * len(after),
        out_specs=WHOLE,
        out_shape=jax.ShapeDtypeStruct(left.shape, left.dtype),
        compiler_params=params(),
        cost_estimate=cost(flops, 10**5),
    )(left, right, *after)


def split3(value):
    high = value.astype(jnp.bfloat16)
    rest = value - high.astype(jnp.float32)
    mid = rest.astype(jnp.bfloat16)
    low = (rest - mid.astype(jnp.float32)).astype(jnp.bfloat16)
    return high, mid, low


def sublane(value, index):
    return jnp.broadcast_to(value[index : index + 1, :], value.shape)


def lane_of(value, index):
    return jnp.take_along_axis(value, jnp.broadcast_to(index, value.shape), axis=1)


def eliminate(columns, panel):
    half = 8
    row = lax.broadcasted_iota(jnp.int32, (half, LANES), 0)
    scales = [jnp.zeros((half, LANES), jnp.float32) for _ in range(2)]
    columns = [list(c) for c in columns]
    panel = [list(p) for p in panel]
    for j in range(0, PANEL, 2):
        h, r = divmod(j, half)
        left, right = columns[j], columns[j + 1]
        a, b, c = sublane(left[h], r), sublane(left[h], r + 1), sublane(right[h], r + 1)
        det = a * c - b * b
        inverse = pl.reciprocal(det, approx=True)
        first, second = [None, None], [None, None]
        for t in range(h, 2):
            x, y = left[t], right[t]
            if t == h:
                x, y = jnp.where(row > r + 1, x, 0.0), jnp.where(row > r + 1, y, 0.0)
            first[t] = (c * x - b * y) * inverse
            second[t] = (a * y - b * x) * inverse
        for later in range(j + 2, PANEL):
            q = later // half
            x, y = sublane(left[q], later % half), sublane(right[q], later % half)
            for t in range(max(h, q), 2):
                columns[later][t] = columns[later][t] - (first[t] * x + second[t] * y)
        inverse_a = pl.reciprocal(a, approx=True)
        first[h] = jnp.where(row == r + 1, b * inverse_a, first[h])
        for group in panel:
            x, y = sublane(group[h], r), sublane(group[h], r + 1)
            for t in range(h, 2):
                group[t] = group[t] - (first[t] * x + second[t] * y)
        scales[h] = jnp.where(row == r, lax.rsqrt(a), scales[h])
        scales[h] = jnp.where(row == r + 1, lax.rsqrt(det * inverse_a), scales[h])
    return [jnp.concatenate([g[0] * scales[0], g[1] * scales[1]], axis=0) for g in panel]


def fill_work(channels, scale, pack_ref, work_ref):
    rows, wide = work_ref.shape
    groups = wide // LANES
    offset = 0
    for g in range(groups):
        top = g * LANES
        size = min(LANES, rows - top)
        column = pack_ref[offset : offset + rows - top, :] * scale
        offset += rows - top
        diag = column[0:size, :]
        if top + LANES > channels:
            row = lax.broadcasted_iota(jnp.int32, diag.shape, 0)
            lane = lax.broadcasted_iota(jnp.int32, diag.shape, 1)
            diag = jnp.where((row == lane) & (lane + top >= channels), 1.0, diag)
        work_ref[top : top + size, top : top + LANES] = diag
        for below in range(g + 1, groups):
            start = (below - g) * LANES
            size_b = min(LANES, rows - below * LANES)
            block = column[start : start + size_b, :]
            if size_b < LANES:
                block = jnp.concatenate(
                    [block, jnp.zeros((LANES - size_b, LANES), jnp.float32)], axis=0
                )
            work_ref[top : top + size, below * LANES : (below + 1) * LANES] = block.T
            work_ref[below * LANES : below * LANES + size_b, top : top + LANES] = jnp.zeros(
                (size_b, LANES), jnp.float32
            )


def eliminate_group(g, work_ref, turned_ref, first=0, last=LANES // PANEL):
    rows, wide = work_ref.shape
    groups = wide // LANES
    row = lax.broadcasted_iota(jnp.int32, (PANEL, LANES), 0)
    lane = lax.broadcasted_iota(jnp.int32, (PANEL, LANES), 1)
    top = g * LANES
    count = min(LANES, rows - top) // PANEL

    def load(local):
        place = pl.ds(pl.multiple_of(top + local, PANEL), PANEL)
        return [work_ref[place, q * LANES : (q + 1) * LANES] for q in range(groups)]

    def panel_step(b, parts, slot):
        local = b * PANEL
        following = jnp.minimum(local + PANEL, (count - 1) * PANEL)
        ahead = load(following)
        pivots = [parts[g][0:8, :], parts[g][8:16, :]]
        columns = [[lane_of(p, local + j) for p in pivots] for j in range(PANEL)]
        inside = (lane >= local) & (lane < local + PANEL)
        identity = jnp.where(lane - local == row, 1.0, 0.0)
        parts = list(parts)
        parts[g] = jnp.where(inside, identity, parts[g])
        done = eliminate(columns, [[p[0:8, :], p[8:16, :]] for p in parts])
        right = []
        for q in range(groups):
            high, mid, low = split3(done[q])
            right.append(jnp.concatenate([high, mid, high, low, mid, high], axis=0))
            if q >= g:
                if q == g:
                    high, mid, low = split3(jnp.where(lane >= local + PANEL, done[q], 0.0))
                left = jnp.concatenate([high, high, mid, high, mid, low], axis=0)
                turned_ref[slot, (q - g) * LANES : (q - g + 1) * LANES, :] = left.T
        right = jnp.concatenate(right, axis=1)
        near = turned_ref[slot, pl.ds(pl.multiple_of(following, PANEL), PANEL), :]
        update = dot(near, right, ((1,), (0,)))
        ahead[g] = jnp.where(inside, 0.0, ahead[g])
        ahead = [ahead[q] - update[:, q * LANES : (q + 1) * LANES] for q in range(groups)]
        for q in range(g, groups):
            low_row = q * LANES
            high_row = min(rows, low_row + LANES)
            base = low_row - top
            update = dot(turned_ref[slot, base : base + high_row - low_row, :], right, ((1,), (0,)))
            for c in range(groups):
                lanes = slice(c * LANES, (c + 1) * LANES)
                old = work_ref[low_row:high_row, lanes]
                if c == g:
                    here = lax.broadcasted_iota(jnp.int32, old.shape, 1)
                    old = jnp.where((here >= local) & (here < local + PANEL), 0.0, old)
                work_ref[low_row:high_row, lanes] = old - update[:, lanes]
        for q in range(groups):
            if q == g:
                done[q] = jnp.where(lane < local + PANEL, done[q], 0.0)
            elif q > g:
                done[q] = jnp.zeros_like(done[q])
            place = pl.ds(pl.multiple_of(top + local, PANEL), PANEL)
            work_ref[place, q * LANES : (q + 1) * LANES] = done[q]
        return ahead

    def two_panels(i, parts):
        return panel_step(first + 2 * i + 1, panel_step(first + 2 * i, parts, 0), 1)

    last = min(last, count)
    parts = lax.fori_loop(0, (last - first) // 2, two_panels, load(first * PANEL))
    if (last - first) % 2:
        panel_step(jnp.int32(last - 1), parts, 0)


def first_stage_kernel(
    channels, scale, core_ref, mine_ref, other_ref, work_ref, pack_ref, folded_ref, turned_ref
):
    join(folded_ref, core_ref[0], mine_ref[...], other_ref[...])
    unfold(folded_ref, pack_ref, channels, True)
    fill_work(channels, scale, pack_ref, work_ref)
    eliminate_group(0, work_ref, turned_ref)
    if work_ref.shape[1] > LANES:
        eliminate_group(1, work_ref, turned_ref, 0, EARLY_PANELS)


def last_stages_kernel(
    channels, before_ref, after_ref, work_ref, folded_ref, pack_ref, turned_ref
):
    work_ref[...] = before_ref[...]
    rows, wide = work_ref.shape
    for g in range(1 if EARLY_PANELS * PANEL < LANES else 2, wide // LANES):
        eliminate_group(g, work_ref, turned_ref, EARLY_PANELS if g == 1 else 0)
    offset = 0
    for q in range(wide // LANES):
        tall = rows - q * LANES
        pack_ref[offset : offset + tall, :] = work_ref[q * LANES : rows, q * LANES : (q + 1) * LANES]
        offset += tall
    fold(pack_ref, folded_ref, channels, False)


def turned_scratch(channels):
    return pltpu.VMEM((2, round_up(channels, LANES), 6 * PANEL), jnp.bfloat16)


def work_shape(channels):
    return jax.ShapeDtypeStruct((round_up(channels, PANEL), round_up(channels, LANES)), jnp.float32)


def first_stage(core, mine, other, channels, total_rows):
    return pl.pallas_call(
        functools.partial(first_stage_kernel, channels, 1.0 / total_rows),
        in_specs=[SCALARS] + [WHOLE] * 2,
        out_specs=WHOLE,
        out_shape=work_shape(channels),
        scratch_shapes=[
            pltpu.VMEM((lower_rows(channels), LANES), jnp.float32),
            pltpu.VMEM((folded_rows(channels), LANES), jnp.float32),
            turned_scratch(channels),
        ],
        compiler_params=params(),
        cost_estimate=cost(FIRST_STAGE_FLOPS, 10**6),
    )(core, mine, other)


def last_stages(work, channels, after):
    return pl.pallas_call(
        functools.partial(last_stages_kernel, channels),
        in_specs=[WHOLE, ANYWHERE],
        out_specs=[WHOLE] * 2,
        out_shape=[
            work_shape(channels),
            jax.ShapeDtypeStruct((folded_rows(channels), LANES), jnp.float32),
        ],
        scratch_shapes=[
            pltpu.VMEM((lower_rows(channels), LANES), jnp.float32),
            turned_scratch(channels),
        ],
        compiler_params=params(),
        cost_estimate=cost(LAST_STAGES_FLOPS, 10**5),
    )(work, after)


def split2(value):
    high = value.astype(jnp.bfloat16)
    return high, (value - high.astype(jnp.float32)).astype(jnp.bfloat16)


def dot3(left, right, dims):
    rows = left.shape[0]
    left_high, left_low = split2(left)
    right_high, right_low = split2(right)
    both = dot(jnp.concatenate([left_high, left_low], axis=0), right_high, dims)
    return both[0:rows, :] + both[rows:, :] + dot(left_high, right_low, dims)


def lower_matrix(pack_ref, out_ref):
    rows, wide = out_ref.shape
    offset = 0
    for g in range(wide // LANES):
        top = g * LANES
        lanes = slice(top, top + LANES)
        if top:
            out_ref[0:top, lanes] = jnp.zeros((top, LANES), jnp.float32)
        out_ref[top:rows, lanes] = pack_ref[offset : offset + rows - top, :]
        offset += rows - top


def basis_kernel(inverse_ref, y_ref, q_ref, token_ref):
    channels = y_ref.shape[0]
    image = y_ref[...]
    token_ref[...] = jnp.zeros_like(token_ref)
    for start, size in strips(channels, 2 * LANES):
        used = min(channels, start + size)
        high, low = split2(inverse_ref[start : start + size, 0:used])
        both = dot(jnp.concatenate([high, low], axis=0), image[0:used, :], ((1,), (0,)))
        q_ref[start : start + size, :] = (both[0:size, :] + both[size:, :]).astype(q_ref.dtype)


def basis(inverse, y_t):
    channels, rows = y_t.shape
    return pl.pallas_call(
        basis_kernel,
        in_specs=[WHOLE] * 2,
        out_specs=[WHOLE] * 2,
        out_shape=[
            jax.ShapeDtypeStruct(y_t.shape, y_t.dtype),
            jax.ShapeDtypeStruct((8, LANES), jnp.float32),
        ],
        compiler_params=params(),
        cost_estimate=cost(10**5, 10**5),
    )(inverse, y_t)


def matrix_shape(channels):
    return jax.ShapeDtypeStruct((channels, 1, channels), jnp.float32)


def part_kernel(
    channels, scale, core_ref, mine_ref, chip_ref, inverse_ref, previous_ref, after_ref, out_ref,
    pack_ref, lower_ref, before_ref,
):
    rows, wide = inverse_ref.shape
    half = mine_ref.shape[0]
    mine = mine_ref[...] + chip_ref[...]
    join(pack_ref, core_ref[0], mine, jnp.zeros((half, LANES), jnp.float32))
    turned = dot3(full_matrix(pack_ref, channels), inverse_ref[...], ((1,), (1,)))
    unfold(previous_ref, lower_ref, channels, False)
    lower_matrix(lower_ref, before_ref)
    total = dot3(before_ref[:, 0:rows], turned, ((1,), (0,))) * scale
    out_ref[:, 0:rows] = total.astype(out_ref.dtype)
    if rows < wide:
        out_ref[:, rows:wide] = jnp.zeros((rows, wide - rows), out_ref.dtype)


def correlation_part(core, mine, chip, inverse, previous, after, channels, total_rows):
    return pl.pallas_call(
        functools.partial(part_kernel, channels, 1.0 / total_rows),
        in_specs=[SCALARS] + [WHOLE] * 4 + [ANYWHERE],
        out_specs=WHOLE,
        out_shape=jax.ShapeDtypeStruct(inverse.shape, jnp.bfloat16),
        scratch_shapes=[
            pltpu.VMEM((full_rows(channels), LANES), jnp.float32),
            pltpu.VMEM((lower_rows(channels), LANES), jnp.float32),
            pltpu.VMEM(inverse.shape, jnp.float32),
        ],
        compiler_params=params(),
        cost_estimate=cost(10**5, 10**5),
    )(core, mine, chip, inverse, previous, after)


def both_kernel(
    scale, core_ref, left_ref, right_ref, mine_ref, other_ref, out_ref, ray_ref,
    folded_ref, pack_ref, full_ref,
):
    channels = out_ref.shape[0]
    mine, other = mine_ref[...].astype(jnp.float32), other_ref[...].astype(jnp.float32)
    join(folded_ref, core_ref[0], mine, other)
    unfold(folded_ref, pack_ref, channels, True)
    symmetric_matrix(pack_ref, full_ref)
    ray_ref[:, 0, :] = full_ref[0:channels, 0:channels] * scale
    total = left_ref[...].astype(jnp.float32) + right_ref[...].astype(jnp.float32)
    out_ref[:, 0, :] = total[0:channels, 0:channels]


def both_parts(core, left, right, mine, other, channels, total_rows):
    return pl.pallas_call(
        functools.partial(both_kernel, 1.0 / total_rows),
        in_specs=[SCALARS] + [WHOLE] * 4,
        out_specs=[WHOLE] * 2,
        out_shape=[matrix_shape(channels)] * 2,
        scratch_shapes=[
            pltpu.VMEM((folded_rows(channels), LANES), jnp.float32),
            pltpu.VMEM((lower_rows(channels), LANES), jnp.float32),
            pltpu.VMEM((round_up(channels, PANEL), round_up(channels, LANES)), jnp.float32),
        ],
        compiler_params=params(),
        cost_estimate=cost(10**5, 10**5),
    )(core, left, right, mine, other)


def from_behind(value, axis, steps):
    count = lax.axis_size(axis)
    leading, last = (max(0, -steps), min(count, count - steps))
    return lax.ppermute(value, axis, [(source, source + steps) for source in range(leading, last)])


def other_core(value):
    return lax.ppermute(value, "rows", [(s, s ^ 1) for s in range(lax.axis_size("rows"))])


def chip_rounds():
    count = lax.axis_size("rows")
    bits = []
    while 2 << len(bits) < count:
        bits.append(2 << len(bits))
    return [
        [(s, s ^ (bits[n] if s % 2 == 0 else bits[-1 - n])) for s in range(count)]
        for n in range(len(bits))
    ]


def sum_chips(value, after):
    count = lax.axis_size("rows")
    if count == 8:
        both, first, second = [
            lax.ppermute(value, "rows", [(s, s ^ bits) for s in range(count)]) for bits in (6, 2, 4)
        ]
        return add_four(both, value, first, second, after)
    for pairs in chip_rounds():
        value = add_after(value, lax.ppermute(value, "rows", pairs), after)
    return value


def shards(x_block, h_diag, h_right, pattern):
    x_t = x_block[0].T
    channels, block_rows = x_t.shape
    masks = pattern[0].transpose(1, 0, 2)
    total_rows = lax.axis_size("rows") * block_rows
    core = (lax.axis_index("rows") % 2).astype(jnp.int32).reshape(1)
    later = from_behind(x_t, "rows", -1)
    carried = from_behind(tile_product(1, masks, x_t, h_right[0], x_t.dtype, 53, True), "rows", 1)
    first = tile_product(0, masks, x_t, h_diag[0], jnp.float32, 50, False)
    part = later_product(masks, later, h_right[0], first)
    y_t, g_mine, g_other = gram(core, part, carried)
    previous_y = from_behind(y_t, "sector", 1)
    rounds = chip_rounds()
    g_sum = g_mine + other_core(g_other)
    r_mine, r_other = ray(core, x_t, y_t, g_sum)
    r_sum = add_after(r_mine, other_core(r_other))
    g_sum = sum_chips(g_sum, r_sum)
    r_first = lax.ppermute(r_sum, "rows", rounds[0])
    work = first_stage(core, g_sum, other_core(g_sum), channels, total_rows)
    r_sum = add_after(r_sum, r_first, work)
    m_mine, m_other = cross(core, previous_y, y_t, r_sum, jnp.float32)
    inverse, pack = last_stages(work, channels, m_other)
    m_sum = add_after(m_mine, other_core(m_other), inverse)
    previous = from_behind(pack, "sector", 1)
    q_t, basis_token = basis(inverse, y_t)
    for pairs in rounds[:-1]:
        m_sum = add_after(m_sum, lax.ppermute(m_sum, "rows", pairs))
    chip = lax.ppermute(m_sum, "rows", rounds[-1])
    part = correlation_part(
        core, m_sum, chip, inverse, previous, basis_token, channels, total_rows
    )
    for pairs in rounds[1:]:
        r_sum = add_after(r_sum, lax.ppermute(r_sum, "rows", pairs), flops=LAST_RAY_FLOPS)
    correlation, rayleigh = both_parts(
        core, part, other_core(part), r_sum, other_core(r_sum), channels, total_rows
    )
    return (q_t.T[None], rayleigh.transpose(1, 0, 2), correlation.transpose(1, 0, 2))


def solution(mesh):
    in_specs = (
        P("sector", "rows", None),
        P("sector", "rows", None),
        P("sector", "rows", None),
        P("sector", None, "rows", None),
    )
    out_specs = (P("sector", "rows", None), P("sector", None, None), P("sector", None, None))
    return jax.shard_map(shards, mesh=mesh, in_specs=in_specs, out_specs=out_specs, check_vma=False)
```
